32 devices in a mesh: groups: 2 (over x), tp: 8 (over z, y), attn: 2 (over core).
Axes of the slice: x: 2, y: 2, z: 4, core: 2. Of those that a mesh axis runs over, the one named last changes fastest.
Arguments:
- hidden_in: bfloat16 [256, 8192], P(('groups', 'tp', 'attn')), parts along dimension 0, may hold values from -6 to 6
- norm_gain: float32 [8192], replicated, may hold values from 0.1 to 1.9
- w_query: bfloat16 [8192, 8192], P(None, ('tp', 'attn')), may hold values from -0.0625 to 0.0625
- w_key: bfloat16 [8192, 1024], P(None, ('tp', 'attn')), may hold values from -0.0625 to 0.0625
- w_value: bfloat16 [8192, 1024], P(None, ('tp', 'attn')), may hold values from -0.0625 to 0.0625
- w_out: bfloat16 [8192, 8192], P(('tp', 'attn')), may hold values from -0.5 to 0.5
- key_pages: bfloat16 [32, 64, 32, 1024], P(('groups', 'tp', 'attn')), parts along dimension 0
- value_pages: bfloat16 [32, 64, 32, 1024], P(('groups', 'tp', 'attn')), parts along dimension 0, may hold values from -6 to 6
- page_table: int32 [32, 16, 4], P(('groups', 'tp', 'attn')), parts along dimension 0, may hold values from 0 to 63, as said below
- kv_owner: int32 [256], P('groups'), parts along dimension 0, may hold values from 0 to 15, as said below
- cached: int32 [256], P('groups'), parts along dimension 0, may hold values from 1 to 128, as said below
Outputs:
- hidden_out: bfloat16 [256, 8192], P(('groups', 'tp', 'attn')), parts along dimension 0
The draws below stay inside these ranges and needn't reach their ends.
There are 2 independent parts, one for each index of `groups`. The reference program is written for one: setup_inputs(seed, part) draws one part's arguments, and reference() takes and returns one part's arrays. A program takes and returns all parts, laid end to end along the dimension named above; an argument that names none is the same for every part. Nothing has to cross between parts.
Inputs may be any that keep to these rules, and one draw needn't show every extreme that they name: `kv_owner`: no device holds the caches of more than 16 requests, and some device holds exactly 16. Some request has exactly 128 cached tokens. `page_table`: the pages named in one device's table are all different.
All inputs are finite; a program needn't handle non-finite values.
Results may differ from the reference program's by a relative error of at most 0.0065.
The reference program's roundings to bfloat16 on the way count: a program that leaves them out, or rounds other values in their place, can miss the bound.
Values may be sent and summed in bfloat16 or wider, within the bound.
No kernel may reach another device: no remote copies, remote signals or barrier semaphores. Data moves between devices by JAX's collectives and lax.ppermute only.
A program may use at most 128 MiB of HBM per device.

```python
import jax
import jax.numpy as jnp
from jax import lax

D = 8192
HEADS = 64
KV_HEADS = 8
HEAD = 128
ROWS_DEV = 8
PAGE = 32
MAXP = 4
OWNERS = 16
REQUESTS = 128
CAP = 16
POOL = 64


def draw_kv_owner(key, part):
    key = jax.random.fold_in(key, 11)
    key_one, key_two, key_three = jax.random.split(key, 3)
    order = jax.random.permutation(key_one, OWNERS)
    spread = jax.random.randint(key_two, (OWNERS // 2,), 0, ROWS_DEV + 1)
    spread = spread.at[0].set(ROWS_DEV)
    counts = jnp.zeros((OWNERS,), jnp.int32)
    counts = counts.at[order[0::2]].set(ROWS_DEV + spread).at[order[1::2]].set(ROWS_DEV - spread)
    boundary = jnp.cumsum(counts)
    places = jnp.arange(REQUESTS, dtype=jnp.int32)
    sorted_owner = jnp.sum((boundary[None, :] <= places[:, None]).astype(jnp.int32), axis=1)
    shuffle = jax.random.permutation(key_three, REQUESTS)
    return sorted_owner[shuffle].astype(jnp.int32)


def draw_cached(key, part):
    key = jax.random.fold_in(key, 23)
    lengths = jax.random.randint(key, (REQUESTS,), 1, MAXP * PAGE + 1)
    return lengths.at[0].set(MAXP * PAGE).astype(jnp.int32)


def draw_page_table(key, part):
    key = jax.random.fold_in(key, 31)
    device_keys = jax.random.split(key, OWNERS)

    def one_table(device_key):
        return jax.random.permutation(device_key, POOL)
    tables = jax.vmap(one_table)(device_keys)
    return tables.reshape(OWNERS, CAP, MAXP).astype(jnp.int32)


def draw_key_pages(key, part):
    key = jax.random.fold_in(key, 37)
    key_one = jax.random.fold_in(key, 0)
    base = jax.random.normal(key_one, (OWNERS, POOL, PAGE, KV_HEADS * HEAD), jnp.float32)
    return base.astype(jnp.bfloat16)


def level_of(key, shape, pieces, low, high):
    def one(axis_at, shards_of):
        steps = jax.random.uniform(jax.random.fold_in(jax.random.fold_in(key, 6), axis_at), (shards_of,), jnp.float32, low / len(pieces), high / len(pieces))
        return jnp.repeat(jnp.exp(steps), shape[axis_at] // shards_of).reshape((-1,) + (1,) * (len(shape) - axis_at - 1))

    loudness = one(*pieces[0])
    for cut in pieces[1:]:
        loudness = loudness * one(*cut)
    return loudness


def centred(own_key, shape, scale, reach, pieces=(), held_as=jnp.bfloat16):
    drawn = scale * jax.random.normal(own_key, shape, jnp.float32)
    if pieces:
        drawn = drawn * level_of(own_key, shape, pieces, -0.22, 0.18)
    return jnp.clip(drawn, -reach, reach).astype(held_as)


def setup_inputs(seed: int = 0, part: int = 0) -> dict:
    keys = jax.random.split(jax.random.key(seed), 12)
    part_keys = jax.random.split(jax.random.fold_in(keys[11], part), 12)
    return {
        "hidden_in": centred(part_keys[0], (REQUESTS, D), 1.0, 6.0, ((0, 16),)),
        "norm_gain": jnp.clip(1.0 + 0.18 * jax.random.normal(keys[1], (D,), jnp.float32), 0.1, 1.9),
        "w_query": centred(keys[2], (D, HEADS * HEAD), D ** -0.5, 0.0625, ((1, 16),)),
        "w_key": centred(keys[3], (D, KV_HEADS * HEAD), D ** -0.5, 0.0625, ((1, 16),)),
        "w_value": centred(keys[4], (D, KV_HEADS * HEAD), D ** -0.5, 0.0625, ((1, 16),)),
        "w_out": centred(keys[5], (HEADS * HEAD, D), HEAD ** -0.5, 0.5, ((0, 16),)),
        "key_pages": draw_key_pages(jax.random.fold_in(jax.random.fold_in(keys[11], part), 71), part),
        "value_pages": centred(part_keys[7], (OWNERS, POOL, PAGE, KV_HEADS * HEAD), 1.0, 6.0, ((0, 16),)),
        "page_table": draw_page_table(jax.random.fold_in(jax.random.fold_in(keys[11], part), 71), part),
        "kv_owner": draw_kv_owner(jax.random.fold_in(jax.random.fold_in(keys[11], part), 71), part),
        "cached": draw_cached(jax.random.fold_in(jax.random.fold_in(keys[11], part), 71), part),
    }


epsilon = 1e-05
rope_base = 500000.0

def rotate(vectors, position):
    halfway = vectors.shape[-1] // 2
    offsets = jnp.arange(halfway, dtype=jnp.float32)
    frequency = rope_base ** (-(2.0 * offsets) / vectors.shape[-1])
    angles = position.astype(jnp.float32)[..., None] * frequency
    cosine_part = jnp.cos(angles)
    sine_part = jnp.sin(angles)
    lower = vectors[..., :halfway]
    upper = vectors[..., halfway:]
    return jnp.concatenate([lower * cosine_part - upper * sine_part, upper * cosine_part + lower * sine_part], axis=-1)

def reference(hidden_in, norm_gain, w_query, w_key, w_value, w_out, key_pages, value_pages, page_table, kv_owner, cached):
    inputs = hidden_in.astype(jnp.float32)
    factor = lax.rsqrt(lax.optimization_barrier(jnp.mean(inputs * inputs, axis=1, keepdims=True)) + epsilon)
    normed = (inputs * factor * norm_gain).astype(jnp.bfloat16)
    query_part = jnp.dot(normed, w_query, preferred_element_type=jnp.float32).astype(jnp.bfloat16)
    key_part = jnp.dot(normed, w_key, preferred_element_type=jnp.float32).astype(jnp.bfloat16)
    value_part = jnp.dot(normed, w_value, preferred_element_type=jnp.float32).astype(jnp.bfloat16)
    onehot = (kv_owner[:, None] == jnp.arange(OWNERS, dtype=jnp.int32)[None, :]).astype(jnp.int32)
    slot_index = lax.optimization_barrier(jnp.sum((jnp.cumsum(onehot, axis=0) - onehot) * onehot, axis=1)).astype(jnp.int32)
    query_rot = rotate(query_part.astype(jnp.float32).reshape(REQUESTS, HEADS, HEAD), cached[:, None]).astype(jnp.bfloat16)
    key_rot = rotate(key_part.astype(jnp.float32).reshape(REQUESTS, KV_HEADS, HEAD), cached[:, None]).astype(jnp.bfloat16)
    value_new = value_part.reshape(REQUESTS, KV_HEADS, HEAD)
    group_size = HEADS // KV_HEADS
    positions = jnp.arange(MAXP * PAGE, dtype=jnp.int32)
    score_scale = HEAD ** (-0.5)

    def attend(request_item):
        query_row, key_row, value_row, owner_row, slot_row, length = request_item
        page_rows = page_table[owner_row, slot_row]
        key_rows = jnp.take(key_pages[owner_row], page_rows, axis=0).reshape(MAXP * PAGE, KV_HEADS, HEAD)
        value_rows = jnp.take(value_pages[owner_row], page_rows, axis=0).reshape(MAXP * PAGE, KV_HEADS, HEAD)
        grouped = query_row.astype(jnp.float32).reshape(KV_HEADS, group_size, HEAD)
        scores = jnp.einsum('gjd,lgd->gjl', grouped, key_rows.astype(jnp.float32)) * score_scale
        own_score = jnp.einsum('gjd,gd->gj', grouped, key_row.astype(jnp.float32)) * score_scale
        valid_mask = positions < length
        masked = jnp.where(valid_mask[None, None, :], scores, -1e+30)
        row_max = jnp.maximum(lax.optimization_barrier(jnp.max(masked, axis=2)), own_score)
        exp_terms = jnp.where(valid_mask[None, None, :], jnp.exp(masked - row_max[..., None]), 0.0)
        own_exp = jnp.exp(own_score - row_max)
        denominator = lax.optimization_barrier(jnp.sum(exp_terms, axis=2)) + own_exp
        weights = (exp_terms / denominator[..., None]).astype(jnp.bfloat16)
        own_weight = (own_exp / denominator).astype(jnp.bfloat16)
        mixed_heads = jnp.einsum('gjl,lgd->gjd', weights.astype(jnp.float32), value_rows.astype(jnp.float32))
        mixed_heads = mixed_heads + own_weight.astype(jnp.float32)[..., None] * value_row.astype(jnp.float32)[:, None, :]
        return mixed_heads.reshape(HEADS * HEAD).astype(jnp.bfloat16)
    attended = lax.map(attend, (query_rot, key_rot, value_new, kv_owner, slot_index, cached))
    branch = jnp.dot(attended, w_out, preferred_element_type=jnp.float32)
    return (inputs + branch).astype(jnp.bfloat16)
```

```python
import jax
import jax.numpy as jnp
from jax import lax
from jax.sharding import PartitionSpec as P

HEAD = 128
AXES = ("tp", "attn")

epsilon = 1e-05
rope_base = 500000.0


def rotate(vectors, position):
    halfway = vectors.shape[-1] // 2
    offsets = jnp.arange(halfway, dtype=jnp.float32)
    frequency = rope_base ** (-(2.0 * offsets) / vectors.shape[-1])
    angles = position.astype(jnp.float32)[..., None] * frequency
    cosine_part = jnp.cos(angles)
    sine_part = jnp.sin(angles)
    lower = vectors[..., :halfway]
    upper = vectors[..., halfway:]
    return jnp.concatenate(
        [lower * cosine_part - upper * sine_part, upper * cosine_part + lower * sine_part], axis=-1
    )


class Grid:
    def __init__(self):
        tp = lax.axis_size("tp")
        self.core = lax.axis_size("attn")
        self.near = 2 if tp % 2 == 0 else 1
        self.far = tp // self.near
        self.size = tp * self.core

    def index(self, far, near, core):
        return (far * self.near + near) * self.core + core

    def perm(self, far=0, near=0, core=0):
        pairs = []
        for f in range(self.far):
            for n in range(self.near):
                for c in range(self.core):
                    to = self.index(
                        (f + far) % self.far, (n + near) % self.near, (c + core) % self.core
                    )
                    pairs.append((self.index(f, n, c), to))
        return pairs

    def send(self, x, far=0, near=0, core=0):
        return lax.ppermute(x, AXES, self.perm(far, near, core))

    def blocks(self, sign):
        me = lax.axis_index(AXES)
        c = me % self.core
        n = (me // self.core) % self.near
        f = me // (self.core * self.near)
        places = []
        for dc in range(self.core):
            for dn in range(self.near):
                for df in range(self.far):
                    places.append(
                        self.index(
                            (f + sign * df) % self.far,
                            (n + sign * dn) % self.near,
                            (c + sign * dc) % self.core,
                        )
                    )
        return jnp.stack(places)


def gather_rows(grid, x):
    parts = [x] + [grid.send(x, far=d) for d in range(1, grid.far)]
    x = jnp.concatenate(parts, axis=0)
    x = jnp.concatenate([x] + [grid.send(x, near=d) for d in range(1, grid.near)], axis=0)
    return jnp.concatenate([x] + [grid.send(x, core=d) for d in range(1, grid.core)], axis=0)


def scatter_sum(grid, x):
    for axis, count in (("core", grid.core), ("near", grid.near), ("far", grid.far)):
        rows = x.shape[0] // count
        got = [
            grid.send(x[d * rows : (d + 1) * rows].astype(jnp.bfloat16), **{axis: d})
            for d in range(1, count)
        ]
        x = x[:rows]
        for part in got:
            x = x + part.astype(jnp.float32)
    return x


def on_device(
    hidden_in,
    norm_gain,
    w_query,
    w_key,
    w_value,
    w_out,
    key_pages,
    value_pages,
    page_table,
    kv_owner,
    cached,
):
    grid = Grid()
    owners = grid.size
    slot_count = page_table.shape[1]
    page_count = page_table.shape[2]
    per_query = w_query.shape[1]
    per_key = w_key.shape[1]
    row_width = per_query + 2 * per_key
    heads_dev = per_query // HEAD
    kv_heads = per_key * owners // HEAD
    all_heads = heads_dev * owners
    group_size = all_heads // kv_heads
    page_size = key_pages.shape[2]
    span = page_count * page_size
    score_scale = HEAD ** (-0.5)
    requests = kv_owner.shape[0]
    rows_dev = requests // owners
    width = hidden_in.shape[1]

    onehot = (kv_owner[:, None] == jnp.arange(owners, dtype=jnp.int32)[None, :]).astype(jnp.int32)
    slot_index = jnp.sum((jnp.cumsum(onehot, axis=0) - onehot) * onehot, axis=1)
    place = kv_owner * slot_count + slot_index

    def reordered(blocks):
        pick = blocks[:, None] == jnp.arange(owners, dtype=jnp.int32)[None, :]
        moved = jnp.where(pick[:, :, None], place.reshape(1, owners, rows_dev), 0)
        return jnp.sum(moved, axis=1).reshape(requests)

    slots = jnp.arange(owners * slot_count, dtype=jnp.int32)
    place_in = reordered(grid.blocks(-1))
    place_out = reordered(grid.blocks(1))
    route_in = (slots[:, None] == place_in[None, :]).astype(jnp.bfloat16)
    route_out = (place_out[:, None] == slots[None, :]).astype(jnp.bfloat16)

    inputs = hidden_in.astype(jnp.float32)
    factor = lax.rsqrt(jnp.mean(inputs * inputs, axis=1, keepdims=True) + epsilon)
    normed = (inputs * factor * norm_gain).astype(jnp.bfloat16)

    w_all = jnp.concatenate([w_query, w_key, w_value], axis=1)
    chunks = 2
    step = width // chunks
    projected = 0.0
    for i in range(chunks):
        part = gather_rows(grid, normed[:, i * step : (i + 1) * step])
        projected = projected + jnp.dot(
            part, w_all[i * step : (i + 1) * step], preferred_element_type=jnp.float32
        )
    projected = projected.astype(jnp.bfloat16)
    outbound = jnp.dot(route_in, projected, preferred_element_type=jnp.float32)
    outbound = outbound.astype(jnp.bfloat16).reshape(owners, slot_count, row_width)
    inbound = lax.all_to_all(outbound, AXES, split_axis=0, concat_axis=0, tiled=True)
    device_id = lax.axis_index(AXES)
    mine_mask = (
        (kv_owner == device_id)[:, None]
        & (slot_index[:, None] == jnp.arange(slot_count, dtype=jnp.int32)[None, :])
    ).astype(jnp.int32)
    lengths = jnp.sum(mine_mask * cached[:, None], axis=0)
    query_in = inbound[:, :, :per_query].reshape(owners, slot_count, heads_dev, HEAD)
    query_in = query_in.transpose(0, 2, 1, 3).reshape(all_heads, slot_count, HEAD)
    key_in = (
        inbound[:, :, per_query : per_query + per_key]
        .transpose(1, 0, 2)
        .reshape(slot_count, kv_heads, HEAD)
    )
    value_in = (
        inbound[:, :, per_query + per_key :].transpose(1, 0, 2).reshape(slot_count, kv_heads, HEAD)
    )
    query_rot = rotate(query_in.astype(jnp.float32), lengths[None, :]).astype(jnp.bfloat16)
    key_rot = rotate(key_in.astype(jnp.float32), lengths[:, None]).astype(jnp.bfloat16)
    grouped = query_rot.reshape(kv_heads, group_size, slot_count, HEAD)
    key_rows = jnp.take(key_pages[0], page_table[0], axis=0).reshape(
        slot_count, span, kv_heads, HEAD
    )
    value_rows = jnp.take(value_pages[0], page_table[0], axis=0).reshape(
        slot_count, span, kv_heads, HEAD
    )
    scores = (
        jnp.einsum("gjsd,slgd->gjsl", grouped, key_rows, preferred_element_type=jnp.float32)
        * score_scale
    )
    own_score = (
        jnp.einsum("gjsd,sgd->gjs", grouped, key_rot, preferred_element_type=jnp.float32)
        * score_scale
    )
    positions = jnp.arange(span, dtype=jnp.int32)
    valid_mask = positions[None, :] < lengths[:, None]
    masked = jnp.where(valid_mask[None, None], scores, -1e30)
    row_max = jnp.maximum(jnp.max(masked, axis=3), own_score)
    exp_terms = jnp.where(valid_mask[None, None], jnp.exp(masked - row_max[..., None]), 0.0)
    own_exp = jnp.exp(own_score - row_max)
    denominator = jnp.sum(exp_terms, axis=3) + own_exp
    weights = (exp_terms / denominator[..., None]).astype(jnp.bfloat16)
    own_weight = (own_exp / denominator).astype(jnp.bfloat16)
    mixed_heads = jnp.einsum(
        "gjsl,slgd->gjsd", weights, value_rows, preferred_element_type=jnp.float32
    )
    mixed_heads = (
        mixed_heads
        + own_weight.astype(jnp.float32)[..., None]
        * value_in.transpose(1, 0, 2).astype(jnp.float32)[:, None]
    )
    attended = mixed_heads.astype(jnp.bfloat16).reshape(owners, heads_dev, slot_count, HEAD)
    attended = attended.transpose(0, 2, 1, 3).reshape(owners, slot_count, per_query)
    returned = lax.all_to_all(attended, AXES, split_axis=0, concat_axis=0, tiled=True)
    returned = returned.reshape(owners * slot_count, per_query)
    head_rows = jnp.dot(route_out, returned, preferred_element_type=jnp.float32)
    head_rows = head_rows.astype(jnp.bfloat16)
    sums = []
    for i in range(chunks):
        partial = jnp.dot(
            head_rows, w_out[:, i * step : (i + 1) * step], preferred_element_type=jnp.float32
        )
        sums.append(scatter_sum(grid, partial))
    summed = jnp.concatenate(sums, axis=1)
    return (inputs + summed).astype(jnp.bfloat16)


def solution(mesh):
    placed = (
        P(("groups", "tp", "attn"), None),
        P(),
        P(None, ("tp", "attn")),
        P(None, ("tp", "attn")),
        P(None, ("tp", "attn")),
        P(("tp", "attn"), None),
        P(("groups", "tp", "attn"), None, None, None),
        P(("groups", "tp", "attn"), None, None, None),
        P(("groups", "tp", "attn"), None, None),
        P("groups"),
        P("groups"),
    )
    return jax.shard_map(
        on_device,
        mesh=mesh,
        in_specs=placed,
        out_specs=P(("groups", "tp", "attn"), None),
        check_vma=False,
    )
```

```python
import functools

import jax
import jax.numpy as jnp
from jax import lax
from jax.experimental import pallas as pl
from jax.experimental.pallas import tpu as pltpu
from jax.sharding import PartitionSpec as P

HEAD = 128
AXES = ("tp", "attn")

epsilon = 1e-05
rope_base = 500000.0


class Grid:
    def __init__(self):
        tp = lax.axis_size("tp")
        self.core = lax.axis_size("attn")
        self.near = 2 if tp % 2 == 0 else 1
        self.far = tp // self.near
        self.size = tp * self.core

    def index(self, far, near, core):
        return (far * self.near + near) * self.core + core

    def perm(self, far=0, near=0, core=0):
        pairs = []
        for f in range(self.far):
            for n in range(self.near):
                for c in range(self.core):
                    to = self.index(
                        (f + far) % self.far, (n + near) % self.near, (c + core) % self.core
                    )
                    pairs.append((self.index(f, n, c), to))
        return pairs

    def send(self, x, far=0, near=0, core=0):
        return lax.ppermute(x, AXES, self.perm(far, near, core))

    def blocks(self, sign):
        me = lax.axis_index(AXES)
        c = me % self.core
        n = (me // self.core) % self.near
        f = me // (self.core * self.near)
        places = []
        for dc in range(self.core):
            for dn in range(self.near):
                for df in range(self.far):
                    places.append(
                        self.index(
                            (f + sign * df) % self.far,
                            (n + sign * dn) % self.near,
                            (c + sign * dc) % self.core,
                        )
                    )
        return jnp.stack(places)


def gather_rows(grid, x):
    parts = [x] + [grid.send(x, far=d) for d in range(1, grid.far)]
    x = jnp.concatenate(parts, axis=0)
    x = jnp.concatenate([x] + [grid.send(x, near=d) for d in range(1, grid.near)], axis=0)
    return x, grid.send(x, core=1)


def scatter_sum(grid, x):
    for axis, count in (("core", grid.core), ("near", grid.near), ("far", grid.far)):
        rows = x.shape[0] // count
        got = [
            grid.send(x[d * rows : (d + 1) * rows].astype(jnp.bfloat16), **{axis: d})
            for d in range(1, count)
        ]
        x = x[:rows]
        for part in got:
            x = x + part.astype(jnp.float32)
    return x


def project_kernel(first, last, xa, xb, wq, wk, wv, *refs):
    if not first:
        before, refs = refs[0], refs[1:]
    if last:
        place, refs = refs[0], refs[1:]
    out, total = refs
    step = pl.program_id(0)
    per_query = wq.shape[1]

    @pl.when(step == 0)
    def _():
        total[...] = jnp.zeros_like(total) if first else before[...]

    x = jnp.concatenate([xa[...], xb[...]], axis=0)
    pieces = [wk[...], wv[...]]
    spare = total.shape[1] - per_query - 2 * wk.shape[0]
    if spare:
        pieces.append(jnp.zeros((spare, wk.shape[1]), wk.dtype))
    kv = jnp.concatenate(pieces, axis=0)
    total[:, :per_query] += jnp.dot(x, wq[...], preferred_element_type=jnp.float32)
    total[:, per_query:] += lax.dot_general(
        x, kv, (((1,), (1,)), ((), ())), preferred_element_type=jnp.float32
    )

    @pl.when(step == pl.num_programs(0) - 1)
    def _():
        if last:
            rows = lax.broadcasted_iota(jnp.int32, (out.shape[0], place.shape[1]), 0)
            route = jnp.where(rows == place[...], 1.0, 0.0).astype(jnp.bfloat16)
            moved = jnp.dot(
                route, total[...].astype(jnp.bfloat16), preferred_element_type=jnp.float32
            )
            out[...] = moved.astype(jnp.bfloat16)
        else:
            out[...] = total[...]


def project(chunk, chunks, halves, w_query, w_key_t, w_value_t, before, place, slots, row_width):
    xa, xb = halves
    width = xa.shape[1]
    block = min(1024, width)
    steps = width // block
    start = chunk * steps
    rows = xa.shape[0] + xb.shape[0]
    first, last = chunk == 0, chunk == chunks - 1
    whole = lambda i: (0, 0)
    args = [xa, xb, w_query, w_key_t, w_value_t]
    specs = [
        pl.BlockSpec((xa.shape[0], block), lambda i: (0, i)),
        pl.BlockSpec((xb.shape[0], block), lambda i: (0, i)),
        pl.BlockSpec((block, w_query.shape[1]), lambda i: (start + i, 0)),
        pl.BlockSpec((w_key_t.shape[0], block), lambda i: (0, start + i)),
        pl.BlockSpec((w_value_t.shape[0], block), lambda i: (0, start + i)),
    ]
    if not first:
        args.append(before)
        specs.append(pl.BlockSpec(before.shape, whole))
    if last:
        args.append(place.reshape(1, rows))
        specs.append(pl.BlockSpec((1, rows), whole))
        out = jax.ShapeDtypeStruct((slots, row_width), jnp.bfloat16)
    else:
        out = jax.ShapeDtypeStruct((rows, row_width), jnp.float32)
    return pl.pallas_call(
        functools.partial(project_kernel, first, last),
        grid=(steps,),
        in_specs=specs,
        out_specs=pl.BlockSpec(out.shape, whole),
        out_shape=out,
        scratch_shapes=[pltpu.VMEM((rows, row_width), jnp.float32)],
        compiler_params=pltpu.CompilerParams(vmem_limit_bytes=24 * 2**20),
        cost_estimate=pl.CostEstimate(
            flops=2 * rows * width * row_width,
            bytes_accessed=2 * width * row_width,
            transcendentals=0,
        ),
        name="project",
    )(*args)


def attend_kernel(
    batch,
    per_query,
    per_key,
    table,
    lengths,
    inbound,
    cosine,
    sine,
    key_pages,
    value_pages,
    out,
    keys,
    values,
    query_rot,
    key_own,
    value_own,
    mixed,
    key_sems,
    value_sems,
):
    owners, slots, _ = inbound.shape
    pages = table.shape[1]
    page = key_pages.shape[1]
    kv_heads = key_pages.shape[2] // HEAD
    heads_dev = per_query // HEAD
    heads = owners * heads_dev
    group = heads // kv_heads
    span = pages * page
    pieces = owners // kv_heads

    def fetch(slot, carry):
        for j in range(pages):
            number = table[slot, j]
            rows = pl.ds(j * page, page)
            pltpu.make_async_copy(
                key_pages.at[number], keys.at[slot, rows], key_sems.at[slot]
            ).start()
            pltpu.make_async_copy(
                value_pages.at[number], values.at[slot, rows], value_sems.at[slot]
            ).start()
        return carry

    lax.fori_loop(0, slots, fetch, 0)

    cos = cosine[...]
    sin = sine[...]

    def turn(x):
        turned = x * cos + pltpu.roll(x, HEAD // 2, 1) * sin
        return turned.astype(jnp.bfloat16).astype(jnp.float32)

    for source in range(owners):
        for j in range(heads_dev):
            head = source * heads_dev + j
            x = inbound[source, :, j * HEAD : (j + 1) * HEAD].astype(jnp.float32)
            query_rot[head * slots : (head + 1) * slots, :] = turn(x)

    lane = lax.broadcasted_iota(jnp.int32, (slots, HEAD), 1) // per_key
    for g in range(kv_heads):
        key = jnp.zeros((slots, HEAD), jnp.float32)
        value = jnp.zeros((slots, HEAD), jnp.float32)
        for j in range(pieces):
            tile = inbound[g * pieces + j, :, per_query : per_query + HEAD].astype(jnp.float32)
            shift = j * per_key
            back = (shift - per_key) % HEAD
            key = jnp.where(lane == j, pltpu.roll(tile, shift, 1) if shift else tile, key)
            value = jnp.where(lane == j, pltpu.roll(tile, back, 1) if back else tile, value)
        key_own[g * slots : (g + 1) * slots, :] = turn(key)
        value_own[g * slots : (g + 1) * slots, :] = value

    scale = HEAD ** (-0.5)
    position = lax.broadcasted_iota(jnp.int32, (heads, span), 1)
    pair = 2 * group
    upper = lax.broadcasted_iota(jnp.int32, (pair, HEAD), 0) < group
    zero = jnp.zeros((pair, HEAD), jnp.bfloat16)

    def some(step, carry):
        places = [step * batch + b for b in range(batch)]
        scored = []
        for slot in places:
            pltpu.make_async_copy(keys.at[slot], keys.at[slot], key_sems.at[slot]).wait()
            rotated = query_rot[pl.ds(slot, heads, stride=slots), :]
            low = rotated.astype(jnp.bfloat16)
            parts = []
            for p in range(kv_heads // 2):
                mine = low[p * pair : (p + 1) * pair]
                wide = jnp.concatenate(
                    [jnp.where(upper, mine, zero), jnp.where(upper, zero, mine)], axis=1
                )
                parts.append(
                    lax.dot_general(
                        wide,
                        keys[slot, :, p * 2 * HEAD : (p + 1) * 2 * HEAD],
                        (((1,), (1,)), ((), ())),
                        preferred_element_type=jnp.float32,
                    )
                )
            own_key = key_own[pl.ds(slot, kv_heads, stride=slots), :]
            product = rotated.reshape(kv_heads, group, HEAD) * own_key[:, None, :]
            own = jnp.sum(product.reshape(heads, HEAD), axis=1, keepdims=True) * scale
            scored.append((jnp.concatenate(parts, axis=0) * scale, own))
        chances = []
        for slot, (scores, own) in zip(places, scored):
            valid = position < lengths[slot]
            masked = jnp.where(valid, scores, -1e30)
            top = jnp.maximum(jnp.max(masked, axis=1, keepdims=True), own)
            terms = jnp.where(valid, jnp.exp(masked - top), 0.0)
            own_term = jnp.exp(own - top)
            total = jnp.sum(terms, axis=1, keepdims=True) + own_term
            own_chance = (own_term / total).astype(jnp.bfloat16).astype(jnp.float32)
            chances.append(((terms / total).astype(jnp.bfloat16), own_chance))
        for slot, (chance, own_chance) in zip(places, chances):
            pltpu.make_async_copy(values.at[slot], values.at[slot], value_sems.at[slot]).wait()
            parts = []
            for p in range(kv_heads // 2):
                both = jnp.dot(
                    chance[p * pair : (p + 1) * pair],
                    values[slot, :, p * 2 * HEAD : (p + 1) * 2 * HEAD],
                    preferred_element_type=jnp.float32,
                )
                parts.append(both[:group, :HEAD])
                parts.append(both[group:, HEAD:])
            own_value = value_own[pl.ds(slot, kv_heads, stride=slots), :]
            own_value = jnp.broadcast_to(own_value[:, None, :], (kv_heads, group, HEAD))
            result = jnp.concatenate(parts, axis=0) + own_chance * own_value.reshape(heads, HEAD)
            mixed[pl.ds(slot, heads, stride=slots), :] = result
        return carry

    lax.fori_loop(0, slots // batch, some, 0)

    for target in range(owners):
        for j in range(heads_dev):
            head = target * heads_dev + j
            out[target, :, j * HEAD : (j + 1) * HEAD] = mixed[
                head * slots : (head + 1) * slots, :
            ].astype(jnp.bfloat16)


def attend(inbound, lengths, table, cosine, sine, key_pages, value_pages, per_query, per_key):
    owners, slots, _ = inbound.shape
    pages = table.shape[1]
    page, kv_width = key_pages.shape[1:]
    kv_heads = kv_width // HEAD
    heads = owners * (per_query // HEAD)
    held = (slots, pages * page, kv_width)
    smem = pl.BlockSpec(memory_space=pltpu.SMEM)
    vmem = pl.BlockSpec(memory_space=pltpu.VMEM)
    hbm = pl.BlockSpec(memory_space=pl.ANY)
    return pl.pallas_call(
        functools.partial(attend_kernel, 4, per_query, per_key),
        in_specs=[smem, smem, vmem, vmem, vmem, hbm, hbm],
        out_specs=vmem,
        out_shape=jax.ShapeDtypeStruct((owners, slots, per_query), jnp.bfloat16),
        scratch_shapes=[
            pltpu.VMEM(held, jnp.bfloat16),
            pltpu.VMEM(held, jnp.bfloat16),
            pltpu.VMEM((heads * slots, HEAD), jnp.float32),
            pltpu.VMEM((kv_heads * slots, HEAD), jnp.float32),
            pltpu.VMEM((kv_heads * slots, HEAD), jnp.float32),
            pltpu.VMEM((heads * slots, HEAD), jnp.float32),
            pltpu.SemaphoreType.DMA((slots,)),
            pltpu.SemaphoreType.DMA((slots,)),
        ],
        compiler_params=pltpu.CompilerParams(vmem_limit_bytes=24 * 2**20),
        cost_estimate=pl.CostEstimate(
            flops=8 * slots * heads * pages * page * HEAD,
            bytes_accessed=4 * slots * pages * page * kv_width,
            transcendentals=slots * heads * pages * page,
        ),
        name="attend",
    )(table, lengths, inbound, cosine, sine, key_pages, value_pages)


def on_device(
    hidden_in,
    norm_gain,
    w_query,
    w_key,
    w_value,
    w_out,
    key_pages,
    value_pages,
    page_table,
    kv_owner,
    cached,
):
    grid = Grid()
    owners = grid.size
    slot_count = page_table.shape[1]
    per_query = w_query.shape[1]
    per_key = w_key.shape[1]
    row_width = per_query + -(-2 * per_key // HEAD) * HEAD
    requests = kv_owner.shape[0]
    rows_dev = requests // owners
    width = hidden_in.shape[1]
    all_slots = owners * slot_count

    inputs = hidden_in.astype(jnp.float32)
    factor = lax.rsqrt(jnp.mean(inputs * inputs, axis=1, keepdims=True) + epsilon)
    normed = (inputs * factor * norm_gain).astype(jnp.bfloat16)

    order = jnp.arange(requests, dtype=jnp.int32)
    earlier = (kv_owner[:, None] == kv_owner[None, :]) & (order[None, :] < order[:, None])
    slot_index = jnp.sum(earlier.astype(jnp.int32), axis=1)
    place = kv_owner * slot_count + slot_index

    def reordered(blocks):
        pick = blocks[:, None] == jnp.arange(owners, dtype=jnp.int32)[None, :]
        moved = jnp.where(pick[:, :, None], place.reshape(1, owners, rows_dev), 0)
        return jnp.sum(moved, axis=1).reshape(requests)

    slots = jnp.arange(all_slots, dtype=jnp.int32)
    place_in = reordered(grid.blocks(-1))
    place_out = reordered(grid.blocks(1))
    route_out = (place_out[:, None] == slots[None, :]).astype(jnp.bfloat16)

    mine = lax.axis_index(AXES) * slot_count + jnp.arange(slot_count, dtype=jnp.int32)
    lengths = jnp.sum(jnp.where(place[:, None] == mine[None, :], cached[:, None], 0), axis=0)
    halfway = HEAD // 2
    offsets = jnp.arange(halfway, dtype=jnp.float32)
    frequency = rope_base ** (-(2.0 * offsets) / HEAD)
    angles = lengths.astype(jnp.float32)[:, None] * frequency
    cosine_part = jnp.cos(angles)
    sine_part = jnp.sin(angles)
    cosine = jnp.concatenate([cosine_part, cosine_part], axis=1)
    sine = jnp.concatenate([-sine_part, sine_part], axis=1)

    chunks = 2
    step = width // chunks
    total = None
    for i in range(chunks):
        halves = gather_rows(grid, normed[:, i * step : (i + 1) * step])
        total = project(
            i, chunks, halves, w_query, w_key.T, w_value.T, total, place_in, all_slots, row_width
        )
    outbound = total.reshape(owners, slot_count, row_width)
    inbound = lax.all_to_all(outbound, AXES, split_axis=0, concat_axis=0, tiled=True)
    attended = attend(
        inbound,
        lengths,
        page_table[0],
        cosine,
        sine,
        key_pages[0],
        value_pages[0],
        per_query,
        per_key,
    )
    returned = lax.all_to_all(attended, AXES, split_axis=0, concat_axis=0, tiled=True)
    returned = returned.reshape(all_slots, per_query)
    head_rows = jnp.dot(route_out, returned, preferred_element_type=jnp.float32)
    head_rows = head_rows.astype(jnp.bfloat16)
    sums = []
    for i in range(chunks):
        partial = jnp.dot(
            head_rows, w_out[:, i * step : (i + 1) * step], preferred_element_type=jnp.float32
        )
        sums.append(scatter_sum(grid, partial))
    summed = jnp.concatenate(sums, axis=1)
    return (inputs + summed).astype(jnp.bfloat16)


def solution(mesh):
    placed = (
        P(("groups", "tp", "attn"), None),
        P(),
        P(None, ("tp", "attn")),
        P(None, ("tp", "attn")),
        P(None, ("tp", "attn")),
        P(("tp", "attn"), None),
        P(("groups", "tp", "attn"), None, None, None),
        P(("groups", "tp", "attn"), None, None, None),
        P(("groups", "tp", "attn"), None, None),
        P("groups"),
        P("groups"),
    )
    return jax.shard_map(
        on_device,
        mesh=mesh,
        in_specs=placed,
        out_specs=P(("groups", "tp", "attn"), None),
        check_vma=False,
    )
```

```python
import functools

import jax
import jax.numpy as jnp
import numpy as np
from jax import lax
from jax.experimental import pallas as pl
from jax.experimental.pallas import tpu as pltpu
from jax.sharding import PartitionSpec as P

HEAD = 128
AXES = ("tp", "attn")

epsilon = 1e-05
rope_base = 500000.0


class Grid:
    def __init__(self):
        tp = lax.axis_size("tp")
        self.core = lax.axis_size("attn")
        self.near = 2 if tp % 2 == 0 else 1
        self.far = tp // self.near
        self.size = tp * self.core

    def index(self, far, near, core):
        return (far * self.near + near) * self.core + core

    def perm(self, far=0, near=0, core=0):
        pairs = []
        for f in range(self.far):
            for n in range(self.near):
                for c in range(self.core):
                    to = self.index(
                        (f + far) % self.far, (n + near) % self.near, (c + core) % self.core
                    )
                    pairs.append((self.index(f, n, c), to))
        return pairs

    def send(self, x, far=0, near=0, core=0):
        return lax.ppermute(x, AXES, self.perm(far, near, core))

    def blocks(self, sign):
        rows = []
        for f in range(self.far):
            for n in range(self.near):
                for c in range(self.core):
                    rows.append(
                        [
                            self.index(
                                (f + sign * df) % self.far,
                                (n + sign * dn) % self.near,
                                (c + sign * dc) % self.core,
                            )
                            for dc in range(self.core)
                            for dn in range(self.near)
                            for df in range(self.far)
                        ]
                    )
        return jnp.asarray(np.array(rows, np.int32))[lax.axis_index(AXES)]


def gather_rows(grid, x):
    parts = [x] + [grid.send(x, far=d) for d in range(1, grid.far)]
    x = jnp.concatenate(parts, axis=0)
    x = jnp.concatenate([x] + [grid.send(x, near=d) for d in range(1, grid.near)], axis=0)
    return x, grid.send(x, core=1)


def scatter_sum(grid, x):
    for axis, count in (("core", grid.core), ("near", grid.near), ("far", grid.far)):
        rows = x.shape[0] // count
        got = [
            grid.send(x[d * rows : (d + 1) * rows].astype(jnp.bfloat16), **{axis: d})
            for d in range(1, count)
        ]
        x = x[:rows]
        for part in got:
            x = x + part.astype(jnp.float32)
    return x


def project_kernel(first, last, xa, xb, wq, wk, wv, *refs):
    if not first:
        before, refs = refs[0], refs[1:]
    if last:
        place, refs = refs[0], refs[1:]
    out, total = refs
    step = pl.program_id(0)
    per_query = wq.shape[1]

    @pl.when(step == 0)
    def _():
        total[...] = jnp.zeros_like(total) if first else before[...]

    x = jnp.concatenate([xa[...], xb[...]], axis=0)
    pieces = [wk[...], wv[...]]
    spare = total.shape[1] - per_query - 2 * wk.shape[0]
    if spare:
        pieces.append(jnp.zeros((spare, wk.shape[1]), wk.dtype))
    kv = jnp.concatenate(pieces, axis=0)
    total[:, :per_query] += jnp.dot(x, wq[...], preferred_element_type=jnp.float32)
    total[:, per_query:] += lax.dot_general(
        x, kv, (((1,), (1,)), ((), ())), preferred_element_type=jnp.float32
    )

    @pl.when(step == pl.num_programs(0) - 1)
    def _():
        if last:
            rows = lax.broadcasted_iota(jnp.int32, (out.shape[0], place.shape[1]), 0)
            route = jnp.where(rows == place[...], 1.0, 0.0).astype(jnp.bfloat16)
            moved = jnp.dot(
                route, total[...].astype(jnp.bfloat16), preferred_element_type=jnp.float32
            )
            out[...] = moved.astype(jnp.bfloat16)
        else:
            out[...] = total[...]


def project(chunk, chunks, halves, w_query, w_key_t, w_value_t, before, place, slots, row_width):
    xa, xb = halves
    width = xa.shape[1]
    block = min(1024, width)
    steps = width // block
    start = chunk * steps
    rows = xa.shape[0] + xb.shape[0]
    first, last = chunk == 0, chunk == chunks - 1
    whole = lambda i: (0, 0)
    args = [xa, xb, w_query, w_key_t, w_value_t]
    specs = [
        pl.BlockSpec((xa.shape[0], block), lambda i: (0, i)),
        pl.BlockSpec((xb.shape[0], block), lambda i: (0, i)),
        pl.BlockSpec((block, w_query.shape[1]), lambda i: (start + i, 0)),
        pl.BlockSpec((w_key_t.shape[0], block), lambda i: (0, start + i)),
        pl.BlockSpec((w_value_t.shape[0], block), lambda i: (0, start + i)),
    ]
    if not first:
        args.append(before)
        specs.append(pl.BlockSpec(before.shape, whole))
    if last:
        args.append(place.reshape(1, rows))
        specs.append(pl.BlockSpec((1, rows), whole))
        out = jax.ShapeDtypeStruct((slots, row_width), jnp.bfloat16)
    else:
        out = jax.ShapeDtypeStruct((rows, row_width), jnp.float32)
    return pl.pallas_call(
        functools.partial(project_kernel, first, last),
        grid=(steps,),
        in_specs=specs,
        out_specs=pl.BlockSpec(out.shape, whole),
        out_shape=out,
        scratch_shapes=[pltpu.VMEM((rows, row_width), jnp.float32)],
        compiler_params=pltpu.CompilerParams(vmem_limit_bytes=56 * 2**20),
        cost_estimate=pl.CostEstimate(
            flops=2 * rows * width * row_width,
            bytes_accessed=2 * width * row_width,
            transcendentals=0,
        ),
        name="project",
    )(*args)


def attend_kernel(
    per_query,
    per_key,
    table,
    lengths,
    inbound,
    cosine,
    sine,
    key_pages,
    value_pages,
    out,
    keys,
    values,
    query_rot,
    value_own,
    chance,
    mixed,
    key_sems,
    value_sems,
):
    owners, slots, _ = inbound.shape
    pages = table.shape[1]
    page, kv_width = key_pages.shape[1:]
    kv_heads = kv_width // HEAD
    heads_dev = per_query // HEAD
    heads = owners * heads_dev
    pair = 2 * heads // kv_heads
    pairs = kv_heads // 2
    span = pages * page
    pieces = owners // kv_heads
    batches, held, _ = keys.shape
    batch = slots // batches

    def fetch(pool, place, sems):
        def one(slot, carry):
            for j in range(pages):
                pltpu.make_async_copy(
                    pool.at[table[slot, j]], place(slot, j * page), sems.at[slot // batch]
                ).start()
            return carry

        lax.fori_loop(0, slots, one, 0)

    def key_place(slot, row):
        return keys.at[slot // batch, pl.ds((slot % batch) * span + row, page)]

    def value_place(slot, row):
        return values.at[slot, pl.ds(row, page)]

    fetch(key_pages, key_place, key_sems)
    fetch(value_pages, value_place, value_sems)

    cos = cosine[...]
    sin = sine[...]

    def turn(x):
        return (x * cos + pltpu.roll(x, HEAD // 2, 1) * sin).astype(jnp.bfloat16)

    for source in range(owners):
        for j in range(heads_dev):
            x = inbound[source, :, j * HEAD : (j + 1) * HEAD].astype(jnp.float32)
            x = turn(x).astype(jnp.float32)
            head = source * heads_dev + j
            for b in range(batches):
                rows = pl.ds(head % pair * batch, batch)
                query_rot[head // pair, b, rows] = x[b * batch : (b + 1) * batch]

    piece = lax.broadcasted_iota(jnp.int32, (slots, HEAD), 1) // per_key
    for g in range(kv_heads):
        key = jnp.zeros((slots, HEAD), jnp.float32)
        value = jnp.zeros((slots, HEAD), jnp.float32)
        for j in range(pieces):
            tile = inbound[g * pieces + j, :, per_query : per_query + HEAD].astype(jnp.float32)
            shift = j * per_key
            back = (shift - per_key) % HEAD
            key = jnp.where(piece == j, pltpu.roll(tile, shift, 1) if shift else tile, key)
            value = jnp.where(piece == j, pltpu.roll(tile, back, 1) if back else tile, value)
        for b in range(batches):
            keys[b, batch * span :, g * HEAD : (g + 1) * HEAD] = turn(key)
        value_own[g] = value

    scale = HEAD ** (-0.5)
    columns = pair * batch
    row = lax.broadcasted_iota(jnp.int32, (span, columns), 0)
    place = lax.broadcasted_iota(jnp.int32, (span, columns), 1) % batch
    own_row = lax.broadcasted_iota(jnp.int32, (slots, columns), 0)
    own_place = lax.broadcasted_iota(jnp.int32, (slots, columns), 1) % batch
    first = lax.broadcasted_iota(jnp.int32, (HEAD, columns), 1) < columns // 2
    same = lax.broadcasted_iota(jnp.int32, (columns, columns), 0) == lax.broadcasted_iota(
        jnp.int32, (columns, columns), 1
    )

    own_chances = {}
    for b in range(batches):
        whole = keys.at[b, pl.ds(0, batch * span)]
        pltpu.make_async_copy(whole, whole, key_sems.at[b]).wait()
        valid = row < lengths[b]
        for p in range(pairs):
            turned = query_rot[p, b].T.astype(jnp.bfloat16)
            none = jnp.zeros_like(turned)
            wide = jnp.concatenate(
                [jnp.where(first, turned, none), jnp.where(first, none, turned)], axis=0
            )
            products = jnp.dot(
                keys[b, :, p * 2 * HEAD : (p + 1) * 2 * HEAD],
                wide,
                preferred_element_type=jnp.float32,
            )
            scores = products[:span]
            for s in range(1, batch):
                scores = jnp.where(place == s, products[s * span : (s + 1) * span], scores)
            own = jnp.where(own_row == own_place + b * batch, products[batch * span :], 0.0)
            own = jnp.sum(own, axis=0, keepdims=True) * scale
            masked = jnp.where(valid, scores * scale, -1e30)
            top = jnp.maximum(jnp.max(masked, axis=0, keepdims=True), own)
            terms = jnp.where(valid, jnp.exp(masked - top), 0.0)
            own_term = jnp.exp(own - top)
            total = jnp.sum(terms, axis=0, keepdims=True) + own_term
            chance[p, b] = (terms / total).T.astype(jnp.bfloat16).astype(jnp.float32)
            own_chance = (own_term / total).astype(jnp.bfloat16).astype(jnp.float32)
            own_chances[p, b] = jnp.sum(
                jnp.where(same, own_chance, 0.0), axis=1, keepdims=True
            )

    for b in range(batches):
        whole = values.at[pl.ds(b * batch, batch)]
        pltpu.make_async_copy(whole, whole, value_sems.at[b]).wait()
        for s in range(batch):
            for p in range(pairs):
                mine = chance[p, b, pl.ds(s, pair, stride=batch)].astype(jnp.bfloat16)
                both = jnp.dot(
                    mine,
                    values[b * batch + s, :, p * 2 * HEAD : (p + 1) * 2 * HEAD],
                    preferred_element_type=jnp.float32,
                )
                result = jnp.concatenate(
                    [both[: pair // 2, :HEAD], both[pair // 2 :, HEAD:]], axis=0
                )
                mixed[p, b, pl.ds(s, pair, stride=batch)] = result

    for p in range(pairs):
        for j in range(pair):
            head = p * pair + j
            g = head * kv_heads // heads
            halves = []
            for b in range(batches):
                rows = slice(j * batch, (j + 1) * batch)
                own_value = value_own[g, b * batch : (b + 1) * batch]
                halves.append(mixed[p, b, rows] + own_chances[p, b][rows] * own_value)
            column = head % heads_dev * HEAD
            out[head // heads_dev, :, column : column + HEAD] = jnp.concatenate(
                halves, axis=0
            ).astype(jnp.bfloat16)


def attend(inbound, lengths, table, cosine, sine, key_pages, value_pages, per_query, per_key):
    owners, slots, _ = inbound.shape
    pages = table.shape[1]
    page, kv_width = key_pages.shape[1:]
    kv_heads = kv_width // HEAD
    heads = owners * (per_query // HEAD)
    span = pages * page
    pair = 2 * heads // kv_heads
    pairs = kv_heads // 2
    batches = slots * pair // HEAD
    batch = slots // batches
    columns = pair * batch
    lengths = jnp.tile(lengths.reshape(batches, 1, batch), (1, 1, pair))
    smem = pl.BlockSpec(memory_space=pltpu.SMEM)
    vmem = pl.BlockSpec(memory_space=pltpu.VMEM)
    hbm = pl.BlockSpec(memory_space=pl.ANY)
    return pl.pallas_call(
        functools.partial(attend_kernel, per_query, per_key),
        in_specs=[smem, vmem, vmem, vmem, vmem, hbm, hbm],
        out_specs=vmem,
        out_shape=jax.ShapeDtypeStruct((owners, slots, per_query), jnp.bfloat16),
        scratch_shapes=[
            pltpu.VMEM((batches, batch * span + slots, kv_width), jnp.bfloat16),
            pltpu.VMEM((slots, span, kv_width), jnp.bfloat16),
            pltpu.VMEM((pairs, batches, columns, HEAD), jnp.float32),
            pltpu.VMEM((kv_heads, slots, HEAD), jnp.float32),
            pltpu.VMEM((pairs, batches, columns, span), jnp.float32),
            pltpu.VMEM((pairs, batches, columns, HEAD), jnp.float32),
            pltpu.SemaphoreType.DMA((batches,)),
            pltpu.SemaphoreType.DMA((batches,)),
        ],
        compiler_params=pltpu.CompilerParams(vmem_limit_bytes=56 * 2**20),
        cost_estimate=pl.CostEstimate(
            flops=8 * slots * heads * span * HEAD,
            bytes_accessed=4 * slots * span * kv_width,
            transcendentals=slots * heads * span,
        ),
        name="attend",
    )(table, lengths, inbound, cosine, sine, key_pages, value_pages)


def on_device(
    hidden_in,
    norm_gain,
    w_query,
    w_key,
    w_value,
    w_out,
    key_pages,
    value_pages,
    page_table,
    kv_owner,
    cached,
):
    grid = Grid()
    owners = grid.size
    slot_count = page_table.shape[1]
    per_query = w_query.shape[1]
    per_key = w_key.shape[1]
    row_width = per_query + -(-2 * per_key // HEAD) * HEAD
    requests = kv_owner.shape[0]
    rows_dev = requests // owners
    width = hidden_in.shape[1]
    all_slots = owners * slot_count

    inputs = hidden_in.astype(jnp.float32)
    factor = lax.rsqrt(jnp.mean(inputs * inputs, axis=1, keepdims=True) + epsilon)
    normed = (inputs * factor * norm_gain).astype(jnp.bfloat16)

    order = jnp.arange(requests, dtype=jnp.int32)
    earlier = (kv_owner[:, None] == kv_owner[None, :]) & (order[None, :] < order[:, None])
    slot_index = jnp.sum(earlier.astype(jnp.int32), axis=1)
    place = kv_owner * slot_count + slot_index

    def reordered(blocks):
        pick = blocks[:, None] == jnp.arange(owners, dtype=jnp.int32)[None, :]
        moved = jnp.where(pick[:, :, None], place.reshape(1, owners, rows_dev), 0)
        return jnp.sum(moved, axis=1).reshape(requests)

    slots = jnp.arange(all_slots, dtype=jnp.int32)
    place_in = reordered(grid.blocks(-1))
    place_out = reordered(grid.blocks(1))
    route_out = (place_out[:, None] == slots[None, :]).astype(jnp.bfloat16)

    mine = lax.axis_index(AXES) * slot_count + jnp.arange(slot_count, dtype=jnp.int32)
    lengths = jnp.sum(jnp.where(place[:, None] == mine[None, :], cached[:, None], 0), axis=0)
    halfway = HEAD // 2
    offsets = jnp.arange(halfway, dtype=jnp.float32)
    frequency = rope_base ** (-(2.0 * offsets) / HEAD)
    angles = lengths.astype(jnp.float32)[:, None] * frequency
    cosine_part = jnp.cos(angles)
    sine_part = jnp.sin(angles)
    cosine = jnp.concatenate([cosine_part, cosine_part], axis=1)
    sine = jnp.concatenate([-sine_part, sine_part], axis=1)

    chunks = 2
    step = width // chunks
    total = None
    for i in range(chunks):
        halves = gather_rows(grid, normed[:, i * step : (i + 1) * step])
        total = project(
            i, chunks, halves, w_query, w_key.T, w_value.T, total, place_in, all_slots, row_width
        )
    outbound = total.reshape(owners, slot_count, row_width)
    inbound = lax.all_to_all(outbound, AXES, split_axis=0, concat_axis=0, tiled=True)
    attended = attend(
        inbound,
        lengths,
        page_table[0],
        cosine,
        sine,
        key_pages[0],
        value_pages[0],
        per_query,
        per_key,
    )
    returned = lax.all_to_all(attended, AXES, split_axis=0, concat_axis=0, tiled=True)
    returned = returned.reshape(all_slots, per_query)
    head_rows = jnp.dot(route_out, returned, preferred_element_type=jnp.float32)
    head_rows = head_rows.astype(jnp.bfloat16)
    sums = []
    for i in range(chunks):
        partial = jnp.dot(
            head_rows, w_out[:, i * step : (i + 1) * step], preferred_element_type=jnp.float32
        )
        sums.append(scatter_sum(grid, partial))
    summed = jnp.concatenate(sums, axis=1)
    return (inputs + summed).astype(jnp.bfloat16)


def solution(mesh):
    placed = (
        P(("groups", "tp", "attn"), None),
        P(),
        P(None, ("tp", "attn")),
        P(None, ("tp", "attn")),
        P(None, ("tp", "attn")),
        P(("tp", "attn"), None),
        P(("groups", "tp", "attn"), None, None, None),
        P(("groups", "tp", "attn"), None, None, None),
        P(("groups", "tp", "attn"), None, None),
        P("groups"),
        P("groups"),
    )
    return jax.shard_map(
        on_device,
        mesh=mesh,
        in_specs=placed,
        out_specs=P(("groups", "tp", "attn"), None),
        check_vma=False,
    )
```

```python
import functools

import jax
import jax.numpy as jnp
import numpy as np
from jax import lax
from jax.experimental import pallas as pl
from jax.experimental.pallas import tpu as pltpu
from jax.sharding import PartitionSpec as P

HEAD = 128
AXES = ("tp", "attn")

epsilon = 1e-05
rope_base = 500000.0


class Grid:
    def __init__(self):
        tp = lax.axis_size("tp")
        self.core = lax.axis_size("attn")
        self.near = 2 if tp % 2 == 0 else 1
        self.far = tp // self.near
        self.size = tp * self.core

    def index(self, far, near, core):
        return (far * self.near + near) * self.core + core

    def perm(self, far=0, near=0, core=0):
        pairs = []
        for f in range(self.far):
            for n in range(self.near):
                for c in range(self.core):
                    to = self.index(
                        (f + far) % self.far, (n + near) % self.near, (c + core) % self.core
                    )
                    pairs.append((self.index(f, n, c), to))
        return pairs

    def send(self, x, far=0, near=0, core=0):
        return lax.ppermute(x, AXES, self.perm(far, near, core))

    def blocks(self, sign):
        rows = []
        for f in range(self.far):
            for n in range(self.near):
                for c in range(self.core):
                    rows.append(
                        [
                            self.index(
                                (f + sign * df) % self.far,
                                (n + sign * dn) % self.near,
                                (c + sign * dc) % self.core,
                            )
                            for dc in range(self.core)
                            for dn in range(self.near)
                            for df in range(self.far)
                        ]
                    )
        return jnp.asarray(np.array(rows, np.int32))[lax.axis_index(AXES)]


def after(x, *earlier):
    return lax.optimization_barrier((x, *earlier))[0]


def gather_rows(grid, x):
    line = jnp.concatenate([x] + [grid.send(x, far=d) for d in range(1, grid.far)], axis=0)
    beside = grid.send(line, near=1)
    return line, beside, grid.send(line, core=1), grid.send(beside, core=1)


def scatter_sum(grid, rows, w_out, chunks):
    step = w_out.shape[1] // chunks
    sums = []
    sent = got = None
    for i in range(chunks):
        if i:
            rows = after(rows, sent)
        x = jnp.dot(rows, w_out[:, i * step : (i + 1) * step], preferred_element_type=jnp.float32)
        half = x.shape[0] // 2
        x = x[:half] + grid.send(x[half:].astype(jnp.bfloat16), core=1).astype(jnp.float32)
        half = half // 2
        sent = x[half:].astype(jnp.bfloat16)
        if i:
            sent = after(sent, got)
        got = grid.send(sent, near=1)
        x = x[:half] + got.astype(jnp.float32)
        rows_dev = half // grid.far
        parts = [
            grid.send(x[d * rows_dev : (d + 1) * rows_dev].astype(jnp.bfloat16), far=d)
            for d in range(1, grid.far)
        ]
        x = x[:rows_dev]
        for part in parts:
            x = x + part.astype(jnp.float32)
        sums.append(x)
    return jnp.concatenate(sums, axis=1)


def project_kernel(first, last, count, *refs):
    parts, (wq, wk, wv), refs = refs[:count], refs[count : count + 3], refs[count + 3 :]
    if not first:
        before, refs = refs[0], refs[1:]
    if last:
        place, refs = refs[0], refs[1:]
    out, total = refs
    step = pl.program_id(0)
    per_query = wq.shape[1]

    @pl.when(step == 0)
    def _():
        total[...] = jnp.zeros_like(total) if first else before[...]

    x = jnp.concatenate([part[...] for part in parts], axis=0)
    pieces = [wk[...], wv[...]]
    spare = total.shape[1] - per_query - 2 * wk.shape[0]
    if spare:
        pieces.append(jnp.zeros((spare, wk.shape[1]), wk.dtype))
    kv = jnp.concatenate(pieces, axis=0)
    total[:, :per_query] += jnp.dot(x, wq[...], preferred_element_type=jnp.float32)
    total[:, per_query:] += lax.dot_general(
        x, kv, (((1,), (1,)), ((), ())), preferred_element_type=jnp.float32
    )

    @pl.when(step == pl.num_programs(0) - 1)
    def _():
        if last:
            rows = lax.broadcasted_iota(jnp.int32, (out.shape[0], place.shape[1]), 0)
            route = jnp.where(rows == place[...], 1.0, 0.0).astype(jnp.bfloat16)
            moved = jnp.dot(
                route, total[...].astype(jnp.bfloat16), preferred_element_type=jnp.float32
            )
            out[...] = moved.astype(jnp.bfloat16)
        else:
            out[...] = total[...]


def project(chunk, chunks, parts, w_query, w_key_t, w_value_t, before, place, slots, row_width):
    width = parts[0].shape[1]
    block = min(1024, width)
    steps = width // block
    start = chunk * steps
    rows = sum(part.shape[0] for part in parts)
    first, last = chunk == 0, chunk == chunks - 1
    whole = lambda i: (0, 0)
    args = [*parts, w_query, w_key_t, w_value_t]
    specs = [
        *[pl.BlockSpec((part.shape[0], block), lambda i: (0, i)) for part in parts],
        pl.BlockSpec((block, w_query.shape[1]), lambda i: (start + i, 0)),
        pl.BlockSpec((w_key_t.shape[0], block), lambda i: (0, start + i)),
        pl.BlockSpec((w_value_t.shape[0], block), lambda i: (0, start + i)),
    ]
    if not first:
        args.append(before)
        specs.append(pl.BlockSpec(before.shape, whole))
    if last:
        args.append(place.reshape(1, rows))
        specs.append(pl.BlockSpec((1, rows), whole))
        out = jax.ShapeDtypeStruct((slots, row_width), jnp.bfloat16)
    else:
        out = jax.ShapeDtypeStruct((rows, row_width), jnp.float32)
    return pl.pallas_call(
        functools.partial(project_kernel, first, last, len(parts)),
        grid=(steps,),
        in_specs=specs,
        out_specs=pl.BlockSpec(out.shape, whole),
        out_shape=out,
        scratch_shapes=[pltpu.VMEM((rows, row_width), jnp.float32)],
        compiler_params=pltpu.CompilerParams(vmem_limit_bytes=48 * 2**20),
        cost_estimate=pl.CostEstimate(
            flops=2 * rows * width * row_width,
            bytes_accessed=2 * width * row_width,
            transcendentals=0,
        ),
        name="project",
    )(*args)


def attend_kernel(
    per_query,
    per_key,
    table,
    lengths,
    inbound,
    cosine,
    sine,
    key_pages,
    value_pages,
    out,
    key_new,
    query_rot,
    value_own,
    chance,
    mixed,
):
    owners, slots, _ = inbound.shape
    pages = table.shape[1]
    page, kv_width = key_pages.shape[1:]
    kv_heads = kv_width // HEAD
    heads_dev = per_query // HEAD
    heads = owners * heads_dev
    pair = 2 * heads // kv_heads
    pairs = kv_heads // 2
    span = pages * page
    pieces = owners // kv_heads
    batches = query_rot.shape[1]
    batch = slots // batches

    def held(pool, slot, columns):
        return [pool[table[slot, j], :, columns] for j in range(pages)]

    cos = cosine[...]
    sin = sine[...]

    def turn(x):
        return (x * cos + pltpu.roll(x, HEAD // 2, 1) * sin).astype(jnp.bfloat16)

    for source in range(owners):
        for j in range(heads_dev):
            x = inbound[source, :, j * HEAD : (j + 1) * HEAD].astype(jnp.float32)
            x = turn(x).astype(jnp.float32)
            head = source * heads_dev + j
            for b in range(batches):
                rows = pl.ds(head % pair * batch, batch)
                query_rot[head // pair, b, rows] = x[b * batch : (b + 1) * batch]

    piece = lax.broadcasted_iota(jnp.int32, (slots, HEAD), 1) // per_key
    for g in range(kv_heads):
        key = jnp.zeros((slots, HEAD), jnp.float32)
        value = jnp.zeros((slots, HEAD), jnp.float32)
        for j in range(pieces):
            tile = inbound[g * pieces + j, :, per_query : per_query + HEAD].astype(jnp.float32)
            shift = j * per_key
            back = (shift - per_key) % HEAD
            key = jnp.where(piece == j, pltpu.roll(tile, shift, 1) if shift else tile, key)
            value = jnp.where(piece == j, pltpu.roll(tile, back, 1) if back else tile, value)
        key_new[:, g * HEAD : (g + 1) * HEAD] = turn(key)
        value_own[g] = value

    scale = HEAD ** (-0.5)
    columns = pair * batch
    row = lax.broadcasted_iota(jnp.int32, (span, columns), 0)
    place = lax.broadcasted_iota(jnp.int32, (span, columns), 1) % batch
    own_row = lax.broadcasted_iota(jnp.int32, (slots, columns), 0)
    own_place = lax.broadcasted_iota(jnp.int32, (slots, columns), 1) % batch
    first = lax.broadcasted_iota(jnp.int32, (HEAD, columns), 1) < columns // 2
    same = lax.broadcasted_iota(jnp.int32, (columns, columns), 0) == lax.broadcasted_iota(
        jnp.int32, (columns, columns), 1
    )

    own_chances = {}
    for b in range(batches):
        valid = row < lengths[b]
        for p in range(pairs):
            turned = query_rot[p, b].T.astype(jnp.bfloat16)
            none = jnp.zeros_like(turned)
            wide = jnp.concatenate(
                [jnp.where(first, turned, none), jnp.where(first, none, turned)], axis=0
            )
            columns_p = slice(p * 2 * HEAD, (p + 1) * 2 * HEAD)
            keys = []
            for s in range(batch):
                keys += held(key_pages, b * batch + s, columns_p)
            keys.append(key_new[:, columns_p])
            products = jnp.dot(
                jnp.concatenate(keys, axis=0), wide, preferred_element_type=jnp.float32
            )
            scores = products[:span]
            for s in range(1, batch):
                scores = jnp.where(place == s, products[s * span : (s + 1) * span], scores)
            own = jnp.where(own_row == own_place + b * batch, products[batch * span :], 0.0)
            own = jnp.sum(own, axis=0, keepdims=True) * scale
            masked = jnp.where(valid, scores * scale, -1e30)
            top = jnp.maximum(jnp.max(masked, axis=0, keepdims=True), own)
            terms = jnp.where(valid, jnp.exp(masked - top), 0.0)
            own_term = jnp.exp(own - top)
            total = jnp.sum(terms, axis=0, keepdims=True) + own_term
            chance[p, b] = (terms / total).T.astype(jnp.bfloat16).astype(jnp.float32)
            own_chance = (own_term / total).astype(jnp.bfloat16).astype(jnp.float32)
            own_chances[p, b] = jnp.sum(
                jnp.where(same, own_chance, 0.0), axis=1, keepdims=True
            )

    for b in range(batches):
        for s in range(batch):
            for p in range(pairs):
                mine = chance[p, b, pl.ds(s, pair, stride=batch)].astype(jnp.bfloat16)
                columns_p = slice(p * 2 * HEAD, (p + 1) * 2 * HEAD)
                values = held(value_pages, b * batch + s, columns_p)
                both = jnp.dot(
                    mine, jnp.concatenate(values, axis=0), preferred_element_type=jnp.float32
                )
                result = jnp.concatenate(
                    [both[: pair // 2, :HEAD], both[pair // 2 :, HEAD:]], axis=0
                )
                mixed[p, b, pl.ds(s, pair, stride=batch)] = result

    for p in range(pairs):
        for j in range(pair):
            head = p * pair + j
            g = head * kv_heads // heads
            halves = []
            for b in range(batches):
                rows = slice(j * batch, (j + 1) * batch)
                own_value = value_own[g, b * batch : (b + 1) * batch]
                halves.append(mixed[p, b, rows] + own_chances[p, b][rows] * own_value)
            column = head % heads_dev * HEAD
            out[head // heads_dev, :, column : column + HEAD] = jnp.concatenate(
                halves, axis=0
            ).astype(jnp.bfloat16)


def attend(inbound, lengths, table, cosine, sine, key_pages, value_pages, per_query, per_key):
    owners, slots, _ = inbound.shape
    pages = table.shape[1]
    page, kv_width = key_pages.shape[1:]
    kv_heads = kv_width // HEAD
    heads = owners * (per_query // HEAD)
    span = pages * page
    pair = 2 * heads // kv_heads
    pairs = kv_heads // 2
    batches = slots * pair // HEAD
    batch = slots // batches
    columns = pair * batch
    lengths = jnp.tile(lengths.reshape(batches, 1, batch), (1, 1, pair))
    smem = pl.BlockSpec(memory_space=pltpu.SMEM)
    vmem = pl.BlockSpec(memory_space=pltpu.VMEM)
    return pl.pallas_call(
        functools.partial(attend_kernel, per_query, per_key),
        in_specs=[smem, vmem, vmem, vmem, vmem, vmem, vmem],
        out_specs=vmem,
        out_shape=jax.ShapeDtypeStruct((owners, slots, per_query), jnp.bfloat16),
        scratch_shapes=[
            pltpu.VMEM((slots, kv_width), jnp.bfloat16),
            pltpu.VMEM((pairs, batches, columns, HEAD), jnp.float32),
            pltpu.VMEM((kv_heads, slots, HEAD), jnp.float32),
            pltpu.VMEM((pairs, batches, columns, span), jnp.float32),
            pltpu.VMEM((pairs, batches, columns, HEAD), jnp.float32),
        ],
        compiler_params=pltpu.CompilerParams(vmem_limit_bytes=44 * 2**20),
        cost_estimate=pl.CostEstimate(
            flops=8 * slots * heads * span * HEAD,
            bytes_accessed=4 * slots * span * kv_width,
            transcendentals=slots * heads * span,
        ),
        name="attend",
    )(table, lengths, inbound, cosine, sine, key_pages, value_pages)


def on_device(
    hidden_in,
    norm_gain,
    w_query,
    w_key,
    w_value,
    w_out,
    key_pages,
    value_pages,
    page_table,
    kv_owner,
    cached,
):
    grid = Grid()
    owners = grid.size
    slot_count = page_table.shape[1]
    per_query = w_query.shape[1]
    per_key = w_key.shape[1]
    row_width = per_query + -(-2 * per_key // HEAD) * HEAD
    requests = kv_owner.shape[0]
    rows_dev = requests // owners
    width = hidden_in.shape[1]
    all_slots = owners * slot_count

    inputs = hidden_in.astype(jnp.float32)
    factor = lax.rsqrt(jnp.mean(inputs * inputs, axis=1, keepdims=True) + epsilon)
    normed = (inputs * factor * norm_gain).astype(jnp.bfloat16)

    order = jnp.arange(requests, dtype=jnp.int32)
    earlier = (kv_owner[:, None] == kv_owner[None, :]) & (order[None, :] < order[:, None])
    slot_index = jnp.sum(earlier.astype(jnp.int32), axis=1)
    place = kv_owner * slot_count + slot_index

    def reordered(blocks):
        pick = blocks[:, None] == jnp.arange(owners, dtype=jnp.int32)[None, :]
        moved = jnp.where(pick[:, :, None], place.reshape(1, owners, rows_dev), 0)
        return jnp.sum(moved, axis=1).reshape(requests)

    slots = jnp.arange(all_slots, dtype=jnp.int32)
    place_in = reordered(grid.blocks(-1))
    place_out = reordered(grid.blocks(1))
    route_out = (place_out[:, None] == slots[None, :]).astype(jnp.bfloat16)

    mine = lax.axis_index(AXES) * slot_count + jnp.arange(slot_count, dtype=jnp.int32)
    lengths = jnp.sum(jnp.where(place[:, None] == mine[None, :], cached[:, None], 0), axis=0)
    halfway = HEAD // 2
    offsets = jnp.arange(halfway, dtype=jnp.float32)
    frequency = rope_base ** (-(2.0 * offsets) / HEAD)
    angles = lengths.astype(jnp.float32)[:, None] * frequency
    cosine_part = jnp.cos(angles)
    sine_part = jnp.sin(angles)
    cosine = jnp.concatenate([cosine_part, cosine_part], axis=1)
    sine = jnp.concatenate([-sine_part, sine_part], axis=1)

    chunks = 2
    step = width // chunks
    total = line = None
    for i in range(chunks):
        x = normed[:, i * step : (i + 1) * step]
        if i:
            x = after(x, line)
        parts = gather_rows(grid, x)
        line = parts[0]
        total = project(
            i, chunks, parts, w_query, w_key.T, w_value.T, total, place_in, all_slots, row_width
        )
    outbound = total.reshape(owners, slot_count, row_width)
    inbound = lax.all_to_all(outbound, AXES, split_axis=0, concat_axis=0, tiled=True)
    attended = attend(
        inbound,
        lengths,
        page_table[0],
        cosine,
        sine,
        key_pages[0],
        value_pages[0],
        per_query,
        per_key,
    )
    returned = lax.all_to_all(attended, AXES, split_axis=0, concat_axis=0, tiled=True)
    returned = returned.reshape(all_slots, per_query)
    head_rows = jnp.dot(route_out, returned, preferred_element_type=jnp.float32)
    head_rows = head_rows.astype(jnp.bfloat16)
    summed = scatter_sum(grid, head_rows, w_out, chunks)
    return (inputs + summed).astype(jnp.bfloat16)


def solution(mesh):
    placed = (
        P(("groups", "tp", "attn"), None),
        P(),
        P(None, ("tp", "attn")),
        P(None, ("tp", "attn")),
        P(None, ("tp", "attn")),
        P(("tp", "attn"), None),
        P(("groups", "tp", "attn"), None, None, None),
        P(("groups", "tp", "attn"), None, None, None),
        P(("groups", "tp", "attn"), None, None),
        P("groups"),
        P("groups"),
    )
    return jax.shard_map(
        on_device,
        mesh=mesh,
        in_specs=placed,
        out_specs=P(("groups", "tp", "attn"), None),
        check_vma=False,
    )
```

```python
import functools

import jax
import jax.numpy as jnp
import numpy as np
from jax import lax
from jax.experimental import pallas as pl
from jax.experimental.pallas import tpu as pltpu
from jax.sharding import PartitionSpec as P

HEAD = 128
AXES = ("tp", "attn")

epsilon = 1e-05
rope_base = 500000.0


class Grid:
    def __init__(self):
        tp = lax.axis_size("tp")
        self.core = lax.axis_size("attn")
        self.near = 2 if tp % 2 == 0 else 1
        self.far = tp // self.near
        self.size = tp * self.core

    def index(self, far, near, core):
        return (far * self.near + near) * self.core + core

    def perm(self, far=0, near=0, core=0):
        pairs = []
        for f in range(self.far):
            for n in range(self.near):
                for c in range(self.core):
                    to = self.index(
                        (f + far) % self.far, (n + near) % self.near, (c + core) % self.core
                    )
                    pairs.append((self.index(f, n, c), to))
        return pairs

    def send(self, x, far=0, near=0, core=0):
        return lax.ppermute(x, AXES, self.perm(far, near, core))

    def blocks(self, sign):
        rows = []
        for f in range(self.far):
            for n in range(self.near):
                for c in range(self.core):
                    rows.append(
                        [
                            self.index(
                                (f + sign * df) % self.far,
                                (n + sign * dn) % self.near,
                                (c + sign * dc) % self.core,
                            )
                            for dc in range(self.core)
                            for dn in range(self.near)
                            for df in range(self.far)
                        ]
                    )
        return jnp.asarray(np.array(rows, np.int32))[lax.axis_index(AXES)]

    def crossed(self):
        return [
            (dc * self.near + dn) * self.far + df
            for dc in range(self.core)
            for df in range(self.far)
            for dn in range(self.near)
        ]


def after(x, *earlier):
    return lax.optimization_barrier((x, *earlier))[0]


def gather_rows(grid, xa, xb, meanwhile):
    beside_b = grid.send(xb, near=1)
    line_a = jnp.concatenate([xa] + [grid.send(xa, far=d) for d in range(1, grid.far)], axis=0)
    pair_b = jnp.concatenate([xb, beside_b], axis=0)
    line_a, pair_b = lax.optimization_barrier((line_a, pair_b))
    beside_a = grid.send(line_a, near=1)
    line_b = [grid.send(pair_b, far=d) for d in range(1, grid.far)]
    beside_a, line_b, meanwhile = lax.optimization_barrier((beside_a, line_b, meanwhile))
    parts_a = [line_a, beside_a]
    parts_b = [pair_b, *line_b]
    parts_a += [grid.send(part, core=1) for part in parts_a]
    parts_b += [grid.send(part, core=1) for part in parts_b]
    return parts_a, parts_b, meanwhile


def narrow(x):
    return x.astype(jnp.bfloat16)


def wide(x):
    return x.astype(jnp.float32)


def scatter_sum(grid, rows_a, rows_b, w_out):
    half = w_out.shape[1] // 2

    def start(rows, w):
        x = jnp.dot(rows, w, preferred_element_type=jnp.float32)
        middle = x.shape[0] // 2
        away = narrow(x[middle:])
        return away, x[:middle] + wide(grid.send(away, core=1))

    def along_near(x):
        middle = x.shape[0] // 2
        return x[:middle] + wide(grid.send(narrow(x[middle:]), near=1))

    def along_far(x):
        size = x.shape[0] // grid.far
        parts = [
            grid.send(narrow(x[d * size : (d + 1) * size]), far=d) for d in range(1, grid.far)
        ]
        x = x[:size]
        for part in parts:
            x = x + wide(part)
        return x

    away, xb = start(rows_b, w_out[:, half:])
    _, xa = start(after(rows_a, away), w_out[:, :half])
    xb = along_near(along_far(xb))
    xa = along_far(along_near(xa))
    return jnp.concatenate([xa, xb], axis=1)


def norm_kernel(x, gain, *outs):
    inputs = x[...].astype(jnp.float32)
    factor = lax.rsqrt(jnp.mean(inputs * inputs, axis=1, keepdims=True) + epsilon)
    normed = (inputs * factor * gain[...]).astype(jnp.bfloat16)
    start = 0
    for out in outs:
        out[...] = normed[:, start : start + out.shape[1]]
        start += out.shape[1]


def norm(x, gain, widths):
    vmem = pl.BlockSpec(memory_space=pltpu.VMEM)
    return pl.pallas_call(
        norm_kernel,
        in_specs=[vmem, vmem],
        out_specs=[vmem] * len(widths),
        out_shape=[jax.ShapeDtypeStruct((x.shape[0], w), jnp.bfloat16) for w in widths],
        compiler_params=pltpu.CompilerParams(vmem_limit_bytes=16 * 2**20),
        name="norm",
    )(x, gain.reshape(1, -1))


def project_kernel(first, last, order, *refs):
    count = len(refs) - 4 - (not first) - last
    parts, (wq, w_kv), refs = refs[:count], refs[count : count + 2], refs[count + 2 :]
    if not first:
        before, refs = refs[0], refs[1:]
    if last:
        place, refs = refs[0], refs[1:]
    out, total = refs
    step = pl.program_id(0)
    block, per_query = wq.shape

    @pl.when(step == 0)
    def _():
        total[...] = jnp.zeros_like(total) if first else before[...]

    here = pl.ds(pl.multiple_of(step * block, block), block)
    x = jnp.concatenate([part[:, here] for part in parts], axis=0)
    products = [
        jnp.dot(x, wq[...], preferred_element_type=jnp.float32),
        lax.dot_general(x, w_kv[...], (((1,), (1,)), ((), ())), preferred_element_type=jnp.float32),
    ]
    size = x.shape[0] // len(order)
    for product, columns in zip(products, (slice(0, per_query), slice(per_query, None))):
        for i, place_i in enumerate(order):
            total[place_i * size : (place_i + 1) * size, columns] += product[
                i * size : (i + 1) * size
            ]

    @pl.when(step == pl.num_programs(0) - 1)
    def _():
        if last:
            rows = lax.broadcasted_iota(jnp.int32, (out.shape[0], place.shape[1]), 0)
            route = jnp.where(rows == place[...], 1.0, 0.0).astype(jnp.bfloat16)
            moved = jnp.dot(
                route, total[...].astype(jnp.bfloat16), preferred_element_type=jnp.float32
            )
            out[...] = moved.astype(jnp.bfloat16)
        else:
            out[...] = total[...]


def project(start, parts, order, w_query, w_kv_t, before, place, slots):
    row_width = w_query.shape[1] + w_kv_t.shape[0]
    width = parts[0].shape[1]
    block = 1024
    rows = sum(part.shape[0] for part in parts)
    first, last = before is None, place is not None
    vmem = pl.BlockSpec(memory_space=pltpu.VMEM)
    args = [*parts, w_query, w_kv_t]
    specs = [vmem] * len(parts)
    specs += [
        pl.BlockSpec((block, w_query.shape[1]), lambda i: (start // block + i, 0)),
        pl.BlockSpec((w_kv_t.shape[0], block), lambda i: (0, start // block + i)),
    ]
    if not first:
        args.append(before)
        specs.append(vmem)
    if last:
        args.append(place.reshape(1, rows))
        specs.append(vmem)
        out = jax.ShapeDtypeStruct((slots, row_width), jnp.bfloat16)
    else:
        out = jax.ShapeDtypeStruct((rows, row_width), jnp.float32)
    return pl.pallas_call(
        functools.partial(project_kernel, first, last, order),
        grid=(width // block,),
        in_specs=specs,
        out_specs=vmem,
        out_shape=out,
        scratch_shapes=[pltpu.VMEM((rows, row_width), jnp.float32)],
        compiler_params=pltpu.CompilerParams(vmem_limit_bytes=48 * 2**20),
        cost_estimate=pl.CostEstimate(
            flops=2 * rows * width * row_width,
            bytes_accessed=2 * width * row_width,
            transcendentals=0,
        ),
        name="project",
    )(*args)


def attend_kernel(
    per_query,
    per_key,
    table,
    lengths,
    inbound,
    cosine,
    sine,
    key_pages,
    value_pages,
    out,
    key_pool,
    value_pool,
    sems,
    key_new,
    query_rot,
    value_own,
    chance,
    mixed,
):
    owners, slots, _ = inbound.shape
    pages = table.shape[1]
    page, kv_width = key_pages.shape[1:]
    kv_heads = kv_width // HEAD
    heads_dev = per_query // HEAD
    heads = owners * heads_dev
    pair = 2 * heads // kv_heads
    pairs = kv_heads // 2
    span = pages * page
    pieces = owners // kv_heads
    batches = query_rot.shape[1]
    batch = slots // batches

    cuts = 4
    size = key_pages.shape[0] // cuts
    for i, (pool, on_chip) in enumerate(((key_pages, key_pool), (value_pages, value_pool))):
        for cut in range(cuts):
            part = pl.ds(cut * size, size)
            pltpu.make_async_copy(pool.at[part], on_chip.at[part], sems.at[i]).start()

    def held(pool, slot, columns):
        return [pool[table[slot, j], :, columns] for j in range(pages)]

    cos = cosine[...]
    sin = sine[...]

    def turn(x):
        return (x * cos + pltpu.roll(x, HEAD // 2, 1) * sin).astype(jnp.bfloat16)

    for source in range(owners):
        for j in range(heads_dev):
            x = inbound[source, :, j * HEAD : (j + 1) * HEAD].astype(jnp.float32)
            x = turn(x).astype(jnp.float32)
            head = source * heads_dev + j
            for b in range(batches):
                rows = pl.ds(head % pair * batch, batch)
                query_rot[head // pair, b, rows] = x[b * batch : (b + 1) * batch]

    piece = lax.broadcasted_iota(jnp.int32, (slots, HEAD), 1) // per_key
    for g in range(kv_heads):
        key = jnp.zeros((slots, HEAD), jnp.float32)
        value = jnp.zeros((slots, HEAD), jnp.float32)
        for j in range(pieces):
            tile = inbound[g * pieces + j, :, per_query : per_query + HEAD].astype(jnp.float32)
            shift = j * per_key
            back = (shift - per_key) % HEAD
            key = jnp.where(piece == j, pltpu.roll(tile, shift, 1) if shift else tile, key)
            value = jnp.where(piece == j, pltpu.roll(tile, back, 1) if back else tile, value)
        key_new[:, g * HEAD : (g + 1) * HEAD] = turn(key)
        value_own[g] = value

    scale = HEAD ** (-0.5)
    columns = pair * batch
    row = lax.broadcasted_iota(jnp.int32, (span, columns), 0)
    place = lax.broadcasted_iota(jnp.int32, (span, columns), 1) % batch
    own_row = lax.broadcasted_iota(jnp.int32, (slots, columns), 0)
    own_place = lax.broadcasted_iota(jnp.int32, (slots, columns), 1) % batch
    first = lax.broadcasted_iota(jnp.int32, (HEAD, columns), 1) < columns // 2
    same = lax.broadcasted_iota(jnp.int32, (columns, columns), 0) == lax.broadcasted_iota(
        jnp.int32, (columns, columns), 1
    )

    pltpu.make_async_copy(key_pool, key_pool, sems.at[0]).wait()
    own_chances = {}
    for b in range(batches):
        valid = row < lengths[b]
        for p in range(pairs):
            turned = query_rot[p, b].T.astype(jnp.bfloat16)
            none = jnp.zeros_like(turned)
            wide = jnp.concatenate(
                [jnp.where(first, turned, none), jnp.where(first, none, turned)], axis=0
            )
            columns_p = slice(p * 2 * HEAD, (p + 1) * 2 * HEAD)
            keys = []
            for s in range(batch):
                keys += held(key_pool, b * batch + s, columns_p)
            keys.append(key_new[:, columns_p])
            products = jnp.dot(
                jnp.concatenate(keys, axis=0), wide, preferred_element_type=jnp.float32
            )
            scores = products[:span]
            for s in range(1, batch):
                scores = jnp.where(place == s, products[s * span : (s + 1) * span], scores)
            own = jnp.where(own_row == own_place + b * batch, products[batch * span :], 0.0)
            own = jnp.sum(own, axis=0, keepdims=True) * scale
            masked = jnp.where(valid, scores * scale, -1e30)
            top = jnp.maximum(jnp.max(masked, axis=0, keepdims=True), own)
            terms = jnp.where(valid, jnp.exp(masked - top), 0.0)
            own_term = jnp.exp(own - top)
            total = jnp.sum(terms, axis=0, keepdims=True) + own_term
            chance[p, b] = (terms / total).T.astype(jnp.bfloat16).astype(jnp.float32)
            own_chance = (own_term / total).astype(jnp.bfloat16).astype(jnp.float32)
            own_chances[p, b] = jnp.sum(
                jnp.where(same, own_chance, 0.0), axis=1, keepdims=True
            )

    pltpu.make_async_copy(value_pool, value_pool, sems.at[1]).wait()
    for b in range(batches):
        for s in range(batch):
            for p in range(pairs):
                mine = chance[p, b, pl.ds(s, pair, stride=batch)].astype(jnp.bfloat16)
                columns_p = slice(p * 2 * HEAD, (p + 1) * 2 * HEAD)
                values = held(value_pool, b * batch + s, columns_p)
                both = jnp.dot(
                    mine, jnp.concatenate(values, axis=0), preferred_element_type=jnp.float32
                )
                result = jnp.concatenate(
                    [both[: pair // 2, :HEAD], both[pair // 2 :, HEAD:]], axis=0
                )
                mixed[p, b, pl.ds(s, pair, stride=batch)] = result

    for p in range(pairs):
        for j in range(pair):
            head = p * pair + j
            g = head * kv_heads // heads
            halves = []
            for b in range(batches):
                rows = slice(j * batch, (j + 1) * batch)
                own_value = value_own[g, b * batch : (b + 1) * batch]
                halves.append(mixed[p, b, rows] + own_chances[p, b][rows] * own_value)
            column = head % heads_dev * HEAD
            out[head // heads_dev, :, column : column + HEAD] = jnp.concatenate(
                halves, axis=0
            ).astype(jnp.bfloat16)


def attend(inbound, lengths, table, cosine, sine, key_pages, value_pages, per_query, per_key):
    owners, slots, _ = inbound.shape
    pages = table.shape[1]
    page, kv_width = key_pages.shape[1:]
    kv_heads = kv_width // HEAD
    heads = owners * (per_query // HEAD)
    span = pages * page
    pair = 2 * heads // kv_heads
    pairs = kv_heads // 2
    batches = slots * pair // HEAD
    batch = slots // batches
    columns = pair * batch
    lengths = jnp.tile(lengths.reshape(batches, 1, batch), (1, 1, pair))
    smem = pl.BlockSpec(memory_space=pltpu.SMEM)
    vmem = pl.BlockSpec(memory_space=pltpu.VMEM)
    hbm = pl.BlockSpec(memory_space=pl.ANY)
    return pl.pallas_call(
        functools.partial(attend_kernel, per_query, per_key),
        in_specs=[smem, vmem, vmem, vmem, vmem, hbm, hbm],
        out_specs=vmem,
        out_shape=jax.ShapeDtypeStruct((owners, slots, per_query), jnp.bfloat16),
        scratch_shapes=[
            pltpu.VMEM(key_pages.shape, jnp.bfloat16),
            pltpu.VMEM(value_pages.shape, jnp.bfloat16),
            pltpu.SemaphoreType.DMA((2,)),
            pltpu.VMEM((slots, kv_width), jnp.bfloat16),
            pltpu.VMEM((pairs, batches, columns, HEAD), jnp.float32),
            pltpu.VMEM((kv_heads, slots, HEAD), jnp.float32),
            pltpu.VMEM((pairs, batches, columns, span), jnp.float32),
            pltpu.VMEM((pairs, batches, columns, HEAD), jnp.float32),
        ],
        compiler_params=pltpu.CompilerParams(vmem_limit_bytes=52 * 2**20),
        cost_estimate=pl.CostEstimate(
            flops=8 * slots * heads * span * HEAD,
            bytes_accessed=4 * slots * span * kv_width,
            transcendentals=slots * heads * span,
        ),
        name="attend",
    )(table, lengths, inbound, cosine, sine, key_pages, value_pages)


def on_device(
    hidden_in,
    norm_gain,
    w_query,
    w_key,
    w_value,
    w_out,
    key_pages,
    value_pages,
    page_table,
    kv_owner,
    cached,
):
    grid = Grid()
    owners = grid.size
    slot_count = page_table.shape[1]
    per_query = w_query.shape[1]
    per_key = w_key.shape[1]
    row_width = per_query + -(-2 * per_key // HEAD) * HEAD
    requests = kv_owner.shape[0]
    rows_dev = requests // owners
    width = hidden_in.shape[1]
    all_slots = owners * slot_count

    unit = width // 8
    xa, xb = norm(hidden_in, norm_gain, (5 * unit, 3 * unit))

    order = jnp.arange(requests, dtype=jnp.int32)
    earlier = (kv_owner[:, None] == kv_owner[None, :]) & (order[None, :] < order[:, None])
    slot_index = jnp.sum(earlier.astype(jnp.int32), axis=1)
    place = kv_owner * slot_count + slot_index

    def reordered(blocks):
        pick = blocks[:, None] == jnp.arange(owners, dtype=jnp.int32)[None, :]
        moved = jnp.where(pick[:, :, None], place.reshape(1, owners, rows_dev), 0)
        return jnp.sum(moved, axis=1).reshape(requests)

    slots = jnp.arange(all_slots, dtype=jnp.int32)
    place_in = reordered(grid.blocks(-1))
    place_out = reordered(grid.blocks(1))
    route_out = (place_out[:, None] == slots[None, :]).astype(jnp.bfloat16)
    crossed = grid.crossed()
    crossed_out = place_out.reshape(owners, rows_dev)[np.array(crossed)].reshape(requests)
    route_crossed = (crossed_out[:, None] == slots[None, :]).astype(jnp.bfloat16)

    mine = lax.axis_index(AXES) * slot_count + jnp.arange(slot_count, dtype=jnp.int32)
    lengths = jnp.sum(jnp.where(place[:, None] == mine[None, :], cached[:, None], 0), axis=0)
    halfway = HEAD // 2
    offsets = jnp.arange(halfway, dtype=jnp.float32)
    frequency = rope_base ** (-(2.0 * offsets) / HEAD)
    angles = lengths.astype(jnp.float32)[:, None] * frequency
    cosine_part = jnp.cos(angles)
    sine_part = jnp.sin(angles)
    cosine = jnp.concatenate([cosine_part, cosine_part], axis=1)
    sine = jnp.concatenate([-sine_part, sine_part], axis=1)

    pieces = [w_key.T, w_value.T]
    spare = row_width - per_query - 2 * per_key
    if spare:
        pieces.append(jnp.zeros((spare, width), w_key.dtype))
    w_kv_t = jnp.concatenate(pieces, axis=0)
    parts_a, parts_b, (w_kv_t, place_in, place_out, cosine, sine) = gather_rows(
        grid, xa, xb, (w_kv_t, place_in, place_out, cosine, sine)
    )
    plain = list(range(owners))
    total = project(0, parts_a, plain, w_query, w_kv_t, None, None, all_slots)
    total = project(5 * unit, parts_b, crossed, w_query, w_kv_t, total, place_in, all_slots)
    outbound = total.reshape(owners, slot_count, row_width)
    inbound = lax.all_to_all(outbound, AXES, split_axis=0, concat_axis=0, tiled=True)
    attended = attend(
        inbound,
        lengths,
        page_table[0],
        cosine,
        sine,
        key_pages[0],
        value_pages[0],
        per_query,
        per_key,
    )
    returned = lax.all_to_all(attended, AXES, split_axis=0, concat_axis=0, tiled=True)
    returned = returned.reshape(all_slots, per_query)
    rows_a = narrow(jnp.dot(route_out, returned, preferred_element_type=jnp.float32))
    rows_b = narrow(jnp.dot(route_crossed, returned, preferred_element_type=jnp.float32))
    summed = scatter_sum(grid, rows_a, rows_b, w_out)
    return narrow(wide(hidden_in) + summed)


def solution(mesh):
    placed = (
        P(("groups", "tp", "attn"), None),
        P(),
        P(None, ("tp", "attn")),
        P(None, ("tp", "attn")),
        P(None, ("tp", "attn")),
        P(("tp", "attn"), None),
        P(("groups", "tp", "attn"), None, None, None),
        P(("groups", "tp", "attn"), None, None, None),
        P(("groups", "tp", "attn"), None, None),
        P("groups"),
        P("groups"),
    )
    return jax.shard_map(
        on_device,
        mesh=mesh,
        in_specs=placed,
        out_specs=P(("groups", "tp", "attn"), None),
        check_vma=False,
    )
```

```python
import functools

import jax
import jax.numpy as jnp
import numpy as np
from jax import lax
from jax.experimental import pallas as pl
from jax.experimental.pallas import tpu as pltpu
from jax.sharding import PartitionSpec as P

HEAD = 128
AXES = ("tp", "attn")

epsilon = 1e-05
rope_base = 500000.0


class Grid:
    def __init__(self):
        tp = lax.axis_size("tp")
        self.core = lax.axis_size("attn")
        self.near = 2 if tp % 2 == 0 else 1
        self.far = tp // self.near
        self.size = tp * self.core

    def index(self, far, near, core):
        return (far * self.near + near) * self.core + core

    def perm(self, far=0, near=0, core=0):
        pairs = []
        for f in range(self.far):
            for n in range(self.near):
                for c in range(self.core):
                    to = self.index(
                        (f + far) % self.far, (n + near) % self.near, (c + core) % self.core
                    )
                    pairs.append((self.index(f, n, c), to))
        return pairs

    def send(self, x, far=0, near=0, core=0):
        return lax.ppermute(x, AXES, self.perm(far, near, core))

    def blocks(self, sign):
        rows = []
        for f in range(self.far):
            for n in range(self.near):
                for c in range(self.core):
                    rows.append(
                        [
                            self.index(
                                (f + sign * df) % self.far,
                                (n + sign * dn) % self.near,
                                (c + sign * dc) % self.core,
                            )
                            for dc in range(self.core)
                            for dn in range(self.near)
                            for df in range(self.far)
                        ]
                    )
        return jnp.asarray(np.array(rows, np.int32))[lax.axis_index(AXES)]

    def crossed(self):
        return [
            (dc * self.near + dn) * self.far + df
            for dc in range(self.core)
            for df in range(self.far)
            for dn in range(self.near)
        ]


def after(x, *earlier):
    return lax.optimization_barrier((x, *earlier))[0]


def gather_rows(grid, xa, xb, meanwhile):
    beside_b = grid.send(xb, near=1)
    line_a = jnp.concatenate([xa] + [grid.send(xa, far=d) for d in range(1, grid.far)], axis=0)
    pair_b = jnp.concatenate([xb, beside_b], axis=0)
    line_a, pair_b = lax.optimization_barrier((line_a, pair_b))
    beside_a = grid.send(line_a, near=1)
    line_b = [grid.send(pair_b, far=d) for d in range(1, grid.far)]
    beside_a, line_b, meanwhile = lax.optimization_barrier((beside_a, line_b, meanwhile(pair_b)))
    parts_a = [line_a, beside_a]
    parts_b = [pair_b, *line_b]
    parts_a += [grid.send(part, core=1) for part in parts_a]
    parts_b += [grid.send(part, core=1) for part in parts_b]
    return parts_a, parts_b, meanwhile


def narrow(x):
    return x.astype(jnp.bfloat16)


def wide(x):
    return x.astype(jnp.float32)


def scatter_sum(grid, rows_a, rows_b, w_out, cut):
    def start(rows, w):
        x = jnp.dot(rows, w, preferred_element_type=jnp.float32)
        middle = x.shape[0] // 2
        away = narrow(x[middle:])
        return away, x[:middle] + wide(grid.send(away, core=1))

    def along_near(x):
        middle = x.shape[0] // 2
        return x[:middle] + wide(grid.send(narrow(x[middle:]), near=1))

    def along_far(x):
        size = x.shape[0] // grid.far
        parts = [
            grid.send(narrow(x[d * size : (d + 1) * size]), far=d) for d in range(1, grid.far)
        ]
        x = x[:size]
        for part in parts:
            x = x + wide(part)
        return x

    away, xb = start(rows_b, w_out[:, cut:])
    _, xa = start(after(rows_a, away), w_out[:, :cut])
    xb = along_near(along_far(xb))
    xa = along_far(along_near(xa))
    return jnp.concatenate([xa, xb], axis=1)


def norm_kernel(x, gain, *outs):
    inputs = x[...].astype(jnp.float32)
    factor = lax.rsqrt(jnp.mean(inputs * inputs, axis=1, keepdims=True) + epsilon)
    normed = (inputs * factor * gain[...]).astype(jnp.bfloat16)
    start = 0
    for out in outs:
        out[...] = normed[:, start : start + out.shape[1]]
        start += out.shape[1]


def norm(x, gain, widths):
    vmem = pl.BlockSpec(memory_space=pltpu.VMEM)
    return pl.pallas_call(
        norm_kernel,
        in_specs=[vmem, vmem],
        out_specs=[vmem] * len(widths),
        out_shape=[jax.ShapeDtypeStruct((x.shape[0], w), jnp.bfloat16) for w in widths],
        compiler_params=pltpu.CompilerParams(vmem_limit_bytes=16 * 2**20),
        name="norm",
    )(x, gain.reshape(1, -1))


def fetch_kernel(*refs):
    count = len(refs) // 2
    sems = refs[-1]
    copies = [
        pltpu.make_async_copy(refs[i], refs[count + i], sems.at[i]) for i in range(count)
    ]
    for copy in copies:
        copy.start()
    for copy in copies:
        copy.wait()


def fetch(*arrays, limit):
    return pl.pallas_call(
        fetch_kernel,
        in_specs=[pl.BlockSpec(memory_space=pl.ANY)] * len(arrays),
        out_specs=[pl.BlockSpec(memory_space=pltpu.VMEM)] * len(arrays),
        out_shape=[jax.ShapeDtypeStruct(x.shape, x.dtype) for x in arrays],
        scratch_shapes=[pltpu.SemaphoreType.DMA((len(arrays),))],
        compiler_params=pltpu.CompilerParams(vmem_limit_bytes=limit * 2**20),
        cost_estimate=pl.CostEstimate(
            flops=0, bytes_accessed=sum(x.size * 4 for x in arrays), transcendentals=0
        ),
        name="fetch",
    )(*arrays)


def project_kernel(first, last, order, start, block, *refs):
    count = len(refs) - 4 - (not first) - last
    parts, (wq, w_kv), refs = refs[:count], refs[count : count + 2], refs[count + 2 :]
    if not first:
        before, refs = refs[0], refs[1:]
    if last:
        place, refs = refs[0], refs[1:]
    out, total = refs
    step = pl.program_id(0)
    per_query = wq.shape[1]

    @pl.when(step == 0)
    def _():
        total[...] = jnp.zeros_like(total) if first else before[...]

    here = pl.ds(pl.multiple_of(step * block, block), block)
    there = pl.ds(pl.multiple_of(start + step * block, block), block)
    x = jnp.concatenate([part[:, here] for part in parts], axis=0)
    products = [
        jnp.dot(x, wq[there, :], preferred_element_type=jnp.float32),
        lax.dot_general(x, w_kv[:, there], (((1,), (1,)), ((), ())), preferred_element_type=jnp.float32),
    ]
    size = x.shape[0] // len(order)
    for product, columns in zip(products, (slice(0, per_query), slice(per_query, None))):
        for i, place_i in enumerate(order):
            total[place_i * size : (place_i + 1) * size, columns] += product[
                i * size : (i + 1) * size
            ]

    @pl.when(step == pl.num_programs(0) - 1)
    def _():
        if last:
            rows = lax.broadcasted_iota(jnp.int32, (out.shape[0], place.shape[1]), 0)
            route = jnp.where(rows == place[...], 1.0, 0.0).astype(jnp.bfloat16)
            moved = jnp.dot(
                route, total[...].astype(jnp.bfloat16), preferred_element_type=jnp.float32
            )
            out[...] = moved.astype(jnp.bfloat16)
        else:
            out[...] = total[...]


def project(start, parts, order, w_query, w_kv_t, before, place, slots):
    row_width = w_query.shape[1] + w_kv_t.shape[0]
    width = parts[0].shape[1]
    block = 1024
    rows = sum(part.shape[0] for part in parts)
    first, last = before is None, place is not None
    vmem = pl.BlockSpec(memory_space=pltpu.VMEM)
    args = [*parts, w_query, w_kv_t]
    specs = [vmem] * len(parts)
    specs += [
        vmem,
        vmem,
    ]
    if not first:
        args.append(before)
        specs.append(vmem)
    if last:
        args.append(place.reshape(1, rows))
        specs.append(vmem)
        out = jax.ShapeDtypeStruct((slots, row_width), jnp.bfloat16)
    else:
        out = jax.ShapeDtypeStruct((rows, row_width), jnp.float32)
    return pl.pallas_call(
        functools.partial(project_kernel, first, last, order, start, block),
        grid=(width // block,),
        in_specs=specs,
        out_specs=vmem,
        out_shape=out,
        scratch_shapes=[pltpu.VMEM((rows, row_width), jnp.float32)],
        compiler_params=pltpu.CompilerParams(vmem_limit_bytes=24 * 2**20),
        cost_estimate=pl.CostEstimate(
            flops=2 * rows * width * row_width,
            bytes_accessed=2 * width * row_width,
            transcendentals=0,
        ),
        name="project",
    )(*args)


def attend_kernel(
    per_query,
    per_key,
    table,
    lengths,
    inbound,
    cosine,
    sine,
    key_pages,
    value_pages,
    out,
    key_new,
    query_rot,
    value_own,
    chance,
    mixed,
):
    owners, slots, _ = inbound.shape
    pages = table.shape[1]
    page, kv_width = key_pages.shape[1:]
    kv_heads = kv_width // HEAD
    heads_dev = per_query // HEAD
    heads = owners * heads_dev
    pair = 2 * heads // kv_heads
    pairs = kv_heads // 2
    span = pages * page
    pieces = owners // kv_heads
    batches = query_rot.shape[1]
    batch = slots // batches

    def held(pool, slot, columns):
        return [pool[table[slot, j], :, columns] for j in range(pages)]

    cos = cosine[...]
    sin = sine[...]

    def turn(x):
        return (x * cos + pltpu.roll(x, HEAD // 2, 1) * sin).astype(jnp.bfloat16)

    for source in range(owners):
        for j in range(heads_dev):
            x = inbound[source, :, j * HEAD : (j + 1) * HEAD].astype(jnp.float32)
            x = turn(x).astype(jnp.float32)
            head = source * heads_dev + j
            for b in range(batches):
                rows = pl.ds(head % pair * batch, batch)
                query_rot[head // pair, b, rows] = x[b * batch : (b + 1) * batch]

    piece = lax.broadcasted_iota(jnp.int32, (slots, HEAD), 1) // per_key
    for g in range(kv_heads):
        key = jnp.zeros((slots, HEAD), jnp.float32)
        value = jnp.zeros((slots, HEAD), jnp.float32)
        for j in range(pieces):
            tile = inbound[g * pieces + j, :, per_query : per_query + HEAD].astype(jnp.float32)
            shift = j * per_key
            back = (shift - per_key) % HEAD
            key = jnp.where(piece == j, pltpu.roll(tile, shift, 1) if shift else tile, key)
            value = jnp.where(piece == j, pltpu.roll(tile, back, 1) if back else tile, value)
        key_new[:, g * HEAD : (g + 1) * HEAD] = turn(key)
        value_own[g] = value

    scale = HEAD ** (-0.5)
    columns = pair * batch
    row = lax.broadcasted_iota(jnp.int32, (span, columns), 0)
    place = lax.broadcasted_iota(jnp.int32, (span, columns), 1) % batch
    own_row = lax.broadcasted_iota(jnp.int32, (slots, columns), 0)
    own_place = lax.broadcasted_iota(jnp.int32, (slots, columns), 1) % batch
    first = lax.broadcasted_iota(jnp.int32, (HEAD, columns), 1) < columns // 2
    same = lax.broadcasted_iota(jnp.int32, (columns, columns), 0) == lax.broadcasted_iota(
        jnp.int32, (columns, columns), 1
    )

    own_chances = {}
    for b in range(batches):
        valid = row < lengths[b]
        for p in range(pairs):
            turned = query_rot[p, b].T.astype(jnp.bfloat16)
            none = jnp.zeros_like(turned)
            wide = jnp.concatenate(
                [jnp.where(first, turned, none), jnp.where(first, none, turned)], axis=0
            )
            columns_p = slice(p * 2 * HEAD, (p + 1) * 2 * HEAD)
            keys = []
            for s in range(batch):
                keys += held(key_pages, b * batch + s, columns_p)
            keys.append(key_new[:, columns_p])
            products = jnp.dot(
                jnp.concatenate(keys, axis=0), wide, preferred_element_type=jnp.float32
            )
            scores = products[:span]
            for s in range(1, batch):
                scores = jnp.where(place == s, products[s * span : (s + 1) * span], scores)
            own = jnp.where(own_row == own_place + b * batch, products[batch * span :], 0.0)
            own = jnp.sum(own, axis=0, keepdims=True) * scale
            masked = jnp.where(valid, scores * scale, -1e30)
            top = jnp.maximum(jnp.max(masked, axis=0, keepdims=True), own)
            terms = jnp.where(valid, jnp.exp(masked - top), 0.0)
            own_term = jnp.exp(own - top)
            total = jnp.sum(terms, axis=0, keepdims=True) + own_term
            chance[p, b] = (terms / total).T.astype(jnp.bfloat16).astype(jnp.float32)
            own_chance = (own_term / total).astype(jnp.bfloat16).astype(jnp.float32)
            own_chances[p, b] = jnp.sum(
                jnp.where(same, own_chance, 0.0), axis=1, keepdims=True
            )

    for b in range(batches):
        for s in range(batch):
            for p in range(pairs):
                mine = chance[p, b, pl.ds(s, pair, stride=batch)].astype(jnp.bfloat16)
                columns_p = slice(p * 2 * HEAD, (p + 1) * 2 * HEAD)
                values = held(value_pages, b * batch + s, columns_p)
                both = jnp.dot(
                    mine, jnp.concatenate(values, axis=0), preferred_element_type=jnp.float32
                )
                result = jnp.concatenate(
                    [both[: pair // 2, :HEAD], both[pair // 2 :, HEAD:]], axis=0
                )
                mixed[p, b, pl.ds(s, pair, stride=batch)] = result

    for p in range(pairs):
        for j in range(pair):
            head = p * pair + j
            g = head * kv_heads // heads
            halves = []
            for b in range(batches):
                rows = slice(j * batch, (j + 1) * batch)
                own_value = value_own[g, b * batch : (b + 1) * batch]
                halves.append(mixed[p, b, rows] + own_chances[p, b][rows] * own_value)
            column = head % heads_dev * HEAD
            out[head // heads_dev, :, column : column + HEAD] = jnp.concatenate(
                halves, axis=0
            ).astype(jnp.bfloat16)


def attend(inbound, lengths, table, cosine, sine, key_pages, value_pages, per_query, per_key):
    owners, slots, _ = inbound.shape
    pages = table.shape[1]
    page, kv_width = key_pages.shape[1:]
    kv_heads = kv_width // HEAD
    heads = owners * (per_query // HEAD)
    span = pages * page
    pair = 2 * heads // kv_heads
    pairs = kv_heads // 2
    batches = slots * pair // HEAD
    batch = slots // batches
    columns = pair * batch
    lengths = jnp.tile(lengths.reshape(batches, 1, batch), (1, 1, pair))
    smem = pl.BlockSpec(memory_space=pltpu.SMEM)
    vmem = pl.BlockSpec(memory_space=pltpu.VMEM)
    return pl.pallas_call(
        functools.partial(attend_kernel, per_query, per_key),
        in_specs=[smem, vmem, vmem, vmem, vmem, vmem, vmem],
        out_specs=vmem,
        out_shape=jax.ShapeDtypeStruct((owners, slots, per_query), jnp.bfloat16),
        scratch_shapes=[
            pltpu.VMEM((slots, kv_width), jnp.bfloat16),
            pltpu.VMEM((pairs, batches, columns, HEAD), jnp.float32),
            pltpu.VMEM((kv_heads, slots, HEAD), jnp.float32),
            pltpu.VMEM((pairs, batches, columns, span), jnp.float32),
            pltpu.VMEM((pairs, batches, columns, HEAD), jnp.float32),
        ],
        compiler_params=pltpu.CompilerParams(vmem_limit_bytes=24 * 2**20),
        cost_estimate=pl.CostEstimate(
            flops=8 * slots * heads * span * HEAD,
            bytes_accessed=4 * slots * span * kv_width,
            transcendentals=slots * heads * span,
        ),
        name="attend",
    )(table, lengths, inbound, cosine, sine, key_pages, value_pages)


def on_device(
    hidden_in,
    norm_gain,
    w_query,
    w_key,
    w_value,
    w_out,
    key_pages,
    value_pages,
    page_table,
    kv_owner,
    cached,
):
    grid = Grid()
    owners = grid.size
    slot_count = page_table.shape[1]
    per_query = w_query.shape[1]
    per_key = w_key.shape[1]
    row_width = per_query + -(-2 * per_key // HEAD) * HEAD
    requests = kv_owner.shape[0]
    rows_dev = requests // owners
    width = hidden_in.shape[1]
    all_slots = owners * slot_count

    unit = width // 8
    xa, xb = norm(hidden_in, norm_gain, (5 * unit, 3 * unit))

    order = jnp.arange(requests, dtype=jnp.int32)
    earlier = (kv_owner[:, None] == kv_owner[None, :]) & (order[None, :] < order[:, None])
    slot_index = jnp.sum(earlier.astype(jnp.int32), axis=1)
    place = kv_owner * slot_count + slot_index

    def reordered(blocks):
        pick = blocks[:, None] == jnp.arange(owners, dtype=jnp.int32)[None, :]
        moved = jnp.where(pick[:, :, None], place.reshape(1, owners, rows_dev), 0)
        return jnp.sum(moved, axis=1).reshape(requests)

    slots = jnp.arange(all_slots, dtype=jnp.int32)
    place_in = reordered(grid.blocks(-1))
    place_out = reordered(grid.blocks(1))
    route_out = (place_out[:, None] == slots[None, :]).astype(jnp.bfloat16)
    crossed = grid.crossed()
    crossed_out = place_out.reshape(owners, rows_dev)[np.array(crossed)].reshape(requests)
    route_crossed = (crossed_out[:, None] == slots[None, :]).astype(jnp.bfloat16)

    mine = lax.axis_index(AXES) * slot_count + jnp.arange(slot_count, dtype=jnp.int32)
    lengths = jnp.sum(jnp.where(place[:, None] == mine[None, :], cached[:, None], 0), axis=0)
    halfway = HEAD // 2
    offsets = jnp.arange(halfway, dtype=jnp.float32)
    frequency = rope_base ** (-(2.0 * offsets) / HEAD)
    angles = lengths.astype(jnp.float32)[:, None] * frequency
    cosine_part = jnp.cos(angles)
    sine_part = jnp.sin(angles)
    cosine = jnp.concatenate([cosine_part, cosine_part], axis=1)
    sine = jnp.concatenate([-sine_part, sine_part], axis=1)

    pieces = [w_key.T, w_value.T]
    spare = row_width - per_query - 2 * per_key
    if spare:
        pieces.append(jnp.zeros((spare, width), w_key.dtype))
    w_kv_t = jnp.concatenate(pieces, axis=0)

    def beside_gather(x):
        (w,) = fetch(after(w_query, x), limit=44)
        return w, w_kv_t, place_in, place_out, cosine, sine

    parts_a, parts_b, others = gather_rows(grid, xa, xb, beside_gather)
    w_query, w_kv_t, place_in, place_out, cosine, sine = others
    plain = list(range(owners))
    total = project(0, parts_a, plain, w_query, w_kv_t, None, None, all_slots)
    total = project(5 * unit, parts_b, crossed, w_query, w_kv_t, total, place_in, all_slots)
    outbound = total.reshape(owners, slot_count, row_width)
    inbound = lax.all_to_all(outbound, AXES, split_axis=0, concat_axis=0, tiled=True)
    keys, values = fetch(after(key_pages, outbound)[0], value_pages[0], limit=44)
    attended = attend(
        inbound,
        lengths,
        page_table[0],
        cosine,
        sine,
        keys,
        values,
        per_query,
        per_key,
    )
    (w_out,) = fetch(after(w_out, attended), limit=44)
    returned = lax.all_to_all(attended, AXES, split_axis=0, concat_axis=0, tiled=True)
    returned = returned.reshape(all_slots, per_query)
    rows_a = narrow(jnp.dot(route_out, returned, preferred_element_type=jnp.float32))
    rows_b = narrow(jnp.dot(route_crossed, returned, preferred_element_type=jnp.float32))
    summed = scatter_sum(grid, rows_a, rows_b, w_out, 5 * unit)
    return narrow(wide(hidden_in) + summed)


def solution(mesh):
    placed = (
        P(("groups", "tp", "attn"), None),
        P(),
        P(None, ("tp", "attn")),
        P(None, ("tp", "attn")),
        P(None, ("tp", "attn")),
        P(("tp", "attn"), None),
        P(("groups", "tp", "attn"), None, None, None),
        P(("groups", "tp", "attn"), None, None, None),
        P(("groups", "tp", "attn"), None, None),
        P("groups"),
        P("groups"),
    )
    return jax.shard_map(
        on_device,
        mesh=mesh,
        in_specs=placed,
        out_specs=P(("groups", "tp", "attn"), None),
        check_vma=False,
    )
```

```python
import functools

import jax
import jax.numpy as jnp
import numpy as np
from jax import lax
from jax.experimental import pallas as pl
from jax.experimental.pallas import tpu as pltpu
from jax.sharding import PartitionSpec as P

HEAD = 128
AXES = ("tp", "attn")

epsilon = 1e-05
rope_base = 500000.0


class Grid:
    def __init__(self):
        tp = lax.axis_size("tp")
        self.core = lax.axis_size("attn")
        self.near = 2 if tp % 2 == 0 else 1
        self.far = tp // self.near
        self.size = tp * self.core

    def index(self, far, near, core):
        return (far * self.near + near) * self.core + core

    def perm(self, far=0, near=0, core=0):
        pairs = []
        for f in range(self.far):
            for n in range(self.near):
                for c in range(self.core):
                    to = self.index(
                        (f + far) % self.far, (n + near) % self.near, (c + core) % self.core
                    )
                    pairs.append((self.index(f, n, c), to))
        return pairs

    def send(self, x, far=0, near=0, core=0):
        return lax.ppermute(x, AXES, self.perm(far, near, core))

    def blocks(self, sign, order=None):
        rows = []
        for f in range(self.far):
            for n in range(self.near):
                for c in range(self.core):
                    row = [
                        self.index(
                            (f + sign * df) % self.far,
                            (n + sign * dn) % self.near,
                            (c + sign * dc) % self.core,
                        )
                        for dc in range(self.core)
                        for dn in range(self.near)
                        for df in range(self.far)
                    ]
                    rows.append([row[i] for i in order] if order else row)
        return jnp.asarray(np.array(rows, np.int32))[lax.axis_index(AXES)]

    def crossed(self):
        return [
            (dc * self.near + dn) * self.far + df
            for dc in range(self.core)
            for df in range(self.far)
            for dn in range(self.near)
        ]


def after(x, *earlier):
    return lax.optimization_barrier((x, *earlier))[0]


def gather_rows(grid, xa, xb, meanwhile):
    beside_b = grid.send(xb, near=1)
    line_a = jnp.concatenate([xa] + [grid.send(xa, far=d) for d in range(1, grid.far)], axis=0)
    pair_b = jnp.concatenate([xb, beside_b], axis=0)
    line_a, pair_b = lax.optimization_barrier((line_a, pair_b))
    beside_a = grid.send(line_a, near=1)
    line_b = [grid.send(pair_b, far=d) for d in range(1, grid.far)]
    beside_a, line_b, meanwhile = lax.optimization_barrier((beside_a, line_b, meanwhile(pair_b)))
    parts_a = [line_a, beside_a]
    parts_b = [pair_b, *line_b]
    parts_a += [grid.send(part, core=1) for part in parts_a]
    parts_b += [grid.send(part, core=1) for part in parts_b]
    return parts_a, parts_b, meanwhile


def narrow(x):
    return x.astype(jnp.bfloat16)


def wide(x):
    return x.astype(jnp.float32)


def product_kernel(start, step, place, returned, w_out, away, keep, held, sems):
    copies = []
    for i in range(held.shape[1] // step):
        here = pl.ds(i * step, step)
        copies.append(
            pltpu.make_async_copy(
                w_out.at[:, pl.ds(start + i * step, step)], held.at[:, here], sems.at[i]
            )
        )
        copies[-1].start()
    slots = lax.broadcasted_iota(jnp.int32, (returned.shape[0], place.shape[1]), 0)
    route = jnp.where(slots == place[...], 1.0, 0.0).astype(jnp.bfloat16)
    rows = lax.dot_general(
        route, returned[...], (((0,), (0,)), ((), ())), preferred_element_type=jnp.float32
    ).astype(jnp.bfloat16)
    half = keep.shape[0]
    for i, copy in enumerate(copies):
        copy.wait()
        here = slice(i * step, (i + 1) * step)
        x = jnp.dot(rows, held[:, here], preferred_element_type=jnp.float32)
        keep[:, here] = x[:half]
        away[:, here] = x[half:].astype(jnp.bfloat16)


def product(place, returned, w_out, start, width):
    rows = place.shape[0]
    step = 512
    vmem = pl.BlockSpec(memory_space=pltpu.VMEM)
    return pl.pallas_call(
        functools.partial(product_kernel, start, step),
        in_specs=[vmem, vmem, pl.BlockSpec(memory_space=pl.ANY)],
        out_specs=[vmem, vmem],
        out_shape=[
            jax.ShapeDtypeStruct((rows // 2, width), jnp.bfloat16),
            jax.ShapeDtypeStruct((rows // 2, width), jnp.float32),
        ],
        scratch_shapes=[
            pltpu.VMEM((w_out.shape[0], width), jnp.bfloat16),
            pltpu.SemaphoreType.DMA((width // step,)),
        ],
        compiler_params=pltpu.CompilerParams(vmem_limit_bytes=48 * 2**20),
        cost_estimate=pl.CostEstimate(
            flops=2 * rows * w_out.shape[0] * width,
            bytes_accessed=2 * w_out.shape[0] * width,
            transcendentals=0,
        ),
        name="product",
    )(place.reshape(1, rows), returned, w_out)


def scatter_sum(grid, place_a, place_b, returned, w_out, cut):
    def along_far(x):
        size = x.shape[0] // grid.far
        parts = [
            grid.send(narrow(x[d * size : (d + 1) * size]), far=d) for d in range(1, grid.far)
        ]
        x = x[:size]
        for part in parts:
            x = x + wide(part)
        return x

    away_a, keep_a = product(place_a, returned, w_out, 0, cut)
    xa = keep_a + wide(grid.send(away_a, core=1))
    middle = xa.shape[0] // 2
    sent_a = narrow(xa[middle:])
    xa = xa[:middle] + wide(grid.send(sent_a, near=1))
    away_b, keep_b = product(
        place_b, after(returned, sent_a), w_out, cut, w_out.shape[1] - cut
    )
    xb = keep_b + wide(grid.send(away_b, core=1))
    xb = along_far(xb)
    middle = xb.shape[0] // 2
    xb = xb[:middle] + wide(grid.send(narrow(xb[middle:]), near=1))
    xa = along_far(xa)
    return jnp.concatenate([xa, xb], axis=1)


def norm_kernel(x, gain, *outs):
    inputs = x[...].astype(jnp.float32)
    factor = lax.rsqrt(jnp.mean(inputs * inputs, axis=1, keepdims=True) + epsilon)
    normed = (inputs * factor * gain[...]).astype(jnp.bfloat16)
    start = 0
    for out in outs:
        out[...] = normed[:, start : start + out.shape[1]]
        start += out.shape[1]


def norm(x, gain, widths):
    vmem = pl.BlockSpec(memory_space=pltpu.VMEM)
    return pl.pallas_call(
        norm_kernel,
        in_specs=[vmem, vmem],
        out_specs=[vmem] * len(widths),
        out_shape=[jax.ShapeDtypeStruct((x.shape[0], w), jnp.bfloat16) for w in widths],
        compiler_params=pltpu.CompilerParams(vmem_limit_bytes=16 * 2**20),
        name="norm",
    )(x, gain.reshape(1, -1))


def fetch_kernel(*refs):
    count = len(refs) // 2
    sems = refs[-1]
    copies = [
        pltpu.make_async_copy(refs[i], refs[count + i], sems.at[i]) for i in range(count)
    ]
    for copy in copies:
        copy.start()
    for copy in copies:
        copy.wait()


def fetch(*arrays, limit):
    return pl.pallas_call(
        fetch_kernel,
        in_specs=[pl.BlockSpec(memory_space=pl.ANY)] * len(arrays),
        out_specs=[pl.BlockSpec(memory_space=pltpu.VMEM)] * len(arrays),
        out_shape=[jax.ShapeDtypeStruct(x.shape, x.dtype) for x in arrays],
        scratch_shapes=[pltpu.SemaphoreType.DMA((len(arrays),))],
        compiler_params=pltpu.CompilerParams(vmem_limit_bytes=limit * 2**20),
        cost_estimate=pl.CostEstimate(
            flops=0, bytes_accessed=sum(x.size * 4 for x in arrays), transcendentals=0
        ),
        name="fetch",
    )(*arrays)


def project_kernel(first, last, order, start, block, *refs):
    count = len(refs) - 4 - (not first) - last
    parts, (wq, w_kv), refs = refs[:count], refs[count : count + 2], refs[count + 2 :]
    if not first:
        before, refs = refs[0], refs[1:]
    if last:
        place, refs = refs[0], refs[1:]
    out, total = refs
    step = pl.program_id(0)
    per_query = wq.shape[1]

    @pl.when(step == 0)
    def _():
        total[...] = jnp.zeros_like(total) if first else before[...]

    here = pl.ds(pl.multiple_of(step * block, block), block)
    there = pl.ds(pl.multiple_of(start + step * block, block), block)
    x = jnp.concatenate([part[:, here] for part in parts], axis=0)
    products = [
        jnp.dot(x, wq[there, :], preferred_element_type=jnp.float32),
        lax.dot_general(x, w_kv[:, there], (((1,), (1,)), ((), ())), preferred_element_type=jnp.float32),
    ]
    size = x.shape[0] // len(order)
    for product, columns in zip(products, (slice(0, per_query), slice(per_query, None))):
        for i, place_i in enumerate(order):
            total[place_i * size : (place_i + 1) * size, columns] += product[
                i * size : (i + 1) * size
            ]

    @pl.when(step == pl.num_programs(0) - 1)
    def _():
        if last:
            rows = lax.broadcasted_iota(jnp.int32, (out.shape[0], place.shape[1]), 0)
            route = jnp.where(rows == place[...], 1.0, 0.0).astype(jnp.bfloat16)
            moved = jnp.dot(
                route, total[...].astype(jnp.bfloat16), preferred_element_type=jnp.float32
            )
            out[...] = moved.astype(jnp.bfloat16)
        else:
            out[...] = total[...]


def project(start, parts, order, w_query, w_kv_t, before, place, slots):
    row_width = w_query.shape[1] + w_kv_t.shape[0]
    width = parts[0].shape[1]
    block = next(b for b in (2816, 2560, 1024, 512) if width % b == 0)
    rows = sum(part.shape[0] for part in parts)
    first, last = before is None, place is not None
    vmem = pl.BlockSpec(memory_space=pltpu.VMEM)
    args = [*parts, w_query, w_kv_t]
    specs = [vmem] * len(parts)
    specs += [
        vmem,
        vmem,
    ]
    if not first:
        args.append(before)
        specs.append(vmem)
    if last:
        args.append(place.reshape(1, rows))
        specs.append(vmem)
        out = jax.ShapeDtypeStruct((slots, row_width), jnp.bfloat16)
    else:
        out = jax.ShapeDtypeStruct((rows, row_width), jnp.float32)
    return pl.pallas_call(
        functools.partial(project_kernel, first, last, order, start, block),
        grid=(width // block,),
        in_specs=specs,
        out_specs=vmem,
        out_shape=out,
        scratch_shapes=[pltpu.VMEM((rows, row_width), jnp.float32)],
        compiler_params=pltpu.CompilerParams(vmem_limit_bytes=24 * 2**20),
        cost_estimate=pl.CostEstimate(
            flops=2 * rows * width * row_width,
            bytes_accessed=2 * width * row_width,
            transcendentals=0,
        ),
        name="project",
    )(*args)


def attend_kernel(
    per_query,
    per_key,
    table,
    lengths,
    inbound,
    cosine,
    sine,
    key_pages,
    value_pages,
    out,
    key_pool,
    value_pool,
    sems,
    key_new,
    query_rot,
    value_own,
    chance,
    mixed,
):
    owners, slots, _ = inbound.shape
    pages = table.shape[1]
    page, kv_width = key_pages.shape[1:]
    kv_heads = kv_width // HEAD
    heads_dev = per_query // HEAD
    heads = owners * heads_dev
    pair = 2 * heads // kv_heads
    pairs = kv_heads // 2
    span = pages * page
    pieces = owners // kv_heads
    batches = query_rot.shape[1]
    batch = slots // batches

    cuts = 4
    size = key_pages.shape[0] // cuts
    for i, (pool, on_chip) in enumerate(((key_pages, key_pool), (value_pages, value_pool))):
        for cut in range(cuts):
            part = pl.ds(cut * size, size)
            pltpu.make_async_copy(pool.at[part], on_chip.at[part], sems.at[i]).start()

    def held(pool, slot, columns):
        return [pool[table[slot, j], :, columns] for j in range(pages)]

    cos = cosine[...]
    sin = sine[...]

    def turn(x):
        return (x * cos + pltpu.roll(x, HEAD // 2, 1) * sin).astype(jnp.bfloat16)

    for source in range(owners):
        for j in range(heads_dev):
            x = inbound[source, :, j * HEAD : (j + 1) * HEAD].astype(jnp.float32)
            x = turn(x).astype(jnp.float32)
            head = source * heads_dev + j
            for b in range(batches):
                rows = pl.ds(head % pair * batch, batch)
                query_rot[head // pair, b, rows] = x[b * batch : (b + 1) * batch]

    piece = lax.broadcasted_iota(jnp.int32, (slots, HEAD), 1) // per_key
    for g in range(kv_heads):
        key = jnp.zeros((slots, HEAD), jnp.float32)
        value = jnp.zeros((slots, HEAD), jnp.float32)
        for j in range(pieces):
            tile = inbound[g * pieces + j, :, per_query : per_query + HEAD].astype(jnp.float32)
            shift = j * per_key
            back = (shift - per_key) % HEAD
            key = jnp.where(piece == j, pltpu.roll(tile, shift, 1) if shift else tile, key)
            value = jnp.where(piece == j, pltpu.roll(tile, back, 1) if back else tile, value)
        key_new[:, g * HEAD : (g + 1) * HEAD] = turn(key)
        value_own[g] = value

    scale = HEAD ** (-0.5)
    columns = pair * batch
    row = lax.broadcasted_iota(jnp.int32, (span, columns), 0)
    place = lax.broadcasted_iota(jnp.int32, (span, columns), 1) % batch
    own_row = lax.broadcasted_iota(jnp.int32, (slots, columns), 0)
    own_place = lax.broadcasted_iota(jnp.int32, (slots, columns), 1) % batch
    first = lax.broadcasted_iota(jnp.int32, (HEAD, columns), 1) < columns // 2
    same = lax.broadcasted_iota(jnp.int32, (columns, columns), 0) == lax.broadcasted_iota(
        jnp.int32, (columns, columns), 1
    )

    pltpu.make_async_copy(key_pool, key_pool, sems.at[0]).wait()
    own_chances = {}
    for b in range(batches):
        valid = row < lengths[b]
        for p in range(pairs):
            turned = query_rot[p, b].T.astype(jnp.bfloat16)
            none = jnp.zeros_like(turned)
            wide = jnp.concatenate(
                [jnp.where(first, turned, none), jnp.where(first, none, turned)], axis=0
            )
            columns_p = slice(p * 2 * HEAD, (p + 1) * 2 * HEAD)
            keys = []
            for s in range(batch):
                keys += held(key_pool, b * batch + s, columns_p)
            keys.append(key_new[:, columns_p])
            products = jnp.dot(
                jnp.concatenate(keys, axis=0), wide, preferred_element_type=jnp.float32
            )
            scores = products[:span]
            for s in range(1, batch):
                scores = jnp.where(place == s, products[s * span : (s + 1) * span], scores)
            own = jnp.where(own_row == own_place + b * batch, products[batch * span :], 0.0)
            own = jnp.sum(own, axis=0, keepdims=True) * scale
            masked = jnp.where(valid, scores * scale, -1e30)
            top = jnp.maximum(jnp.max(masked, axis=0, keepdims=True), own)
            terms = jnp.where(valid, jnp.exp(masked - top), 0.0)
            own_term = jnp.exp(own - top)
            total = jnp.sum(terms, axis=0, keepdims=True) + own_term
            chance[p, b] = (terms / total).T.astype(jnp.bfloat16).astype(jnp.float32)
            own_chance = (own_term / total).astype(jnp.bfloat16).astype(jnp.float32)
            own_chances[p, b] = jnp.sum(
                jnp.where(same, own_chance, 0.0), axis=1, keepdims=True
            )

    pltpu.make_async_copy(value_pool, value_pool, sems.at[1]).wait()
    for b in range(batches):
        for s in range(batch):
            for p in range(pairs):
                mine = chance[p, b, pl.ds(s, pair, stride=batch)].astype(jnp.bfloat16)
                columns_p = slice(p * 2 * HEAD, (p + 1) * 2 * HEAD)
                values = held(value_pool, b * batch + s, columns_p)
                both = jnp.dot(
                    mine, jnp.concatenate(values, axis=0), preferred_element_type=jnp.float32
                )
                result = jnp.concatenate(
                    [both[: pair // 2, :HEAD], both[pair // 2 :, HEAD:]], axis=0
                )
                mixed[p, b, pl.ds(s, pair, stride=batch)] = result

    for p in range(pairs):
        for j in range(pair):
            head = p * pair + j
            g = head * kv_heads // heads
            halves = []
            for b in range(batches):
                rows = slice(j * batch, (j + 1) * batch)
                own_value = value_own[g, b * batch : (b + 1) * batch]
                halves.append(mixed[p, b, rows] + own_chances[p, b][rows] * own_value)
            column = head % heads_dev * HEAD
            out[head // heads_dev, :, column : column + HEAD] = jnp.concatenate(
                halves, axis=0
            ).astype(jnp.bfloat16)


def attend(inbound, lengths, table, cosine, sine, key_pages, value_pages, per_query, per_key):
    owners, slots, _ = inbound.shape
    pages = table.shape[1]
    page, kv_width = key_pages.shape[1:]
    kv_heads = kv_width // HEAD
    heads = owners * (per_query // HEAD)
    span = pages * page
    pair = 2 * heads // kv_heads
    pairs = kv_heads // 2
    batches = slots * pair // HEAD
    batch = slots // batches
    columns = pair * batch
    lengths = jnp.tile(lengths.reshape(batches, 1, batch), (1, 1, pair))
    smem = pl.BlockSpec(memory_space=pltpu.SMEM)
    vmem = pl.BlockSpec(memory_space=pltpu.VMEM)
    hbm = pl.BlockSpec(memory_space=pl.ANY)
    return pl.pallas_call(
        functools.partial(attend_kernel, per_query, per_key),
        in_specs=[smem, vmem, vmem, vmem, vmem, hbm, hbm],
        out_specs=vmem,
        out_shape=jax.ShapeDtypeStruct((owners, slots, per_query), jnp.bfloat16),
        scratch_shapes=[
            pltpu.VMEM(key_pages.shape, jnp.bfloat16),
            pltpu.VMEM(value_pages.shape, jnp.bfloat16),
            pltpu.SemaphoreType.DMA((2,)),
            pltpu.VMEM((slots, kv_width), jnp.bfloat16),
            pltpu.VMEM((pairs, batches, columns, HEAD), jnp.float32),
            pltpu.VMEM((kv_heads, slots, HEAD), jnp.float32),
            pltpu.VMEM((pairs, batches, columns, span), jnp.float32),
            pltpu.VMEM((pairs, batches, columns, HEAD), jnp.float32),
        ],
        compiler_params=pltpu.CompilerParams(vmem_limit_bytes=52 * 2**20),
        cost_estimate=pl.CostEstimate(
            flops=8 * slots * heads * span * HEAD,
            bytes_accessed=4 * slots * span * kv_width,
            transcendentals=slots * heads * span,
        ),
        name="attend",
    )(table, lengths, inbound, cosine, sine, key_pages, value_pages)


def on_device(
    hidden_in,
    norm_gain,
    w_query,
    w_key,
    w_value,
    w_out,
    key_pages,
    value_pages,
    page_table,
    kv_owner,
    cached,
):
    grid = Grid()
    owners = grid.size
    slot_count = page_table.shape[1]
    per_query = w_query.shape[1]
    per_key = w_key.shape[1]
    row_width = per_query + -(-2 * per_key // HEAD) * HEAD
    requests = kv_owner.shape[0]
    rows_dev = requests // owners
    width = hidden_in.shape[1]
    all_slots = owners * slot_count

    crossed = grid.crossed()
    cut = width // 16 * 11
    xa, xb = norm(hidden_in, norm_gain, (cut, width - cut))

    def placed(kv_owner):
        order = jnp.arange(requests, dtype=jnp.int32)
        earlier = (kv_owner[:, None] == kv_owner[None, :]) & (order[None, :] < order[:, None])
        return kv_owner * slot_count + jnp.sum(earlier.astype(jnp.int32), axis=1)

    def reordered(place, blocks):
        pick = blocks[:, None] == jnp.arange(owners, dtype=jnp.int32)[None, :]
        moved = jnp.where(pick[:, :, None], place.reshape(1, owners, rows_dev), 0)
        return jnp.sum(moved, axis=1).reshape(requests)

    def beside_gather(x):
        (w,) = fetch(after(w_query, x), limit=44)
        pieces = [after(w_key, x).T, w_value.T]
        spare = row_width - per_query - 2 * per_key
        if spare:
            pieces.append(jnp.zeros((spare, width), w_key.dtype))
        place = placed(after(kv_owner, x))
        return w, jnp.concatenate(pieces, axis=0), place, reordered(place, grid.blocks(-1))

    parts_a, parts_b, others = gather_rows(grid, xa, xb, beside_gather)
    w_query, w_kv_t, place, place_in = others
    plain = list(range(owners))
    total = project(0, parts_a, plain, w_query, w_kv_t, None, None, all_slots)
    total = project(cut, parts_b, crossed, w_query, w_kv_t, total, place_in, all_slots)
    outbound = total.reshape(owners, slot_count, row_width)
    place = after(place, outbound)
    place_out = reordered(place, grid.blocks(1))
    crossed_out = reordered(place, grid.blocks(1, crossed))
    mine = lax.axis_index(AXES) * slot_count + jnp.arange(slot_count, dtype=jnp.int32)
    lengths = jnp.sum(jnp.where(place[:, None] == mine[None, :], cached[:, None], 0), axis=0)
    halfway = HEAD // 2
    offsets = jnp.arange(halfway, dtype=jnp.float32)
    frequency = rope_base ** (-(2.0 * offsets) / HEAD)
    angles = lengths.astype(jnp.float32)[:, None] * frequency
    cosine_part = jnp.cos(angles)
    sine_part = jnp.sin(angles)
    cosine = jnp.concatenate([cosine_part, cosine_part], axis=1)
    sine = jnp.concatenate([-sine_part, sine_part], axis=1)
    inbound = lax.all_to_all(outbound, AXES, split_axis=0, concat_axis=0, tiled=True)
    attended = attend(
        inbound,
        lengths,
        page_table[0],
        cosine,
        sine,
        key_pages[0],
        value_pages[0],
        per_query,
        per_key,
    )
    returned = lax.all_to_all(attended, AXES, split_axis=0, concat_axis=0, tiled=True)
    returned = returned.reshape(all_slots, per_query)
    summed = scatter_sum(grid, place_out, crossed_out, returned, w_out, cut)
    return narrow(wide(hidden_in) + summed)


def solution(mesh):
    placed = (
        P(("groups", "tp", "attn"), None),
        P(),
        P(None, ("tp", "attn")),
        P(None, ("tp", "attn")),
        P(None, ("tp", "attn")),
        P(("tp", "attn"), None),
        P(("groups", "tp", "attn"), None, None, None),
        P(("groups", "tp", "attn"), None, None, None),
        P(("groups", "tp", "attn"), None, None),
        P("groups"),
        P("groups"),
    )
    return jax.shard_map(
        on_device,
        mesh=mesh,
        in_specs=placed,
        out_specs=P(("groups", "tp", "attn"), None),
        check_vma=False,
    )
```

```python
import functools

import jax
import jax.numpy as jnp
import numpy as np
from jax import lax
from jax.experimental import pallas as pl
from jax.experimental.pallas import tpu as pltpu
from jax.sharding import PartitionSpec as P

HEAD = 128
AXES = ("tp", "attn")

epsilon = 1e-05
rope_base = 500000.0


class Grid:
    def __init__(self):
        tp = lax.axis_size("tp")
        self.core = lax.axis_size("attn")
        self.near = 2 if tp % 2 == 0 else 1
        self.far = tp // self.near
        self.size = tp * self.core

    def index(self, far, near, core):
        return (far * self.near + near) * self.core + core

    def perm(self, far=0, near=0, core=0):
        pairs = []
        for f in range(self.far):
            for n in range(self.near):
                for c in range(self.core):
                    to = self.index(
                        (f + far) % self.far, (n + near) % self.near, (c + core) % self.core
                    )
                    pairs.append((self.index(f, n, c), to))
        return pairs

    def send(self, x, far=0, near=0, core=0):
        return lax.ppermute(x, AXES, self.perm(far, near, core))

    def blocks(self, sign, order=None):
        rows = []
        for f in range(self.far):
            for n in range(self.near):
                for c in range(self.core):
                    row = [
                        self.index(
                            (f + sign * df) % self.far,
                            (n + sign * dn) % self.near,
                            (c + sign * dc) % self.core,
                        )
                        for dc in range(self.core)
                        for dn in range(self.near)
                        for df in range(self.far)
                    ]
                    rows.append([row[i] for i in order] if order else row)
        return jnp.asarray(np.array(rows, np.int32))[lax.axis_index(AXES)]

    def crossed(self):
        return [
            (dc * self.near + dn) * self.far + df
            for dc in range(self.core)
            for df in range(self.far)
            for dn in range(self.near)
        ]


def after(x, *earlier):
    return lax.optimization_barrier((x, *earlier))[0]


def gather_rows(grid, xa, xb, meanwhile):
    beside_b = grid.send(xb, near=1)
    line_a = jnp.concatenate([xa] + [grid.send(xa, far=d) for d in range(1, grid.far)], axis=0)
    pair_b = jnp.concatenate([xb, beside_b], axis=0)
    line_a, pair_b = lax.optimization_barrier((line_a, pair_b))
    beside_a = grid.send(line_a, near=1)
    line_b = [grid.send(pair_b, far=d) for d in range(1, grid.far)]
    beside_a, line_b, meanwhile = lax.optimization_barrier((beside_a, line_b, meanwhile(pair_b)))
    parts_a = [line_a, beside_a]
    parts_b = [pair_b, *line_b]
    parts_a += [grid.send(part, core=1) for part in parts_a]
    parts_b += [grid.send(part, core=1) for part in parts_b]
    return parts_a, parts_b, meanwhile


def narrow(x):
    return x.astype(jnp.bfloat16)


def wide(x):
    return x.astype(jnp.float32)


def product_kernel(cuts, place_a, place_b, returned, w_out, away_a, keep_a, away_b, keep_b, held, sems):
    copies = []
    for i, (start, stop) in enumerate(cuts):
        here = pl.ds(start, stop - start)
        copies.append(pltpu.make_async_copy(w_out.at[:, here], held.at[:, here], sems.at[i]))
        copies[-1].start()
    slots = lax.broadcasted_iota(jnp.int32, (returned.shape[0], place_a.shape[1]), 0)

    def picked(place):
        route = jnp.where(slots == place[...], 1.0, 0.0).astype(jnp.bfloat16)
        rows = lax.dot_general(
            route, returned[...], (((0,), (0,)), ((), ())), preferred_element_type=jnp.float32
        )
        return rows.astype(jnp.bfloat16)

    rows_a, rows_b = picked(place_a), picked(place_b)
    half = keep_a.shape[0]
    middle = keep_a.shape[1]
    for copy, (start, stop) in zip(copies, cuts):
        copy.wait()
        rows, away, keep = (rows_a, away_a, keep_a) if start < middle else (rows_b, away_b, keep_b)
        x = jnp.dot(rows, held[:, start:stop], preferred_element_type=jnp.float32)
        begin = start if start < middle else start - middle
        here = slice(begin, begin + stop - start)
        keep[:, here] = x[:half]
        away[:, here] = x[half:].astype(jnp.bfloat16)


def product(place_a, place_b, returned, w_out, cut):
    rows = place_a.shape[0]
    depth, width = w_out.shape
    cuts = []
    for start, stop in ((0, cut), (cut, width)):
        while start < stop:
            cuts.append((start, min(start + 1024, stop)))
            start = cuts[-1][1]
    vmem = pl.BlockSpec(memory_space=pltpu.VMEM)
    out = []
    for size in (cut, width - cut):
        out.append(jax.ShapeDtypeStruct((rows // 2, size), jnp.bfloat16))
        out.append(jax.ShapeDtypeStruct((rows // 2, size), jnp.float32))
    return pl.pallas_call(
        functools.partial(product_kernel, tuple(cuts)),
        in_specs=[vmem, vmem, vmem, pl.BlockSpec(memory_space=pl.ANY)],
        out_specs=[vmem] * 4,
        out_shape=out,
        scratch_shapes=[
            pltpu.VMEM(w_out.shape, jnp.bfloat16),
            pltpu.SemaphoreType.DMA((len(cuts),)),
        ],
        compiler_params=pltpu.CompilerParams(vmem_limit_bytes=48 * 2**20),
        cost_estimate=pl.CostEstimate(
            flops=2 * rows * depth * width, bytes_accessed=2 * depth * width, transcendentals=0
        ),
        name="product",
    )(place_a.reshape(1, rows), place_b.reshape(1, rows), returned, w_out)


def scatter_sum(grid, place_a, place_b, returned, w_out, cut):
    def send_far(x):
        size = x.shape[0] // grid.far
        return x[:size], [
            grid.send(narrow(x[d * size : (d + 1) * size]), far=d) for d in range(1, grid.far)
        ]

    def total(x, parts):
        for part in parts:
            x = x + wide(part)
        return x

    away_a, keep_a, away_b, keep_b = product(place_a, place_b, returned, w_out, cut)
    xa = keep_a + wide(grid.send(away_a, core=1))
    middle = xa.shape[0] // 2
    sent_a = narrow(xa[middle:])
    got_a = grid.send(sent_a, near=1)
    xb = keep_b + wide(grid.send(after(away_b, sent_a), core=1))
    xb, got_b = send_far(xb)
    got_a, got_b = lax.optimization_barrier((got_a, got_b))
    xa, parts_a = send_far(xa[:middle] + wide(got_a))
    xb = total(xb, got_b)
    middle = xb.shape[0] // 2
    xb = xb[:middle] + wide(grid.send(narrow(xb[middle:]), near=1))
    xa = total(xa, parts_a)
    return jnp.concatenate([xa, xb], axis=1)


def norm_kernel(x, gain, *outs):
    inputs = x[...].astype(jnp.float32)
    factor = lax.rsqrt(jnp.mean(inputs * inputs, axis=1, keepdims=True) + epsilon)
    normed = (inputs * factor * gain[...]).astype(jnp.bfloat16)
    start = 0
    for out in outs:
        out[...] = normed[:, start : start + out.shape[1]]
        start += out.shape[1]


def norm(x, gain, widths):
    vmem = pl.BlockSpec(memory_space=pltpu.VMEM)
    return pl.pallas_call(
        norm_kernel,
        in_specs=[vmem, vmem],
        out_specs=[vmem] * len(widths),
        out_shape=[jax.ShapeDtypeStruct((x.shape[0], w), jnp.bfloat16) for w in widths],
        compiler_params=pltpu.CompilerParams(vmem_limit_bytes=16 * 2**20),
        name="norm",
    )(x, gain.reshape(1, -1))


def fetch_kernel(*refs):
    count = len(refs) // 2
    sems = refs[-1]
    copies = [
        pltpu.make_async_copy(refs[i], refs[count + i], sems.at[i]) for i in range(count)
    ]
    for copy in copies:
        copy.start()
    for copy in copies:
        copy.wait()


def fetch(*arrays, limit):
    return pl.pallas_call(
        fetch_kernel,
        in_specs=[pl.BlockSpec(memory_space=pl.ANY)] * len(arrays),
        out_specs=[pl.BlockSpec(memory_space=pltpu.VMEM)] * len(arrays),
        out_shape=[jax.ShapeDtypeStruct(x.shape, x.dtype) for x in arrays],
        scratch_shapes=[pltpu.SemaphoreType.DMA((len(arrays),))],
        compiler_params=pltpu.CompilerParams(vmem_limit_bytes=limit * 2**20),
        cost_estimate=pl.CostEstimate(
            flops=0, bytes_accessed=sum(x.size * 4 for x in arrays), transcendentals=0
        ),
        name="fetch",
    )(*arrays)


def project_kernel(first, last, order, start, block, *refs):
    count = len(refs) - 4 - (not first) - last
    parts, (wq, w_kv), refs = refs[:count], refs[count : count + 2], refs[count + 2 :]
    if not first:
        before, refs = refs[0], refs[1:]
    if last:
        place, refs = refs[0], refs[1:]
    out, total = refs
    step = pl.program_id(0)
    per_query = wq.shape[1]

    @pl.when(step == 0)
    def _():
        total[...] = jnp.zeros_like(total) if first else before[...]

    here = pl.ds(pl.multiple_of(step * block, block), block)
    there = pl.ds(pl.multiple_of(start + step * block, block), block)
    x = jnp.concatenate([part[:, here] for part in parts], axis=0)
    products = [
        jnp.dot(x, wq[there, :], preferred_element_type=jnp.float32),
        lax.dot_general(x, w_kv[:, there], (((1,), (1,)), ((), ())), preferred_element_type=jnp.float32),
    ]
    size = x.shape[0] // len(order)
    for product, columns in zip(products, (slice(0, per_query), slice(per_query, None))):
        for i, place_i in enumerate(order):
            total[place_i * size : (place_i + 1) * size, columns] += product[
                i * size : (i + 1) * size
            ]

    @pl.when(step == pl.num_programs(0) - 1)
    def _():
        if last:
            rows = lax.broadcasted_iota(jnp.int32, (out.shape[0], place.shape[1]), 0)
            route = jnp.where(rows == place[...], 1.0, 0.0).astype(jnp.bfloat16)
            moved = jnp.dot(
                route, total[...].astype(jnp.bfloat16), preferred_element_type=jnp.float32
            )
            out[...] = moved.astype(jnp.bfloat16)
        else:
            out[...] = total[...]


def project(start, parts, order, w_query, w_kv_t, before, place, slots):
    row_width = w_query.shape[1] + w_kv_t.shape[0]
    width = parts[0].shape[1]
    block = next(b for b in (2816, 2688, 1024, 512) if width % b == 0)
    rows = sum(part.shape[0] for part in parts)
    first, last = before is None, place is not None
    vmem = pl.BlockSpec(memory_space=pltpu.VMEM)
    args = [*parts, w_query, w_kv_t]
    specs = [vmem] * len(parts)
    specs += [
        vmem,
        vmem,
    ]
    if not first:
        args.append(before)
        specs.append(vmem)
    if last:
        args.append(place.reshape(1, rows))
        specs.append(vmem)
        out = jax.ShapeDtypeStruct((slots, row_width), jnp.bfloat16)
    else:
        out = jax.ShapeDtypeStruct((rows, row_width), jnp.float32)
    return pl.pallas_call(
        functools.partial(project_kernel, first, last, order, start, block),
        grid=(width // block,),
        in_specs=specs,
        out_specs=vmem,
        out_shape=out,
        scratch_shapes=[pltpu.VMEM((rows, row_width), jnp.float32)],
        compiler_params=pltpu.CompilerParams(vmem_limit_bytes=24 * 2**20),
        cost_estimate=pl.CostEstimate(
            flops=2 * rows * width * row_width,
            bytes_accessed=2 * width * row_width,
            transcendentals=0,
        ),
        name="project",
    )(*args)


def attend_kernel(
    per_query,
    per_key,
    table,
    lengths,
    inbound,
    cosine,
    sine,
    key_pages,
    value_pages,
    out,
    key_pool,
    value_pool,
    sems,
    key_new,
    query_rot,
    value_own,
    chance,
    mixed,
):
    owners, slots, _ = inbound.shape
    pages = table.shape[1]
    page, kv_width = key_pages.shape[1:]
    kv_heads = kv_width // HEAD
    heads_dev = per_query // HEAD
    heads = owners * heads_dev
    pair = 2 * heads // kv_heads
    pairs = kv_heads // 2
    span = pages * page
    pieces = owners // kv_heads
    batches = query_rot.shape[1]
    batch = slots // batches

    cuts = 4
    size = key_pages.shape[0] // cuts
    for i, (pool, on_chip) in enumerate(((key_pages, key_pool), (value_pages, value_pool))):
        for cut in range(cuts):
            part = pl.ds(cut * size, size)
            pltpu.make_async_copy(pool.at[part], on_chip.at[part], sems.at[i]).start()

    def held(pool, slot, columns):
        return [pool[table[slot, j], :, columns] for j in range(pages)]

    cos = cosine[...]
    sin = sine[...]

    def turn(x):
        return (x * cos + pltpu.roll(x, HEAD // 2, 1) * sin).astype(jnp.bfloat16)

    for source in range(owners):
        for j in range(heads_dev):
            x = inbound[source, :, j * HEAD : (j + 1) * HEAD].astype(jnp.float32)
            x = turn(x).astype(jnp.float32)
            head = source * heads_dev + j
            for b in range(batches):
                rows = pl.ds(head % pair * batch, batch)
                query_rot[head // pair, b, rows] = x[b * batch : (b + 1) * batch]

    piece = lax.broadcasted_iota(jnp.int32, (slots, HEAD), 1) // per_key
    for g in range(kv_heads):
        key = jnp.zeros((slots, HEAD), jnp.float32)
        value = jnp.zeros((slots, HEAD), jnp.float32)
        for j in range(pieces):
            tile = inbound[g * pieces + j, :, per_query : per_query + HEAD].astype(jnp.float32)
            shift = j * per_key
            back = (shift - per_key) % HEAD
            key = jnp.where(piece == j, pltpu.roll(tile, shift, 1) if shift else tile, key)
            value = jnp.where(piece == j, pltpu.roll(tile, back, 1) if back else tile, value)
        key_new[:, g * HEAD : (g + 1) * HEAD] = turn(key)
        value_own[g] = value

    scale = HEAD ** (-0.5)
    columns = pair * batch
    row = lax.broadcasted_iota(jnp.int32, (span, columns), 0)
    place = lax.broadcasted_iota(jnp.int32, (span, columns), 1) % batch
    own_row = lax.broadcasted_iota(jnp.int32, (slots, columns), 0)
    own_place = lax.broadcasted_iota(jnp.int32, (slots, columns), 1) % batch
    first = lax.broadcasted_iota(jnp.int32, (HEAD, columns), 1) < columns // 2
    same = lax.broadcasted_iota(jnp.int32, (columns, columns), 0) == lax.broadcasted_iota(
        jnp.int32, (columns, columns), 1
    )

    pltpu.make_async_copy(key_pool, key_pool, sems.at[0]).wait()
    own_chances = {}
    for b in range(batches):
        valid = row < lengths[b]
        for p in range(pairs):
            turned = query_rot[p, b].T.astype(jnp.bfloat16)
            none = jnp.zeros_like(turned)
            wide = jnp.concatenate(
                [jnp.where(first, turned, none), jnp.where(first, none, turned)], axis=0
            )
            columns_p = slice(p * 2 * HEAD, (p + 1) * 2 * HEAD)
            keys = []
            for s in range(batch):
                keys += held(key_pool, b * batch + s, columns_p)
            keys.append(key_new[:, columns_p])
            products = jnp.dot(
                jnp.concatenate(keys, axis=0), wide, preferred_element_type=jnp.float32
            )
            scores = products[:span]
            for s in range(1, batch):
                scores = jnp.where(place == s, products[s * span : (s + 1) * span], scores)
            own = jnp.where(own_row == own_place + b * batch, products[batch * span :], 0.0)
            own = jnp.sum(own, axis=0, keepdims=True) * scale
            masked = jnp.where(valid, scores * scale, -1e30)
            top = jnp.maximum(jnp.max(masked, axis=0, keepdims=True), own)
            terms = jnp.where(valid, jnp.exp(masked - top), 0.0)
            own_term = jnp.exp(own - top)
            total = jnp.sum(terms, axis=0, keepdims=True) + own_term
            chance[p, b] = (terms / total).T.astype(jnp.bfloat16).astype(jnp.float32)
            own_chance = (own_term / total).astype(jnp.bfloat16).astype(jnp.float32)
            own_chances[p, b] = jnp.sum(
                jnp.where(same, own_chance, 0.0), axis=1, keepdims=True
            )

    pltpu.make_async_copy(value_pool, value_pool, sems.at[1]).wait()
    for b in range(batches):
        for s in range(batch):
            for p in range(pairs):
                mine = chance[p, b, pl.ds(s, pair, stride=batch)].astype(jnp.bfloat16)
                columns_p = slice(p * 2 * HEAD, (p + 1) * 2 * HEAD)
                values = held(value_pool, b * batch + s, columns_p)
                both = jnp.dot(
                    mine, jnp.concatenate(values, axis=0), preferred_element_type=jnp.float32
                )
                result = jnp.concatenate(
                    [both[: pair // 2, :HEAD], both[pair // 2 :, HEAD:]], axis=0
                )
                mixed[p, b, pl.ds(s, pair, stride=batch)] = result

    for p in range(pairs):
        for j in range(pair):
            head = p * pair + j
            g = head * kv_heads // heads
            halves = []
            for b in range(batches):
                rows = slice(j * batch, (j + 1) * batch)
                own_value = value_own[g, b * batch : (b + 1) * batch]
                halves.append(mixed[p, b, rows] + own_chances[p, b][rows] * own_value)
            column = head % heads_dev * HEAD
            out[head // heads_dev, :, column : column + HEAD] = jnp.concatenate(
                halves, axis=0
            ).astype(jnp.bfloat16)


def attend(inbound, lengths, table, cosine, sine, key_pages, value_pages, per_query, per_key):
    owners, slots, _ = inbound.shape
    pages = table.shape[1]
    page, kv_width = key_pages.shape[1:]
    kv_heads = kv_width // HEAD
    heads = owners * (per_query // HEAD)
    span = pages * page
    pair = 2 * heads // kv_heads
    pairs = kv_heads // 2
    batches = slots * pair // HEAD
    batch = slots // batches
    columns = pair * batch
    lengths = jnp.tile(lengths.reshape(batches, 1, batch), (1, 1, pair))
    smem = pl.BlockSpec(memory_space=pltpu.SMEM)
    vmem = pl.BlockSpec(memory_space=pltpu.VMEM)
    hbm = pl.BlockSpec(memory_space=pl.ANY)
    return pl.pallas_call(
        functools.partial(attend_kernel, per_query, per_key),
        in_specs=[smem, vmem, vmem, vmem, vmem, hbm, hbm],
        out_specs=vmem,
        out_shape=jax.ShapeDtypeStruct((owners, slots, per_query), jnp.bfloat16),
        scratch_shapes=[
            pltpu.VMEM(key_pages.shape, jnp.bfloat16),
            pltpu.VMEM(value_pages.shape, jnp.bfloat16),
            pltpu.SemaphoreType.DMA((2,)),
            pltpu.VMEM((slots, kv_width), jnp.bfloat16),
            pltpu.VMEM((pairs, batches, columns, HEAD), jnp.float32),
            pltpu.VMEM((kv_heads, slots, HEAD), jnp.float32),
            pltpu.VMEM((pairs, batches, columns, span), jnp.float32),
            pltpu.VMEM((pairs, batches, columns, HEAD), jnp.float32),
        ],
        compiler_params=pltpu.CompilerParams(vmem_limit_bytes=52 * 2**20),
        cost_estimate=pl.CostEstimate(
            flops=8 * slots * heads * span * HEAD,
            bytes_accessed=4 * slots * span * kv_width,
            transcendentals=slots * heads * span,
        ),
        name="attend",
    )(table, lengths, inbound, cosine, sine, key_pages, value_pages)


def on_device(
    hidden_in,
    norm_gain,
    w_query,
    w_key,
    w_value,
    w_out,
    key_pages,
    value_pages,
    page_table,
    kv_owner,
    cached,
):
    grid = Grid()
    owners = grid.size
    slot_count = page_table.shape[1]
    per_query = w_query.shape[1]
    per_key = w_key.shape[1]
    row_width = per_query + -(-2 * per_key // HEAD) * HEAD
    requests = kv_owner.shape[0]
    rows_dev = requests // owners
    width = hidden_in.shape[1]
    all_slots = owners * slot_count

    crossed = grid.crossed()
    cut = width // 32 * 21
    xa, xb = norm(hidden_in, norm_gain, (cut, width - cut))

    def placed(kv_owner):
        order = jnp.arange(requests, dtype=jnp.int32)
        earlier = (kv_owner[:, None] == kv_owner[None, :]) & (order[None, :] < order[:, None])
        return kv_owner * slot_count + jnp.sum(earlier.astype(jnp.int32), axis=1)

    def reordered(place, blocks):
        pick = blocks[:, None] == jnp.arange(owners, dtype=jnp.int32)[None, :]
        moved = jnp.where(pick[:, :, None], place.reshape(1, owners, rows_dev), 0)
        return jnp.sum(moved, axis=1).reshape(requests)

    def beside_gather(x):
        (w,) = fetch(after(w_query, x), limit=44)
        pieces = [after(w_key, x).T, w_value.T]
        spare = row_width - per_query - 2 * per_key
        if spare:
            pieces.append(jnp.zeros((spare, width), w_key.dtype))
        place = placed(after(kv_owner, x))
        return w, jnp.concatenate(pieces, axis=0), place, reordered(place, grid.blocks(-1))

    parts_a, parts_b, others = gather_rows(grid, xa, xb, beside_gather)
    w_query, w_kv_t, place, place_in = others
    plain = list(range(owners))
    total = project(0, parts_a, plain, w_query, w_kv_t, None, None, all_slots)
    total = project(cut, parts_b, crossed, w_query, w_kv_t, total, place_in, all_slots)
    outbound = total.reshape(owners, slot_count, row_width)
    place = after(place, outbound)
    place_out = reordered(place, grid.blocks(1))
    crossed_out = reordered(place, grid.blocks(1, crossed))
    mine = jnp.asarray(np.arange(all_slots, dtype=np.int32).reshape(owners, slot_count))
    mine = mine[lax.axis_index(AXES)]
    lengths = jnp.sum(jnp.where(place[:, None] == mine[None, :], cached[:, None], 0), axis=0)
    halfway = HEAD // 2
    offsets = jnp.arange(halfway, dtype=jnp.float32)
    frequency = rope_base ** (-(2.0 * offsets) / HEAD)
    angles = lengths.astype(jnp.float32)[:, None] * frequency
    cosine_part = jnp.cos(angles)
    sine_part = jnp.sin(angles)
    cosine = jnp.concatenate([cosine_part, cosine_part], axis=1)
    sine = jnp.concatenate([-sine_part, sine_part], axis=1)
    inbound = lax.all_to_all(outbound, AXES, split_axis=0, concat_axis=0, tiled=True)
    attended = attend(
        inbound,
        lengths,
        after(page_table, outbound)[0],
        cosine,
        sine,
        key_pages[0],
        value_pages[0],
        per_query,
        per_key,
    )
    returned = lax.all_to_all(attended, AXES, split_axis=0, concat_axis=0, tiled=True)
    returned = returned.reshape(all_slots, per_query)
    summed = scatter_sum(grid, place_out, crossed_out, returned, w_out, cut)
    return narrow(wide(hidden_in) + summed)


def solution(mesh):
    placed = (
        P(("groups", "tp", "attn"), None),
        P(),
        P(None, ("tp", "attn")),
        P(None, ("tp", "attn")),
        P(None, ("tp", "attn")),
        P(("tp", "attn"), None),
        P(("groups", "tp", "attn"), None, None, None),
        P(("groups", "tp", "attn"), None, None, None),
        P(("groups", "tp", "attn"), None, None),
        P("groups"),
        P("groups"),
    )
    return jax.shard_map(
        on_device,
        mesh=mesh,
        in_specs=placed,
        out_specs=P(("groups", "tp", "attn"), None),
        check_vma=False,
    )
```

```python
import functools

import jax
import jax.numpy as jnp
import numpy as np
from jax import lax
from jax.experimental import pallas as pl
from jax.experimental.pallas import tpu as pltpu
from jax.sharding import PartitionSpec as P

HEAD = 128
AXES = ("tp", "attn")

epsilon = 1e-05
rope_base = 500000.0


class Grid:
    def __init__(self):
        self.half = lax.axis_size("tp") // 4
        self.sizes = (self.half, 2, 2, lax.axis_size("attn"))
        self.size = int(np.prod(self.sizes))

    def shifted(self, place, moves):
        return np.ravel_multi_index(
            tuple((p + m) % n for p, m, n in zip(place, moves, self.sizes)), self.sizes
        )

    def send(self, x, half=0, pair=0, near=0, core=0):
        pairs = [
            (i, int(self.shifted(np.unravel_index(i, self.sizes), (half, pair, near, core))))
            for i in range(self.size)
        ]
        return lax.ppermute(x, AXES, pairs)

    def moves(self, order):
        counts = [self.sizes[axis] for axis in order]
        places = []
        for steps in np.ndindex(*counts):
            move = [0, 0, 0, 0]
            for axis, step in zip(order, steps):
                move[axis] = step
            places.append(tuple(move))
        return places

    def blocks(self, sign, order):
        rows = [
            [
                int(self.shifted(np.unravel_index(i, self.sizes), [sign * m for m in move]))
                for move in self.moves(order)
            ]
            for i in range(self.size)
        ]
        return jnp.asarray(np.array(rows, np.int32))[lax.axis_index(AXES)]


HALF, PAIR, NEAR, CORE = range(4)
ORDER_A = (CORE, NEAR, PAIR, HALF)
ORDER_B = (CORE, PAIR, HALF, NEAR)


def after(x, *earlier):
    return lax.optimization_barrier((x, *earlier))[0]


def gather_line(grid, x):
    crossed = [grid.send(x, half=d) for d in range(1, grid.half)]
    crossed = crossed[0] if len(crossed) == 1 else jnp.concatenate(crossed, axis=0)
    return [x, crossed, grid.send(x, pair=1), grid.send(crossed, pair=1)]


def gather_rows(grid, xa, xb, meanwhile):
    beside_b = grid.send(xb, near=1)
    line_a = jnp.concatenate(gather_line(grid, xa), axis=0)
    pair_b = jnp.concatenate([xb, beside_b], axis=0)
    line_a, pair_b = lax.optimization_barrier((line_a, pair_b))
    beside_a = grid.send(line_a, near=1)
    parts_b = gather_line(grid, pair_b)
    beside_a, parts_b, meanwhile = lax.optimization_barrier(
        (beside_a, parts_b, meanwhile(pair_b))
    )
    parts_a = [line_a, beside_a]
    parts_a += [grid.send(part, core=1) for part in parts_a]
    parts_b += [grid.send(part, core=1) for part in parts_b]
    return parts_a, parts_b, meanwhile


def narrow(x):
    return x.astype(jnp.bfloat16)


def wide(x):
    return x.astype(jnp.float32)


def product_kernel(cuts, place_a, place_b, returned, w_out, away_a, keep_a, away_b, keep_b, held, sems):
    copies = []
    for i, (start, stop) in enumerate(cuts):
        here = pl.ds(start, stop - start)
        copies.append(pltpu.make_async_copy(w_out.at[:, here], held.at[:, here], sems.at[i]))
        copies[-1].start()
    slots = lax.broadcasted_iota(jnp.int32, (returned.shape[0], place_a.shape[1]), 0)

    def picked(place):
        route = jnp.where(slots == place[...], 1.0, 0.0).astype(jnp.bfloat16)
        rows = lax.dot_general(
            route, returned[...], (((0,), (0,)), ((), ())), preferred_element_type=jnp.float32
        )
        return rows.astype(jnp.bfloat16)

    rows_a, rows_b = picked(place_a), picked(place_b)
    half = keep_a.shape[0]
    middle = keep_a.shape[1]
    for copy, (start, stop) in zip(copies, cuts):
        copy.wait()
        rows, away, keep = (rows_a, away_a, keep_a) if start < middle else (rows_b, away_b, keep_b)
        x = jnp.dot(rows, held[:, start:stop], preferred_element_type=jnp.float32)
        begin = start if start < middle else start - middle
        here = slice(begin, begin + stop - start)
        keep[:, here] = x[:half]
        away[:, here] = x[half:].astype(jnp.bfloat16)


def product(place_a, place_b, returned, w_out, cut):
    rows = place_a.shape[0]
    depth, width = w_out.shape
    cuts = []
    for start, stop in ((0, cut), (cut, width)):
        while start < stop:
            cuts.append((start, min(start + 1024, stop)))
            start = cuts[-1][1]
    vmem = pl.BlockSpec(memory_space=pltpu.VMEM)
    out = []
    for size in (cut, width - cut):
        out.append(jax.ShapeDtypeStruct((rows // 2, size), jnp.bfloat16))
        out.append(jax.ShapeDtypeStruct((rows // 2, size), jnp.float32))
    return pl.pallas_call(
        functools.partial(product_kernel, tuple(cuts)),
        in_specs=[vmem, vmem, vmem, pl.BlockSpec(memory_space=pl.ANY)],
        out_specs=[vmem] * 4,
        out_shape=out,
        scratch_shapes=[
            pltpu.VMEM(w_out.shape, jnp.bfloat16),
            pltpu.SemaphoreType.DMA((len(cuts),)),
        ],
        compiler_params=pltpu.CompilerParams(vmem_limit_bytes=48 * 2**20),
        cost_estimate=pl.CostEstimate(
            flops=2 * rows * depth * width, bytes_accessed=2 * depth * width, transcendentals=0
        ),
        name="product",
    )(place_a.reshape(1, rows), place_b.reshape(1, rows), returned, w_out)


def scatter_sum(grid, place_a, place_b, returned, w_out, cut):
    def along_line(x):
        size = x.shape[0] // 2 // grid.half
        middle = x.shape[0] // 2
        first = grid.send(narrow(x[middle + size :]), pair=1)
        second = grid.send(narrow(x[middle : middle + size]), pair=1)
        far = x[size:middle] + wide(first)
        third = [
            grid.send(narrow(far[d * size : (d + 1) * size]), half=d + 1)
            for d in range(grid.half - 1)
        ]
        return x[:size], [second] + third

    def total(x, parts):
        for part in parts:
            x = x + wide(part)
        return x

    away_a, keep_a, away_b, keep_b = product(place_a, place_b, returned, w_out, cut)
    xa = keep_a + wide(grid.send(away_a, core=1))
    middle = xa.shape[0] // 2
    sent_a = narrow(xa[middle:])
    got_a = grid.send(sent_a, near=1)
    xb = keep_b + wide(grid.send(after(away_b, sent_a), core=1))
    xb, got_b = along_line(xb)
    got_a, got_b = lax.optimization_barrier((got_a, got_b))
    xa, parts_a = along_line(xa[:middle] + wide(got_a))
    xb = total(xb, got_b)
    middle = xb.shape[0] // 2
    xb = xb[:middle] + wide(grid.send(narrow(xb[middle:]), near=1))
    xa = total(xa, parts_a)
    return jnp.concatenate([xa, xb], axis=1)


def norm_kernel(x, gain, *outs):
    inputs = x[...].astype(jnp.float32)
    factor = lax.rsqrt(jnp.mean(inputs * inputs, axis=1, keepdims=True) + epsilon)
    normed = (inputs * factor * gain[...]).astype(jnp.bfloat16)
    start = 0
    for out in outs:
        out[...] = normed[:, start : start + out.shape[1]]
        start += out.shape[1]


def norm(x, gain, widths):
    vmem = pl.BlockSpec(memory_space=pltpu.VMEM)
    return pl.pallas_call(
        norm_kernel,
        in_specs=[vmem, vmem],
        out_specs=[vmem] * len(widths),
        out_shape=[jax.ShapeDtypeStruct((x.shape[0], w), jnp.bfloat16) for w in widths],
        compiler_params=pltpu.CompilerParams(vmem_limit_bytes=16 * 2**20),
        name="norm",
    )(x, gain.reshape(1, -1))


def fetch_kernel(*refs):
    count = len(refs) // 2
    sems = refs[-1]
    copies = [
        pltpu.make_async_copy(refs[i], refs[count + i], sems.at[i]) for i in range(count)
    ]
    for copy in copies:
        copy.start()
    for copy in copies:
        copy.wait()


def fetch(*arrays, limit):
    return pl.pallas_call(
        fetch_kernel,
        in_specs=[pl.BlockSpec(memory_space=pl.ANY)] * len(arrays),
        out_specs=[pl.BlockSpec(memory_space=pltpu.VMEM)] * len(arrays),
        out_shape=[jax.ShapeDtypeStruct(x.shape, x.dtype) for x in arrays],
        scratch_shapes=[pltpu.SemaphoreType.DMA((len(arrays),))],
        compiler_params=pltpu.CompilerParams(vmem_limit_bytes=limit * 2**20),
        cost_estimate=pl.CostEstimate(
            flops=0, bytes_accessed=sum(x.size * 4 for x in arrays), transcendentals=0
        ),
        name="fetch",
    )(*arrays)


def project_kernel(first, last, order, start, block, *refs):
    count = len(refs) - 4 - (not first) - last
    parts, (wq, w_kv), refs = refs[:count], refs[count : count + 2], refs[count + 2 :]
    if not first:
        before, refs = refs[0], refs[1:]
    if last:
        place, refs = refs[0], refs[1:]
    out, total = refs
    step = pl.program_id(0)
    per_query = wq.shape[1]

    @pl.when(step == 0)
    def _():
        total[...] = jnp.zeros_like(total) if first else before[...]

    here = pl.ds(pl.multiple_of(step * block, block), block)
    there = pl.ds(pl.multiple_of(start + step * block, block), block)
    x = jnp.concatenate([part[:, here] for part in parts], axis=0)
    products = [
        jnp.dot(x, wq[there, :], preferred_element_type=jnp.float32),
        lax.dot_general(x, w_kv[:, there], (((1,), (1,)), ((), ())), preferred_element_type=jnp.float32),
    ]
    size = x.shape[0] // len(order)
    for product, columns in zip(products, (slice(0, per_query), slice(per_query, None))):
        for i, place_i in enumerate(order):
            total[place_i * size : (place_i + 1) * size, columns] += product[
                i * size : (i + 1) * size
            ]

    @pl.when(step == pl.num_programs(0) - 1)
    def _():
        if last:
            rows = lax.broadcasted_iota(jnp.int32, (out.shape[0], place.shape[1]), 0)
            route = jnp.where(rows == place[...], 1.0, 0.0).astype(jnp.bfloat16)
            moved = jnp.dot(
                route, total[...].astype(jnp.bfloat16), preferred_element_type=jnp.float32
            )
            out[...] = moved.astype(jnp.bfloat16)
        else:
            out[...] = total[...]


def project(start, parts, order, w_query, w_kv_t, before, place, slots):
    row_width = w_query.shape[1] + w_kv_t.shape[0]
    width = parts[0].shape[1]
    block = width
    rows = sum(part.shape[0] for part in parts)
    first, last = before is None, place is not None
    vmem = pl.BlockSpec(memory_space=pltpu.VMEM)
    args = [*parts, w_query, w_kv_t]
    specs = [vmem] * len(parts)
    specs += [
        vmem,
        vmem,
    ]
    if not first:
        args.append(before)
        specs.append(vmem)
    if last:
        args.append(place.reshape(1, rows))
        specs.append(vmem)
        out = jax.ShapeDtypeStruct((slots, row_width), jnp.bfloat16)
    else:
        out = jax.ShapeDtypeStruct((rows, row_width), jnp.float32)
    return pl.pallas_call(
        functools.partial(project_kernel, first, last, order, start, block),
        grid=(width // block,),
        in_specs=specs,
        out_specs=vmem,
        out_shape=out,
        scratch_shapes=[pltpu.VMEM((rows, row_width), jnp.float32)],
        compiler_params=pltpu.CompilerParams(vmem_limit_bytes=24 * 2**20),
        cost_estimate=pl.CostEstimate(
            flops=2 * rows * width * row_width,
            bytes_accessed=2 * width * row_width,
            transcendentals=0,
        ),
        name="project",
    )(*args)


def attend_kernel(
    per_query,
    per_key,
    table,
    lengths,
    inbound,
    cosine,
    sine,
    key_pages,
    value_pages,
    out,
    key_pool,
    value_pool,
    sems,
    key_new,
    query_rot,
    value_own,
    chance,
    mixed,
):
    owners, slots, _ = inbound.shape
    pages = table.shape[1]
    page, kv_width = key_pages.shape[1:]
    kv_heads = kv_width // HEAD
    heads_dev = per_query // HEAD
    heads = owners * heads_dev
    pair = 2 * heads // kv_heads
    pairs = kv_heads // 2
    span = pages * page
    pieces = owners // kv_heads
    batches = query_rot.shape[1]
    batch = slots // batches

    cuts = 4
    size = key_pages.shape[0] // cuts
    for i, (pool, on_chip) in enumerate(((key_pages, key_pool), (value_pages, value_pool))):
        for cut in range(cuts):
            part = pl.ds(cut * size, size)
            pltpu.make_async_copy(pool.at[part], on_chip.at[part], sems.at[i]).start()

    def held(pool, slot, columns):
        return [pool[table[slot, j], :, columns] for j in range(pages)]

    cos = cosine[...]
    sin = sine[...]

    def turn(x):
        return (x * cos + pltpu.roll(x, HEAD // 2, 1) * sin).astype(jnp.bfloat16)

    for source in range(owners):
        for j in range(heads_dev):
            x = inbound[source, :, j * HEAD : (j + 1) * HEAD].astype(jnp.float32)
            x = turn(x).astype(jnp.float32)
            head = source * heads_dev + j
            for b in range(batches):
                rows = pl.ds(head % pair * batch, batch)
                query_rot[head // pair, b, rows] = x[b * batch : (b + 1) * batch]

    piece = lax.broadcasted_iota(jnp.int32, (slots, HEAD), 1) // per_key
    for g in range(kv_heads):
        key = jnp.zeros((slots, HEAD), jnp.float32)
        value = jnp.zeros((slots, HEAD), jnp.float32)
        for j in range(pieces):
            tile = inbound[g * pieces + j, :, per_query : per_query + HEAD].astype(jnp.float32)
            shift = j * per_key
            back = (shift - per_key) % HEAD
            key = jnp.where(piece == j, pltpu.roll(tile, shift, 1) if shift else tile, key)
            value = jnp.where(piece == j, pltpu.roll(tile, back, 1) if back else tile, value)
        key_new[:, g * HEAD : (g + 1) * HEAD] = turn(key)
        value_own[g] = value

    scale = HEAD ** (-0.5)
    columns = pair * batch
    row = lax.broadcasted_iota(jnp.int32, (span, columns), 0)
    place = lax.broadcasted_iota(jnp.int32, (span, columns), 1) % batch
    own_row = lax.broadcasted_iota(jnp.int32, (slots, columns), 0)
    own_place = lax.broadcasted_iota(jnp.int32, (slots, columns), 1) % batch
    first = lax.broadcasted_iota(jnp.int32, (HEAD, columns), 1) < columns // 2
    same = lax.broadcasted_iota(jnp.int32, (columns, columns), 0) == lax.broadcasted_iota(
        jnp.int32, (columns, columns), 1
    )

    pltpu.make_async_copy(key_pool, key_pool, sems.at[0]).wait()
    own_chances = {}
    for b in range(batches):
        valid = row < lengths[b]
        for p in range(pairs):
            turned = query_rot[p, b].T.astype(jnp.bfloat16)
            none = jnp.zeros_like(turned)
            wide = jnp.concatenate(
                [jnp.where(first, turned, none), jnp.where(first, none, turned)], axis=0
            )
            columns_p = slice(p * 2 * HEAD, (p + 1) * 2 * HEAD)
            keys = []
            for s in range(batch):
                keys += held(key_pool, b * batch + s, columns_p)
            keys.append(key_new[:, columns_p])
            products = jnp.dot(
                jnp.concatenate(keys, axis=0), wide, preferred_element_type=jnp.float32
            )
            scores = products[:span]
            for s in range(1, batch):
                scores = jnp.where(place == s, products[s * span : (s + 1) * span], scores)
            own = jnp.where(own_row == own_place + b * batch, products[batch * span :], 0.0)
            own = jnp.sum(own, axis=0, keepdims=True) * scale
            masked = jnp.where(valid, scores * scale, -1e30)
            top = jnp.maximum(jnp.max(masked, axis=0, keepdims=True), own)
            terms = jnp.where(valid, jnp.exp(masked - top), 0.0)
            own_term = jnp.exp(own - top)
            total = jnp.sum(terms, axis=0, keepdims=True) + own_term
            chance[p, b] = (terms / total).T.astype(jnp.bfloat16).astype(jnp.float32)
            own_chance = (own_term / total).astype(jnp.bfloat16).astype(jnp.float32)
            own_chances[p, b] = jnp.sum(
                jnp.where(same, own_chance, 0.0), axis=1, keepdims=True
            )

    pltpu.make_async_copy(value_pool, value_pool, sems.at[1]).wait()
    for b in range(batches):
        for s in range(batch):
            for p in range(pairs):
                mine = chance[p, b, pl.ds(s, pair, stride=batch)].astype(jnp.bfloat16)
                columns_p = slice(p * 2 * HEAD, (p + 1) * 2 * HEAD)
                values = held(value_pool, b * batch + s, columns_p)
                both = jnp.dot(
                    mine, jnp.concatenate(values, axis=0), preferred_element_type=jnp.float32
                )
                result = jnp.concatenate(
                    [both[: pair // 2, :HEAD], both[pair // 2 :, HEAD:]], axis=0
                )
                mixed[p, b, pl.ds(s, pair, stride=batch)] = result

    for p in range(pairs):
        for j in range(pair):
            head = p * pair + j
            g = head * kv_heads // heads
            halves = []
            for b in range(batches):
                rows = slice(j * batch, (j + 1) * batch)
                own_value = value_own[g, b * batch : (b + 1) * batch]
                halves.append(mixed[p, b, rows] + own_chances[p, b][rows] * own_value)
            column = head % heads_dev * HEAD
            out[head // heads_dev, :, column : column + HEAD] = jnp.concatenate(
                halves, axis=0
            ).astype(jnp.bfloat16)


def attend(inbound, lengths, table, cosine, sine, key_pages, value_pages, per_query, per_key):
    owners, slots, _ = inbound.shape
    pages = table.shape[1]
    page, kv_width = key_pages.shape[1:]
    kv_heads = kv_width // HEAD
    heads = owners * (per_query // HEAD)
    span = pages * page
    pair = 2 * heads // kv_heads
    pairs = kv_heads // 2
    batches = slots * pair // HEAD
    batch = slots // batches
    columns = pair * batch
    lengths = jnp.tile(lengths.reshape(batches, 1, batch), (1, 1, pair))
    smem = pl.BlockSpec(memory_space=pltpu.SMEM)
    vmem = pl.BlockSpec(memory_space=pltpu.VMEM)
    hbm = pl.BlockSpec(memory_space=pl.ANY)
    return pl.pallas_call(
        functools.partial(attend_kernel, per_query, per_key),
        in_specs=[smem, vmem, vmem, vmem, vmem, hbm, hbm],
        out_specs=vmem,
        out_shape=jax.ShapeDtypeStruct((owners, slots, per_query), jnp.bfloat16),
        scratch_shapes=[
            pltpu.VMEM(key_pages.shape, jnp.bfloat16),
            pltpu.VMEM(value_pages.shape, jnp.bfloat16),
            pltpu.SemaphoreType.DMA((2,)),
            pltpu.VMEM((slots, kv_width), jnp.bfloat16),
            pltpu.VMEM((pairs, batches, columns, HEAD), jnp.float32),
            pltpu.VMEM((kv_heads, slots, HEAD), jnp.float32),
            pltpu.VMEM((pairs, batches, columns, span), jnp.float32),
            pltpu.VMEM((pairs, batches, columns, HEAD), jnp.float32),
        ],
        compiler_params=pltpu.CompilerParams(vmem_limit_bytes=52 * 2**20),
        cost_estimate=pl.CostEstimate(
            flops=8 * slots * heads * span * HEAD,
            bytes_accessed=4 * slots * span * kv_width,
            transcendentals=slots * heads * span,
        ),
        name="attend",
    )(table, lengths, inbound, cosine, sine, key_pages, value_pages)


def on_device(
    hidden_in,
    norm_gain,
    w_query,
    w_key,
    w_value,
    w_out,
    key_pages,
    value_pages,
    page_table,
    kv_owner,
    cached,
):
    grid = Grid()
    owners = grid.size
    slot_count = page_table.shape[1]
    per_query = w_query.shape[1]
    per_key = w_key.shape[1]
    row_width = per_query + -(-2 * per_key // HEAD) * HEAD
    requests = kv_owner.shape[0]
    rows_dev = requests // owners
    width = hidden_in.shape[1]
    all_slots = owners * slot_count

    moves_a = grid.moves(ORDER_A)
    order_b = [moves_a.index(move) for move in grid.moves(ORDER_B)]
    cut = width // 8 * 5
    xa, xb = norm(hidden_in, norm_gain, (cut, width - cut))

    def placed(kv_owner):
        order = jnp.arange(requests, dtype=jnp.int32)
        earlier = (kv_owner[:, None] == kv_owner[None, :]) & (order[None, :] < order[:, None])
        return kv_owner * slot_count + jnp.sum(earlier.astype(jnp.int32), axis=1)

    def reordered(place, blocks):
        pick = blocks[:, None] == jnp.arange(owners, dtype=jnp.int32)[None, :]
        moved = jnp.where(pick[:, :, None], place.reshape(1, owners, rows_dev), 0)
        return jnp.sum(moved, axis=1).reshape(requests)

    def beside_gather(x):
        (w,) = fetch(after(w_query, x), limit=44)
        pieces = [after(w_key, x).T, w_value.T]
        spare = row_width - per_query - 2 * per_key
        if spare:
            pieces.append(jnp.zeros((spare, width), w_key.dtype))
        place = placed(after(kv_owner, x))
        return w, jnp.concatenate(pieces, axis=0), place, reordered(place, grid.blocks(-1, ORDER_A))

    parts_a, parts_b, others = gather_rows(grid, xa, xb, beside_gather)
    w_query, w_kv_t, place, place_in = others
    plain = list(range(owners))
    total = project(0, parts_a, plain, w_query, w_kv_t, None, None, all_slots)
    total = project(cut, parts_b, order_b, w_query, w_kv_t, total, place_in, all_slots)
    outbound = total.reshape(owners, slot_count, row_width)
    place = after(place, outbound)
    place_a = reordered(place, grid.blocks(1, ORDER_A))
    place_b = reordered(place, grid.blocks(1, ORDER_B))
    mine = jnp.asarray(np.arange(all_slots, dtype=np.int32).reshape(owners, slot_count))
    mine = mine[lax.axis_index(AXES)]
    lengths = jnp.sum(jnp.where(place[:, None] == mine[None, :], cached[:, None], 0), axis=0)
    halfway = HEAD // 2
    offsets = jnp.arange(halfway, dtype=jnp.float32)
    frequency = rope_base ** (-(2.0 * offsets) / HEAD)
    angles = lengths.astype(jnp.float32)[:, None] * frequency
    cosine_part = jnp.cos(angles)
    sine_part = jnp.sin(angles)
    cosine = jnp.concatenate([cosine_part, cosine_part], axis=1)
    sine = jnp.concatenate([-sine_part, sine_part], axis=1)
    inbound = lax.all_to_all(outbound, AXES, split_axis=0, concat_axis=0, tiled=True)
    attended = attend(
        inbound,
        lengths,
        after(page_table, outbound)[0],
        cosine,
        sine,
        key_pages[0],
        value_pages[0],
        per_query,
        per_key,
    )
    returned = lax.all_to_all(attended, AXES, split_axis=0, concat_axis=0, tiled=True)
    returned = returned.reshape(all_slots, per_query)
    summed = scatter_sum(grid, place_a, place_b, returned, w_out, cut)
    return narrow(wide(hidden_in) + summed)


def solution(mesh):
    placed = (
        P(("groups", "tp", "attn"), None),
        P(),
        P(None, ("tp", "attn")),
        P(None, ("tp", "attn")),
        P(None, ("tp", "attn")),
        P(("tp", "attn"), None),
        P(("groups", "tp", "attn"), None, None, None),
        P(("groups", "tp", "attn"), None, None, None),
        P(("groups", "tp", "attn"), None, None),
        P("groups"),
        P("groups"),
    )
    return jax.shard_map(
        on_device,
        mesh=mesh,
        in_specs=placed,
        out_specs=P(("groups", "tp", "attn"), None),
        check_vma=False,
    )
```

```python
import functools

import jax
import jax.numpy as jnp
import numpy as np
from jax import lax
from jax.experimental import pallas as pl
from jax.experimental.pallas import tpu as pltpu
from jax.sharding import PartitionSpec as P

HEAD = 128
AXES = ("tp", "attn")

epsilon = 1e-05
rope_base = 500000.0


class Grid:
    def __init__(self):
        self.half = lax.axis_size("tp") // 4
        self.sizes = (self.half, 2, 2, lax.axis_size("attn"))
        self.size = int(np.prod(self.sizes))

    def shifted(self, place, moves):
        return np.ravel_multi_index(
            tuple((p + m) % n for p, m, n in zip(place, moves, self.sizes)), self.sizes
        )

    def send(self, x, half=0, pair=0, near=0, core=0):
        pairs = [
            (i, int(self.shifted(np.unravel_index(i, self.sizes), (half, pair, near, core))))
            for i in range(self.size)
        ]
        return lax.ppermute(x, AXES, pairs)

    def moves(self, order):
        counts = [self.sizes[axis] for axis in order]
        places = []
        for steps in np.ndindex(*counts):
            move = [0, 0, 0, 0]
            for axis, step in zip(order, steps):
                move[axis] = step
            places.append(tuple(move))
        return places

    def blocks(self, sign, order):
        rows = [
            [
                int(self.shifted(np.unravel_index(i, self.sizes), [sign * m for m in move]))
                for move in self.moves(order)
            ]
            for i in range(self.size)
        ]
        return jnp.asarray(np.array(rows, np.int32))[lax.axis_index(AXES)]


HALF, PAIR, NEAR, CORE = range(4)
ORDER_A = (CORE, NEAR, PAIR, HALF)
ORDER_B = (CORE, PAIR, HALF, NEAR)


def after(x, *earlier):
    return lax.optimization_barrier((x, *earlier))[0]


def gather_line(grid, x):
    crossed = [grid.send(x, half=d) for d in range(1, grid.half)]
    crossed = crossed[0] if len(crossed) == 1 else jnp.concatenate(crossed, axis=0)
    return [x, crossed, grid.send(x, pair=1), grid.send(crossed, pair=1)]


def gather_rows(grid, xa, xb, first, second):
    beside_b = grid.send(xb, near=1)
    line_a = jnp.concatenate(
        [xa]
        + [
            grid.send(xa, half=half, pair=pair)
            for pair in range(2)
            for half in range(grid.half)
            if half or pair
        ],
        axis=0,
    )
    pair_b = jnp.concatenate([xb, beside_b], axis=0)
    line_a, pair_b, first = lax.optimization_barrier((line_a, pair_b, first(xa)))
    beside_a = grid.send(line_a, near=1)
    parts_b = gather_line(grid, pair_b)
    beside_a, parts_b, second = lax.optimization_barrier((beside_a, parts_b, second(pair_b)))
    parts_a = [line_a, beside_a]
    parts_a += [grid.send(part, core=1) for part in parts_a]
    parts_b += [grid.send(part, core=1) for part in parts_b]
    return parts_a, parts_b, first, second


def narrow(x):
    return x.astype(jnp.bfloat16)


def wide(x):
    return x.astype(jnp.float32)


def product_kernel(
    cuts,
    place_a,
    place_b,
    returned,
    w_out,
    w_front,
    away_a,
    keep_a,
    away_b,
    keep_b,
    held,
    sems,
):
    front = w_front.shape[1]
    copies = []
    for i, (start, stop) in enumerate(cuts):
        copy = None
        if start >= front:
            size = pl.ds(start, stop - start), pl.ds(start - front, stop - start)
            copy = pltpu.make_async_copy(
                w_out.at[:, size[0]], held.at[:, size[1]], sems.at[i]
            )
            copy.start()
        copies.append(copy)
    slots = lax.broadcasted_iota(jnp.int32, (returned.shape[0], place_a.shape[1]), 0)

    def picked(place):
        route = jnp.where(slots == place[...], 1.0, 0.0).astype(jnp.bfloat16)
        rows = lax.dot_general(
            route, returned[...], (((0,), (0,)), ((), ())), preferred_element_type=jnp.float32
        )
        return rows.astype(jnp.bfloat16)

    rows_a, rows_b = picked(place_a), picked(place_b)
    half = keep_a.shape[0]
    middle = keep_a.shape[1]
    for copy, (start, stop) in zip(copies, cuts):
        if copy is not None:
            copy.wait()
        rows, away, keep = (rows_a, away_a, keep_a) if start < middle else (rows_b, away_b, keep_b)
        w = w_front[:, start:stop] if copy is None else held[:, start - front : stop - front]
        x = jnp.dot(rows, w, preferred_element_type=jnp.float32)
        begin = start if start < middle else start - middle
        here = slice(begin, begin + stop - start)
        keep[:, here] = x[:half]
        away[:, here] = x[half:].astype(jnp.bfloat16)


def product(place_a, place_b, returned, w_out, w_front, cut):
    rows = place_a.shape[0]
    depth, width = w_out.shape
    cuts = []
    front = w_front.shape[1]
    for start, stop in ((0, front), (front, cut), (cut, width)):
        while start < stop:
            cuts.append((start, min(start + 1024, stop)))
            start = cuts[-1][1]
    vmem = pl.BlockSpec(memory_space=pltpu.VMEM)
    out = []
    for size in (cut, width - cut):
        out.append(jax.ShapeDtypeStruct((rows // 2, size), jnp.bfloat16))
        out.append(jax.ShapeDtypeStruct((rows // 2, size), jnp.float32))
    return pl.pallas_call(
        functools.partial(product_kernel, tuple(cuts)),
        in_specs=[vmem, vmem, vmem, pl.BlockSpec(memory_space=pl.ANY), vmem],
        out_specs=[vmem] * 4,
        out_shape=out,
        scratch_shapes=[
            pltpu.VMEM((depth, width - front), jnp.bfloat16),
            pltpu.SemaphoreType.DMA((len(cuts),)),
        ],
        compiler_params=pltpu.CompilerParams(vmem_limit_bytes=48 * 2**20),
        cost_estimate=pl.CostEstimate(
            flops=2 * rows * depth * width, bytes_accessed=2 * depth * width, transcendentals=0
        ),
        name="product",
    )(place_a.reshape(1, rows), place_b.reshape(1, rows), returned, w_out, w_front)


def scatter_sum(grid, place_a, place_b, returned, w_out, w_front, cut):
    def along_line(x):
        size = x.shape[0] // 2 // grid.half
        middle = x.shape[0] // 2
        first = grid.send(narrow(x[middle + size :]), pair=1)
        second = grid.send(narrow(x[middle : middle + size]), pair=1)
        far = x[size:middle] + wide(first)
        third = [
            grid.send(narrow(far[d * size : (d + 1) * size]), half=d + 1)
            for d in range(grid.half - 1)
        ]
        return x[:size], [second] + third

    def direct(x):
        size = x.shape[0] // 2 // grid.half
        parts = []
        for pair in range(2):
            for half in range(grid.half):
                begin = (pair * grid.half + half) * size
                if begin:
                    sent = narrow(x[begin : begin + size])
                    parts.append(grid.send(sent, half=half, pair=pair))
        return x[:size], parts

    def total(x, parts):
        for part in parts:
            x = x + wide(part)
        return x

    away_a, keep_a, away_b, keep_b = product(place_a, place_b, returned, w_out, w_front, cut)
    xa = keep_a + wide(grid.send(away_a, core=1))
    middle = xa.shape[0] // 2
    sent_a = narrow(xa[middle:])
    got_a = grid.send(sent_a, near=1)
    xb = keep_b + wide(grid.send(after(away_b, sent_a), core=1))
    xb, got_b = along_line(xb)
    got_a, got_b = lax.optimization_barrier((got_a, got_b))
    xa, parts_a = direct(xa[:middle] + wide(got_a))
    xb = total(xb, got_b)
    middle = xb.shape[0] // 2
    xb = xb[:middle] + wide(grid.send(narrow(xb[middle:]), near=1))
    xa = total(xa, parts_a)
    return jnp.concatenate([xa, xb], axis=1)


def norm_kernel(x, gain, *outs):
    inputs = x[...].astype(jnp.float32)
    factor = lax.rsqrt(jnp.mean(inputs * inputs, axis=1, keepdims=True) + epsilon)
    normed = (inputs * factor * gain[...]).astype(jnp.bfloat16)
    start = 0
    for out in outs:
        out[...] = normed[:, start : start + out.shape[1]]
        start += out.shape[1]


def norm(x, gain, widths):
    vmem = pl.BlockSpec(memory_space=pltpu.VMEM)
    return pl.pallas_call(
        norm_kernel,
        in_specs=[vmem, vmem],
        out_specs=[vmem] * len(widths),
        out_shape=[jax.ShapeDtypeStruct((x.shape[0], w), jnp.bfloat16) for w in widths],
        compiler_params=pltpu.CompilerParams(vmem_limit_bytes=16 * 2**20),
        name="norm",
    )(x, gain.reshape(1, -1))


def fetch_kernel(starts, *refs):
    count = len(starts)
    sems = refs[-1]
    copies = []
    for i, start in enumerate(starts):
        source, target = refs[i], refs[count + i]
        if start is not None:
            columns = pl.ds(start, target.shape[-1])
            source = source.at[(slice(None),) * (len(target.shape) - 1) + (columns,)]
        copies.append(pltpu.make_async_copy(source, target, sems.at[i]))
        copies[-1].start()
    for copy in copies:
        copy.wait()


def fetch(*wanted, limit):
    arrays = [x for x, _ in wanted]
    starts = [columns and columns[0] for _, columns in wanted]
    out = [
        jax.ShapeDtypeStruct(x.shape[:-1] + (columns[1],) if columns else x.shape, x.dtype)
        for x, columns in wanted
    ]
    return pl.pallas_call(
        functools.partial(fetch_kernel, starts),
        in_specs=[pl.BlockSpec(memory_space=pl.ANY)] * len(arrays),
        out_specs=[pl.BlockSpec(memory_space=pltpu.VMEM)] * len(arrays),
        out_shape=out,
        scratch_shapes=[pltpu.SemaphoreType.DMA((len(arrays),))],
        compiler_params=pltpu.CompilerParams(vmem_limit_bytes=limit * 2**20),
        cost_estimate=pl.CostEstimate(
            flops=0, bytes_accessed=sum(x.size * 4 for x in out), transcendentals=0
        ),
        name="fetch",
    )(*arrays)


def project_kernel(first, last, order, start, block, *refs):
    count = len(refs) - 4 - (not first) - last
    parts, (wq, w_kv), refs = refs[:count], refs[count : count + 2], refs[count + 2 :]
    if not first:
        before, refs = refs[0], refs[1:]
    if last:
        place, refs = refs[0], refs[1:]
    out, total = refs
    step = pl.program_id(0)
    per_query = wq.shape[1]

    @pl.when(step == 0)
    def _():
        total[...] = jnp.zeros_like(total) if first else before[...]

    here = pl.ds(pl.multiple_of(step * block, block), block)
    there = pl.ds(pl.multiple_of(start + step * block, block), block)
    x = jnp.concatenate([part[:, here] for part in parts], axis=0)
    products = [
        jnp.dot(x, wq[there, :], preferred_element_type=jnp.float32),
        lax.dot_general(x, w_kv[:, there], (((1,), (1,)), ((), ())), preferred_element_type=jnp.float32),
    ]
    size = x.shape[0] // len(order)
    for product, columns in zip(products, (slice(0, per_query), slice(per_query, None))):
        for i, place_i in enumerate(order):
            total[place_i * size : (place_i + 1) * size, columns] += product[
                i * size : (i + 1) * size
            ]

    @pl.when(step == pl.num_programs(0) - 1)
    def _():
        if last:
            rows = lax.broadcasted_iota(jnp.int32, (out.shape[0], place.shape[1]), 0)
            route = jnp.where(rows == place[...], 1.0, 0.0).astype(jnp.bfloat16)
            moved = jnp.dot(
                route, total[...].astype(jnp.bfloat16), preferred_element_type=jnp.float32
            )
            out[...] = moved.astype(jnp.bfloat16)
        else:
            out[...] = total[...]


def project(start, parts, order, w_query, w_kv_t, before, place, slots):
    row_width = w_query.shape[1] + w_kv_t.shape[0]
    width = parts[0].shape[1]
    block = width
    rows = sum(part.shape[0] for part in parts)
    first, last = before is None, place is not None
    vmem = pl.BlockSpec(memory_space=pltpu.VMEM)
    args = [*parts, w_query, w_kv_t]
    specs = [vmem] * len(parts)
    specs += [
        vmem,
        vmem,
    ]
    if not first:
        args.append(before)
        specs.append(vmem)
    if last:
        args.append(place.reshape(1, rows))
        specs.append(vmem)
        out = jax.ShapeDtypeStruct((slots, row_width), jnp.bfloat16)
    else:
        out = jax.ShapeDtypeStruct((rows, row_width), jnp.float32)
    return pl.pallas_call(
        functools.partial(project_kernel, first, last, order, start, block),
        grid=(width // block,),
        in_specs=specs,
        out_specs=vmem,
        out_shape=out,
        scratch_shapes=[pltpu.VMEM((rows, row_width), jnp.float32)],
        compiler_params=pltpu.CompilerParams(vmem_limit_bytes=24 * 2**20),
        cost_estimate=pl.CostEstimate(
            flops=2 * rows * width * row_width,
            bytes_accessed=2 * width * row_width,
            transcendentals=0,
        ),
        name="project",
    )(*args)


def attend_kernel(
    per_query,
    per_key,
    table,
    lengths,
    inbound,
    cosine,
    sine,
    key_pages,
    value_pages,
    key_front,
    out,
    key_pool,
    value_pool,
    sems,
    key_new,
    query_rot,
    value_own,
    chance,
    mixed,
):
    owners, slots, _ = inbound.shape
    pages = table.shape[1]
    page, kv_width = key_pages.shape[1:]
    kv_heads = kv_width // HEAD
    heads_dev = per_query // HEAD
    heads = owners * heads_dev
    pair = 2 * heads // kv_heads
    pairs = kv_heads // 2
    span = pages * page
    pieces = owners // kv_heads
    batches = query_rot.shape[1]
    batch = slots // batches

    cuts = 4
    size = key_pages.shape[0] // cuts
    front = key_front.shape[2]
    back = key_pages.at[:, :, pl.ds(front, kv_width - front)]
    for i, (pool, on_chip) in enumerate(((back, key_pool), (value_pages, value_pool))):
        for cut in range(cuts):
            part = pl.ds(cut * size, size)
            pltpu.make_async_copy(pool.at[part], on_chip.at[part], sems.at[i]).start()

    def held(pool, slot, columns):
        return [pool[table[slot, j], :, columns] for j in range(pages)]

    cos = cosine[...]
    sin = sine[...]

    def turn(x):
        return (x * cos + pltpu.roll(x, HEAD // 2, 1) * sin).astype(jnp.bfloat16)

    for source in range(owners):
        for j in range(heads_dev):
            x = inbound[source, :, j * HEAD : (j + 1) * HEAD].astype(jnp.float32)
            x = turn(x).astype(jnp.float32)
            head = source * heads_dev + j
            for b in range(batches):
                rows = pl.ds(head % pair * batch, batch)
                query_rot[head // pair, b, rows] = x[b * batch : (b + 1) * batch]

    piece = lax.broadcasted_iota(jnp.int32, (slots, HEAD), 1) // per_key
    for g in range(kv_heads):
        key = jnp.zeros((slots, HEAD), jnp.float32)
        value = jnp.zeros((slots, HEAD), jnp.float32)
        for j in range(pieces):
            tile = inbound[g * pieces + j, :, per_query : per_query + HEAD].astype(jnp.float32)
            shift = j * per_key
            back = (shift - per_key) % HEAD
            key = jnp.where(piece == j, pltpu.roll(tile, shift, 1) if shift else tile, key)
            value = jnp.where(piece == j, pltpu.roll(tile, back, 1) if back else tile, value)
        key_new[:, g * HEAD : (g + 1) * HEAD] = turn(key)
        value_own[g] = value

    scale = HEAD ** (-0.5)
    columns = pair * batch
    row = lax.broadcasted_iota(jnp.int32, (span, columns), 0)
    place = lax.broadcasted_iota(jnp.int32, (span, columns), 1) % batch
    own_row = lax.broadcasted_iota(jnp.int32, (slots, columns), 0)
    own_place = lax.broadcasted_iota(jnp.int32, (slots, columns), 1) % batch
    first = lax.broadcasted_iota(jnp.int32, (HEAD, columns), 1) < columns // 2
    same = lax.broadcasted_iota(jnp.int32, (columns, columns), 0) == lax.broadcasted_iota(
        jnp.int32, (columns, columns), 1
    )

    own_chances = {}
    for p in range(pairs):
        begin = p * 2 * HEAD
        if begin == front:
            pltpu.make_async_copy(key_pool, key_pool, sems.at[0]).wait()
        source = key_front if begin < front else key_pool
        inside = begin if begin < front else begin - front
        for b in range(batches):
            valid = row < lengths[b]
            turned = query_rot[p, b].T.astype(jnp.bfloat16)
            none = jnp.zeros_like(turned)
            wide = jnp.concatenate(
                [jnp.where(first, turned, none), jnp.where(first, none, turned)], axis=0
            )
            columns_p = slice(p * 2 * HEAD, (p + 1) * 2 * HEAD)
            keys = []
            for s in range(batch):
                keys += held(source, b * batch + s, slice(inside, inside + 2 * HEAD))
            keys.append(key_new[:, columns_p])
            products = jnp.dot(
                jnp.concatenate(keys, axis=0), wide, preferred_element_type=jnp.float32
            )
            scores = products[:span]
            for s in range(1, batch):
                scores = jnp.where(place == s, products[s * span : (s + 1) * span], scores)
            own = jnp.where(own_row == own_place + b * batch, products[batch * span :], 0.0)
            own = jnp.sum(own, axis=0, keepdims=True) * scale
            masked = jnp.where(valid, scores * scale, -1e30)
            top = jnp.maximum(jnp.max(masked, axis=0, keepdims=True), own)
            terms = jnp.where(valid, jnp.exp(masked - top), 0.0)
            own_term = jnp.exp(own - top)
            total = jnp.sum(terms, axis=0, keepdims=True) + own_term
            chance[p, b] = (terms / total).T.astype(jnp.bfloat16).astype(jnp.float32)
            own_chance = (own_term / total).astype(jnp.bfloat16).astype(jnp.float32)
            own_chances[p, b] = jnp.sum(
                jnp.where(same, own_chance, 0.0), axis=1, keepdims=True
            )

    pltpu.make_async_copy(value_pool, value_pool, sems.at[1]).wait()
    for b in range(batches):
        for s in range(batch):
            for p in range(pairs):
                mine = chance[p, b, pl.ds(s, pair, stride=batch)].astype(jnp.bfloat16)
                columns_p = slice(p * 2 * HEAD, (p + 1) * 2 * HEAD)
                values = held(value_pool, b * batch + s, columns_p)
                both = jnp.dot(
                    mine, jnp.concatenate(values, axis=0), preferred_element_type=jnp.float32
                )
                result = jnp.concatenate(
                    [both[: pair // 2, :HEAD], both[pair // 2 :, HEAD:]], axis=0
                )
                mixed[p, b, pl.ds(s, pair, stride=batch)] = result

    for p in range(pairs):
        for j in range(pair):
            head = p * pair + j
            g = head * kv_heads // heads
            halves = []
            for b in range(batches):
                rows = slice(j * batch, (j + 1) * batch)
                own_value = value_own[g, b * batch : (b + 1) * batch]
                halves.append(mixed[p, b, rows] + own_chances[p, b][rows] * own_value)
            column = head % heads_dev * HEAD
            out[head // heads_dev, :, column : column + HEAD] = jnp.concatenate(
                halves, axis=0
            ).astype(jnp.bfloat16)


def attend(
    inbound, lengths, table, cosine, sine, key_pages, value_pages, key_front, per_query, per_key
):
    owners, slots, _ = inbound.shape
    pages = table.shape[1]
    page, kv_width = key_pages.shape[1:]
    kv_heads = kv_width // HEAD
    heads = owners * (per_query // HEAD)
    span = pages * page
    pair = 2 * heads // kv_heads
    pairs = kv_heads // 2
    batches = slots * pair // HEAD
    batch = slots // batches
    columns = pair * batch
    lengths = jnp.tile(lengths.reshape(batches, 1, batch), (1, 1, pair))
    smem = pl.BlockSpec(memory_space=pltpu.SMEM)
    vmem = pl.BlockSpec(memory_space=pltpu.VMEM)
    hbm = pl.BlockSpec(memory_space=pl.ANY)
    return pl.pallas_call(
        functools.partial(attend_kernel, per_query, per_key),
        in_specs=[smem, vmem, vmem, vmem, vmem, hbm, hbm, vmem],
        out_specs=vmem,
        out_shape=jax.ShapeDtypeStruct((owners, slots, per_query), jnp.bfloat16),
        scratch_shapes=[
            pltpu.VMEM(key_pages.shape[:2] + (kv_width - key_front.shape[2],), jnp.bfloat16),
            pltpu.VMEM(value_pages.shape, jnp.bfloat16),
            pltpu.SemaphoreType.DMA((2,)),
            pltpu.VMEM((slots, kv_width), jnp.bfloat16),
            pltpu.VMEM((pairs, batches, columns, HEAD), jnp.float32),
            pltpu.VMEM((kv_heads, slots, HEAD), jnp.float32),
            pltpu.VMEM((pairs, batches, columns, span), jnp.float32),
            pltpu.VMEM((pairs, batches, columns, HEAD), jnp.float32),
        ],
        compiler_params=pltpu.CompilerParams(vmem_limit_bytes=52 * 2**20),
        cost_estimate=pl.CostEstimate(
            flops=8 * slots * heads * span * HEAD,
            bytes_accessed=4 * slots * span * kv_width,
            transcendentals=slots * heads * span,
        ),
        name="attend",
    )(table, lengths, inbound, cosine, sine, key_pages, value_pages, key_front)


def on_device(
    hidden_in,
    norm_gain,
    w_query,
    w_key,
    w_value,
    w_out,
    key_pages,
    value_pages,
    page_table,
    kv_owner,
    cached,
):
    grid = Grid()
    owners = grid.size
    slot_count = page_table.shape[1]
    per_query = w_query.shape[1]
    per_key = w_key.shape[1]
    row_width = per_query + -(-2 * per_key // HEAD) * HEAD
    requests = kv_owner.shape[0]
    rows_dev = requests // owners
    width = hidden_in.shape[1]
    all_slots = owners * slot_count

    moves_a = grid.moves(ORDER_A)
    order_b = [moves_a.index(move) for move in grid.moves(ORDER_B)]
    cut = width // 8 * 5
    xa, xb = norm(hidden_in, norm_gain, (cut, width - cut))

    def placed(kv_owner):
        order = jnp.arange(requests, dtype=jnp.int32)
        earlier = (kv_owner[:, None] == kv_owner[None, :]) & (order[None, :] < order[:, None])
        return kv_owner * slot_count + jnp.sum(earlier.astype(jnp.int32), axis=1)

    def reordered(place, blocks):
        pick = blocks[:, None] == jnp.arange(owners, dtype=jnp.int32)[None, :]
        moved = jnp.where(pick[:, :, None], place.reshape(1, owners, rows_dev), 0)
        return jnp.sum(moved, axis=1).reshape(requests)

    def first(x):
        place = placed(after(kv_owner, x))
        place_in = reordered(place, grid.blocks(-1, ORDER_A))
        (w,) = fetch((after(w_query, place_in), None), limit=44)
        return w, place, place_in

    def second(x):
        pieces = [after(w_key, x).T, w_value.T]
        spare = row_width - per_query - 2 * per_key
        if spare:
            pieces.append(jnp.zeros((spare, width), w_key.dtype))
        return jnp.concatenate(pieces, axis=0)

    parts_a, parts_b, others, w_kv_t = gather_rows(grid, xa, xb, first, second)
    w_query, place, place_in = others
    plain = list(range(owners))
    total = project(0, parts_a, plain, w_query, w_kv_t, None, None, all_slots)
    total = project(cut, parts_b, order_b, w_query, w_kv_t, total, place_in, all_slots)
    outbound = total.reshape(owners, slot_count, row_width)
    place = after(place, outbound)
    place_a = reordered(place, grid.blocks(1, ORDER_A))
    place_b = reordered(place, grid.blocks(1, ORDER_B))
    mine = jnp.asarray(np.arange(all_slots, dtype=np.int32).reshape(owners, slot_count))
    mine = mine[lax.axis_index(AXES)]
    lengths = jnp.sum(jnp.where(place[:, None] == mine[None, :], cached[:, None], 0), axis=0)
    halfway = HEAD // 2
    offsets = jnp.arange(halfway, dtype=jnp.float32)
    frequency = rope_base ** (-(2.0 * offsets) / HEAD)
    angles = lengths.astype(jnp.float32)[:, None] * frequency
    cosine_part = jnp.cos(angles)
    sine_part = jnp.sin(angles)
    cosine = jnp.concatenate([cosine_part, cosine_part], axis=1)
    sine = jnp.concatenate([-sine_part, sine_part], axis=1)
    inbound = lax.all_to_all(outbound, AXES, split_axis=0, concat_axis=0, tiled=True)
    kv_half = key_pages.shape[3] // 2
    (key_front,) = fetch((after(key_pages, outbound)[0], (0, kv_half)), limit=51)
    attended = attend(
        inbound,
        lengths,
        after(page_table, outbound)[0],
        cosine,
        sine,
        key_pages[0],
        value_pages[0],
        key_front,
        per_query,
        per_key,
    )
    (w_front,) = fetch((after(w_out, attended), (0, width // 32 * 10)), limit=48)
    returned = lax.all_to_all(attended, AXES, split_axis=0, concat_axis=0, tiled=True)
    returned = returned.reshape(all_slots, per_query)
    summed = scatter_sum(grid, place_a, place_b, returned, w_out, w_front, width // 32 * 19)
    return narrow(wide(hidden_in) + summed)


def solution(mesh):
    placed = (
        P(("groups", "tp", "attn"), None),
        P(),
        P(None, ("tp", "attn")),
        P(None, ("tp", "attn")),
        P(None, ("tp", "attn")),
        P(("tp", "attn"), None),
        P(("groups", "tp", "attn"), None, None, None),
        P(("groups", "tp", "attn"), None, None, None),
        P(("groups", "tp", "attn"), None, None),
        P("groups"),
        P("groups"),
    )
    return jax.shard_map(
        on_device,
        mesh=mesh,
        in_specs=placed,
        out_specs=P(("groups", "tp", "attn"), None),
        check_vma=False,
    )
```

```python
import functools

import jax
import jax.numpy as jnp
import numpy as np
from jax import lax
from jax.experimental import pallas as pl
from jax.experimental.pallas import tpu as pltpu
from jax.sharding import PartitionSpec as P

HEAD = 128
AXES = ("tp", "attn")

epsilon = 1e-05
rope_base = 500000.0


class Grid:
    def __init__(self):
        self.half = lax.axis_size("tp") // 4
        self.sizes = (self.half, 2, 2, lax.axis_size("attn"))
        self.size = int(np.prod(self.sizes))

    def shifted(self, place, moves):
        return np.ravel_multi_index(
            tuple((p + m) % n for p, m, n in zip(place, moves, self.sizes)), self.sizes
        )

    def send(self, x, half=0, pair=0, near=0, core=0):
        pairs = [
            (i, int(self.shifted(np.unravel_index(i, self.sizes), (half, pair, near, core))))
            for i in range(self.size)
        ]
        return lax.ppermute(x, AXES, pairs)

    def moves(self, order):
        counts = [self.sizes[axis] for axis in order]
        places = []
        for steps in np.ndindex(*counts):
            move = [0, 0, 0, 0]
            for axis, step in zip(order, steps):
                move[axis] = step
            places.append(tuple(move))
        return places

    def blocks(self, sign, order):
        rows = [
            [
                int(self.shifted(np.unravel_index(i, self.sizes), [sign * m for m in move]))
                for move in self.moves(order)
            ]
            for i in range(self.size)
        ]
        return jnp.asarray(np.array(rows, np.int32))[lax.axis_index(AXES)]


HALF, PAIR, NEAR, CORE = range(4)
ORDER_A = (CORE, NEAR, PAIR, HALF)
ORDER_B = (CORE, PAIR, HALF, NEAR)


def after(x, *earlier):
    return lax.optimization_barrier((x, *earlier))[0]


def gather_rows(grid, xa, xb, first, second):
    beside_b = grid.send(xb, near=1)
    line_a = jnp.concatenate(
        [xa]
        + [
            grid.send(xa, half=half, pair=pair)
            for pair in range(2)
            for half in range(grid.half)
            if half or pair
        ],
        axis=0,
    )
    pair_b = jnp.concatenate([xb, beside_b], axis=0)
    line_a, pair_b, first = lax.optimization_barrier((line_a, pair_b, first(xa)))
    beside_a = grid.send(line_a, near=1)
    parts_b = [pair_b] + [
        grid.send(pair_b, half=half, pair=pair)
        for pair in range(2)
        for half in range(grid.half)
        if half or pair
    ]
    beside_a, parts_b[1], second = lax.optimization_barrier((beside_a, parts_b[1], second(pair_b)))
    parts_a = [line_a, beside_a]
    parts_a += [grid.send(part, core=1) for part in parts_a]
    parts_b += [grid.send(part, core=1) for part in parts_b]
    return parts_a, parts_b, first, second


def narrow(x):
    return x.astype(jnp.bfloat16)


def wide(x):
    return x.astype(jnp.float32)


def product_kernel(
    cuts,
    place_a,
    place_b,
    returned,
    w_out,
    w_front,
    away_a,
    keep_a,
    away_b,
    keep_b,
    held,
    sems,
):
    front = w_front.shape[1]
    copies = []
    for i, (start, stop) in enumerate(cuts):
        copy = None
        if start >= front:
            size = pl.ds(start, stop - start), pl.ds(start - front, stop - start)
            copy = pltpu.make_async_copy(
                w_out.at[:, size[0]], held.at[:, size[1]], sems.at[i]
            )
            copy.start()
        copies.append(copy)
    slots = lax.broadcasted_iota(jnp.int32, (returned.shape[0], place_a.shape[1]), 0)

    def picked(place):
        route = jnp.where(slots == place[...], 1.0, 0.0).astype(jnp.bfloat16)
        rows = lax.dot_general(
            route, returned[...], (((0,), (0,)), ((), ())), preferred_element_type=jnp.float32
        )
        return rows.astype(jnp.bfloat16)

    rows_a, rows_b = picked(place_a), picked(place_b)
    half = keep_a.shape[0]
    middle = keep_a.shape[1]
    for copy, (start, stop) in zip(copies, cuts):
        if copy is not None:
            copy.wait()
        rows, away, keep = (rows_a, away_a, keep_a) if start < middle else (rows_b, away_b, keep_b)
        w = w_front[:, start:stop] if copy is None else held[:, start - front : stop - front]
        x = jnp.dot(rows, w, preferred_element_type=jnp.float32)
        begin = start if start < middle else start - middle
        here = slice(begin, begin + stop - start)
        keep[:, here] = x[:half]
        away[:, here] = x[half:].astype(jnp.bfloat16)


def product(place_a, place_b, returned, w_out, w_front, cut):
    rows = place_a.shape[0]
    depth, width = w_out.shape
    cuts = []
    front = w_front.shape[1]
    for start, stop in ((0, front), (front, cut), (cut, width)):
        while start < stop:
            cuts.append((start, min(start + 1024, stop)))
            start = cuts[-1][1]
    vmem = pl.BlockSpec(memory_space=pltpu.VMEM)
    out = []
    for size in (cut, width - cut):
        out.append(jax.ShapeDtypeStruct((rows // 2, size), jnp.bfloat16))
        out.append(jax.ShapeDtypeStruct((rows // 2, size), jnp.float32))
    return pl.pallas_call(
        functools.partial(product_kernel, tuple(cuts)),
        in_specs=[vmem, vmem, vmem, pl.BlockSpec(memory_space=pl.ANY), vmem],
        out_specs=[vmem] * 4,
        out_shape=out,
        scratch_shapes=[
            pltpu.VMEM((depth, width - front), jnp.bfloat16),
            pltpu.SemaphoreType.DMA((len(cuts),)),
        ],
        compiler_params=pltpu.CompilerParams(vmem_limit_bytes=48 * 2**20),
        cost_estimate=pl.CostEstimate(
            flops=2 * rows * depth * width, bytes_accessed=2 * depth * width, transcendentals=0
        ),
        name="product",
    )(place_a.reshape(1, rows), place_b.reshape(1, rows), returned, w_out, w_front)


def scatter_sum(grid, place_a, place_b, returned, w_out, w_front, cut):
    def direct(x):
        size = x.shape[0] // 2 // grid.half
        parts = []
        for pair in range(2):
            for half in range(grid.half):
                begin = (pair * grid.half + half) * size
                if begin:
                    sent = narrow(x[begin : begin + size])
                    parts.append(grid.send(sent, half=half, pair=pair))
        return x[:size], parts

    def total(x, parts):
        for part in parts:
            x = x + wide(part)
        return x

    away_a, keep_a, away_b, keep_b = product(place_a, place_b, returned, w_out, w_front, cut)
    xa = keep_a + wide(grid.send(away_a, core=1))
    middle = xa.shape[0] // 2
    sent_a = narrow(xa[middle:])
    got_a = grid.send(sent_a, near=1)
    xb = keep_b + wide(grid.send(after(away_b, sent_a), core=1))
    xb, got_b = direct(xb)
    got_a, got_b[0] = lax.optimization_barrier((got_a, got_b[0]))
    xa, parts_a = direct(xa[:middle] + wide(got_a))
    xb = total(xb, got_b)
    middle = xb.shape[0] // 2
    sent_b = after(narrow(xb[middle:]), parts_a[0])
    xb = xb[:middle] + wide(grid.send(sent_b, near=1))
    xa = total(xa, parts_a)
    return jnp.concatenate([xa, xb], axis=1)


def norm_kernel(x, gain, *outs):
    inputs = x[...].astype(jnp.float32)
    factor = lax.rsqrt(jnp.mean(inputs * inputs, axis=1, keepdims=True) + epsilon)
    normed = (inputs * factor * gain[...]).astype(jnp.bfloat16)
    start = 0
    for out in outs:
        out[...] = normed[:, start : start + out.shape[1]]
        start += out.shape[1]


def norm(x, gain, widths):
    vmem = pl.BlockSpec(memory_space=pltpu.VMEM)
    return pl.pallas_call(
        norm_kernel,
        in_specs=[vmem, vmem],
        out_specs=[vmem] * len(widths),
        out_shape=[jax.ShapeDtypeStruct((x.shape[0], w), jnp.bfloat16) for w in widths],
        compiler_params=pltpu.CompilerParams(vmem_limit_bytes=16 * 2**20),
        name="norm",
    )(x, gain.reshape(1, -1))


def fetch_kernel(starts, *refs):
    count = len(starts)
    sems = refs[-1]
    copies = []
    for i, start in enumerate(starts):
        source, target = refs[i], refs[count + i]
        if start is not None:
            columns = pl.ds(start, target.shape[-1])
            source = source.at[(slice(None),) * (len(target.shape) - 1) + (columns,)]
        copies.append(pltpu.make_async_copy(source, target, sems.at[i]))
        copies[-1].start()
    for copy in copies:
        copy.wait()


def fetch(*wanted, limit):
    arrays = [x for x, _ in wanted]
    starts = [columns and columns[0] for _, columns in wanted]
    out = [
        jax.ShapeDtypeStruct(x.shape[:-1] + (columns[1],) if columns else x.shape, x.dtype)
        for x, columns in wanted
    ]
    return pl.pallas_call(
        functools.partial(fetch_kernel, starts),
        in_specs=[pl.BlockSpec(memory_space=pl.ANY)] * len(arrays),
        out_specs=[pl.BlockSpec(memory_space=pltpu.VMEM)] * len(arrays),
        out_shape=out,
        scratch_shapes=[pltpu.SemaphoreType.DMA((len(arrays),))],
        compiler_params=pltpu.CompilerParams(vmem_limit_bytes=limit * 2**20),
        cost_estimate=pl.CostEstimate(
            flops=0, bytes_accessed=sum(x.size * 4 for x in out), transcendentals=0
        ),
        name="fetch",
    )(*arrays)


def project_kernel(first, last, order, start, block, *refs):
    count = len(refs) - 4 - (not first) - last
    parts, (wq, w_kv), refs = refs[:count], refs[count : count + 2], refs[count + 2 :]
    if not first:
        before, refs = refs[0], refs[1:]
    if last:
        place, refs = refs[0], refs[1:]
    out, total = refs
    step = pl.program_id(0)
    per_query = wq.shape[1]

    @pl.when(step == 0)
    def _():
        total[...] = jnp.zeros_like(total) if first else before[...]

    here = pl.ds(pl.multiple_of(step * block, block), block)
    there = pl.ds(pl.multiple_of(start + step * block, block), block)
    x = jnp.concatenate([part[:, here] for part in parts], axis=0)
    products = [
        jnp.dot(x, wq[there, :], preferred_element_type=jnp.float32),
        lax.dot_general(x, w_kv[:, there], (((1,), (1,)), ((), ())), preferred_element_type=jnp.float32),
    ]
    size = x.shape[0] // len(order)
    for product, columns in zip(products, (slice(0, per_query), slice(per_query, None))):
        for i, place_i in enumerate(order):
            total[place_i * size : (place_i + 1) * size, columns] += product[
                i * size : (i + 1) * size
            ]

    @pl.when(step == pl.num_programs(0) - 1)
    def _():
        if last:
            rows = lax.broadcasted_iota(jnp.int32, (out.shape[0], place.shape[1]), 0)
            route = jnp.where(rows == place[...], 1.0, 0.0).astype(jnp.bfloat16)
            moved = jnp.dot(
                route, total[...].astype(jnp.bfloat16), preferred_element_type=jnp.float32
            )
            out[...] = moved.astype(jnp.bfloat16)
        else:
            out[...] = total[...]


def project(start, parts, order, w_query, w_kv_t, before, place, slots):
    row_width = w_query.shape[1] + w_kv_t.shape[0]
    width = parts[0].shape[1]
    block = width
    rows = sum(part.shape[0] for part in parts)
    first, last = before is None, place is not None
    vmem = pl.BlockSpec(memory_space=pltpu.VMEM)
    args = [*parts, w_query, w_kv_t]
    specs = [vmem] * len(parts)
    specs += [
        vmem,
        vmem,
    ]
    if not first:
        args.append(before)
        specs.append(vmem)
    if last:
        args.append(place.reshape(1, rows))
        specs.append(vmem)
        out = jax.ShapeDtypeStruct((slots, row_width), jnp.bfloat16)
    else:
        out = jax.ShapeDtypeStruct((rows, row_width), jnp.float32)
    return pl.pallas_call(
        functools.partial(project_kernel, first, last, order, start, block),
        grid=(width // block,),
        in_specs=specs,
        out_specs=vmem,
        out_shape=out,
        scratch_shapes=[pltpu.VMEM((rows, row_width), jnp.float32)],
        compiler_params=pltpu.CompilerParams(vmem_limit_bytes=24 * 2**20),
        cost_estimate=pl.CostEstimate(
            flops=2 * rows * width * row_width,
            bytes_accessed=2 * width * row_width,
            transcendentals=0,
        ),
        name="project",
    )(*args)


def attend_kernel(
    per_query,
    per_key,
    table,
    lengths,
    inbound,
    cosine,
    sine,
    key_pages,
    value_pages,
    out,
    key_pool,
    value_pool,
    sems,
    key_new,
    query_rot,
    value_own,
    chance,
    mixed,
):
    owners, slots, _ = inbound.shape
    pages = table.shape[1]
    page, kv_width = key_pages.shape[1:]
    kv_heads = kv_width // HEAD
    heads_dev = per_query // HEAD
    heads = owners * heads_dev
    pair = 2 * heads // kv_heads
    pairs = kv_heads // 2
    span = pages * page
    pieces = owners // kv_heads
    batches = query_rot.shape[1]
    batch = slots // batches

    cuts = 4
    size = key_pages.shape[0] // cuts
    for i, (pool, on_chip) in enumerate(((key_pages, key_pool), (value_pages, value_pool))):
        for cut in range(cuts):
            part = pl.ds(cut * size, size)
            pltpu.make_async_copy(pool.at[part], on_chip.at[part], sems.at[i]).start()

    def held(pool, slot, columns):
        return [pool[table[slot, j], :, columns] for j in range(pages)]

    cos = cosine[...]
    sin = sine[...]

    def turn(x):
        return (x * cos + pltpu.roll(x, HEAD // 2, 1) * sin).astype(jnp.bfloat16)

    for source in range(owners):
        for j in range(heads_dev):
            x = inbound[source, :, j * HEAD : (j + 1) * HEAD].astype(jnp.float32)
            x = turn(x).astype(jnp.float32)
            head = source * heads_dev + j
            for b in range(batches):
                rows = pl.ds(head % pair * batch, batch)
                query_rot[head // pair, b, rows] = x[b * batch : (b + 1) * batch]

    piece = lax.broadcasted_iota(jnp.int32, (slots, HEAD), 1) // per_key
    for g in range(kv_heads):
        key = jnp.zeros((slots, HEAD), jnp.float32)
        value = jnp.zeros((slots, HEAD), jnp.float32)
        for j in range(pieces):
            tile = inbound[g * pieces + j, :, per_query : per_query + HEAD].astype(jnp.float32)
            shift = j * per_key
            back = (shift - per_key) % HEAD
            key = jnp.where(piece == j, pltpu.roll(tile, shift, 1) if shift else tile, key)
            value = jnp.where(piece == j, pltpu.roll(tile, back, 1) if back else tile, value)
        key_new[:, g * HEAD : (g + 1) * HEAD] = turn(key)
        value_own[g] = value

    scale = HEAD ** (-0.5)
    columns = pair * batch
    row = lax.broadcasted_iota(jnp.int32, (span, columns), 0)
    place = lax.broadcasted_iota(jnp.int32, (span, columns), 1) % batch
    own_row = lax.broadcasted_iota(jnp.int32, (slots, columns), 0)
    own_place = lax.broadcasted_iota(jnp.int32, (slots, columns), 1) % batch
    first = lax.broadcasted_iota(jnp.int32, (HEAD, columns), 1) < columns // 2
    same = lax.broadcasted_iota(jnp.int32, (columns, columns), 0) == lax.broadcasted_iota(
        jnp.int32, (columns, columns), 1
    )

    pltpu.make_async_copy(key_pool, key_pool, sems.at[0]).wait()
    own_chances = {}
    for b in range(batches):
        valid = row < lengths[b]
        for p in range(pairs):
            turned = query_rot[p, b].T.astype(jnp.bfloat16)
            none = jnp.zeros_like(turned)
            wide = jnp.concatenate(
                [jnp.where(first, turned, none), jnp.where(first, none, turned)], axis=0
            )
            columns_p = slice(p * 2 * HEAD, (p + 1) * 2 * HEAD)
            keys = []
            for s in range(batch):
                keys += held(key_pool, b * batch + s, columns_p)
            keys.append(key_new[:, columns_p])
            products = jnp.dot(
                jnp.concatenate(keys, axis=0), wide, preferred_element_type=jnp.float32
            )
            scores = products[:span]
            for s in range(1, batch):
                scores = jnp.where(place == s, products[s * span : (s + 1) * span], scores)
            own = jnp.where(own_row == own_place + b * batch, products[batch * span :], 0.0)
            own = jnp.sum(own, axis=0, keepdims=True) * scale
            masked = jnp.where(valid, scores * scale, -1e30)
            top = jnp.maximum(jnp.max(masked, axis=0, keepdims=True), own)
            terms = jnp.where(valid, jnp.exp(masked - top), 0.0)
            own_term = jnp.exp(own - top)
            total = jnp.sum(terms, axis=0, keepdims=True) + own_term
            chance[p, b] = (terms / total).T.astype(jnp.bfloat16).astype(jnp.float32)
            own_chance = (own_term / total).astype(jnp.bfloat16).astype(jnp.float32)
            own_chances[p, b] = jnp.sum(
                jnp.where(same, own_chance, 0.0), axis=1, keepdims=True
            )

    pltpu.make_async_copy(value_pool, value_pool, sems.at[1]).wait()
    for b in range(batches):
        for s in range(batch):
            for p in range(pairs):
                mine = chance[p, b, pl.ds(s, pair, stride=batch)].astype(jnp.bfloat16)
                columns_p = slice(p * 2 * HEAD, (p + 1) * 2 * HEAD)
                values = held(value_pool, b * batch + s, columns_p)
                both = jnp.dot(
                    mine, jnp.concatenate(values, axis=0), preferred_element_type=jnp.float32
                )
                result = jnp.concatenate(
                    [both[: pair // 2, :HEAD], both[pair // 2 :, HEAD:]], axis=0
                )
                mixed[p, b, pl.ds(s, pair, stride=batch)] = result

    for p in range(pairs):
        for j in range(pair):
            head = p * pair + j
            g = head * kv_heads // heads
            halves = []
            for b in range(batches):
                rows = slice(j * batch, (j + 1) * batch)
                own_value = value_own[g, b * batch : (b + 1) * batch]
                halves.append(mixed[p, b, rows] + own_chances[p, b][rows] * own_value)
            column = head % heads_dev * HEAD
            out[head // heads_dev, :, column : column + HEAD] = jnp.concatenate(
                halves, axis=0
            ).astype(jnp.bfloat16)


def attend(inbound, lengths, table, cosine, sine, key_pages, value_pages, per_query, per_key):
    owners, slots, _ = inbound.shape
    pages = table.shape[1]
    page, kv_width = key_pages.shape[1:]
    kv_heads = kv_width // HEAD
    heads = owners * (per_query // HEAD)
    span = pages * page
    pair = 2 * heads // kv_heads
    pairs = kv_heads // 2
    batches = slots * pair // HEAD
    batch = slots // batches
    columns = pair * batch
    lengths = jnp.tile(lengths.reshape(batches, 1, batch), (1, 1, pair))
    smem = pl.BlockSpec(memory_space=pltpu.SMEM)
    vmem = pl.BlockSpec(memory_space=pltpu.VMEM)
    hbm = pl.BlockSpec(memory_space=pl.ANY)
    return pl.pallas_call(
        functools.partial(attend_kernel, per_query, per_key),
        in_specs=[smem, vmem, vmem, vmem, vmem, hbm, hbm],
        out_specs=vmem,
        out_shape=jax.ShapeDtypeStruct((owners, slots, per_query), jnp.bfloat16),
        scratch_shapes=[
            pltpu.VMEM(key_pages.shape, jnp.bfloat16),
            pltpu.VMEM(value_pages.shape, jnp.bfloat16),
            pltpu.SemaphoreType.DMA((2,)),
            pltpu.VMEM((slots, kv_width), jnp.bfloat16),
            pltpu.VMEM((pairs, batches, columns, HEAD), jnp.float32),
            pltpu.VMEM((kv_heads, slots, HEAD), jnp.float32),
            pltpu.VMEM((pairs, batches, columns, span), jnp.float32),
            pltpu.VMEM((pairs, batches, columns, HEAD), jnp.float32),
        ],
        compiler_params=pltpu.CompilerParams(vmem_limit_bytes=52 * 2**20),
        cost_estimate=pl.CostEstimate(
            flops=8 * slots * heads * span * HEAD,
            bytes_accessed=4 * slots * span * kv_width,
            transcendentals=slots * heads * span,
        ),
        name="attend",
    )(table, lengths, inbound, cosine, sine, key_pages, value_pages)


def on_device(
    hidden_in,
    norm_gain,
    w_query,
    w_key,
    w_value,
    w_out,
    key_pages,
    value_pages,
    page_table,
    kv_owner,
    cached,
):
    grid = Grid()
    owners = grid.size
    slot_count = page_table.shape[1]
    per_query = w_query.shape[1]
    per_key = w_key.shape[1]
    row_width = per_query + -(-2 * per_key // HEAD) * HEAD
    requests = kv_owner.shape[0]
    rows_dev = requests // owners
    width = hidden_in.shape[1]
    all_slots = owners * slot_count

    moves_a = grid.moves(ORDER_A)
    order_b = [moves_a.index(move) for move in grid.moves(ORDER_B)]
    cut = width // 8 * 5
    xa, xb = norm(hidden_in, norm_gain, (cut, width - cut))

    def placed(kv_owner):
        order = jnp.arange(requests, dtype=jnp.int32)
        earlier = (kv_owner[:, None] == kv_owner[None, :]) & (order[None, :] < order[:, None])
        return kv_owner * slot_count + jnp.sum(earlier.astype(jnp.int32), axis=1)

    def reordered(place, blocks):
        pick = blocks[:, None] == jnp.arange(owners, dtype=jnp.int32)[None, :]
        moved = jnp.where(pick[:, :, None], place.reshape(1, owners, rows_dev), 0)
        return jnp.sum(moved, axis=1).reshape(requests)

    def first(x):
        place = placed(after(kv_owner, x))
        pieces = [after(w_key, x).T, w_value.T]
        spare = row_width - per_query - 2 * per_key
        if spare:
            pieces.append(jnp.zeros((spare, width), w_key.dtype))
        return place, reordered(place, grid.blocks(-1, ORDER_A)), jnp.concatenate(pieces, axis=0)

    def second(x):
        return fetch((after(w_query, x), None), limit=44)[0]

    parts_a, parts_b, others, w_query = gather_rows(grid, xa, xb, first, second)
    place, place_in, w_kv_t = others
    plain = list(range(owners))
    total = project(0, parts_a, plain, w_query, w_kv_t, None, None, all_slots)
    total = project(cut, parts_b, order_b, w_query, w_kv_t, total, place_in, all_slots)
    outbound = total.reshape(owners, slot_count, row_width)
    place = after(place, outbound)
    place_a = reordered(place, grid.blocks(1, ORDER_A))
    place_b = reordered(place, grid.blocks(1, ORDER_B))
    mine = jnp.asarray(np.arange(all_slots, dtype=np.int32).reshape(owners, slot_count))
    mine = mine[lax.axis_index(AXES)]
    lengths = jnp.sum(jnp.where(place[:, None] == mine[None, :], cached[:, None], 0), axis=0)
    halfway = HEAD // 2
    offsets = jnp.arange(halfway, dtype=jnp.float32)
    frequency = rope_base ** (-(2.0 * offsets) / HEAD)
    angles = lengths.astype(jnp.float32)[:, None] * frequency
    cosine_part = jnp.cos(angles)
    sine_part = jnp.sin(angles)
    cosine = jnp.concatenate([cosine_part, cosine_part], axis=1)
    sine = jnp.concatenate([-sine_part, sine_part], axis=1)
    inbound = lax.all_to_all(outbound, AXES, split_axis=0, concat_axis=0, tiled=True)
    attended = attend(
        inbound,
        lengths,
        after(page_table, outbound)[0],
        cosine,
        sine,
        key_pages[0],
        value_pages[0],
        per_query,
        per_key,
    )
    (w_front,) = fetch((after(w_out, attended), (0, width // 32 * 10)), limit=48)
    returned = lax.all_to_all(attended, AXES, split_axis=0, concat_axis=0, tiled=True)
    returned = returned.reshape(all_slots, per_query)
    summed = scatter_sum(grid, place_a, place_b, returned, w_out, w_front, width // 32 * 21)
    return narrow(wide(hidden_in) + summed)


def solution(mesh):
    placed = (
        P(("groups", "tp", "attn"), None),
        P(),
        P(None, ("tp", "attn")),
        P(None, ("tp", "attn")),
        P(None, ("tp", "attn")),
        P(("tp", "attn"), None),
        P(("groups", "tp", "attn"), None, None, None),
        P(("groups", "tp", "attn"), None, None, None),
        P(("groups", "tp", "attn"), None, None),
        P("groups"),
        P("groups"),
    )
    return jax.shard_map(
        on_device,
        mesh=mesh,
        in_specs=placed,
        out_specs=P(("groups", "tp", "attn"), None),
        check_vma=False,
    )
```

```python
import functools

import jax
import jax.numpy as jnp
import numpy as np
from jax import lax
from jax.experimental import pallas as pl
from jax.experimental.pallas import tpu as pltpu
from jax.sharding import PartitionSpec as P

HEAD = 128
AXES = ("tp", "attn")

epsilon = 1e-05
rope_base = 500000.0


class Grid:
    def __init__(self):
        self.half = lax.axis_size("tp") // 4
        self.sizes = (self.half, 2, 2, lax.axis_size("attn"))
        self.size = int(np.prod(self.sizes))

    def shifted(self, place, moves):
        return np.ravel_multi_index(
            tuple((p + m) % n for p, m, n in zip(place, moves, self.sizes)), self.sizes
        )

    def send(self, x, half=0, pair=0, near=0, core=0):
        pairs = [
            (i, int(self.shifted(np.unravel_index(i, self.sizes), (half, pair, near, core))))
            for i in range(self.size)
        ]
        return lax.ppermute(x, AXES, pairs)

    def moves(self, order):
        counts = [self.sizes[axis] for axis in order]
        places = []
        for steps in np.ndindex(*counts):
            move = [0, 0, 0, 0]
            for axis, step in zip(order, steps):
                move[axis] = step
            places.append(tuple(move))
        return places

    def blocks(self, sign, order):
        rows = [
            [
                int(self.shifted(np.unravel_index(i, self.sizes), [sign * m for m in move]))
                for move in self.moves(order)
            ]
            for i in range(self.size)
        ]
        return jnp.asarray(np.array(rows, np.int32))[lax.axis_index(AXES)]


HALF, PAIR, NEAR, CORE = range(4)
ORDER_A = (CORE, NEAR, PAIR, HALF)
ORDER_B = (CORE, PAIR, HALF, NEAR)


def after(x, *earlier):
    return lax.optimization_barrier((x, *earlier))[0]


def gather_rows(grid, xa, xb, first, second):
    beside_b = grid.send(xb, near=1)
    line_a = jnp.concatenate(
        [xa]
        + [
            grid.send(xa, half=half, pair=pair)
            for pair in range(2)
            for half in range(grid.half)
            if half or pair
        ],
        axis=0,
    )
    pair_b = jnp.concatenate([xb, beside_b], axis=0)
    line_a, pair_b, first = lax.optimization_barrier((line_a, pair_b, first(xa)))
    beside_a = grid.send(line_a, near=1)
    parts_b = [pair_b] + [
        grid.send(pair_b, half=half, pair=pair)
        for pair in range(2)
        for half in range(grid.half)
        if half or pair
    ]
    beside_a, parts_b, second = lax.optimization_barrier((beside_a, parts_b, second(pair_b)))
    parts_a = [line_a, beside_a]
    parts_a += [grid.send(part, core=1) for part in parts_a]
    parts_b += [grid.send(part, core=1) for part in parts_b]
    return parts_a, parts_b, first, second


def narrow(x):
    return x.astype(jnp.bfloat16)


def wide(x):
    return x.astype(jnp.float32)


def product_kernel(
    cuts,
    place_a,
    place_b,
    returned,
    w_out,
    w_front,
    away_a,
    keep_a,
    away_b,
    keep_b,
    held,
    sems,
):
    front = w_front.shape[1]
    copies = []
    for i, (start, stop) in enumerate(cuts):
        copy = None
        if start >= front:
            size = pl.ds(start, stop - start), pl.ds(start - front, stop - start)
            copy = pltpu.make_async_copy(
                w_out.at[:, size[0]], held.at[:, size[1]], sems.at[i]
            )
            copy.start()
        copies.append(copy)
    slots = lax.broadcasted_iota(jnp.int32, (returned.shape[0], place_a.shape[1]), 0)

    def picked(place):
        route = jnp.where(slots == place[...], 1.0, 0.0).astype(jnp.bfloat16)
        rows = lax.dot_general(
            route, returned[...], (((0,), (0,)), ((), ())), preferred_element_type=jnp.float32
        )
        return rows.astype(jnp.bfloat16)

    rows_a, rows_b = picked(place_a), picked(place_b)
    half = keep_a.shape[0]
    middle = keep_a.shape[1]
    for copy, (start, stop) in zip(copies, cuts):
        if copy is not None:
            copy.wait()
        rows, away, keep = (rows_a, away_a, keep_a) if start < middle else (rows_b, away_b, keep_b)
        w = w_front[:, start:stop] if copy is None else held[:, start - front : stop - front]
        x = jnp.dot(rows, w, preferred_element_type=jnp.float32)
        begin = start if start < middle else start - middle
        here = slice(begin, begin + stop - start)
        keep[:, here] = x[:half]
        away[:, here] = x[half:].astype(jnp.bfloat16)


def product(place_a, place_b, returned, w_out, w_front, cut):
    rows = place_a.shape[0]
    depth, width = w_out.shape
    cuts = []
    front = w_front.shape[1]
    for start, stop in ((0, front), (front, cut), (cut, width)):
        while start < stop:
            cuts.append((start, min(start + 1024, stop)))
            start = cuts[-1][1]
    vmem = pl.BlockSpec(memory_space=pltpu.VMEM)
    out = []
    for size in (cut, width - cut):
        out.append(jax.ShapeDtypeStruct((rows // 2, size), jnp.bfloat16))
        out.append(jax.ShapeDtypeStruct((rows // 2, size), jnp.float32))
    return pl.pallas_call(
        functools.partial(product_kernel, tuple(cuts)),
        in_specs=[vmem, vmem, vmem, pl.BlockSpec(memory_space=pl.ANY), vmem],
        out_specs=[vmem] * 4,
        out_shape=out,
        scratch_shapes=[
            pltpu.VMEM((depth, width - front), jnp.bfloat16),
            pltpu.SemaphoreType.DMA((len(cuts),)),
        ],
        compiler_params=pltpu.CompilerParams(vmem_limit_bytes=48 * 2**20),
        cost_estimate=pl.CostEstimate(
            flops=2 * rows * depth * width, bytes_accessed=2 * depth * width, transcendentals=0
        ),
        name="product",
    )(place_a.reshape(1, rows), place_b.reshape(1, rows), returned, w_out, w_front)


def scatter_sum(grid, place_a, place_b, returned, w_out, w_front, cut):
    def along_line(x):
        size = x.shape[0] // 2 // grid.half
        middle = x.shape[0] // 2
        first = grid.send(narrow(x[middle + size :]), pair=1)
        second = grid.send(after(narrow(x[middle : middle + size]), first), pair=1)
        far = x[size:middle] + wide(first)
        third = [
            grid.send(narrow(far[d * size : (d + 1) * size]), half=d + 1)
            for d in range(grid.half - 1)
        ]
        return x[:size], [second] + third

    def direct(x):
        size = x.shape[0] // 2 // grid.half
        parts = []
        for pair in range(2):
            for half in range(grid.half):
                begin = (pair * grid.half + half) * size
                if begin:
                    sent = narrow(x[begin : begin + size])
                    parts.append(grid.send(sent, half=half, pair=pair))
        return x[:size], parts

    def total(x, parts):
        for part in parts:
            x = x + wide(part)
        return x

    away_a, keep_a, away_b, keep_b = product(place_a, place_b, returned, w_out, w_front, cut)
    xa = keep_a + wide(grid.send(away_a, core=1))
    middle = xa.shape[0] // 2
    sent_a = narrow(xa[middle:])
    got_a = grid.send(sent_a, near=1)
    xb = keep_b + wide(grid.send(after(away_b, sent_a), core=1))
    xb, got_b = along_line(xb)
    got_a, got_b = lax.optimization_barrier((got_a, got_b))
    xa, parts_a = direct(xa[:middle] + wide(got_a))
    xb = total(xb, got_b)
    middle = xb.shape[0] // 2
    xb = xb[:middle] + wide(grid.send(narrow(xb[middle:]), near=1))
    xa = total(xa, parts_a)
    return jnp.concatenate([xa, xb], axis=1)


def norm_kernel(x, gain, *outs):
    inputs = x[...].astype(jnp.float32)
    factor = lax.rsqrt(jnp.mean(inputs * inputs, axis=1, keepdims=True) + epsilon)
    normed = (inputs * factor * gain[...]).astype(jnp.bfloat16)
    start = 0
    for out in outs:
        out[...] = normed[:, start : start + out.shape[1]]
        start += out.shape[1]


def norm(x, gain, widths):
    vmem = pl.BlockSpec(memory_space=pltpu.VMEM)
    return pl.pallas_call(
        norm_kernel,
        in_specs=[vmem, vmem],
        out_specs=[vmem] * len(widths),
        out_shape=[jax.ShapeDtypeStruct((x.shape[0], w), jnp.bfloat16) for w in widths],
        compiler_params=pltpu.CompilerParams(vmem_limit_bytes=16 * 2**20),
        name="norm",
    )(x, gain.reshape(1, -1))


def fetch_kernel(starts, *refs):
    count = len(starts)
    sems = refs[-1]
    copies = []
    for i, start in enumerate(starts):
        source, target = refs[i], refs[count + i]
        if start is not None:
            columns = pl.ds(start, target.shape[-1])
            source = source.at[(slice(None),) * (len(target.shape) - 1) + (columns,)]
        copies.append(pltpu.make_async_copy(source, target, sems.at[i]))
        copies[-1].start()
    for copy in copies:
        copy.wait()


def fetch(*wanted, limit):
    arrays = [x for x, _ in wanted]
    starts = [columns and columns[0] for _, columns in wanted]
    out = [
        jax.ShapeDtypeStruct(x.shape[:-1] + (columns[1],) if columns else x.shape, x.dtype)
        for x, columns in wanted
    ]
    return pl.pallas_call(
        functools.partial(fetch_kernel, starts),
        in_specs=[pl.BlockSpec(memory_space=pl.ANY)] * len(arrays),
        out_specs=[pl.BlockSpec(memory_space=pltpu.VMEM)] * len(arrays),
        out_shape=out,
        scratch_shapes=[pltpu.SemaphoreType.DMA((len(arrays),))],
        compiler_params=pltpu.CompilerParams(vmem_limit_bytes=limit * 2**20),
        cost_estimate=pl.CostEstimate(
            flops=0, bytes_accessed=sum(x.size * 4 for x in out), transcendentals=0
        ),
        name="fetch",
    )(*arrays)


def project_kernel(first, last, order, start, block, *refs):
    count = len(refs) - 4 - (not first) - last
    parts, (wq, w_kv), refs = refs[:count], refs[count : count + 2], refs[count + 2 :]
    if not first:
        before, refs = refs[0], refs[1:]
    if last:
        place, refs = refs[0], refs[1:]
    out, total = refs
    step = pl.program_id(0)
    per_query = wq.shape[1]

    @pl.when(step == 0)
    def _():
        total[...] = jnp.zeros_like(total) if first else before[...]

    here = pl.ds(pl.multiple_of(step * block, block), block)
    there = pl.ds(pl.multiple_of(start + step * block, block), block)
    x = jnp.concatenate([part[:, here] for part in parts], axis=0)
    products = [
        jnp.dot(x, wq[there, :], preferred_element_type=jnp.float32),
        lax.dot_general(x, w_kv[:, there], (((1,), (1,)), ((), ())), preferred_element_type=jnp.float32),
    ]
    size = x.shape[0] // len(order)
    for product, columns in zip(products, (slice(0, per_query), slice(per_query, None))):
        for i, place_i in enumerate(order):
            total[place_i * size : (place_i + 1) * size, columns] += product[
                i * size : (i + 1) * size
            ]

    @pl.when(step == pl.num_programs(0) - 1)
    def _():
        if last:
            rows = lax.broadcasted_iota(jnp.int32, (out.shape[0], place.shape[1]), 0)
            route = jnp.where(rows == place[...], 1.0, 0.0).astype(jnp.bfloat16)
            moved = jnp.dot(
                route, total[...].astype(jnp.bfloat16), preferred_element_type=jnp.float32
            )
            out[...] = moved.astype(jnp.bfloat16)
        else:
            out[...] = total[...]


def project(start, parts, order, w_query, w_kv_t, before, place, slots):
    row_width = w_query.shape[1] + w_kv_t.shape[0]
    width = parts[0].shape[1]
    block = width
    rows = sum(part.shape[0] for part in parts)
    first, last = before is None, place is not None
    vmem = pl.BlockSpec(memory_space=pltpu.VMEM)
    args = [*parts, w_query, w_kv_t]
    specs = [vmem] * len(parts)
    specs += [
        vmem,
        vmem,
    ]
    if not first:
        args.append(before)
        specs.append(vmem)
    if last:
        args.append(place.reshape(1, rows))
        specs.append(vmem)
        out = jax.ShapeDtypeStruct((slots, row_width), jnp.bfloat16)
    else:
        out = jax.ShapeDtypeStruct((rows, row_width), jnp.float32)
    return pl.pallas_call(
        functools.partial(project_kernel, first, last, order, start, block),
        grid=(width // block,),
        in_specs=specs,
        out_specs=vmem,
        out_shape=out,
        scratch_shapes=[pltpu.VMEM((rows, row_width), jnp.float32)],
        compiler_params=pltpu.CompilerParams(vmem_limit_bytes=24 * 2**20),
        cost_estimate=pl.CostEstimate(
            flops=2 * rows * width * row_width,
            bytes_accessed=2 * width * row_width,
            transcendentals=0,
        ),
        name="project",
    )(*args)


def attend_kernel(
    per_query,
    per_key,
    table,
    lengths,
    inbound,
    cosine,
    sine,
    key_pages,
    value_pages,
    out,
    key_pool,
    value_pool,
    sems,
    key_new,
    query_rot,
    value_own,
    chance,
    mixed,
):
    owners, slots, _ = inbound.shape
    pages = table.shape[1]
    page, kv_width = key_pages.shape[1:]
    kv_heads = kv_width // HEAD
    heads_dev = per_query // HEAD
    heads = owners * heads_dev
    pair = 2 * heads // kv_heads
    pairs = kv_heads // 2
    span = pages * page
    pieces = owners // kv_heads
    batches = query_rot.shape[1]
    batch = slots // batches

    width = kv_width // 2
    copies = []
    for i, (pool, on_chip) in enumerate(((key_pages, key_pool), (value_pages, value_pool))):
        for half in range(2):
            part = pool.at[:, :, pl.ds(half * width, width)]
            copies.append(pltpu.make_async_copy(part, on_chip.at[half], sems.at[i, half]))
            copies[-1].start()

    def held(pool, slot, columns):
        return [pool[table[slot, j], :, columns] for j in range(pages)]

    cos = cosine[...]
    sin = sine[...]

    def turn(x):
        return (x * cos + pltpu.roll(x, HEAD // 2, 1) * sin).astype(jnp.bfloat16)

    for source in range(owners):
        for j in range(heads_dev):
            x = inbound[source, :, j * HEAD : (j + 1) * HEAD].astype(jnp.float32)
            x = turn(x).astype(jnp.float32)
            head = source * heads_dev + j
            for b in range(batches):
                rows = pl.ds(head % pair * batch, batch)
                query_rot[head // pair, b, rows] = x[b * batch : (b + 1) * batch]

    piece = lax.broadcasted_iota(jnp.int32, (slots, HEAD), 1) // per_key
    for g in range(kv_heads):
        key = jnp.zeros((slots, HEAD), jnp.float32)
        value = jnp.zeros((slots, HEAD), jnp.float32)
        for j in range(pieces):
            tile = inbound[g * pieces + j, :, per_query : per_query + HEAD].astype(jnp.float32)
            shift = j * per_key
            back = (shift - per_key) % HEAD
            key = jnp.where(piece == j, pltpu.roll(tile, shift, 1) if shift else tile, key)
            value = jnp.where(piece == j, pltpu.roll(tile, back, 1) if back else tile, value)
        key_new[:, g * HEAD : (g + 1) * HEAD] = turn(key)
        value_own[g] = value

    scale = HEAD ** (-0.5)
    columns = pair * batch
    row = lax.broadcasted_iota(jnp.int32, (span, columns), 0)
    place = lax.broadcasted_iota(jnp.int32, (span, columns), 1) % batch
    own_row = lax.broadcasted_iota(jnp.int32, (slots, columns), 0)
    own_place = lax.broadcasted_iota(jnp.int32, (slots, columns), 1) % batch
    first = lax.broadcasted_iota(jnp.int32, (HEAD, columns), 1) < columns // 2
    same = lax.broadcasted_iota(jnp.int32, (columns, columns), 0) == lax.broadcasted_iota(
        jnp.int32, (columns, columns), 1
    )

    own_chances = {}
    for p in range(pairs):
        half, inside = divmod(p * 2 * HEAD, width)
        columns_p = slice(inside, inside + 2 * HEAD)
        if inside == 0:
            copies[half].wait()
        for b in range(batches):
            valid = row < lengths[b]
            turned = query_rot[p, b].T.astype(jnp.bfloat16)
            none = jnp.zeros_like(turned)
            wide = jnp.concatenate(
                [jnp.where(first, turned, none), jnp.where(first, none, turned)], axis=0
            )
            keys = []
            for s in range(batch):
                keys += held(key_pool.at[half], b * batch + s, columns_p)
            keys.append(key_new[:, p * 2 * HEAD : (p + 1) * 2 * HEAD])
            products = jnp.dot(
                jnp.concatenate(keys, axis=0), wide, preferred_element_type=jnp.float32
            )
            scores = products[:span]
            for s in range(1, batch):
                scores = jnp.where(place == s, products[s * span : (s + 1) * span], scores)
            own = jnp.where(own_row == own_place + b * batch, products[batch * span :], 0.0)
            own = jnp.sum(own, axis=0, keepdims=True) * scale
            masked = jnp.where(valid, scores * scale, -1e30)
            top = jnp.maximum(jnp.max(masked, axis=0, keepdims=True), own)
            terms = jnp.where(valid, jnp.exp(masked - top), 0.0)
            own_term = jnp.exp(own - top)
            total = jnp.sum(terms, axis=0, keepdims=True) + own_term
            chance[p, b] = (terms / total).T.astype(jnp.bfloat16).astype(jnp.float32)
            own_chance = (own_term / total).astype(jnp.bfloat16).astype(jnp.float32)
            own_chances[p, b] = jnp.sum(
                jnp.where(same, own_chance, 0.0), axis=1, keepdims=True
            )

    for p in range(pairs):
        half, inside = divmod(p * 2 * HEAD, width)
        columns_p = slice(inside, inside + 2 * HEAD)
        if inside == 0:
            copies[2 + half].wait()
        for b in range(batches):
            for s in range(batch):
                mine = chance[p, b, pl.ds(s, pair, stride=batch)].astype(jnp.bfloat16)
                values = held(value_pool.at[half], b * batch + s, columns_p)
                both = jnp.dot(
                    mine, jnp.concatenate(values, axis=0), preferred_element_type=jnp.float32
                )
                result = jnp.concatenate(
                    [both[: pair // 2, :HEAD], both[pair // 2 :, HEAD:]], axis=0
                )
                mixed[p, b, pl.ds(s, pair, stride=batch)] = result
        for j in range(pair):
            head = p * pair + j
            g = head * kv_heads // heads
            halves = []
            for b in range(batches):
                rows = slice(j * batch, (j + 1) * batch)
                own_value = value_own[g, b * batch : (b + 1) * batch]
                halves.append(mixed[p, b, rows] + own_chances[p, b][rows] * own_value)
            column = head % heads_dev * HEAD
            out[head // heads_dev, :, column : column + HEAD] = jnp.concatenate(
                halves, axis=0
            ).astype(jnp.bfloat16)


def attend(inbound, lengths, table, cosine, sine, key_pages, value_pages, per_query, per_key):
    owners, slots, _ = inbound.shape
    pages = table.shape[1]
    page, kv_width = key_pages.shape[1:]
    kv_heads = kv_width // HEAD
    heads = owners * (per_query // HEAD)
    span = pages * page
    pair = 2 * heads // kv_heads
    pairs = kv_heads // 2
    batches = slots * pair // HEAD
    batch = slots // batches
    columns = pair * batch
    lengths = jnp.tile(lengths.reshape(batches, 1, batch), (1, 1, pair))
    smem = pl.BlockSpec(memory_space=pltpu.SMEM)
    vmem = pl.BlockSpec(memory_space=pltpu.VMEM)
    hbm = pl.BlockSpec(memory_space=pl.ANY)
    return pl.pallas_call(
        functools.partial(attend_kernel, per_query, per_key),
        in_specs=[smem, vmem, vmem, vmem, vmem, hbm, hbm],
        out_specs=vmem,
        out_shape=jax.ShapeDtypeStruct((owners, slots, per_query), jnp.bfloat16),
        scratch_shapes=[
            pltpu.VMEM((2, *key_pages.shape[:2], kv_width // 2), jnp.bfloat16),
            pltpu.VMEM((2, *key_pages.shape[:2], kv_width // 2), jnp.bfloat16),
            pltpu.SemaphoreType.DMA((2, 2)),
            pltpu.VMEM((slots, kv_width), jnp.bfloat16),
            pltpu.VMEM((pairs, batches, columns, HEAD), jnp.float32),
            pltpu.VMEM((kv_heads, slots, HEAD), jnp.float32),
            pltpu.VMEM((pairs, batches, columns, span), jnp.float32),
            pltpu.VMEM((pairs, batches, columns, HEAD), jnp.float32),
        ],
        compiler_params=pltpu.CompilerParams(vmem_limit_bytes=52 * 2**20),
        cost_estimate=pl.CostEstimate(
            flops=8 * slots * heads * span * HEAD,
            bytes_accessed=4 * slots * span * kv_width,
            transcendentals=slots * heads * span,
        ),
        name="attend",
    )(table, lengths, inbound, cosine, sine, key_pages, value_pages)


def on_device(
    hidden_in,
    norm_gain,
    w_query,
    w_key,
    w_value,
    w_out,
    key_pages,
    value_pages,
    page_table,
    kv_owner,
    cached,
):
    grid = Grid()
    owners = grid.size
    slot_count = page_table.shape[1]
    per_query = w_query.shape[1]
    per_key = w_key.shape[1]
    row_width = per_query + -(-2 * per_key // HEAD) * HEAD
    requests = kv_owner.shape[0]
    rows_dev = requests // owners
    width = hidden_in.shape[1]
    all_slots = owners * slot_count

    moves_a = grid.moves(ORDER_A)
    order_b = [moves_a.index(move) for move in grid.moves(ORDER_B)]
    cut = width // 8 * 5
    xa, xb = norm(hidden_in, norm_gain, (cut, width - cut))

    def placed(kv_owner):
        order = jnp.arange(requests, dtype=jnp.int32)
        earlier = (kv_owner[:, None] == kv_owner[None, :]) & (order[None, :] < order[:, None])
        return kv_owner * slot_count + jnp.sum(earlier.astype(jnp.int32), axis=1)

    def reordered(place, blocks):
        pick = blocks[:, None] == jnp.arange(owners, dtype=jnp.int32)[None, :]
        moved = jnp.where(pick[:, :, None], place.reshape(1, owners, rows_dev), 0)
        return jnp.sum(moved, axis=1).reshape(requests)

    def first(x):
        place = placed(after(kv_owner, x))
        pieces = [after(w_key, x).T, w_value.T]
        spare = row_width - per_query - 2 * per_key
        if spare:
            pieces.append(jnp.zeros((spare, width), w_key.dtype))
        return place, reordered(place, grid.blocks(-1, ORDER_A)), jnp.concatenate(pieces, axis=0)

    def second(x):
        return fetch((after(w_query, x), None), limit=44)[0]

    parts_a, parts_b, others, w_query = gather_rows(grid, xa, xb, first, second)
    place, place_in, w_kv_t = others
    plain = list(range(owners))
    total = project(0, parts_a, plain, w_query, w_kv_t, None, None, all_slots)
    total = project(cut, parts_b, order_b, w_query, w_kv_t, total, place_in, all_slots)
    outbound = total.reshape(owners, slot_count, row_width)
    place = after(place, outbound)
    place_a = reordered(place, grid.blocks(1, ORDER_A))
    place_b = reordered(place, grid.blocks(1, ORDER_B))
    mine = jnp.asarray(np.arange(all_slots, dtype=np.int32).reshape(owners, slot_count))
    mine = mine[lax.axis_index(AXES)]
    lengths = jnp.sum(jnp.where(place[:, None] == mine[None, :], cached[:, None], 0), axis=0)
    halfway = HEAD // 2
    offsets = jnp.arange(halfway, dtype=jnp.float32)
    frequency = rope_base ** (-(2.0 * offsets) / HEAD)
    angles = lengths.astype(jnp.float32)[:, None] * frequency
    cosine_part = jnp.cos(angles)
    sine_part = jnp.sin(angles)
    cosine = jnp.concatenate([cosine_part, cosine_part], axis=1)
    sine = jnp.concatenate([-sine_part, sine_part], axis=1)
    inbound = lax.all_to_all(outbound, AXES, split_axis=0, concat_axis=0, tiled=True)
    attended = attend(
        inbound,
        lengths,
        after(page_table, outbound)[0],
        cosine,
        sine,
        key_pages[0],
        value_pages[0],
        per_query,
        per_key,
    )
    (w_front,) = fetch((after(w_out, attended), (0, width // 32 * 10)), limit=48)
    returned = lax.all_to_all(attended, AXES, split_axis=0, concat_axis=0, tiled=True)
    returned = returned.reshape(all_slots, per_query)
    summed = scatter_sum(grid, place_a, place_b, returned, w_out, w_front, width // 32 * 19)
    return narrow(wide(hidden_in) + summed)


def solution(mesh):
    placed = (
        P(("groups", "tp", "attn"), None),
        P(),
        P(None, ("tp", "attn")),
        P(None, ("tp", "attn")),
        P(None, ("tp", "attn")),
        P(("tp", "attn"), None),
        P(("groups", "tp", "attn"), None, None, None),
        P(("groups", "tp", "attn"), None, None, None),
        P(("groups", "tp", "attn"), None, None),
        P("groups"),
        P("groups"),
    )
    return jax.shard_map(
        on_device,
        mesh=mesh,
        in_specs=placed,
        out_specs=P(("groups", "tp", "attn"), None),
        check_vma=False,
    )
```

```python
import functools

import jax
import jax.numpy as jnp
import numpy as np
from jax import lax
from jax.experimental import pallas as pl
from jax.experimental.pallas import tpu as pltpu
from jax.sharding import PartitionSpec as P

HEAD = 128
AXES = ("tp", "attn")

epsilon = 1e-05
rope_base = 500000.0


class Grid:
    def __init__(self):
        self.half = lax.axis_size("tp") // 4
        self.sizes = (self.half, 2, 2, lax.axis_size("attn"))
        self.size = int(np.prod(self.sizes))

    def shifted(self, place, moves):
        return np.ravel_multi_index(
            tuple((p + m) % n for p, m, n in zip(place, moves, self.sizes)), self.sizes
        )

    def send(self, x, half=0, pair=0, near=0, core=0):
        pairs = [
            (i, int(self.shifted(np.unravel_index(i, self.sizes), (half, pair, near, core))))
            for i in range(self.size)
        ]
        return lax.ppermute(x, AXES, pairs)

    def moves(self, order):
        counts = [self.sizes[axis] for axis in order]
        places = []
        for steps in np.ndindex(*counts):
            move = [0, 0, 0, 0]
            for axis, step in zip(order, steps):
                move[axis] = step
            places.append(tuple(move))
        return places

    def blocks(self, sign, order):
        rows = [
            [
                int(self.shifted(np.unravel_index(i, self.sizes), [sign * m for m in move]))
                for move in self.moves(order)
            ]
            for i in range(self.size)
        ]
        return jnp.asarray(np.array(rows, np.int32))[lax.axis_index(AXES)]


HALF, PAIR, NEAR, CORE = range(4)
ORDER_A = (CORE, NEAR, PAIR, HALF)
ORDER_B = (CORE, PAIR, HALF, NEAR)


def after(x, *earlier):
    return lax.optimization_barrier((x, *earlier))[0]


def gather_rows(grid, xa, xb, first, second):
    beside_b = grid.send(xb, near=1)
    line_a = jnp.concatenate(
        [xa]
        + [
            grid.send(xa, half=half, pair=pair)
            for pair in range(2)
            for half in range(grid.half)
            if half or pair
        ],
        axis=0,
    )
    pair_b = jnp.concatenate([xb, beside_b], axis=0)
    line_a, pair_b, first = lax.optimization_barrier((line_a, pair_b, first(xa)))
    beside_a = grid.send(line_a, near=1)
    parts_b = [pair_b] + [
        grid.send(pair_b, half=half, pair=pair)
        for pair in range(2)
        for half in range(grid.half)
        if half or pair
    ]
    beside_a, parts_b, second = lax.optimization_barrier((beside_a, parts_b, second(pair_b)))
    parts_a = [line_a, beside_a]
    parts_a += [grid.send(part, core=1) for part in parts_a]
    parts_b += [grid.send(part, core=1) for part in parts_b]
    return parts_a, parts_b, first, second


def narrow(x):
    return x.astype(jnp.bfloat16)


def wide(x):
    return x.astype(jnp.float32)


def product_kernel(start, cuts, place, returned, w_out, *refs):
    front = refs[0].shape[1] if len(refs) == 5 else 0
    away, keep, held, sems = refs[-4:]
    copies = []
    for i, (begin, end) in enumerate(cuts):
        copy = None
        if begin >= front:
            source = w_out.at[:, pl.ds(start + begin, end - begin)]
            copy = pltpu.make_async_copy(
                source, held.at[:, pl.ds(begin - front, end - begin)], sems.at[i]
            )
            copy.start()
        copies.append(copy)
    slots = lax.broadcasted_iota(jnp.int32, (returned.shape[0], place.shape[1]), 0)
    route = jnp.where(slots == place[...], 1.0, 0.0).astype(jnp.bfloat16)
    rows = lax.dot_general(
        route, returned[...], (((0,), (0,)), ((), ())), preferred_element_type=jnp.float32
    ).astype(jnp.bfloat16)
    half = keep.shape[0]
    for copy, (begin, end) in zip(copies, cuts):
        if copy is None:
            w = refs[0][:, begin:end]
        else:
            copy.wait()
            w = held[:, begin - front : end - front]
        x = jnp.dot(rows, w, preferred_element_type=jnp.float32)
        keep[:, begin:end] = x[:half]
        away[:, begin:end] = x[half:].astype(jnp.bfloat16)


def product(place, returned, w_out, start, width, w_front=None):
    rows = place.shape[0]
    depth = w_out.shape[0]
    front = 0 if w_front is None else w_front.shape[1]
    cuts = []
    for begin, end in ((0, front), (front, width)):
        while begin < end:
            cuts.append((begin, min(begin + 1024, end)))
            begin = cuts[-1][1]
    vmem = pl.BlockSpec(memory_space=pltpu.VMEM)
    args = [place.reshape(1, rows), returned, w_out]
    specs = [vmem, vmem, pl.BlockSpec(memory_space=pl.ANY)]
    if front:
        args.append(w_front)
        specs.append(vmem)
    return pl.pallas_call(
        functools.partial(product_kernel, start, tuple(cuts)),
        in_specs=specs,
        out_specs=[vmem, vmem],
        out_shape=[
            jax.ShapeDtypeStruct((rows // 2, width), jnp.bfloat16),
            jax.ShapeDtypeStruct((rows // 2, width), jnp.float32),
        ],
        scratch_shapes=[
            pltpu.VMEM((depth, width - front), jnp.bfloat16),
            pltpu.SemaphoreType.DMA((len(cuts),)),
        ],
        compiler_params=pltpu.CompilerParams(vmem_limit_bytes=48 * 2**20),
        cost_estimate=pl.CostEstimate(
            flops=2 * rows * depth * width,
            bytes_accessed=2 * depth * (width - front),
            transcendentals=0,
        ),
        name="product",
    )(*args)


def scatter_sum(grid, place_a, place_b, returned, w_out, w_front, cut):
    def direct(x):
        size = x.shape[0] // 2 // grid.half
        parts = []
        for pair in range(2):
            for half in range(grid.half):
                begin = (pair * grid.half + half) * size
                if begin:
                    sent = narrow(x[begin : begin + size])
                    parts.append(grid.send(sent, half=half, pair=pair))
        return x[:size], parts

    def total(x, parts):
        for part in parts:
            x = x + wide(part)
        return x

    away_a, keep_a = product(place_a, returned, w_out, 0, cut, w_front)
    away_b, keep_b = product(
        place_b, after(returned, away_a), w_out, cut, w_out.shape[1] - cut
    )
    xa = keep_a + wide(grid.send(away_a, core=1))
    middle = xa.shape[0] // 2
    sent_a = narrow(xa[middle:])
    got_a = grid.send(sent_a, near=1)
    xb = keep_b + wide(grid.send(after(away_b, sent_a), core=1))
    xb, got_b = direct(xb)
    got_a, got_b = lax.optimization_barrier((got_a, got_b))
    xa, parts_a = direct(xa[:middle] + wide(got_a))
    xb = total(xb, got_b)
    middle = xb.shape[0] // 2
    xb = xb[:middle] + wide(grid.send(narrow(xb[middle:]), near=1))
    xa = total(xa, parts_a)
    return jnp.concatenate([xa, xb], axis=1)


def norm_kernel(x, gain, *outs):
    inputs = x[...].astype(jnp.float32)
    factor = lax.rsqrt(jnp.mean(inputs * inputs, axis=1, keepdims=True) + epsilon)
    normed = (inputs * factor * gain[...]).astype(jnp.bfloat16)
    start = 0
    for out in outs:
        out[...] = normed[:, start : start + out.shape[1]]
        start += out.shape[1]


def norm(x, gain, widths):
    vmem = pl.BlockSpec(memory_space=pltpu.VMEM)
    return pl.pallas_call(
        norm_kernel,
        in_specs=[vmem, vmem],
        out_specs=[vmem] * len(widths),
        out_shape=[jax.ShapeDtypeStruct((x.shape[0], w), jnp.bfloat16) for w in widths],
        compiler_params=pltpu.CompilerParams(vmem_limit_bytes=16 * 2**20),
        name="norm",
    )(x, gain.reshape(1, -1))


def fetch_kernel(starts, *refs):
    count = len(starts)
    sems = refs[-1]
    copies = []
    for i, start in enumerate(starts):
        source, target = refs[i], refs[count + i]
        if start is not None:
            columns = pl.ds(start, target.shape[-1])
            source = source.at[(slice(None),) * (len(target.shape) - 1) + (columns,)]
        copies.append(pltpu.make_async_copy(source, target, sems.at[i]))
        copies[-1].start()
    for copy in copies:
        copy.wait()


def fetch(*wanted, limit):
    arrays = [x for x, _ in wanted]
    starts = [columns and columns[0] for _, columns in wanted]
    out = [
        jax.ShapeDtypeStruct(x.shape[:-1] + (columns[1],) if columns else x.shape, x.dtype)
        for x, columns in wanted
    ]
    return pl.pallas_call(
        functools.partial(fetch_kernel, starts),
        in_specs=[pl.BlockSpec(memory_space=pl.ANY)] * len(arrays),
        out_specs=[pl.BlockSpec(memory_space=pltpu.VMEM)] * len(arrays),
        out_shape=out,
        scratch_shapes=[pltpu.SemaphoreType.DMA((len(arrays),))],
        compiler_params=pltpu.CompilerParams(vmem_limit_bytes=limit * 2**20),
        cost_estimate=pl.CostEstimate(
            flops=0, bytes_accessed=sum(x.size * 4 for x in out), transcendentals=0
        ),
        name="fetch",
    )(*arrays)


def project_kernel(first, last, order, start, block, *refs):
    count = len(refs) - 4 - (not first) - last
    parts, (wq, w_kv), refs = refs[:count], refs[count : count + 2], refs[count + 2 :]
    if not first:
        before, refs = refs[0], refs[1:]
    if last:
        place, refs = refs[0], refs[1:]
    out, total = refs
    step = pl.program_id(0)
    per_query = wq.shape[1]

    @pl.when(step == 0)
    def _():
        total[...] = jnp.zeros_like(total) if first else before[...]

    here = pl.ds(pl.multiple_of(step * block, block), block)
    there = pl.ds(pl.multiple_of(start + step * block, block), block)
    x = jnp.concatenate([part[:, here] for part in parts], axis=0)
    products = [
        jnp.dot(x, wq[there, :], preferred_element_type=jnp.float32),
        lax.dot_general(x, w_kv[:, there], (((1,), (1,)), ((), ())), preferred_element_type=jnp.float32),
    ]
    size = x.shape[0] // len(order)
    for product, columns in zip(products, (slice(0, per_query), slice(per_query, None))):
        for i, place_i in enumerate(order):
            total[place_i * size : (place_i + 1) * size, columns] += product[
                i * size : (i + 1) * size
            ]

    @pl.when(step == pl.num_programs(0) - 1)
    def _():
        if last:
            rows = lax.broadcasted_iota(jnp.int32, (out.shape[0], place.shape[1]), 0)
            route = jnp.where(rows == place[...], 1.0, 0.0).astype(jnp.bfloat16)
            moved = jnp.dot(
                route, total[...].astype(jnp.bfloat16), preferred_element_type=jnp.float32
            )
            out[...] = moved.astype(jnp.bfloat16)
        else:
            out[...] = total[...]


def project(start, parts, order, w_query, w_kv_t, before, place, slots):
    row_width = w_query.shape[1] + w_kv_t.shape[0]
    width = parts[0].shape[1]
    block = width
    rows = sum(part.shape[0] for part in parts)
    first, last = before is None, place is not None
    vmem = pl.BlockSpec(memory_space=pltpu.VMEM)
    args = [*parts, w_query, w_kv_t]
    specs = [vmem] * len(parts)
    specs += [
        vmem,
        vmem,
    ]
    if not first:
        args.append(before)
        specs.append(vmem)
    if last:
        args.append(place.reshape(1, rows))
        specs.append(vmem)
        out = jax.ShapeDtypeStruct((slots, row_width), jnp.bfloat16)
    else:
        out = jax.ShapeDtypeStruct((rows, row_width), jnp.float32)
    return pl.pallas_call(
        functools.partial(project_kernel, first, last, order, start, block),
        grid=(width // block,),
        in_specs=specs,
        out_specs=vmem,
        out_shape=out,
        scratch_shapes=[pltpu.VMEM((rows, row_width), jnp.float32)],
        compiler_params=pltpu.CompilerParams(vmem_limit_bytes=24 * 2**20),
        cost_estimate=pl.CostEstimate(
            flops=2 * rows * width * row_width,
            bytes_accessed=2 * width * row_width,
            transcendentals=0,
        ),
        name="project",
    )(*args)


def attend_kernel(
    per_query,
    per_key,
    table,
    lengths,
    inbound,
    cosine,
    sine,
    key_pages,
    value_pages,
    out,
    key_pool,
    value_pool,
    sems,
    key_new,
    query_rot,
    value_own,
    chance,
    mixed,
):
    owners, slots, _ = inbound.shape
    pages = table.shape[1]
    page, kv_width = key_pages.shape[1:]
    kv_heads = kv_width // HEAD
    heads_dev = per_query // HEAD
    heads = owners * heads_dev
    pair = 2 * heads // kv_heads
    pairs = kv_heads // 2
    span = pages * page
    pieces = owners // kv_heads
    batches = query_rot.shape[1]
    batch = slots // batches

    width = 2 * HEAD
    copies = []
    for i, (pool, on_chip) in enumerate(((key_pages, key_pool), (value_pages, value_pool))):
        for p in range(pairs):
            part = pool.at[:, :, pl.ds(p * width, width)]
            copies.append(pltpu.make_async_copy(part, on_chip.at[p], sems.at[i, p]))
    ahead = 2
    for copy in copies[:ahead]:
        copy.start()

    def arrived(i):
        copies[i].wait()
        if i + ahead < len(copies):
            copies[i + ahead].start()

    def held(pool, slot):
        return [pool[table[slot, j]] for j in range(pages)]

    cos = cosine[...]
    sin = sine[...]

    def turn(x):
        return (x * cos + pltpu.roll(x, HEAD // 2, 1) * sin).astype(jnp.bfloat16)

    for source in range(owners):
        for j in range(heads_dev):
            x = inbound[source, :, j * HEAD : (j + 1) * HEAD].astype(jnp.float32)
            x = turn(x).astype(jnp.float32)
            head = source * heads_dev + j
            for b in range(batches):
                rows = pl.ds(head % pair * batch, batch)
                query_rot[head // pair, b, rows] = x[b * batch : (b + 1) * batch]

    piece = lax.broadcasted_iota(jnp.int32, (slots, HEAD), 1) // per_key
    for g in range(kv_heads):
        key = jnp.zeros((slots, HEAD), jnp.float32)
        value = jnp.zeros((slots, HEAD), jnp.float32)
        for j in range(pieces):
            tile = inbound[g * pieces + j, :, per_query : per_query + HEAD].astype(jnp.float32)
            shift = j * per_key
            back = (shift - per_key) % HEAD
            key = jnp.where(piece == j, pltpu.roll(tile, shift, 1) if shift else tile, key)
            value = jnp.where(piece == j, pltpu.roll(tile, back, 1) if back else tile, value)
        key_new[:, g * HEAD : (g + 1) * HEAD] = turn(key)
        value_own[g] = value

    scale = HEAD ** (-0.5)
    columns = pair * batch
    row = lax.broadcasted_iota(jnp.int32, (span, columns), 0)
    place = lax.broadcasted_iota(jnp.int32, (span, columns), 1) % batch
    own_row = lax.broadcasted_iota(jnp.int32, (slots, columns), 0)
    own_place = lax.broadcasted_iota(jnp.int32, (slots, columns), 1) % batch
    first = lax.broadcasted_iota(jnp.int32, (HEAD, columns), 1) < columns // 2
    same = lax.broadcasted_iota(jnp.int32, (columns, columns), 0) == lax.broadcasted_iota(
        jnp.int32, (columns, columns), 1
    )

    own_chances = {}
    for p in range(pairs):
        arrived(p)
        for b in range(batches):
            valid = row < lengths[b]
            turned = query_rot[p, b].T.astype(jnp.bfloat16)
            none = jnp.zeros_like(turned)
            wide = jnp.concatenate(
                [jnp.where(first, turned, none), jnp.where(first, none, turned)], axis=0
            )
            keys = []
            for s in range(batch):
                keys += held(key_pool.at[p], b * batch + s)
            keys.append(key_new[:, p * 2 * HEAD : (p + 1) * 2 * HEAD])
            products = jnp.dot(
                jnp.concatenate(keys, axis=0), wide, preferred_element_type=jnp.float32
            )
            scores = products[:span]
            for s in range(1, batch):
                scores = jnp.where(place == s, products[s * span : (s + 1) * span], scores)
            own = jnp.where(own_row == own_place + b * batch, products[batch * span :], 0.0)
            own = jnp.sum(own, axis=0, keepdims=True) * scale
            masked = jnp.where(valid, scores * scale, -1e30)
            top = jnp.maximum(jnp.max(masked, axis=0, keepdims=True), own)
            terms = jnp.where(valid, jnp.exp(masked - top), 0.0)
            own_term = jnp.exp(own - top)
            total = jnp.sum(terms, axis=0, keepdims=True) + own_term
            chance[p, b] = (terms / total).T.astype(jnp.bfloat16).astype(jnp.float32)
            own_chance = (own_term / total).astype(jnp.bfloat16).astype(jnp.float32)
            own_chances[p, b] = jnp.sum(
                jnp.where(same, own_chance, 0.0), axis=1, keepdims=True
            )

    for p in range(pairs):
        arrived(pairs + p)
        for b in range(batches):
            for s in range(batch):
                mine = chance[p, b, pl.ds(s, pair, stride=batch)].astype(jnp.bfloat16)
                values = held(value_pool.at[p], b * batch + s)
                both = jnp.dot(
                    mine, jnp.concatenate(values, axis=0), preferred_element_type=jnp.float32
                )
                result = jnp.concatenate(
                    [both[: pair // 2, :HEAD], both[pair // 2 :, HEAD:]], axis=0
                )
                mixed[p, b, pl.ds(s, pair, stride=batch)] = result
        for j in range(pair):
            head = p * pair + j
            g = head * kv_heads // heads
            halves = []
            for b in range(batches):
                rows = slice(j * batch, (j + 1) * batch)
                own_value = value_own[g, b * batch : (b + 1) * batch]
                halves.append(mixed[p, b, rows] + own_chances[p, b][rows] * own_value)
            column = head % heads_dev * HEAD
            out[head // heads_dev, :, column : column + HEAD] = jnp.concatenate(
                halves, axis=0
            ).astype(jnp.bfloat16)


def attend(inbound, lengths, table, cosine, sine, key_pages, value_pages, per_query, per_key):
    owners, slots, _ = inbound.shape
    pages = table.shape[1]
    page, kv_width = key_pages.shape[1:]
    kv_heads = kv_width // HEAD
    heads = owners * (per_query // HEAD)
    span = pages * page
    pair = 2 * heads // kv_heads
    pairs = kv_heads // 2
    batches = slots * pair // HEAD
    batch = slots // batches
    columns = pair * batch
    lengths = jnp.tile(lengths.reshape(batches, 1, batch), (1, 1, pair))
    smem = pl.BlockSpec(memory_space=pltpu.SMEM)
    vmem = pl.BlockSpec(memory_space=pltpu.VMEM)
    hbm = pl.BlockSpec(memory_space=pl.ANY)
    return pl.pallas_call(
        functools.partial(attend_kernel, per_query, per_key),
        in_specs=[smem, vmem, vmem, vmem, vmem, hbm, hbm],
        out_specs=vmem,
        out_shape=jax.ShapeDtypeStruct((owners, slots, per_query), jnp.bfloat16),
        scratch_shapes=[
            pltpu.VMEM((pairs, *key_pages.shape[:2], 2 * HEAD), jnp.bfloat16),
            pltpu.VMEM((pairs, *key_pages.shape[:2], 2 * HEAD), jnp.bfloat16),
            pltpu.SemaphoreType.DMA((2, pairs)),
            pltpu.VMEM((slots, kv_width), jnp.bfloat16),
            pltpu.VMEM((pairs, batches, columns, HEAD), jnp.float32),
            pltpu.VMEM((kv_heads, slots, HEAD), jnp.float32),
            pltpu.VMEM((pairs, batches, columns, span), jnp.float32),
            pltpu.VMEM((pairs, batches, columns, HEAD), jnp.float32),
        ],
        compiler_params=pltpu.CompilerParams(vmem_limit_bytes=52 * 2**20),
        cost_estimate=pl.CostEstimate(
            flops=8 * slots * heads * span * HEAD,
            bytes_accessed=4 * slots * span * kv_width,
            transcendentals=slots * heads * span,
        ),
        name="attend",
    )(table, lengths, inbound, cosine, sine, key_pages, value_pages)


def on_device(
    hidden_in,
    norm_gain,
    w_query,
    w_key,
    w_value,
    w_out,
    key_pages,
    value_pages,
    page_table,
    kv_owner,
    cached,
):
    grid = Grid()
    owners = grid.size
    slot_count = page_table.shape[1]
    per_query = w_query.shape[1]
    per_key = w_key.shape[1]
    row_width = per_query + -(-2 * per_key // HEAD) * HEAD
    requests = kv_owner.shape[0]
    rows_dev = requests // owners
    width = hidden_in.shape[1]
    all_slots = owners * slot_count

    moves_a = grid.moves(ORDER_A)
    order_b = [moves_a.index(move) for move in grid.moves(ORDER_B)]
    cut = width // 8 * 5
    xa, xb = norm(hidden_in, norm_gain, (cut, width - cut))

    def placed(kv_owner):
        order = jnp.arange(requests, dtype=jnp.int32)
        earlier = (kv_owner[:, None] == kv_owner[None, :]) & (order[None, :] < order[:, None])
        return kv_owner * slot_count + jnp.sum(earlier.astype(jnp.int32), axis=1)

    def reordered(place, blocks):
        pick = blocks[:, None] == jnp.arange(owners, dtype=jnp.int32)[None, :]
        moved = jnp.where(pick[:, :, None], place.reshape(1, owners, rows_dev), 0)
        return jnp.sum(moved, axis=1).reshape(requests)

    def first(x):
        place = placed(after(kv_owner, x))
        pieces = [after(w_key, x).T, w_value.T]
        spare = row_width - per_query - 2 * per_key
        if spare:
            pieces.append(jnp.zeros((spare, width), w_key.dtype))
        return place, reordered(place, grid.blocks(-1, ORDER_A)), jnp.concatenate(pieces, axis=0)

    def second(x):
        return fetch((after(w_query, x), None), limit=44)[0]

    parts_a, parts_b, others, w_query = gather_rows(grid, xa, xb, first, second)
    place, place_in, w_kv_t = others
    plain = list(range(owners))
    total = project(0, parts_a, plain, w_query, w_kv_t, None, None, all_slots)
    total = project(cut, parts_b, order_b, w_query, w_kv_t, total, place_in, all_slots)
    outbound = total.reshape(owners, slot_count, row_width)
    place = after(place, outbound)
    place_a = reordered(place, grid.blocks(1, ORDER_A))
    place_b = reordered(place, grid.blocks(1, ORDER_B))
    mine = jnp.asarray(np.arange(all_slots, dtype=np.int32).reshape(owners, slot_count))
    mine = mine[lax.axis_index(AXES)]
    lengths = jnp.sum(jnp.where(place[:, None] == mine[None, :], cached[:, None], 0), axis=0)
    halfway = HEAD // 2
    offsets = jnp.arange(halfway, dtype=jnp.float32)
    frequency = rope_base ** (-(2.0 * offsets) / HEAD)
    angles = lengths.astype(jnp.float32)[:, None] * frequency
    cosine_part = jnp.cos(angles)
    sine_part = jnp.sin(angles)
    cosine = jnp.concatenate([cosine_part, cosine_part], axis=1)
    sine = jnp.concatenate([-sine_part, sine_part], axis=1)
    inbound = lax.all_to_all(outbound, AXES, split_axis=0, concat_axis=0, tiled=True)
    attended = attend(
        inbound,
        lengths,
        after(page_table, outbound)[0],
        cosine,
        sine,
        key_pages[0],
        value_pages[0],
        per_query,
        per_key,
    )
    (w_front,) = fetch((after(w_out, attended), (0, width // 32 * 10)), limit=48)
    returned = lax.all_to_all(attended, AXES, split_axis=0, concat_axis=0, tiled=True)
    returned = returned.reshape(all_slots, per_query)
    summed = scatter_sum(grid, place_a, place_b, returned, w_out, w_front, width // 32 * 21)
    return narrow(wide(hidden_in) + summed)


def solution(mesh):
    placed = (
        P(("groups", "tp", "attn"), None),
        P(),
        P(None, ("tp", "attn")),
        P(None, ("tp", "attn")),
        P(None, ("tp", "attn")),
        P(("tp", "attn"), None),
        P(("groups", "tp", "attn"), None, None, None),
        P(("groups", "tp", "attn"), None, None, None),
        P(("groups", "tp", "attn"), None, None),
        P("groups"),
        P("groups"),
    )
    return jax.shard_map(
        on_device,
        mesh=mesh,
        in_specs=placed,
        out_specs=P(("groups", "tp", "attn"), None),
        check_vma=False,
    )
```

```python
import functools

import jax
import jax.numpy as jnp
import numpy as np
from jax import lax
from jax.experimental import pallas as pl
from jax.experimental.pallas import tpu as pltpu
from jax.sharding import PartitionSpec as P

HEAD = 128
AXES = ("tp", "attn")

epsilon = 1e-05
rope_base = 500000.0


class Grid:
    def __init__(self):
        self.half = lax.axis_size("tp") // 4
        self.sizes = (self.half, 2, 2, lax.axis_size("attn"))
        self.size = int(np.prod(self.sizes))

    def shifted(self, place, moves):
        return np.ravel_multi_index(
            tuple((p + m) % n for p, m, n in zip(place, moves, self.sizes)), self.sizes
        )

    def send(self, x, half=0, pair=0, near=0, core=0):
        pairs = [
            (i, int(self.shifted(np.unravel_index(i, self.sizes), (half, pair, near, core))))
            for i in range(self.size)
        ]
        return lax.ppermute(x, AXES, pairs)

    def moves(self, order):
        counts = [self.sizes[axis] for axis in order]
        places = []
        for steps in np.ndindex(*counts):
            move = [0, 0, 0, 0]
            for axis, step in zip(order, steps):
                move[axis] = step
            places.append(tuple(move))
        return places

    def blocks(self, sign, order):
        rows = [
            [
                int(self.shifted(np.unravel_index(i, self.sizes), [sign * m for m in move]))
                for move in self.moves(order)
            ]
            for i in range(self.size)
        ]
        return jnp.asarray(np.array(rows, np.int32))[lax.axis_index(AXES)]


HALF, PAIR, NEAR, CORE = range(4)
ORDER_A = (CORE, NEAR, PAIR, HALF)
ORDER_B = (CORE, PAIR, HALF, NEAR)


def after(x, *earlier):
    return lax.optimization_barrier((x, *earlier))[0]


def gather_rows(grid, xa, xb, first, second):
    beside_b = grid.send(xb, near=1)
    line_a = jnp.concatenate(
        [xa]
        + [
            grid.send(xa, half=half, pair=pair)
            for pair in range(2)
            for half in range(grid.half)
            if half or pair
        ],
        axis=0,
    )
    pair_b = jnp.concatenate([xb, beside_b], axis=0)
    line_a, pair_b, first = lax.optimization_barrier((line_a, pair_b, first(xa)))
    beside_a = grid.send(line_a, near=1)
    parts_b = [pair_b] + [
        grid.send(pair_b, half=half, pair=pair)
        for pair in range(2)
        for half in range(grid.half)
        if half or pair
    ]
    beside_a, parts_b, second = lax.optimization_barrier((beside_a, parts_b, second(pair_b)))
    parts_a = [line_a, beside_a]
    parts_a += [grid.send(part, core=1) for part in parts_a]
    parts_b += [grid.send(part, core=1) for part in parts_b]
    return parts_a, parts_b, first, second


def narrow(x):
    return x.astype(jnp.bfloat16)


def wide(x):
    return x.astype(jnp.float32)


def product_kernel(
    cuts,
    place_a,
    place_b,
    returned,
    w_out,
    w_front,
    away_a,
    keep_a,
    away_b,
    keep_b,
    held,
    sems,
):
    front = w_front.shape[1]
    copies = []
    for i, (start, stop) in enumerate(cuts):
        copy = None
        if start >= front:
            size = pl.ds(start, stop - start), pl.ds(start - front, stop - start)
            copy = pltpu.make_async_copy(
                w_out.at[:, size[0]], held.at[:, size[1]], sems.at[i]
            )
            copy.start()
        copies.append(copy)
    slots = lax.broadcasted_iota(jnp.int32, (returned.shape[0], place_a.shape[1]), 0)

    def picked(place):
        route = jnp.where(slots == place[...], 1.0, 0.0).astype(jnp.bfloat16)
        rows = lax.dot_general(
            route, returned[...], (((0,), (0,)), ((), ())), preferred_element_type=jnp.float32
        )
        return rows.astype(jnp.bfloat16)

    rows_a, rows_b = picked(place_a), picked(place_b)
    half = keep_a.shape[0]
    middle = keep_a.shape[1]
    for copy, (start, stop) in zip(copies, cuts):
        if copy is not None:
            copy.wait()
        rows, away, keep = (rows_a, away_a, keep_a) if start < middle else (rows_b, away_b, keep_b)
        w = w_front[:, start:stop] if copy is None else held[:, start - front : stop - front]
        x = jnp.dot(rows, w, preferred_element_type=jnp.float32)
        begin = start if start < middle else start - middle
        here = slice(begin, begin + stop - start)
        keep[:, here] = x[:half]
        away[:, here] = x[half:].astype(jnp.bfloat16)


def product(place_a, place_b, returned, w_out, w_front, cut):
    rows = place_a.shape[0]
    depth, width = w_out.shape
    cuts = []
    front = w_front.shape[1]
    for start, stop in ((0, front), (front, cut), (cut, width)):
        while start < stop:
            cuts.append((start, min(start + 1024, stop)))
            start = cuts[-1][1]
    vmem = pl.BlockSpec(memory_space=pltpu.VMEM)
    out = []
    for size in (cut, width - cut):
        out.append(jax.ShapeDtypeStruct((rows // 2, size), jnp.bfloat16))
        out.append(jax.ShapeDtypeStruct((rows // 2, size), jnp.float32))
    return pl.pallas_call(
        functools.partial(product_kernel, tuple(cuts)),
        in_specs=[vmem, vmem, vmem, pl.BlockSpec(memory_space=pl.ANY), vmem],
        out_specs=[vmem] * 4,
        out_shape=out,
        scratch_shapes=[
            pltpu.VMEM((depth, width - front), jnp.bfloat16),
            pltpu.SemaphoreType.DMA((len(cuts),)),
        ],
        compiler_params=pltpu.CompilerParams(vmem_limit_bytes=48 * 2**20),
        cost_estimate=pl.CostEstimate(
            flops=2 * rows * depth * width, bytes_accessed=2 * depth * width, transcendentals=0
        ),
        name="product",
    )(place_a.reshape(1, rows), place_b.reshape(1, rows), returned, w_out, w_front)


def scatter_sum(grid, place_a, place_b, returned, w_out, w_front, cut):
    def direct(x):
        size = x.shape[0] // 2 // grid.half
        parts = []
        for pair in range(2):
            for half in range(grid.half):
                begin = (pair * grid.half + half) * size
                if begin:
                    sent = narrow(x[begin : begin + size])
                    parts.append(grid.send(sent, half=half, pair=pair))
        return x[:size], parts

    def total(x, parts):
        for part in parts:
            x = x + wide(part)
        return x

    away_a, keep_a, away_b, keep_b = product(place_a, place_b, returned, w_out, w_front, cut)
    xa = keep_a + wide(grid.send(away_a, core=1))
    middle = xa.shape[0] // 2
    sent_a = narrow(xa[middle:])
    got_a = grid.send(sent_a, near=1)
    xb = keep_b + wide(grid.send(after(away_b, sent_a), core=1))
    xb, got_b = direct(xb)
    got_a, got_b = lax.optimization_barrier((got_a, got_b))
    xa, parts_a = direct(xa[:middle] + wide(got_a))
    xb = total(xb, got_b)
    middle = xb.shape[0] // 2
    xb = xb[:middle] + wide(grid.send(narrow(xb[middle:]), near=1))
    xa = total(xa, parts_a)
    return jnp.concatenate([xa, xb], axis=1)


def norm_kernel(x, gain, *outs):
    inputs = x[...].astype(jnp.float32)
    factor = lax.rsqrt(jnp.mean(inputs * inputs, axis=1, keepdims=True) + epsilon)
    normed = (inputs * factor * gain[...]).astype(jnp.bfloat16)
    start = 0
    for out in outs:
        out[...] = normed[:, start : start + out.shape[1]]
        start += out.shape[1]


def norm(x, gain, widths):
    vmem = pl.BlockSpec(memory_space=pltpu.VMEM)
    return pl.pallas_call(
        norm_kernel,
        in_specs=[vmem, vmem],
        out_specs=[vmem] * len(widths),
        out_shape=[jax.ShapeDtypeStruct((x.shape[0], w), jnp.bfloat16) for w in widths],
        compiler_params=pltpu.CompilerParams(vmem_limit_bytes=16 * 2**20),
        name="norm",
    )(x, gain.reshape(1, -1))


def fetch_kernel(starts, *refs):
    count = len(starts)
    sems = refs[-1]
    copies = []
    for i, start in enumerate(starts):
        source, target = refs[i], refs[count + i]
        if start is not None:
            columns = pl.ds(start, target.shape[-1])
            source = source.at[(slice(None),) * (len(target.shape) - 1) + (columns,)]
        copies.append(pltpu.make_async_copy(source, target, sems.at[i]))
        copies[-1].start()
    for copy in copies:
        copy.wait()


def fetch(*wanted, limit):
    arrays = [x for x, _ in wanted]
    starts = [columns and columns[0] for _, columns in wanted]
    out = [
        jax.ShapeDtypeStruct(x.shape[:-1] + (columns[1],) if columns else x.shape, x.dtype)
        for x, columns in wanted
    ]
    return pl.pallas_call(
        functools.partial(fetch_kernel, starts),
        in_specs=[pl.BlockSpec(memory_space=pl.ANY)] * len(arrays),
        out_specs=[pl.BlockSpec(memory_space=pltpu.VMEM)] * len(arrays),
        out_shape=out,
        scratch_shapes=[pltpu.SemaphoreType.DMA((len(arrays),))],
        compiler_params=pltpu.CompilerParams(vmem_limit_bytes=limit * 2**20),
        cost_estimate=pl.CostEstimate(
            flops=0, bytes_accessed=sum(x.size * 4 for x in out), transcendentals=0
        ),
        name="fetch",
    )(*arrays)


def project_kernel(first, last, order, start, block, *refs):
    count = len(refs) - 4 - (not first) - last
    parts, (wq, w_kv), refs = refs[:count], refs[count : count + 2], refs[count + 2 :]
    if not first:
        before, refs = refs[0], refs[1:]
    if last:
        place, refs = refs[0], refs[1:]
    out, total = refs
    step = pl.program_id(0)
    per_query = wq.shape[1]

    @pl.when(step == 0)
    def _():
        total[...] = jnp.zeros_like(total) if first else before[...]

    here = pl.ds(pl.multiple_of(step * block, block), block)
    there = pl.ds(pl.multiple_of(start + step * block, block), block)
    x = jnp.concatenate([part[:, here] for part in parts], axis=0)
    products = [
        jnp.dot(x, wq[there, :], preferred_element_type=jnp.float32),
        lax.dot_general(x, w_kv[:, there], (((1,), (1,)), ((), ())), preferred_element_type=jnp.float32),
    ]
    size = x.shape[0] // len(order)
    for product, columns in zip(products, (slice(0, per_query), slice(per_query, None))):
        for i, place_i in enumerate(order):
            total[place_i * size : (place_i + 1) * size, columns] += product[
                i * size : (i + 1) * size
            ]

    @pl.when(step == pl.num_programs(0) - 1)
    def _():
        if last:
            rows = lax.broadcasted_iota(jnp.int32, (out.shape[0], place.shape[1]), 0)
            route = jnp.where(rows == place[...], 1.0, 0.0).astype(jnp.bfloat16)
            moved = jnp.dot(
                route, total[...].astype(jnp.bfloat16), preferred_element_type=jnp.float32
            )
            out[...] = moved.astype(jnp.bfloat16)
        else:
            out[...] = total[...]


def project(start, parts, order, w_query, w_kv_t, before, place, slots):
    row_width = w_query.shape[1] + w_kv_t.shape[0]
    width = parts[0].shape[1]
    block = width
    rows = sum(part.shape[0] for part in parts)
    first, last = before is None, place is not None
    vmem = pl.BlockSpec(memory_space=pltpu.VMEM)
    args = [*parts, w_query, w_kv_t]
    specs = [vmem] * len(parts)
    specs += [
        vmem,
        vmem,
    ]
    if not first:
        args.append(before)
        specs.append(vmem)
    if last:
        args.append(place.reshape(1, rows))
        specs.append(vmem)
        out = jax.ShapeDtypeStruct((slots, row_width), jnp.bfloat16)
    else:
        out = jax.ShapeDtypeStruct((rows, row_width), jnp.float32)
    return pl.pallas_call(
        functools.partial(project_kernel, first, last, order, start, block),
        grid=(width // block,),
        in_specs=specs,
        out_specs=vmem,
        out_shape=out,
        scratch_shapes=[pltpu.VMEM((rows, row_width), jnp.float32)],
        compiler_params=pltpu.CompilerParams(vmem_limit_bytes=24 * 2**20),
        cost_estimate=pl.CostEstimate(
            flops=2 * rows * width * row_width,
            bytes_accessed=2 * width * row_width,
            transcendentals=0,
        ),
        name="project",
    )(*args)


def attend_kernel(
    per_query,
    per_key,
    table,
    lengths,
    inbound,
    cosine,
    sine,
    key_pages,
    value_pages,
    out,
    key_pool,
    value_pool,
    sems,
    key_new,
    query_rot,
    value_own,
    chance,
    mixed,
):
    owners, slots, _ = inbound.shape
    pages = table.shape[1]
    page, kv_width = key_pages.shape[1:]
    kv_heads = kv_width // HEAD
    heads_dev = per_query // HEAD
    heads = owners * heads_dev
    pair = 2 * heads // kv_heads
    pairs = kv_heads // 2
    span = pages * page
    pieces = owners // kv_heads
    batches = query_rot.shape[1]
    batch = slots // batches

    cuts = 4
    size = key_pages.shape[0] // cuts

    def fetch_pool(pool, on_chip, sem):
        for cut in range(cuts):
            part = pl.ds(cut * size, size)
            pltpu.make_async_copy(pool.at[part], on_chip.at[part], sem).start()

    fetch_pool(key_pages, key_pool, sems.at[0])

    def held(pool, slot, columns):
        return [pool[table[slot, j], :, columns] for j in range(pages)]

    cos = cosine[...]
    sin = sine[...]

    def turn(x):
        return (x * cos + pltpu.roll(x, HEAD // 2, 1) * sin).astype(jnp.bfloat16)

    for source in range(owners):
        for j in range(heads_dev):
            x = inbound[source, :, j * HEAD : (j + 1) * HEAD].astype(jnp.float32)
            x = turn(x).astype(jnp.float32)
            head = source * heads_dev + j
            for b in range(batches):
                rows = pl.ds(head % pair * batch, batch)
                query_rot[head // pair, b, rows] = x[b * batch : (b + 1) * batch]

    piece = lax.broadcasted_iota(jnp.int32, (slots, HEAD), 1) // per_key
    for g in range(kv_heads):
        key = jnp.zeros((slots, HEAD), jnp.float32)
        value = jnp.zeros((slots, HEAD), jnp.float32)
        for j in range(pieces):
            tile = inbound[g * pieces + j, :, per_query : per_query + HEAD].astype(jnp.float32)
            shift = j * per_key
            back = (shift - per_key) % HEAD
            key = jnp.where(piece == j, pltpu.roll(tile, shift, 1) if shift else tile, key)
            value = jnp.where(piece == j, pltpu.roll(tile, back, 1) if back else tile, value)
        key_new[:, g * HEAD : (g + 1) * HEAD] = turn(key)
        value_own[g] = value

    scale = HEAD ** (-0.5)
    columns = pair * batch
    row = lax.broadcasted_iota(jnp.int32, (span, columns), 0)
    place = lax.broadcasted_iota(jnp.int32, (span, columns), 1) % batch
    own_row = lax.broadcasted_iota(jnp.int32, (slots, columns), 0)
    own_place = lax.broadcasted_iota(jnp.int32, (slots, columns), 1) % batch
    first = lax.broadcasted_iota(jnp.int32, (HEAD, columns), 1) < columns // 2
    same = lax.broadcasted_iota(jnp.int32, (columns, columns), 0) == lax.broadcasted_iota(
        jnp.int32, (columns, columns), 1
    )

    own_chances = {}
    pltpu.make_async_copy(key_pool, key_pool, sems.at[0]).wait()
    fetch_pool(value_pages, value_pool, sems.at[1])
    for p in range(pairs):
        columns_p = slice(p * 2 * HEAD, (p + 1) * 2 * HEAD)
        for b in range(batches):
            valid = row < lengths[b]
            turned = query_rot[p, b].T.astype(jnp.bfloat16)
            none = jnp.zeros_like(turned)
            wide = jnp.concatenate(
                [jnp.where(first, turned, none), jnp.where(first, none, turned)], axis=0
            )
            keys = []
            for s in range(batch):
                keys += held(key_pool, b * batch + s, columns_p)
            keys.append(key_new[:, columns_p])
            products = jnp.dot(
                jnp.concatenate(keys, axis=0), wide, preferred_element_type=jnp.float32
            )
            scores = products[:span]
            for s in range(1, batch):
                scores = jnp.where(place == s, products[s * span : (s + 1) * span], scores)
            own = jnp.where(own_row == own_place + b * batch, products[batch * span :], 0.0)
            own = jnp.sum(own, axis=0, keepdims=True) * scale
            masked = jnp.where(valid, scores * scale, -1e30)
            top = jnp.maximum(jnp.max(masked, axis=0, keepdims=True), own)
            terms = jnp.where(valid, jnp.exp(masked - top), 0.0)
            own_term = jnp.exp(own - top)
            total = jnp.sum(terms, axis=0, keepdims=True) + own_term
            chance[p, b] = (terms / total).T.astype(jnp.bfloat16).astype(jnp.float32)
            own_chance = (own_term / total).astype(jnp.bfloat16).astype(jnp.float32)
            own_chances[p, b] = jnp.sum(
                jnp.where(same, own_chance, 0.0), axis=1, keepdims=True
            )

    pltpu.make_async_copy(value_pool, value_pool, sems.at[1]).wait()
    for p in range(pairs):
        columns_p = slice(p * 2 * HEAD, (p + 1) * 2 * HEAD)
        for b in range(batches):
            for s in range(batch):
                mine = chance[p, b, pl.ds(s, pair, stride=batch)].astype(jnp.bfloat16)
                values = held(value_pool, b * batch + s, columns_p)
                both = jnp.dot(
                    mine, jnp.concatenate(values, axis=0), preferred_element_type=jnp.float32
                )
                result = jnp.concatenate(
                    [both[: pair // 2, :HEAD], both[pair // 2 :, HEAD:]], axis=0
                )
                mixed[p, b, pl.ds(s, pair, stride=batch)] = result
        for j in range(pair):
            head = p * pair + j
            g = head * kv_heads // heads
            halves = []
            for b in range(batches):
                rows = slice(j * batch, (j + 1) * batch)
                own_value = value_own[g, b * batch : (b + 1) * batch]
                halves.append(mixed[p, b, rows] + own_chances[p, b][rows] * own_value)
            column = head % heads_dev * HEAD
            out[head // heads_dev, :, column : column + HEAD] = jnp.concatenate(
                halves, axis=0
            ).astype(jnp.bfloat16)


def attend(inbound, lengths, table, cosine, sine, key_pages, value_pages, per_query, per_key):
    owners, slots, _ = inbound.shape
    pages = table.shape[1]
    page, kv_width = key_pages.shape[1:]
    kv_heads = kv_width // HEAD
    heads = owners * (per_query // HEAD)
    span = pages * page
    pair = 2 * heads // kv_heads
    pairs = kv_heads // 2
    batches = slots * pair // HEAD
    batch = slots // batches
    columns = pair * batch
    lengths = jnp.tile(lengths.reshape(batches, 1, batch), (1, 1, pair))
    smem = pl.BlockSpec(memory_space=pltpu.SMEM)
    vmem = pl.BlockSpec(memory_space=pltpu.VMEM)
    hbm = pl.BlockSpec(memory_space=pl.ANY)
    return pl.pallas_call(
        functools.partial(attend_kernel, per_query, per_key),
        in_specs=[smem, vmem, vmem, vmem, vmem, hbm, hbm],
        out_specs=vmem,
        out_shape=jax.ShapeDtypeStruct((owners, slots, per_query), jnp.bfloat16),
        scratch_shapes=[
            pltpu.VMEM(key_pages.shape, jnp.bfloat16),
            pltpu.VMEM(value_pages.shape, jnp.bfloat16),
            pltpu.SemaphoreType.DMA((2,)),
            pltpu.VMEM((slots, kv_width), jnp.bfloat16),
            pltpu.VMEM((pairs, batches, columns, HEAD), jnp.float32),
            pltpu.VMEM((kv_heads, slots, HEAD), jnp.float32),
            pltpu.VMEM((pairs, batches, columns, span), jnp.float32),
            pltpu.VMEM((pairs, batches, columns, HEAD), jnp.float32),
        ],
        compiler_params=pltpu.CompilerParams(vmem_limit_bytes=52 * 2**20),
        cost_estimate=pl.CostEstimate(
            flops=8 * slots * heads * span * HEAD,
            bytes_accessed=4 * slots * span * kv_width,
            transcendentals=slots * heads * span,
        ),
        name="attend",
    )(table, lengths, inbound, cosine, sine, key_pages, value_pages)


def on_device(
    hidden_in,
    norm_gain,
    w_query,
    w_key,
    w_value,
    w_out,
    key_pages,
    value_pages,
    page_table,
    kv_owner,
    cached,
):
    grid = Grid()
    owners = grid.size
    slot_count = page_table.shape[1]
    per_query = w_query.shape[1]
    per_key = w_key.shape[1]
    row_width = per_query + -(-2 * per_key // HEAD) * HEAD
    requests = kv_owner.shape[0]
    rows_dev = requests // owners
    width = hidden_in.shape[1]
    all_slots = owners * slot_count

    moves_a = grid.moves(ORDER_A)
    order_b = [moves_a.index(move) for move in grid.moves(ORDER_B)]
    cut = width // 8 * 5
    xa, xb = norm(hidden_in, norm_gain, (cut, width - cut))

    def placed(kv_owner):
        order = jnp.arange(requests, dtype=jnp.int32)
        earlier = (kv_owner[:, None] == kv_owner[None, :]) & (order[None, :] < order[:, None])
        return kv_owner * slot_count + jnp.sum(earlier.astype(jnp.int32), axis=1)

    def reordered(place, blocks):
        pick = blocks[:, None] == jnp.arange(owners, dtype=jnp.int32)[None, :]
        moved = jnp.where(pick[:, :, None], place.reshape(1, owners, rows_dev), 0)
        return jnp.sum(moved, axis=1).reshape(requests)

    def first(x):
        place = placed(after(kv_owner, x))
        pieces = [after(w_key, x).T, w_value.T]
        spare = row_width - per_query - 2 * per_key
        if spare:
            pieces.append(jnp.zeros((spare, width), w_key.dtype))
        return place, reordered(place, grid.blocks(-1, ORDER_A)), jnp.concatenate(pieces, axis=0)

    def second(x):
        return fetch((after(w_query, x), None), limit=44)[0]

    parts_a, parts_b, others, w_query = gather_rows(grid, xa, xb, first, second)
    place, place_in, w_kv_t = others
    plain = list(range(owners))
    total = project(0, parts_a, plain, w_query, w_kv_t, None, None, all_slots)
    total = project(cut, parts_b, order_b, w_query, w_kv_t, total, place_in, all_slots)
    outbound = total.reshape(owners, slot_count, row_width)
    place = after(place, outbound)
    place_a = reordered(place, grid.blocks(1, ORDER_A))
    place_b = reordered(place, grid.blocks(1, ORDER_B))
    mine = jnp.asarray(np.arange(all_slots, dtype=np.int32).reshape(owners, slot_count))
    mine = mine[lax.axis_index(AXES)]
    lengths = jnp.sum(jnp.where(place[:, None] == mine[None, :], cached[:, None], 0), axis=0)
    halfway = HEAD // 2
    offsets = jnp.arange(halfway, dtype=jnp.float32)
    frequency = rope_base ** (-(2.0 * offsets) / HEAD)
    angles = lengths.astype(jnp.float32)[:, None] * frequency
    cosine_part = jnp.cos(angles)
    sine_part = jnp.sin(angles)
    cosine = jnp.concatenate([cosine_part, cosine_part], axis=1)
    sine = jnp.concatenate([-sine_part, sine_part], axis=1)
    inbound = lax.all_to_all(outbound, AXES, split_axis=0, concat_axis=0, tiled=True)
    attended = attend(
        inbound,
        lengths,
        after(page_table, outbound)[0],
        cosine,
        sine,
        key_pages[0],
        value_pages[0],
        per_query,
        per_key,
    )
    (w_front,) = fetch((after(w_out, attended), (0, width // 32 * 10)), limit=48)
    returned = lax.all_to_all(attended, AXES, split_axis=0, concat_axis=0, tiled=True)
    returned = returned.reshape(all_slots, per_query)
    summed = scatter_sum(grid, place_a, place_b, returned, w_out, w_front, width // 32 * 21)
    return narrow(wide(hidden_in) + summed)


def solution(mesh):
    placed = (
        P(("groups", "tp", "attn"), None),
        P(),
        P(None, ("tp", "attn")),
        P(None, ("tp", "attn")),
        P(None, ("tp", "attn")),
        P(("tp", "attn"), None),
        P(("groups", "tp", "attn"), None, None, None),
        P(("groups", "tp", "attn"), None, None, None),
        P(("groups", "tp", "attn"), None, None),
        P("groups"),
        P("groups"),
    )
    return jax.shard_map(
        on_device,
        mesh=mesh,
        in_specs=placed,
        out_specs=P(("groups", "tp", "attn"), None),
        check_vma=False,
    )
```

```python
import functools

import jax
import jax.numpy as jnp
import numpy as np
from jax import lax
from jax.experimental import pallas as pl
from jax.experimental.pallas import tpu as pltpu
from jax.sharding import PartitionSpec as P

HEAD = 128
AXES = ("tp", "attn")

epsilon = 1e-05
rope_base = 500000.0


class Grid:
    def __init__(self):
        self.half = lax.axis_size("tp") // 4
        self.sizes = (self.half, 2, 2, lax.axis_size("attn"))
        self.size = int(np.prod(self.sizes))

    def shifted(self, place, moves):
        return np.ravel_multi_index(
            tuple((p + m) % n for p, m, n in zip(place, moves, self.sizes)), self.sizes
        )

    def send(self, x, half=0, pair=0, near=0, core=0):
        pairs = [
            (i, int(self.shifted(np.unravel_index(i, self.sizes), (half, pair, near, core))))
            for i in range(self.size)
        ]
        return lax.ppermute(x, AXES, pairs)

    def moves(self, order):
        counts = [self.sizes[axis] for axis in order]
        places = []
        for steps in np.ndindex(*counts):
            move = [0, 0, 0, 0]
            for axis, step in zip(order, steps):
                move[axis] = step
            places.append(tuple(move))
        return places


HALF, PAIR, NEAR, CORE = range(4)
ORDER_A = (CORE, NEAR, PAIR, HALF)
ORDER_B = (CORE, PAIR, HALF, NEAR)


def after(x, *earlier):
    return lax.optimization_barrier((x, *earlier))[0]


def gather_rows(grid, xa, xb, first, second):
    beside_b = grid.send(xb, near=1)
    line_a = jnp.concatenate(
        [xa]
        + [
            grid.send(xa, half=half, pair=pair)
            for pair in range(2)
            for half in range(grid.half)
            if half or pair
        ],
        axis=0,
    )
    pair_b = jnp.concatenate([xb, beside_b], axis=0)
    line_a, pair_b, first = lax.optimization_barrier((line_a, pair_b, first(xa)))
    beside_a = grid.send(line_a, near=1)
    parts_b = [pair_b] + [
        grid.send(pair_b, half=half, pair=pair)
        for pair in range(2)
        for half in range(grid.half)
        if half or pair
    ]
    beside_a, parts_b, second = lax.optimization_barrier((beside_a, parts_b, second(pair_b)))
    parts_a = [line_a, beside_a]
    parts_a += [grid.send(part, core=1) for part in parts_a]
    parts_b += [grid.send(part, core=1) for part in parts_b]
    return parts_a, parts_b, first, second


def narrow(x):
    return x.astype(jnp.bfloat16)


def wide(x):
    return x.astype(jnp.float32)


def product_kernel(
    cuts,
    place_a,
    place_b,
    returned,
    w_out,
    w_front,
    away_a,
    keep_a,
    away_b,
    keep_b,
    held,
    sems,
):
    front = w_front.shape[1]
    copies = []
    for i, (start, stop) in enumerate(cuts):
        copy = None
        if start >= front:
            size = pl.ds(start, stop - start), pl.ds(start - front, stop - start)
            copy = pltpu.make_async_copy(
                w_out.at[:, size[0]], held.at[:, size[1]], sems.at[i]
            )
            copy.start()
        copies.append(copy)
    slots = lax.broadcasted_iota(jnp.int32, (returned.shape[0], place_a.shape[1]), 0)

    def picked(place):
        route = jnp.where(slots == place[...], 1.0, 0.0).astype(jnp.bfloat16)
        rows = lax.dot_general(
            route, returned[...], (((0,), (0,)), ((), ())), preferred_element_type=jnp.float32
        )
        return rows.astype(jnp.bfloat16)

    rows_a, rows_b = picked(place_a), picked(place_b)
    half = keep_a.shape[0]
    middle = keep_a.shape[1]
    for copy, (start, stop) in zip(copies, cuts):
        if copy is not None:
            copy.wait()
        rows, away, keep = (rows_a, away_a, keep_a) if start < middle else (rows_b, away_b, keep_b)
        w = w_front[:, start:stop] if copy is None else held[:, start - front : stop - front]
        x = jnp.dot(rows, w, preferred_element_type=jnp.float32)
        begin = start if start < middle else start - middle
        here = slice(begin, begin + stop - start)
        keep[:, here] = x[:half]
        away[:, here] = x[half:].astype(jnp.bfloat16)


def product(place_a, place_b, returned, w_out, w_front, cut):
    rows = place_a.shape[1]
    depth, width = w_out.shape
    cuts = []
    front = w_front.shape[1]
    for start, stop in ((0, front), (front, cut), (cut, width)):
        while start < stop:
            cuts.append((start, min(start + 1024, stop)))
            start = cuts[-1][1]
    vmem = pl.BlockSpec(memory_space=pltpu.VMEM)
    out = []
    for size in (cut, width - cut):
        out.append(jax.ShapeDtypeStruct((rows // 2, size), jnp.bfloat16))
        out.append(jax.ShapeDtypeStruct((rows // 2, size), jnp.float32))
    return pl.pallas_call(
        functools.partial(product_kernel, tuple(cuts)),
        in_specs=[vmem, vmem, vmem, pl.BlockSpec(memory_space=pl.ANY), vmem],
        out_specs=[vmem] * 4,
        out_shape=out,
        scratch_shapes=[
            pltpu.VMEM((depth, width - front), jnp.bfloat16),
            pltpu.SemaphoreType.DMA((len(cuts),)),
        ],
        compiler_params=pltpu.CompilerParams(vmem_limit_bytes=48 * 2**20),
        cost_estimate=pl.CostEstimate(
            flops=2 * rows * depth * width, bytes_accessed=2 * depth * width, transcendentals=0
        ),
        name="product",
    )(place_a, place_b, returned, w_out, w_front)


def scatter_sum(grid, place_a, place_b, returned, w_out, w_front, cut):
    def direct(x):
        size = x.shape[0] // 2 // grid.half
        parts = []
        for pair in range(2):
            for half in range(grid.half):
                begin = (pair * grid.half + half) * size
                if begin:
                    sent = narrow(x[begin : begin + size])
                    parts.append(grid.send(sent, half=half, pair=pair))
        return x[:size], parts

    def total(x, parts):
        for part in parts:
            x = x + wide(part)
        return x

    away_a, keep_a, away_b, keep_b = product(place_a, place_b, returned, w_out, w_front, cut)
    xa = keep_a + wide(grid.send(away_a, core=1))
    middle = xa.shape[0] // 2
    sent_a = narrow(xa[middle:])
    got_a = grid.send(sent_a, near=1)
    xb = keep_b + wide(grid.send(after(away_b, sent_a), core=1))
    xb, got_b = direct(xb)
    got_a, got_b = lax.optimization_barrier((got_a, got_b))
    xa, parts_a = direct(xa[:middle] + wide(got_a))
    xb = total(xb, got_b)
    middle = xb.shape[0] // 2
    xb = xb[:middle] + wide(grid.send(narrow(xb[middle:]), near=1))
    xa = total(xa, parts_a)
    return jnp.concatenate([xa, xb], axis=1)


def norm_kernel(x, gain, *outs):
    inputs = x[...].astype(jnp.float32)
    factor = lax.rsqrt(jnp.mean(inputs * inputs, axis=1, keepdims=True) + epsilon)
    normed = (inputs * factor * gain[...]).astype(jnp.bfloat16)
    start = 0
    for out in outs:
        out[...] = normed[:, start : start + out.shape[1]]
        start += out.shape[1]


def norm(x, gain, widths):
    vmem = pl.BlockSpec(memory_space=pltpu.VMEM)
    return pl.pallas_call(
        norm_kernel,
        in_specs=[vmem, vmem],
        out_specs=[vmem] * len(widths),
        out_shape=[jax.ShapeDtypeStruct((x.shape[0], w), jnp.bfloat16) for w in widths],
        compiler_params=pltpu.CompilerParams(vmem_limit_bytes=60 * 2**20),
        name="norm",
    )(x, gain.reshape(1, -1))


def placing_kernel(sizes, slots, orders, kv_owner, *outs):
    requests = kv_owner.shape[1]
    row = lax.broadcasted_iota(jnp.int32, (requests, requests), 0)
    column = lax.broadcasted_iota(jnp.int32, (requests, requests), 1)

    def upright(x):
        return jnp.sum(jnp.where(row == column, x, 0.0), axis=1, keepdims=True)

    owner = kv_owner[...].astype(jnp.float32)
    earlier = (upright(owner) == owner) & (row < column)
    slot = jnp.sum(jnp.where(earlier, 1.0, 0.0), axis=0, keepdims=True)
    place = owner * slots + slot
    upright_place = upright(place)

    tp = lax.axis_index("tp")
    me = (lax.div(tp, 4), lax.rem(lax.div(tp, 2), 2), lax.rem(tp, 2), lax.axis_index("attn"))
    rows_dev = requests // int(np.prod(sizes))
    lane = lax.broadcasted_iota(jnp.int32, (1, requests), 1)
    for order, out in zip(orders, outs):
        if order is None:
            out[...] = place.astype(jnp.int32)
            continue
        if not order:
            out[...] = (tp * sizes[CORE] + me[CORE]) * slots + lane
            continue
        sign, axes = order
        rest = lax.div(lane, rows_dev)
        where = [None] * len(sizes)
        for axis in reversed(axes):
            move = lax.rem(rest, sizes[axis])
            rest = lax.div(rest, sizes[axis])
            where[axis] = lax.rem(me[axis] + sizes[axis] + sign * move, sizes[axis])
        block = where[0]
        for axis in range(1, len(sizes)):
            block = block * sizes[axis] + where[axis]
        source = block * rows_dev + lax.rem(lane, rows_dev)
        moved = jnp.sum(jnp.where(row == source, upright_place, 0.0), axis=0, keepdims=True)
        out[...] = moved.astype(jnp.int32)


def placing(kv_owner, sizes, slots, orders):
    requests = kv_owner.shape[0]
    vmem = pl.BlockSpec(memory_space=pltpu.VMEM)
    return pl.pallas_call(
        functools.partial(placing_kernel, sizes, slots, orders),
        in_specs=[vmem],
        out_specs=[vmem] * len(orders),
        out_shape=[jax.ShapeDtypeStruct((1, requests), jnp.int32)] * len(orders),
        compiler_params=pltpu.CompilerParams(vmem_limit_bytes=16 * 2**20),
        name="placing",
    )(kv_owner.reshape(1, requests))


def fetch_kernel(starts, *refs):
    count = len(starts)
    sems = refs[-1]
    copies = []
    for i, start in enumerate(starts):
        source, target = refs[i], refs[count + i]
        if start is not None:
            columns = pl.ds(start, target.shape[-1])
            source = source.at[(slice(None),) * (len(target.shape) - 1) + (columns,)]
        copies.append(pltpu.make_async_copy(source, target, sems.at[i]))
        copies[-1].start()
    for copy in copies:
        copy.wait()


def fetch(*wanted, limit):
    arrays = [x for x, _ in wanted]
    starts = [columns and columns[0] for _, columns in wanted]
    out = [
        jax.ShapeDtypeStruct(x.shape[:-1] + (columns[1],) if columns else x.shape, x.dtype)
        for x, columns in wanted
    ]
    return pl.pallas_call(
        functools.partial(fetch_kernel, starts),
        in_specs=[pl.BlockSpec(memory_space=pl.ANY)] * len(arrays),
        out_specs=[pl.BlockSpec(memory_space=pltpu.VMEM)] * len(arrays),
        out_shape=out,
        scratch_shapes=[pltpu.SemaphoreType.DMA((len(arrays),))],
        compiler_params=pltpu.CompilerParams(vmem_limit_bytes=limit * 2**20),
        cost_estimate=pl.CostEstimate(
            flops=0, bytes_accessed=sum(x.size * 4 for x in out), transcendentals=0
        ),
        name="fetch",
    )(*arrays)


def project_kernel(first, last, order, start, block, *refs):
    count = len(refs) - 4 - (not first) - last
    parts, (wq, w_kv), refs = refs[:count], refs[count : count + 2], refs[count + 2 :]
    if not first:
        before, refs = refs[0], refs[1:]
    if last:
        place, refs = refs[0], refs[1:]
    out, total = refs
    step = pl.program_id(0)
    per_query = wq.shape[1]

    @pl.when(step == 0)
    def _():
        total[...] = jnp.zeros_like(total) if first else before[...]

    here = pl.ds(pl.multiple_of(step * block, block), block)
    there = pl.ds(pl.multiple_of(start + step * block, block), block)
    x = jnp.concatenate([part[:, here] for part in parts], axis=0)
    products = [
        jnp.dot(x, wq[there, :], preferred_element_type=jnp.float32),
        lax.dot_general(x, w_kv[:, there], (((1,), (1,)), ((), ())), preferred_element_type=jnp.float32),
    ]
    size = x.shape[0] // len(order)
    for product, columns in zip(products, (slice(0, per_query), slice(per_query, None))):
        for i, place_i in enumerate(order):
            total[place_i * size : (place_i + 1) * size, columns] += product[
                i * size : (i + 1) * size
            ]

    @pl.when(step == pl.num_programs(0) - 1)
    def _():
        if last:
            rows = lax.broadcasted_iota(jnp.int32, (out.shape[0], place.shape[1]), 0)
            route = jnp.where(rows == place[...], 1.0, 0.0).astype(jnp.bfloat16)
            moved = jnp.dot(
                route, total[...].astype(jnp.bfloat16), preferred_element_type=jnp.float32
            )
            out[...] = moved.astype(jnp.bfloat16)
        else:
            out[...] = total[...]


def project(start, parts, order, w_query, w_kv_t, before, place, slots):
    row_width = w_query.shape[1] + w_kv_t.shape[0]
    width = parts[0].shape[1]
    block = width
    rows = sum(part.shape[0] for part in parts)
    first, last = before is None, place is not None
    vmem = pl.BlockSpec(memory_space=pltpu.VMEM)
    args = [*parts, w_query, w_kv_t]
    specs = [vmem] * len(parts)
    specs += [
        vmem,
        vmem,
    ]
    if not first:
        args.append(before)
        specs.append(vmem)
    if last:
        args.append(place)
        specs.append(vmem)
        out = jax.ShapeDtypeStruct((slots, row_width), jnp.bfloat16)
    else:
        out = jax.ShapeDtypeStruct((rows, row_width), jnp.float32)
    return pl.pallas_call(
        functools.partial(project_kernel, first, last, order, start, block),
        grid=(width // block,),
        in_specs=specs,
        out_specs=vmem,
        out_shape=out,
        scratch_shapes=[pltpu.VMEM((rows, row_width), jnp.float32)],
        compiler_params=pltpu.CompilerParams(vmem_limit_bytes=24 * 2**20),
        cost_estimate=pl.CostEstimate(
            flops=2 * rows * width * row_width,
            bytes_accessed=2 * width * row_width,
            transcendentals=0,
        ),
        name="project",
    )(*args)


def attend_kernel(
    per_query,
    per_key,
    table,
    lengths,
    inbound,
    cosine,
    sine,
    key_pages,
    value_pages,
    out,
    key_pool,
    value_pool,
    sems,
    key_new,
    query_rot,
    value_own,
    chance,
    mixed,
):
    owners, slots, _ = inbound.shape
    pages = table.shape[1]
    page, kv_width = key_pages.shape[1:]
    kv_heads = kv_width // HEAD
    heads_dev = per_query // HEAD
    heads = owners * heads_dev
    pair = 2 * heads // kv_heads
    pairs = kv_heads // 2
    span = pages * page
    pieces = owners // kv_heads
    batches = query_rot.shape[1]
    batch = slots // batches

    cuts = 16
    size = key_pages.shape[0] // cuts

    def fetch_pool(pool, on_chip, sem):
        for cut in range(cuts):
            part = pl.ds(cut * size, size)
            pltpu.make_async_copy(pool.at[part], on_chip.at[part], sem).start()

    fetch_pool(key_pages, key_pool, sems.at[0])
    fetch_pool(value_pages, value_pool, sems.at[1])

    def held(pool, slot, columns):
        return [pool[table[slot, j], :, columns] for j in range(pages)]

    cos = cosine[...]
    sin = sine[...]

    def turn(x):
        return (x * cos + pltpu.roll(x, HEAD // 2, 1) * sin).astype(jnp.bfloat16)

    for source in range(owners):
        for j in range(heads_dev):
            x = inbound[source, :, j * HEAD : (j + 1) * HEAD].astype(jnp.float32)
            x = turn(x).astype(jnp.float32)
            head = source * heads_dev + j
            for b in range(batches):
                rows = pl.ds(head % pair * batch, batch)
                query_rot[head // pair, b, rows] = x[b * batch : (b + 1) * batch]

    piece = lax.broadcasted_iota(jnp.int32, (slots, HEAD), 1) // per_key
    for g in range(kv_heads):
        key = jnp.zeros((slots, HEAD), jnp.float32)
        value = jnp.zeros((slots, HEAD), jnp.float32)
        for j in range(pieces):
            tile = inbound[g * pieces + j, :, per_query : per_query + HEAD].astype(jnp.float32)
            shift = j * per_key
            back = (shift - per_key) % HEAD
            key = jnp.where(piece == j, pltpu.roll(tile, shift, 1) if shift else tile, key)
            value = jnp.where(piece == j, pltpu.roll(tile, back, 1) if back else tile, value)
        key_new[:, g * HEAD : (g + 1) * HEAD] = turn(key)
        value_own[g] = value

    scale = HEAD ** (-0.5)
    columns = pair * batch
    row = lax.broadcasted_iota(jnp.int32, (span, columns), 0)
    place = lax.broadcasted_iota(jnp.int32, (span, columns), 1) % batch
    own_row = lax.broadcasted_iota(jnp.int32, (slots, columns), 0)
    own_place = lax.broadcasted_iota(jnp.int32, (slots, columns), 1) % batch
    first = lax.broadcasted_iota(jnp.int32, (HEAD, columns), 1) < columns // 2
    same = lax.broadcasted_iota(jnp.int32, (columns, columns), 0) == lax.broadcasted_iota(
        jnp.int32, (columns, columns), 1
    )

    own_chances = {}
    pltpu.make_async_copy(key_pool, key_pool, sems.at[0]).wait()
    for p in range(pairs):
        columns_p = slice(p * 2 * HEAD, (p + 1) * 2 * HEAD)
        for b in range(batches):
            valid = row < lengths[b]
            turned = query_rot[p, b].T.astype(jnp.bfloat16)
            none = jnp.zeros_like(turned)
            wide = jnp.concatenate(
                [jnp.where(first, turned, none), jnp.where(first, none, turned)], axis=0
            )
            keys = []
            for s in range(batch):
                keys += held(key_pool, b * batch + s, columns_p)
            keys.append(key_new[:, columns_p])
            products = jnp.dot(
                jnp.concatenate(keys, axis=0), wide, preferred_element_type=jnp.float32
            )
            scores = products[:span]
            for s in range(1, batch):
                scores = jnp.where(place == s, products[s * span : (s + 1) * span], scores)
            own = jnp.where(own_row == own_place + b * batch, products[batch * span :], 0.0)
            own = jnp.sum(own, axis=0, keepdims=True) * scale
            masked = jnp.where(valid, scores * scale, -1e30)
            top = jnp.maximum(jnp.max(masked, axis=0, keepdims=True), own)
            terms = jnp.where(valid, jnp.exp(masked - top), 0.0)
            own_term = jnp.exp(own - top)
            total = jnp.sum(terms, axis=0, keepdims=True) + own_term
            chance[p, b] = (terms / total).T.astype(jnp.bfloat16).astype(jnp.float32)
            own_chance = (own_term / total).astype(jnp.bfloat16).astype(jnp.float32)
            own_chances[p, b] = jnp.sum(
                jnp.where(same, own_chance, 0.0), axis=1, keepdims=True
            )

    pltpu.make_async_copy(value_pool, value_pool, sems.at[1]).wait()
    for p in range(pairs):
        columns_p = slice(p * 2 * HEAD, (p + 1) * 2 * HEAD)
        for b in range(batches):
            for s in range(batch):
                mine = chance[p, b, pl.ds(s, pair, stride=batch)].astype(jnp.bfloat16)
                values = held(value_pool, b * batch + s, columns_p)
                both = jnp.dot(
                    mine, jnp.concatenate(values, axis=0), preferred_element_type=jnp.float32
                )
                result = jnp.concatenate(
                    [both[: pair // 2, :HEAD], both[pair // 2 :, HEAD:]], axis=0
                )
                mixed[p, b, pl.ds(s, pair, stride=batch)] = result
        for j in range(pair):
            head = p * pair + j
            g = head * kv_heads // heads
            halves = []
            for b in range(batches):
                rows = slice(j * batch, (j + 1) * batch)
                own_value = value_own[g, b * batch : (b + 1) * batch]
                halves.append(mixed[p, b, rows] + own_chances[p, b][rows] * own_value)
            column = head % heads_dev * HEAD
            out[head // heads_dev, :, column : column + HEAD] = jnp.concatenate(
                halves, axis=0
            ).astype(jnp.bfloat16)


def attend(inbound, lengths, table, cosine, sine, key_pages, value_pages, per_query, per_key):
    owners, slots, _ = inbound.shape
    pages = table.shape[1]
    page, kv_width = key_pages.shape[1:]
    kv_heads = kv_width // HEAD
    heads = owners * (per_query // HEAD)
    span = pages * page
    pair = 2 * heads // kv_heads
    pairs = kv_heads // 2
    batches = slots * pair // HEAD
    batch = slots // batches
    columns = pair * batch
    lengths = jnp.tile(lengths.reshape(batches, 1, batch), (1, 1, pair))
    smem = pl.BlockSpec(memory_space=pltpu.SMEM)
    vmem = pl.BlockSpec(memory_space=pltpu.VMEM)
    hbm = pl.BlockSpec(memory_space=pl.ANY)
    return pl.pallas_call(
        functools.partial(attend_kernel, per_query, per_key),
        in_specs=[smem, vmem, vmem, vmem, vmem, hbm, hbm],
        out_specs=vmem,
        out_shape=jax.ShapeDtypeStruct((owners, slots, per_query), jnp.bfloat16),
        scratch_shapes=[
            pltpu.VMEM(key_pages.shape, jnp.bfloat16),
            pltpu.VMEM(value_pages.shape, jnp.bfloat16),
            pltpu.SemaphoreType.DMA((2,)),
            pltpu.VMEM((slots, kv_width), jnp.bfloat16),
            pltpu.VMEM((pairs, batches, columns, HEAD), jnp.float32),
            pltpu.VMEM((kv_heads, slots, HEAD), jnp.float32),
            pltpu.VMEM((pairs, batches, columns, span), jnp.float32),
            pltpu.VMEM((pairs, batches, columns, HEAD), jnp.float32),
        ],
        compiler_params=pltpu.CompilerParams(vmem_limit_bytes=52 * 2**20),
        cost_estimate=pl.CostEstimate(
            flops=8 * slots * heads * span * HEAD,
            bytes_accessed=4 * slots * span * kv_width,
            transcendentals=slots * heads * span,
        ),
        name="attend",
    )(table, lengths, inbound, cosine, sine, key_pages, value_pages)


def on_device(
    hidden_in,
    norm_gain,
    w_query,
    w_key,
    w_value,
    w_out,
    key_pages,
    value_pages,
    page_table,
    kv_owner,
    cached,
):
    grid = Grid()
    owners = grid.size
    slot_count = page_table.shape[1]
    per_query = w_query.shape[1]
    per_key = w_key.shape[1]
    row_width = per_query + -(-2 * per_key // HEAD) * HEAD
    requests = kv_owner.shape[0]
    rows_dev = requests // owners
    width = hidden_in.shape[1]
    all_slots = owners * slot_count

    moves_a = grid.moves(ORDER_A)
    order_b = [moves_a.index(move) for move in grid.moves(ORDER_B)]
    cut = width // 8 * 5
    xa, xb = norm(hidden_in, norm_gain, (cut, width - cut))

    def first(x):
        orders = (None, (-1, ORDER_A), (1, ORDER_A), (1, ORDER_B), ())
        places = placing(after(kv_owner, x), grid.sizes, slot_count, orders)
        pieces = [after(w_key, x).T, w_value.T]
        spare = row_width - per_query - 2 * per_key
        if spare:
            pieces.append(jnp.zeros((spare, width), w_key.dtype))
        return places, jnp.concatenate(pieces, axis=0)

    def second(x):
        return fetch((after(w_query, x), None), limit=44)[0]

    parts_a, parts_b, others, w_query = gather_rows(grid, xa, xb, first, second)
    (place, place_in, place_a, place_b, mine), w_kv_t = others
    plain = list(range(owners))
    total = project(0, parts_a, plain, w_query, w_kv_t, None, None, all_slots)
    total = project(cut, parts_b, order_b, w_query, w_kv_t, total, place_in, all_slots)
    outbound = total.reshape(owners, slot_count, row_width)
    place = after(place, outbound).reshape(requests)
    mine = mine[0, :slot_count]
    lengths = jnp.sum(jnp.where(place[:, None] == mine[None, :], cached[:, None], 0), axis=0)
    halfway = HEAD // 2
    offsets = jnp.arange(halfway, dtype=jnp.float32)
    frequency = rope_base ** (-(2.0 * offsets) / HEAD)
    angles = lengths.astype(jnp.float32)[:, None] * frequency
    cosine_part = jnp.cos(angles)
    sine_part = jnp.sin(angles)
    cosine = jnp.concatenate([cosine_part, cosine_part], axis=1)
    sine = jnp.concatenate([-sine_part, sine_part], axis=1)
    inbound = lax.all_to_all(outbound, AXES, split_axis=0, concat_axis=0, tiled=True)
    attended = attend(
        inbound,
        lengths,
        after(page_table, outbound)[0],
        cosine,
        sine,
        key_pages[0],
        value_pages[0],
        per_query,
        per_key,
    )
    (w_front,) = fetch((after(w_out, attended), (0, width // 32 * 10)), limit=48)
    returned = lax.all_to_all(attended, AXES, split_axis=0, concat_axis=0, tiled=True)
    returned = returned.reshape(all_slots, per_query)
    summed = scatter_sum(grid, place_a, place_b, returned, w_out, w_front, width // 32 * 21)
    return narrow(wide(hidden_in) + summed)


def solution(mesh):
    placed = (
        P(("groups", "tp", "attn"), None),
        P(),
        P(None, ("tp", "attn")),
        P(None, ("tp", "attn")),
        P(None, ("tp", "attn")),
        P(("tp", "attn"), None),
        P(("groups", "tp", "attn"), None, None, None),
        P(("groups", "tp", "attn"), None, None, None),
        P(("groups", "tp", "attn"), None, None),
        P("groups"),
        P("groups"),
    )
    return jax.shard_map(
        on_device,
        mesh=mesh,
        in_specs=placed,
        out_specs=P(("groups", "tp", "attn"), None),
        check_vma=False,
    )
```

```python
import functools

import jax
import jax.numpy as jnp
import numpy as np
from jax import lax
from jax.experimental import pallas as pl
from jax.experimental.pallas import tpu as pltpu
from jax.sharding import PartitionSpec as P

HEAD = 128
AXES = ("tp", "attn")

epsilon = 1e-05
rope_base = 500000.0


class Grid:
    def __init__(self):
        self.half = lax.axis_size("tp") // 4
        self.sizes = (self.half, 2, 2, lax.axis_size("attn"))
        self.size = int(np.prod(self.sizes))

    def shifted(self, place, moves):
        return np.ravel_multi_index(
            tuple((p + m) % n for p, m, n in zip(place, moves, self.sizes)), self.sizes
        )

    def send(self, x, half=0, pair=0, near=0, core=0):
        pairs = [
            (i, int(self.shifted(np.unravel_index(i, self.sizes), (half, pair, near, core))))
            for i in range(self.size)
        ]
        return lax.ppermute(x, AXES, pairs)

    def moves(self, order):
        counts = [self.sizes[axis] for axis in order]
        places = []
        for steps in np.ndindex(*counts):
            move = [0, 0, 0, 0]
            for axis, step in zip(order, steps):
                move[axis] = step
            places.append(tuple(move))
        return places


HALF, PAIR, NEAR, CORE = range(4)
ORDER_A = (CORE, NEAR, PAIR, HALF)
ORDER_B = (CORE, PAIR, HALF, NEAR)


def after(x, *earlier):
    return lax.optimization_barrier((x, *earlier))[0]


def gather_rows(grid, xa, xb, first, second):
    beside_b = grid.send(xb, near=1)
    line_a = jnp.concatenate(
        [xa]
        + [
            grid.send(xa, half=half, pair=pair)
            for pair in range(2)
            for half in range(grid.half)
            if half or pair
        ],
        axis=0,
    )
    pair_b = jnp.concatenate([xb, beside_b], axis=0)
    line_a, pair_b, first = lax.optimization_barrier((line_a, pair_b, first(xa)))
    beside_a = grid.send(line_a, near=1)
    parts_b = [pair_b] + [
        grid.send(pair_b, half=half, pair=pair)
        for pair in range(2)
        for half in range(grid.half)
        if half or pair
    ]
    beside_a, parts_b, second = lax.optimization_barrier((beside_a, parts_b, second(pair_b)))
    parts_a = [line_a, beside_a]
    parts_a += [grid.send(part, core=1) for part in parts_a]
    parts_b += [grid.send(part, core=1) for part in parts_b]
    return parts_a, parts_b, first, second


def narrow(x):
    return x.astype(jnp.bfloat16)


def wide(x):
    return x.astype(jnp.float32)


def product_kernel(
    cuts,
    place_a,
    place_b,
    returned,
    w_out,
    w_front,
    away_a,
    keep_a,
    away_b,
    keep_b,
    held,
    sems,
):
    front = w_front.shape[1]
    copies = []
    for i, (start, stop) in enumerate(cuts):
        copy = None
        if start >= front:
            size = pl.ds(start, stop - start), pl.ds(start - front, stop - start)
            copy = pltpu.make_async_copy(
                w_out.at[:, size[0]], held.at[:, size[1]], sems.at[i]
            )
            copy.start()
        copies.append(copy)
    slots = lax.broadcasted_iota(jnp.int32, (returned.shape[0], place_a.shape[1]), 0)

    def picked(place):
        route = jnp.where(slots == place[...], 1.0, 0.0).astype(jnp.bfloat16)
        rows = lax.dot_general(
            route, returned[...], (((0,), (0,)), ((), ())), preferred_element_type=jnp.float32
        )
        return rows.astype(jnp.bfloat16)

    rows_a, rows_b = picked(place_a), picked(place_b)
    half = keep_a.shape[0]
    middle = keep_a.shape[1]
    for copy, (start, stop) in zip(copies, cuts):
        if copy is not None:
            copy.wait()
        rows, away, keep = (rows_a, away_a, keep_a) if start < middle else (rows_b, away_b, keep_b)
        w = w_front[:, start:stop] if copy is None else held[:, start - front : stop - front]
        x = jnp.dot(rows, w, preferred_element_type=jnp.float32)
        begin = start if start < middle else start - middle
        here = slice(begin, begin + stop - start)
        keep[:, here] = x[:half]
        away[:, here] = x[half:].astype(jnp.bfloat16)


def product(place_a, place_b, returned, w_out, w_front, cut):
    rows = place_a.shape[1]
    depth, width = w_out.shape
    cuts = []
    front = w_front.shape[1]
    for start, stop in ((0, front), (front, cut), (cut, width)):
        while start < stop:
            cuts.append((start, min(start + 1024, stop)))
            start = cuts[-1][1]
    vmem = pl.BlockSpec(memory_space=pltpu.VMEM)
    out = []
    for size in (cut, width - cut):
        out.append(jax.ShapeDtypeStruct((rows // 2, size), jnp.bfloat16))
        out.append(jax.ShapeDtypeStruct((rows // 2, size), jnp.float32))
    return pl.pallas_call(
        functools.partial(product_kernel, tuple(cuts)),
        in_specs=[vmem, vmem, vmem, pl.BlockSpec(memory_space=pl.ANY), vmem],
        out_specs=[vmem] * 4,
        out_shape=out,
        scratch_shapes=[
            pltpu.VMEM((depth, width - front), jnp.bfloat16),
            pltpu.SemaphoreType.DMA((len(cuts),)),
        ],
        compiler_params=pltpu.CompilerParams(vmem_limit_bytes=48 * 2**20),
        cost_estimate=pl.CostEstimate(
            flops=2 * rows * depth * width, bytes_accessed=2 * depth * width, transcendentals=0
        ),
        name="product",
    )(place_a, place_b, returned, w_out, w_front)


def scatter_sum(grid, place_a, place_b, returned, w_out, w_front, cut):
    def direct(x):
        size = x.shape[0] // 2 // grid.half
        parts = []
        for pair in range(2):
            for half in range(grid.half):
                begin = (pair * grid.half + half) * size
                if begin:
                    sent = narrow(x[begin : begin + size])
                    parts.append(grid.send(sent, half=half, pair=pair))
        return x[:size], parts

    def total(x, parts):
        for part in parts:
            x = x + wide(part)
        return x

    away_a, keep_a, away_b, keep_b = product(place_a, place_b, returned, w_out, w_front, cut)
    xa = keep_a + wide(grid.send(away_a, core=1))
    middle = xa.shape[0] // 2
    sent_a = narrow(xa[middle:])
    got_a = grid.send(sent_a, near=1)
    xb = keep_b + wide(grid.send(after(away_b, sent_a), core=1))
    xb, got_b = direct(xb)
    got_a, got_b = lax.optimization_barrier((got_a, got_b))
    xa, parts_a = direct(xa[:middle] + wide(got_a))
    xb = total(xb, got_b)
    middle = xb.shape[0] // 2
    xb = xb[:middle] + wide(grid.send(narrow(xb[middle:]), near=1))
    xa = total(xa, parts_a)
    return jnp.concatenate([xa, xb], axis=1)


def norm_kernel(x, gain, *refs):
    outs, (rows, gains, sems) = refs[:-3], refs[-3:]
    copies = [
        pltpu.make_async_copy(x, rows, sems.at[0]),
        pltpu.make_async_copy(gain, gains, sems.at[1]),
    ]
    for copy in copies:
        copy.start()
    copies[0].wait()
    inputs = rows[...].astype(jnp.float32)
    factor = lax.rsqrt(jnp.mean(inputs * inputs, axis=1, keepdims=True) + epsilon)
    copies[1].wait()
    normed = (inputs * factor * gains[...]).astype(jnp.bfloat16)
    start = 0
    for out in outs:
        out[...] = normed[:, start : start + out.shape[1]]
        start += out.shape[1]


def norm(x, gain, widths):
    vmem = pl.BlockSpec(memory_space=pltpu.VMEM)
    hbm = pl.BlockSpec(memory_space=pl.ANY)
    return pl.pallas_call(
        norm_kernel,
        in_specs=[hbm, hbm],
        out_specs=[vmem] * len(widths),
        out_shape=[jax.ShapeDtypeStruct((x.shape[0], w), jnp.bfloat16) for w in widths],
        scratch_shapes=[
            pltpu.VMEM(x.shape, jnp.bfloat16),
            pltpu.VMEM((1, x.shape[1]), jnp.float32),
            pltpu.SemaphoreType.DMA((2,)),
        ],
        compiler_params=pltpu.CompilerParams(vmem_limit_bytes=60 * 2**20),
        name="norm",
    )(x, gain.reshape(1, -1))


def placing_kernel(sizes, slots, orders, kv_owner, *outs):
    requests = kv_owner.shape[1]
    row = lax.broadcasted_iota(jnp.int32, (requests, requests), 0)
    column = lax.broadcasted_iota(jnp.int32, (requests, requests), 1)

    def upright(x):
        return jnp.sum(jnp.where(row == column, x, 0.0), axis=1, keepdims=True)

    owner = kv_owner[...].astype(jnp.float32)
    earlier = (upright(owner) == owner) & (row < column)
    slot = jnp.sum(jnp.where(earlier, 1.0, 0.0), axis=0, keepdims=True)
    place = owner * slots + slot
    upright_place = upright(place)

    tp = lax.axis_index("tp")
    me = (lax.div(tp, 4), lax.rem(lax.div(tp, 2), 2), lax.rem(tp, 2), lax.axis_index("attn"))
    rows_dev = requests // int(np.prod(sizes))
    lane = lax.broadcasted_iota(jnp.int32, (1, requests), 1)
    for order, out in zip(orders, outs):
        if order is None:
            out[...] = place.astype(jnp.int32)
            continue
        if not order:
            out[...] = (tp * sizes[CORE] + me[CORE]) * slots + lane
            continue
        sign, axes = order
        rest = lax.div(lane, rows_dev)
        where = [None] * len(sizes)
        for axis in reversed(axes):
            move = lax.rem(rest, sizes[axis])
            rest = lax.div(rest, sizes[axis])
            where[axis] = lax.rem(me[axis] + sizes[axis] + sign * move, sizes[axis])
        block = where[0]
        for axis in range(1, len(sizes)):
            block = block * sizes[axis] + where[axis]
        source = block * rows_dev + lax.rem(lane, rows_dev)
        moved = jnp.sum(jnp.where(row == source, upright_place, 0.0), axis=0, keepdims=True)
        out[...] = moved.astype(jnp.int32)


def placing(kv_owner, sizes, slots, orders):
    requests = kv_owner.shape[0]
    vmem = pl.BlockSpec(memory_space=pltpu.VMEM)
    return pl.pallas_call(
        functools.partial(placing_kernel, sizes, slots, orders),
        in_specs=[vmem],
        out_specs=[vmem] * len(orders),
        out_shape=[jax.ShapeDtypeStruct((1, requests), jnp.int32)] * len(orders),
        compiler_params=pltpu.CompilerParams(vmem_limit_bytes=16 * 2**20),
        name="placing",
    )(kv_owner.reshape(1, requests))


def fetch_kernel(starts, *refs):
    count = len(starts)
    sems = refs[-1]
    copies = []
    for i, start in enumerate(starts):
        source, target = refs[i], refs[count + i]
        if start is not None:
            columns = pl.ds(start, target.shape[-1])
            source = source.at[(slice(None),) * (len(target.shape) - 1) + (columns,)]
        copies.append(pltpu.make_async_copy(source, target, sems.at[i]))
        copies[-1].start()
    for copy in copies:
        copy.wait()


def fetch(*wanted, limit):
    arrays = [x for x, _ in wanted]
    starts = [columns and columns[0] for _, columns in wanted]
    out = [
        jax.ShapeDtypeStruct(x.shape[:-1] + (columns[1],) if columns else x.shape, x.dtype)
        for x, columns in wanted
    ]
    return pl.pallas_call(
        functools.partial(fetch_kernel, starts),
        in_specs=[pl.BlockSpec(memory_space=pl.ANY)] * len(arrays),
        out_specs=[pl.BlockSpec(memory_space=pltpu.VMEM)] * len(arrays),
        out_shape=out,
        scratch_shapes=[pltpu.SemaphoreType.DMA((len(arrays),))],
        compiler_params=pltpu.CompilerParams(vmem_limit_bytes=limit * 2**20),
        cost_estimate=pl.CostEstimate(
            flops=0, bytes_accessed=sum(x.size * 4 for x in out), transcendentals=0
        ),
        name="fetch",
    )(*arrays)


def project_kernel(first, last, order, start, block, *refs):
    count = len(refs) - 4 - (not first) - last
    parts, (wq, w_kv), refs = refs[:count], refs[count : count + 2], refs[count + 2 :]
    if not first:
        before, refs = refs[0], refs[1:]
    if last:
        place, refs = refs[0], refs[1:]
    out, total = refs
    step = pl.program_id(0)
    per_query = wq.shape[1]

    @pl.when(step == 0)
    def _():
        total[...] = jnp.zeros_like(total) if first else before[...]

    here = pl.ds(pl.multiple_of(step * block, block), block)
    there = pl.ds(pl.multiple_of(start + step * block, block), block)
    x = jnp.concatenate([part[:, here] for part in parts], axis=0)
    products = [
        jnp.dot(x, wq[there, :], preferred_element_type=jnp.float32),
        lax.dot_general(x, w_kv[:, there], (((1,), (1,)), ((), ())), preferred_element_type=jnp.float32),
    ]
    size = x.shape[0] // len(order)
    for product, columns in zip(products, (slice(0, per_query), slice(per_query, None))):
        for i, place_i in enumerate(order):
            total[place_i * size : (place_i + 1) * size, columns] += product[
                i * size : (i + 1) * size
            ]

    @pl.when(step == pl.num_programs(0) - 1)
    def _():
        if last:
            rows = lax.broadcasted_iota(jnp.int32, (out.shape[0], place.shape[1]), 0)
            route = jnp.where(rows == place[...], 1.0, 0.0).astype(jnp.bfloat16)
            moved = jnp.dot(
                route, total[...].astype(jnp.bfloat16), preferred_element_type=jnp.float32
            )
            out[...] = moved.astype(jnp.bfloat16)
        else:
            out[...] = total[...]


def project(start, parts, order, w_query, w_kv_t, before, place, slots):
    row_width = w_query.shape[1] + w_kv_t.shape[0]
    width = parts[0].shape[1]
    block = width
    rows = sum(part.shape[0] for part in parts)
    first, last = before is None, place is not None
    vmem = pl.BlockSpec(memory_space=pltpu.VMEM)
    args = [*parts, w_query, w_kv_t]
    specs = [vmem] * len(parts)
    specs += [
        vmem,
        vmem,
    ]
    if not first:
        args.append(before)
        specs.append(vmem)
    if last:
        args.append(place)
        specs.append(vmem)
        out = jax.ShapeDtypeStruct((slots, row_width), jnp.bfloat16)
    else:
        out = jax.ShapeDtypeStruct((rows, row_width), jnp.float32)
    return pl.pallas_call(
        functools.partial(project_kernel, first, last, order, start, block),
        grid=(width // block,),
        in_specs=specs,
        out_specs=vmem,
        out_shape=out,
        scratch_shapes=[pltpu.VMEM((rows, row_width), jnp.float32)],
        compiler_params=pltpu.CompilerParams(vmem_limit_bytes=24 * 2**20),
        cost_estimate=pl.CostEstimate(
            flops=2 * rows * width * row_width,
            bytes_accessed=2 * width * row_width,
            transcendentals=0,
        ),
        name="project",
    )(*args)


def attend_kernel(
    per_query,
    per_key,
    table,
    counts,
    lengths,
    inbound,
    cosine,
    sine,
    key_pages,
    value_pages,
    out,
    key_pool,
    value_pool,
    key_sems,
    value_sems,
    key_new,
    query_rot,
    value_own,
    chance,
    mixed,
):
    owners, slots, _ = inbound.shape
    pages = table.shape[1]
    page, kv_width = key_pages.shape[1:]
    kv_heads = kv_width // HEAD
    heads_dev = per_query // HEAD
    heads = owners * heads_dev
    pair = 2 * heads // kv_heads
    pairs = kv_heads // 2
    span = pages * page
    pieces = owners // kv_heads
    batches = query_rot.shape[1]
    batch = slots // batches

    def page_copy(pool, on_chip, sems, slot, j):
        rows = pl.ds(j * page, page)
        return pltpu.make_async_copy(
            pool.at[table[slot, j]], on_chip.at[slot, rows], sems.at[slot, j]
        )

    def each_page(act, otherwise=None):
        def one(slot, carry):
            for j in range(pages):
                needed = counts[slot] > j * page

                @pl.when(needed)
                def _():
                    act(slot, j)

                if otherwise is not None:

                    @pl.when(jnp.logical_not(needed))
                    def _():
                        otherwise(slot, j)

            return carry

        lax.fori_loop(0, slots, one, 0)

    def clear(slot, j):
        value_pool[slot, pl.ds(j * page, page)] = jnp.zeros((page, kv_width), jnp.bfloat16)

    each_page(lambda slot, j: page_copy(key_pages, key_pool, key_sems, slot, j).start())
    each_page(lambda slot, j: page_copy(value_pages, value_pool, value_sems, slot, j).start(), clear)

    cos = cosine[...]
    sin = sine[...]

    def turn(x):
        return (x * cos + pltpu.roll(x, HEAD // 2, 1) * sin).astype(jnp.bfloat16)

    for source in range(owners):
        for j in range(heads_dev):
            x = inbound[source, :, j * HEAD : (j + 1) * HEAD].astype(jnp.float32)
            x = turn(x).astype(jnp.float32)
            head = source * heads_dev + j
            for b in range(batches):
                rows = pl.ds(head % pair * batch, batch)
                query_rot[head // pair, b, rows] = x[b * batch : (b + 1) * batch]

    piece = lax.broadcasted_iota(jnp.int32, (slots, HEAD), 1) // per_key
    for g in range(kv_heads):
        key = jnp.zeros((slots, HEAD), jnp.float32)
        value = jnp.zeros((slots, HEAD), jnp.float32)
        for j in range(pieces):
            tile = inbound[g * pieces + j, :, per_query : per_query + HEAD].astype(jnp.float32)
            shift = j * per_key
            back = (shift - per_key) % HEAD
            key = jnp.where(piece == j, pltpu.roll(tile, shift, 1) if shift else tile, key)
            value = jnp.where(piece == j, pltpu.roll(tile, back, 1) if back else tile, value)
        key_new[:, g * HEAD : (g + 1) * HEAD] = turn(key)
        value_own[g] = value

    scale = HEAD ** (-0.5)
    columns = pair * batch
    row = lax.broadcasted_iota(jnp.int32, (span, columns), 0)
    place = lax.broadcasted_iota(jnp.int32, (span, columns), 1) % batch
    own_row = lax.broadcasted_iota(jnp.int32, (slots, columns), 0)
    own_place = lax.broadcasted_iota(jnp.int32, (slots, columns), 1) % batch
    first = lax.broadcasted_iota(jnp.int32, (HEAD, columns), 1) < columns // 2
    same = lax.broadcasted_iota(jnp.int32, (columns, columns), 0) == lax.broadcasted_iota(
        jnp.int32, (columns, columns), 1
    )

    own_chances = {}
    each_page(lambda slot, j: page_copy(key_pages, key_pool, key_sems, slot, j).wait())
    for p in range(pairs):
        columns_p = slice(p * 2 * HEAD, (p + 1) * 2 * HEAD)
        for b in range(batches):
            valid = row < lengths[b]
            turned = query_rot[p, b].T.astype(jnp.bfloat16)
            none = jnp.zeros_like(turned)
            wide = jnp.concatenate(
                [jnp.where(first, turned, none), jnp.where(first, none, turned)], axis=0
            )
            keys = key_pool[b * batch : (b + 1) * batch, :, columns_p]
            keys = [keys.reshape(batch * span, 2 * HEAD), key_new[:, columns_p]]
            products = jnp.dot(
                jnp.concatenate(keys, axis=0), wide, preferred_element_type=jnp.float32
            )
            scores = products[:span]
            for s in range(1, batch):
                scores = jnp.where(place == s, products[s * span : (s + 1) * span], scores)
            own = jnp.where(own_row == own_place + b * batch, products[batch * span :], 0.0)
            own = jnp.sum(own, axis=0, keepdims=True) * scale
            masked = jnp.where(valid, scores * scale, -1e30)
            top = jnp.maximum(jnp.max(masked, axis=0, keepdims=True), own)
            terms = jnp.where(valid, jnp.exp(masked - top), 0.0)
            own_term = jnp.exp(own - top)
            total = jnp.sum(terms, axis=0, keepdims=True) + own_term
            chance[p, b] = (terms / total).T.astype(jnp.bfloat16).astype(jnp.float32)
            own_chance = (own_term / total).astype(jnp.bfloat16).astype(jnp.float32)
            own_chances[p, b] = jnp.sum(
                jnp.where(same, own_chance, 0.0), axis=1, keepdims=True
            )

    each_page(lambda slot, j: page_copy(value_pages, value_pool, value_sems, slot, j).wait())
    for p in range(pairs):
        columns_p = slice(p * 2 * HEAD, (p + 1) * 2 * HEAD)
        for b in range(batches):
            for s in range(batch):
                mine = chance[p, b, pl.ds(s, pair, stride=batch)].astype(jnp.bfloat16)
                both = jnp.dot(
                    mine,
                    value_pool[b * batch + s, :, columns_p],
                    preferred_element_type=jnp.float32,
                )
                result = jnp.concatenate(
                    [both[: pair // 2, :HEAD], both[pair // 2 :, HEAD:]], axis=0
                )
                mixed[p, b, pl.ds(s, pair, stride=batch)] = result
        for j in range(pair):
            head = p * pair + j
            g = head * kv_heads // heads
            halves = []
            for b in range(batches):
                rows = slice(j * batch, (j + 1) * batch)
                own_value = value_own[g, b * batch : (b + 1) * batch]
                halves.append(mixed[p, b, rows] + own_chances[p, b][rows] * own_value)
            column = head % heads_dev * HEAD
            out[head // heads_dev, :, column : column + HEAD] = jnp.concatenate(
                halves, axis=0
            ).astype(jnp.bfloat16)


def attend(inbound, lengths, table, cosine, sine, key_pages, value_pages, per_query, per_key):
    owners, slots, _ = inbound.shape
    pages = table.shape[1]
    page, kv_width = key_pages.shape[1:]
    kv_heads = kv_width // HEAD
    heads = owners * (per_query // HEAD)
    span = pages * page
    pair = 2 * heads // kv_heads
    pairs = kv_heads // 2
    batches = slots * pair // HEAD
    batch = slots // batches
    columns = pair * batch
    counts = lengths
    lengths = jnp.tile(lengths.reshape(batches, 1, batch), (1, 1, pair))
    smem = pl.BlockSpec(memory_space=pltpu.SMEM)
    vmem = pl.BlockSpec(memory_space=pltpu.VMEM)
    hbm = pl.BlockSpec(memory_space=pl.ANY)
    return pl.pallas_call(
        functools.partial(attend_kernel, per_query, per_key),
        in_specs=[smem, smem, vmem, vmem, vmem, vmem, hbm, hbm],
        out_specs=vmem,
        out_shape=jax.ShapeDtypeStruct((owners, slots, per_query), jnp.bfloat16),
        scratch_shapes=[
            pltpu.VMEM((slots, span, kv_width), jnp.bfloat16),
            pltpu.VMEM((slots, span, kv_width), jnp.bfloat16),
            pltpu.SemaphoreType.DMA((slots, pages)),
            pltpu.SemaphoreType.DMA((slots, pages)),
            pltpu.VMEM((slots, kv_width), jnp.bfloat16),
            pltpu.VMEM((pairs, batches, columns, HEAD), jnp.float32),
            pltpu.VMEM((kv_heads, slots, HEAD), jnp.float32),
            pltpu.VMEM((pairs, batches, columns, span), jnp.float32),
            pltpu.VMEM((pairs, batches, columns, HEAD), jnp.float32),
        ],
        compiler_params=pltpu.CompilerParams(vmem_limit_bytes=52 * 2**20),
        cost_estimate=pl.CostEstimate(
            flops=8 * slots * heads * span * HEAD,
            bytes_accessed=4 * slots * span * kv_width,
            transcendentals=slots * heads * span,
        ),
        name="attend",
    )(table, counts, lengths, inbound, cosine, sine, key_pages, value_pages)


def on_device(
    hidden_in,
    norm_gain,
    w_query,
    w_key,
    w_value,
    w_out,
    key_pages,
    value_pages,
    page_table,
    kv_owner,
    cached,
):
    grid = Grid()
    owners = grid.size
    slot_count = page_table.shape[1]
    per_query = w_query.shape[1]
    per_key = w_key.shape[1]
    row_width = per_query + -(-2 * per_key // HEAD) * HEAD
    requests = kv_owner.shape[0]
    rows_dev = requests // owners
    width = hidden_in.shape[1]
    all_slots = owners * slot_count

    moves_a = grid.moves(ORDER_A)
    order_b = [moves_a.index(move) for move in grid.moves(ORDER_B)]
    cut = width // 16 * 11
    xa, xb = norm(hidden_in, norm_gain, (cut, width - cut))

    def first(x):
        orders = (None, (-1, ORDER_A), (1, ORDER_A), (1, ORDER_B), ())
        places = placing(after(kv_owner, x), grid.sizes, slot_count, orders)
        pieces = [after(w_key, x).T, w_value.T]
        spare = row_width - per_query - 2 * per_key
        if spare:
            pieces.append(jnp.zeros((spare, width), w_key.dtype))
        return places, jnp.concatenate(pieces, axis=0)

    def second(x):
        return fetch((after(w_query, x), None), limit=44)[0]

    parts_a, parts_b, others, w_query = gather_rows(grid, xa, xb, first, second)
    (place, place_in, place_a, place_b, mine), w_kv_t = others
    plain = list(range(owners))
    total = project(0, parts_a, plain, w_query, w_kv_t, None, None, all_slots)
    total = project(cut, parts_b, order_b, w_query, w_kv_t, total, place_in, all_slots)
    outbound = total.reshape(owners, slot_count, row_width)
    place = after(place, outbound).reshape(requests)
    mine = mine[0, :slot_count]
    lengths = jnp.sum(jnp.where(place[:, None] == mine[None, :], cached[:, None], 0), axis=0)
    halfway = HEAD // 2
    offsets = jnp.arange(halfway, dtype=jnp.float32)
    frequency = rope_base ** (-(2.0 * offsets) / HEAD)
    angles = lengths.astype(jnp.float32)[:, None] * frequency
    cosine_part = jnp.cos(angles)
    sine_part = jnp.sin(angles)
    cosine = jnp.concatenate([cosine_part, cosine_part], axis=1)
    sine = jnp.concatenate([-sine_part, sine_part], axis=1)
    inbound = lax.all_to_all(outbound, AXES, split_axis=0, concat_axis=0, tiled=True)
    attended = attend(
        inbound,
        lengths,
        after(page_table, outbound)[0],
        cosine,
        sine,
        key_pages[0],
        value_pages[0],
        per_query,
        per_key,
    )
    (w_front,) = fetch((after(w_out, attended), (0, width // 32 * 10)), limit=48)
    returned = lax.all_to_all(attended, AXES, split_axis=0, concat_axis=0, tiled=True)
    returned = returned.reshape(all_slots, per_query)
    summed = scatter_sum(grid, place_a, place_b, returned, w_out, w_front, width // 32 * 21)
    return narrow(wide(hidden_in) + summed)


def solution(mesh):
    placed = (
        P(("groups", "tp", "attn"), None),
        P(),
        P(None, ("tp", "attn")),
        P(None, ("tp", "attn")),
        P(None, ("tp", "attn")),
        P(("tp", "attn"), None),
        P(("groups", "tp", "attn"), None, None, None),
        P(("groups", "tp", "attn"), None, None, None),
        P(("groups", "tp", "attn"), None, None),
        P("groups"),
        P("groups"),
    )
    return jax.shard_map(
        on_device,
        mesh=mesh,
        in_specs=placed,
        out_specs=P(("groups", "tp", "attn"), None),
        check_vma=False,
    )
```

```python
import functools

import jax
import jax.numpy as jnp
import numpy as np
from jax import lax
from jax.experimental import pallas as pl
from jax.experimental.pallas import tpu as pltpu
from jax.sharding import PartitionSpec as P

HEAD = 128
AXES = ("tp", "attn")

epsilon = 1e-05
rope_base = 500000.0


class Grid:
    def __init__(self):
        self.half = lax.axis_size("tp") // 4
        self.sizes = (self.half, 2, 2, lax.axis_size("attn"))
        self.size = int(np.prod(self.sizes))

    def shifted(self, place, moves):
        return np.ravel_multi_index(
            tuple((p + m) % n for p, m, n in zip(place, moves, self.sizes)), self.sizes
        )

    def send(self, x, half=0, pair=0, near=0, core=0):
        pairs = [
            (i, int(self.shifted(np.unravel_index(i, self.sizes), (half, pair, near, core))))
            for i in range(self.size)
        ]
        return lax.ppermute(x, AXES, pairs)

    def moves(self, order):
        counts = [self.sizes[axis] for axis in order]
        places = []
        for steps in np.ndindex(*counts):
            move = [0, 0, 0, 0]
            for axis, step in zip(order, steps):
                move[axis] = step
            places.append(tuple(move))
        return places


HALF, PAIR, NEAR, CORE = range(4)
ORDER_A = (CORE, NEAR, PAIR, HALF)
ORDER_B = (CORE, PAIR, HALF, NEAR)


def after(x, *earlier):
    return lax.optimization_barrier((x, *earlier))[0]


def gather_rows(grid, xa, xb, first, second):
    beside_b = grid.send(xb, near=1)
    line_a = jnp.concatenate(
        [xa]
        + [
            grid.send(xa, half=half, pair=pair)
            for pair in range(2)
            for half in range(grid.half)
            if half or pair
        ],
        axis=0,
    )
    pair_b = jnp.concatenate([xb, beside_b], axis=0)
    line_a, pair_b, first = lax.optimization_barrier((line_a, pair_b, first(xa)))
    beside_a = grid.send(line_a, near=1)
    parts_b = [pair_b] + [
        grid.send(pair_b, half=half, pair=pair)
        for pair in range(2)
        for half in range(grid.half)
        if half or pair
    ]
    beside_a, parts_b, second = lax.optimization_barrier((beside_a, parts_b, second(pair_b)))
    parts_a = [line_a, beside_a]
    parts_a += [grid.send(part, core=1) for part in parts_a]
    parts_b += [grid.send(part, core=1) for part in parts_b]
    return parts_a, parts_b, first, second


def narrow(x):
    return x.astype(jnp.bfloat16)


def wide(x):
    return x.astype(jnp.float32)


def product_kernel(
    cuts,
    place_a,
    place_b,
    returned,
    w_out,
    w_front,
    away_a,
    keep_a,
    away_b,
    keep_b,
    held,
    sems,
):
    front = w_front.shape[1]
    copies = []
    for i, (start, stop) in enumerate(cuts):
        copy = None
        if start >= front:
            size = pl.ds(start, stop - start), pl.ds(start - front, stop - start)
            copy = pltpu.make_async_copy(
                w_out.at[:, size[0]], held.at[:, size[1]], sems.at[i]
            )
            copy.start()
        copies.append(copy)
    slots = lax.broadcasted_iota(jnp.int32, (returned.shape[0], place_a.shape[1]), 0)

    def picked(place):
        route = jnp.where(slots == place[...], 1.0, 0.0).astype(jnp.bfloat16)
        rows = lax.dot_general(
            route, returned[...], (((0,), (0,)), ((), ())), preferred_element_type=jnp.float32
        )
        return rows.astype(jnp.bfloat16)

    rows_a, rows_b = picked(place_a), picked(place_b)
    half = keep_a.shape[0]
    middle = keep_a.shape[1]
    for copy, (start, stop) in zip(copies, cuts):
        if copy is not None:
            copy.wait()
        rows, away, keep = (rows_a, away_a, keep_a) if start < middle else (rows_b, away_b, keep_b)
        w = w_front[:, start:stop] if copy is None else held[:, start - front : stop - front]
        x = jnp.dot(rows, w, preferred_element_type=jnp.float32)
        begin = start if start < middle else start - middle
        here = slice(begin, begin + stop - start)
        keep[:, here] = x[:half]
        away[:, here] = x[half:].astype(jnp.bfloat16)


def product(place_a, place_b, returned, w_out, w_front, cut):
    rows = place_a.shape[1]
    depth, width = w_out.shape
    cuts = []
    front = w_front.shape[1]
    for start, stop in ((0, front), (front, cut), (cut, width)):
        while start < stop:
            cuts.append((start, min(start + 1024, stop)))
            start = cuts[-1][1]
    vmem = pl.BlockSpec(memory_space=pltpu.VMEM)
    out = []
    for size in (cut, width - cut):
        out.append(jax.ShapeDtypeStruct((rows // 2, size), jnp.bfloat16))
        out.append(jax.ShapeDtypeStruct((rows // 2, size), jnp.float32))
    return pl.pallas_call(
        functools.partial(product_kernel, tuple(cuts)),
        in_specs=[vmem, vmem, vmem, pl.BlockSpec(memory_space=pl.ANY), vmem],
        out_specs=[vmem] * 4,
        out_shape=out,
        scratch_shapes=[
            pltpu.VMEM((depth, width - front), jnp.bfloat16),
            pltpu.SemaphoreType.DMA((len(cuts),)),
        ],
        compiler_params=pltpu.CompilerParams(vmem_limit_bytes=48 * 2**20),
        cost_estimate=pl.CostEstimate(
            flops=2 * rows * depth * width, bytes_accessed=2 * depth * width, transcendentals=0
        ),
        name="product",
    )(place_a, place_b, returned, w_out, w_front)


def scatter_sum(grid, place_a, place_b, returned, w_out, w_front, cut):
    def pieces(x):
        size = x.shape[0] // 2 // grid.half
        return x[:size], [narrow(x[i * size : (i + 1) * size]) for i in range(1, 2 * grid.half)]

    def direct(sent):
        return [
            grid.send(x, half=i % grid.half, pair=i // grid.half)
            for i, x in enumerate(sent, start=1)
        ]

    def total(x, parts):
        for part in parts:
            x = x + wide(part)
        return x

    away_a, keep_a, away_b, keep_b = product(place_a, place_b, returned, w_out, w_front, cut)
    xa = keep_a + wide(grid.send(away_a, core=1))
    middle = xa.shape[0] // 2
    sent_a = narrow(xa[middle:])
    got_a = grid.send(sent_a, near=1)
    xb = keep_b + wide(grid.send(after(away_b, sent_a), core=1))
    xb, sent = pieces(xb)
    got_b = direct(sent)
    got_a, got_b[0] = lax.optimization_barrier((got_a, got_b[0]))
    xa, sent = pieces(xa[:middle] + wide(got_a))
    parts_a = direct(sent)
    xb = total(xb, got_b)
    middle = xb.shape[0] // 2
    sent_b = after(narrow(xb[middle:]), *sent)
    xa = total(xa, parts_a)
    xb = xb[:middle] + wide(after(grid.send(sent_b, near=1), xa))
    return jnp.concatenate([xa, xb], axis=1)


def norm_kernel(x, gain, *refs):
    outs, (rows, gains, sems) = refs[:-3], refs[-3:]
    copies = [
        pltpu.make_async_copy(x, rows, sems.at[0]),
        pltpu.make_async_copy(gain, gains, sems.at[1]),
    ]
    for copy in copies:
        copy.start()
    copies[0].wait()
    inputs = rows[...].astype(jnp.float32)
    factor = lax.rsqrt(jnp.mean(inputs * inputs, axis=1, keepdims=True) + epsilon)
    copies[1].wait()
    normed = (inputs * factor * gains[...]).astype(jnp.bfloat16)
    start = 0
    for out in outs:
        out[...] = normed[:, start : start + out.shape[1]]
        start += out.shape[1]


def norm(x, gain, widths):
    vmem = pl.BlockSpec(memory_space=pltpu.VMEM)
    hbm = pl.BlockSpec(memory_space=pl.ANY)
    return pl.pallas_call(
        norm_kernel,
        in_specs=[hbm, hbm],
        out_specs=[vmem] * len(widths),
        out_shape=[jax.ShapeDtypeStruct((x.shape[0], w), jnp.bfloat16) for w in widths],
        scratch_shapes=[
            pltpu.VMEM(x.shape, jnp.bfloat16),
            pltpu.VMEM((1, x.shape[1]), jnp.float32),
            pltpu.SemaphoreType.DMA((2,)),
        ],
        compiler_params=pltpu.CompilerParams(vmem_limit_bytes=60 * 2**20),
        name="norm",
    )(x, gain.reshape(1, -1))


def placing_kernel(sizes, slots, orders, kv_owner, *outs):
    requests = kv_owner.shape[1]
    row = lax.broadcasted_iota(jnp.int32, (requests, requests), 0)
    column = lax.broadcasted_iota(jnp.int32, (requests, requests), 1)

    def upright(x):
        return jnp.sum(jnp.where(row == column, x, 0.0), axis=1, keepdims=True)

    owner = kv_owner[...].astype(jnp.float32)
    earlier = (upright(owner) == owner) & (row < column)
    slot = jnp.sum(jnp.where(earlier, 1.0, 0.0), axis=0, keepdims=True)
    place = owner * slots + slot
    upright_place = upright(place)

    tp = lax.axis_index("tp")
    me = (lax.div(tp, 4), lax.rem(lax.div(tp, 2), 2), lax.rem(tp, 2), lax.axis_index("attn"))
    rows_dev = requests // int(np.prod(sizes))
    lane = lax.broadcasted_iota(jnp.int32, (1, requests), 1)
    for order, out in zip(orders, outs):
        if order is None:
            out[...] = place.astype(jnp.int32)
            continue
        if not order:
            out[...] = (tp * sizes[CORE] + me[CORE]) * slots + lane
            continue
        sign, axes = order
        rest = lax.div(lane, rows_dev)
        where = [None] * len(sizes)
        for axis in reversed(axes):
            move = lax.rem(rest, sizes[axis])
            rest = lax.div(rest, sizes[axis])
            where[axis] = lax.rem(me[axis] + sizes[axis] + sign * move, sizes[axis])
        block = where[0]
        for axis in range(1, len(sizes)):
            block = block * sizes[axis] + where[axis]
        source = block * rows_dev + lax.rem(lane, rows_dev)
        moved = jnp.sum(jnp.where(row == source, upright_place, 0.0), axis=0, keepdims=True)
        out[...] = moved.astype(jnp.int32)


def placing(kv_owner, sizes, slots, orders):
    requests = kv_owner.shape[0]
    vmem = pl.BlockSpec(memory_space=pltpu.VMEM)
    return pl.pallas_call(
        functools.partial(placing_kernel, sizes, slots, orders),
        in_specs=[vmem],
        out_specs=[vmem] * len(orders),
        out_shape=[jax.ShapeDtypeStruct((1, requests), jnp.int32)] * len(orders),
        compiler_params=pltpu.CompilerParams(vmem_limit_bytes=16 * 2**20),
        name="placing",
    )(kv_owner.reshape(1, requests))


def fetch_kernel(starts, *refs):
    count = len(starts)
    sems = refs[-1]
    copies = []
    for i, start in enumerate(starts):
        source, target = refs[i], refs[count + i]
        if start is not None:
            columns = pl.ds(start, target.shape[-1])
            source = source.at[(slice(None),) * (len(target.shape) - 1) + (columns,)]
        copies.append(pltpu.make_async_copy(source, target, sems.at[i]))
        copies[-1].start()
    for copy in copies:
        copy.wait()


def fetch(*wanted, limit):
    arrays = [x for x, _ in wanted]
    starts = [columns and columns[0] for _, columns in wanted]
    out = [
        jax.ShapeDtypeStruct(x.shape[:-1] + (columns[1],) if columns else x.shape, x.dtype)
        for x, columns in wanted
    ]
    return pl.pallas_call(
        functools.partial(fetch_kernel, starts),
        in_specs=[pl.BlockSpec(memory_space=pl.ANY)] * len(arrays),
        out_specs=[pl.BlockSpec(memory_space=pltpu.VMEM)] * len(arrays),
        out_shape=out,
        scratch_shapes=[pltpu.SemaphoreType.DMA((len(arrays),))],
        compiler_params=pltpu.CompilerParams(vmem_limit_bytes=limit * 2**20),
        cost_estimate=pl.CostEstimate(
            flops=0, bytes_accessed=sum(x.size * 4 for x in out), transcendentals=0
        ),
        name="fetch",
    )(*arrays)


def project_kernel(first, last, order, start, block, *refs):
    count = len(refs) - 4 - (not first) - last
    parts, (wq, w_kv), refs = refs[:count], refs[count : count + 2], refs[count + 2 :]
    if not first:
        before, refs = refs[0], refs[1:]
    if last:
        place, refs = refs[0], refs[1:]
    out, total = refs
    step = pl.program_id(0)
    per_query = wq.shape[1]

    @pl.when(step == 0)
    def _():
        total[...] = jnp.zeros_like(total) if first else before[...]

    here = pl.ds(pl.multiple_of(step * block, block), block)
    there = pl.ds(pl.multiple_of(start + step * block, block), block)
    x = jnp.concatenate([part[:, here] for part in parts], axis=0)
    products = [
        jnp.dot(x, wq[there, :], preferred_element_type=jnp.float32),
        lax.dot_general(x, w_kv[:, there], (((1,), (1,)), ((), ())), preferred_element_type=jnp.float32),
    ]
    size = x.shape[0] // len(order)
    for product, columns in zip(products, (slice(0, per_query), slice(per_query, None))):
        for i, place_i in enumerate(order):
            total[place_i * size : (place_i + 1) * size, columns] += product[
                i * size : (i + 1) * size
            ]

    @pl.when(step == pl.num_programs(0) - 1)
    def _():
        if last:
            rows = lax.broadcasted_iota(jnp.int32, (out.shape[0], place.shape[1]), 0)
            route = jnp.where(rows == place[...], 1.0, 0.0).astype(jnp.bfloat16)
            moved = jnp.dot(
                route, total[...].astype(jnp.bfloat16), preferred_element_type=jnp.float32
            )
            out[...] = moved.astype(jnp.bfloat16)
        else:
            out[...] = total[...]


def project(start, parts, order, w_query, w_kv_t, before, place, slots):
    row_width = w_query.shape[1] + w_kv_t.shape[0]
    width = parts[0].shape[1]
    block = width
    rows = sum(part.shape[0] for part in parts)
    first, last = before is None, place is not None
    vmem = pl.BlockSpec(memory_space=pltpu.VMEM)
    args = [*parts, w_query, w_kv_t]
    specs = [vmem] * len(parts)
    specs += [
        vmem,
        vmem,
    ]
    if not first:
        args.append(before)
        specs.append(vmem)
    if last:
        args.append(place)
        specs.append(vmem)
        out = jax.ShapeDtypeStruct((slots, row_width), jnp.bfloat16)
    else:
        out = jax.ShapeDtypeStruct((rows, row_width), jnp.float32)
    return pl.pallas_call(
        functools.partial(project_kernel, first, last, order, start, block),
        grid=(width // block,),
        in_specs=specs,
        out_specs=vmem,
        out_shape=out,
        scratch_shapes=[pltpu.VMEM((rows, row_width), jnp.float32)],
        compiler_params=pltpu.CompilerParams(vmem_limit_bytes=24 * 2**20),
        cost_estimate=pl.CostEstimate(
            flops=2 * rows * width * row_width,
            bytes_accessed=2 * width * row_width,
            transcendentals=0,
        ),
        name="project",
    )(*args)


def attend_kernel(
    per_query,
    per_key,
    table,
    lengths,
    inbound,
    cosine,
    sine,
    key_pages,
    value_pages,
    out,
    key_pool,
    value_pool,
    sems,
    key_new,
    query_rot,
    value_own,
    chance,
    mixed,
):
    owners, slots, _ = inbound.shape
    pages = table.shape[1]
    page, kv_width = key_pages.shape[1:]
    kv_heads = kv_width // HEAD
    heads_dev = per_query // HEAD
    heads = owners * heads_dev
    pair = 2 * heads // kv_heads
    pairs = kv_heads // 2
    span = pages * page
    pieces = owners // kv_heads
    batches = query_rot.shape[1]
    batch = slots // batches

    cuts = 16
    size = key_pages.shape[0] // cuts

    def fetch_pool(pool, on_chip, sem):
        for cut in range(cuts):
            part = pl.ds(cut * size, size)
            pltpu.make_async_copy(pool.at[part], on_chip.at[part], sem).start()

    fetch_pool(key_pages, key_pool, sems.at[0])
    fetch_pool(value_pages, value_pool, sems.at[1])

    def held(pool, slot, columns):
        return [pool[table[slot, j], :, columns] for j in range(pages)]

    cos = cosine[...]
    sin = sine[...]

    def turn(x):
        return (x * cos + pltpu.roll(x, HEAD // 2, 1) * sin).astype(jnp.bfloat16)

    for source in range(owners):
        for j in range(heads_dev):
            x = inbound[source, :, j * HEAD : (j + 1) * HEAD].astype(jnp.float32)
            x = turn(x).astype(jnp.float32)
            head = source * heads_dev + j
            for b in range(batches):
                rows = pl.ds(head % pair * batch, batch)
                query_rot[head // pair, b, rows] = x[b * batch : (b + 1) * batch]

    piece = lax.broadcasted_iota(jnp.int32, (slots, HEAD), 1) // per_key
    for g in range(kv_heads):
        key = jnp.zeros((slots, HEAD), jnp.float32)
        value = jnp.zeros((slots, HEAD), jnp.float32)
        for j in range(pieces):
            tile = inbound[g * pieces + j, :, per_query : per_query + HEAD].astype(jnp.float32)
            shift = j * per_key
            back = (shift - per_key) % HEAD
            key = jnp.where(piece == j, pltpu.roll(tile, shift, 1) if shift else tile, key)
            value = jnp.where(piece == j, pltpu.roll(tile, back, 1) if back else tile, value)
        key_new[:, g * HEAD : (g + 1) * HEAD] = turn(key)
        value_own[g] = value

    scale = HEAD ** (-0.5)
    columns = pair * batch
    row = lax.broadcasted_iota(jnp.int32, (span, columns), 0)
    place = lax.broadcasted_iota(jnp.int32, (span, columns), 1) % batch
    own_row = lax.broadcasted_iota(jnp.int32, (slots, columns), 0)
    own_place = lax.broadcasted_iota(jnp.int32, (slots, columns), 1) % batch
    first = lax.broadcasted_iota(jnp.int32, (HEAD, columns), 1) < columns // 2
    same = lax.broadcasted_iota(jnp.int32, (columns, columns), 0) == lax.broadcasted_iota(
        jnp.int32, (columns, columns), 1
    )

    own_chances = {}
    pltpu.make_async_copy(key_pool, key_pool, sems.at[0]).wait()
    for p in range(pairs):
        columns_p = slice(p * 2 * HEAD, (p + 1) * 2 * HEAD)
        for b in range(batches):
            valid = row < lengths[b]
            turned = query_rot[p, b].T.astype(jnp.bfloat16)
            none = jnp.zeros_like(turned)
            wide = jnp.concatenate(
                [jnp.where(first, turned, none), jnp.where(first, none, turned)], axis=0
            )
            keys = []
            for s in range(batch):
                keys += held(key_pool, b * batch + s, columns_p)
            keys.append(key_new[:, columns_p])
            products = jnp.dot(
                jnp.concatenate(keys, axis=0), wide, preferred_element_type=jnp.float32
            )
            scores = products[:span]
            for s in range(1, batch):
                scores = jnp.where(place == s, products[s * span : (s + 1) * span], scores)
            own = jnp.where(own_row == own_place + b * batch, products[batch * span :], 0.0)
            own = jnp.sum(own, axis=0, keepdims=True) * scale
            masked = jnp.where(valid, scores * scale, -1e30)
            top = jnp.maximum(jnp.max(masked, axis=0, keepdims=True), own)
            terms = jnp.where(valid, jnp.exp(masked - top), 0.0)
            own_term = jnp.exp(own - top)
            total = jnp.sum(terms, axis=0, keepdims=True) + own_term
            chance[p, b] = (terms / total).T.astype(jnp.bfloat16).astype(jnp.float32)
            own_chance = (own_term / total).astype(jnp.bfloat16).astype(jnp.float32)
            own_chances[p, b] = jnp.sum(
                jnp.where(same, own_chance, 0.0), axis=1, keepdims=True
            )

    pltpu.make_async_copy(value_pool, value_pool, sems.at[1]).wait()
    for p in range(pairs):
        columns_p = slice(p * 2 * HEAD, (p + 1) * 2 * HEAD)
        for b in range(batches):
            for s in range(batch):
                mine = chance[p, b, pl.ds(s, pair, stride=batch)].astype(jnp.bfloat16)
                values = held(value_pool, b * batch + s, columns_p)
                both = jnp.dot(
                    mine, jnp.concatenate(values, axis=0), preferred_element_type=jnp.float32
                )
                result = jnp.concatenate(
                    [both[: pair // 2, :HEAD], both[pair // 2 :, HEAD:]], axis=0
                )
                mixed[p, b, pl.ds(s, pair, stride=batch)] = result
        for j in range(pair):
            head = p * pair + j
            g = head * kv_heads // heads
            halves = []
            for b in range(batches):
                rows = slice(j * batch, (j + 1) * batch)
                own_value = value_own[g, b * batch : (b + 1) * batch]
                halves.append(mixed[p, b, rows] + own_chances[p, b][rows] * own_value)
            column = head % heads_dev * HEAD
            out[head // heads_dev, :, column : column + HEAD] = jnp.concatenate(
                halves, axis=0
            ).astype(jnp.bfloat16)


def attend(inbound, lengths, table, cosine, sine, key_pages, value_pages, per_query, per_key):
    owners, slots, _ = inbound.shape
    pages = table.shape[1]
    page, kv_width = key_pages.shape[1:]
    kv_heads = kv_width // HEAD
    heads = owners * (per_query // HEAD)
    span = pages * page
    pair = 2 * heads // kv_heads
    pairs = kv_heads // 2
    batches = slots * pair // HEAD
    batch = slots // batches
    columns = pair * batch
    lengths = jnp.tile(lengths.reshape(batches, 1, batch), (1, 1, pair))
    smem = pl.BlockSpec(memory_space=pltpu.SMEM)
    vmem = pl.BlockSpec(memory_space=pltpu.VMEM)
    hbm = pl.BlockSpec(memory_space=pl.ANY)
    return pl.pallas_call(
        functools.partial(attend_kernel, per_query, per_key),
        in_specs=[smem, vmem, vmem, vmem, vmem, hbm, hbm],
        out_specs=vmem,
        out_shape=jax.ShapeDtypeStruct((owners, slots, per_query), jnp.bfloat16),
        scratch_shapes=[
            pltpu.VMEM(key_pages.shape, jnp.bfloat16),
            pltpu.VMEM(value_pages.shape, jnp.bfloat16),
            pltpu.SemaphoreType.DMA((2,)),
            pltpu.VMEM((slots, kv_width), jnp.bfloat16),
            pltpu.VMEM((pairs, batches, columns, HEAD), jnp.float32),
            pltpu.VMEM((kv_heads, slots, HEAD), jnp.float32),
            pltpu.VMEM((pairs, batches, columns, span), jnp.float32),
            pltpu.VMEM((pairs, batches, columns, HEAD), jnp.float32),
        ],
        compiler_params=pltpu.CompilerParams(vmem_limit_bytes=52 * 2**20),
        cost_estimate=pl.CostEstimate(
            flops=8 * slots * heads * span * HEAD,
            bytes_accessed=4 * slots * span * kv_width,
            transcendentals=slots * heads * span,
        ),
        name="attend",
    )(table, lengths, inbound, cosine, sine, key_pages, value_pages)


def on_device(
    hidden_in,
    norm_gain,
    w_query,
    w_key,
    w_value,
    w_out,
    key_pages,
    value_pages,
    page_table,
    kv_owner,
    cached,
):
    grid = Grid()
    owners = grid.size
    slot_count = page_table.shape[1]
    per_query = w_query.shape[1]
    per_key = w_key.shape[1]
    row_width = per_query + -(-2 * per_key // HEAD) * HEAD
    requests = kv_owner.shape[0]
    rows_dev = requests // owners
    width = hidden_in.shape[1]
    all_slots = owners * slot_count

    moves_a = grid.moves(ORDER_A)
    order_b = [moves_a.index(move) for move in grid.moves(ORDER_B)]
    cut = width // 16 * 11
    xa, xb = norm(hidden_in, norm_gain, (cut, width - cut))

    def first(x):
        orders = (None, (-1, ORDER_A), (1, ORDER_A), (1, ORDER_B), ())
        places = placing(after(kv_owner, x), grid.sizes, slot_count, orders)
        pieces = [after(w_key, x).T, w_value.T]
        spare = row_width - per_query - 2 * per_key
        if spare:
            pieces.append(jnp.zeros((spare, width), w_key.dtype))
        return places, jnp.concatenate(pieces, axis=0)

    def second(x):
        return fetch((after(w_query, x), None), limit=44)[0]

    parts_a, parts_b, others, w_query = gather_rows(grid, xa, xb, first, second)
    (place, place_in, place_a, place_b, mine), w_kv_t = others
    plain = list(range(owners))
    total = project(0, parts_a, plain, w_query, w_kv_t, None, None, all_slots)
    total = project(cut, parts_b, order_b, w_query, w_kv_t, total, place_in, all_slots)
    outbound = total.reshape(owners, slot_count, row_width)
    place = after(place, outbound).reshape(requests)
    mine = mine[0, :slot_count]
    lengths = jnp.sum(jnp.where(place[:, None] == mine[None, :], cached[:, None], 0), axis=0)
    halfway = HEAD // 2
    offsets = jnp.arange(halfway, dtype=jnp.float32)
    frequency = rope_base ** (-(2.0 * offsets) / HEAD)
    angles = lengths.astype(jnp.float32)[:, None] * frequency
    cosine_part = jnp.cos(angles)
    sine_part = jnp.sin(angles)
    cosine = jnp.concatenate([cosine_part, cosine_part], axis=1)
    sine = jnp.concatenate([-sine_part, sine_part], axis=1)
    inbound = lax.all_to_all(outbound, AXES, split_axis=0, concat_axis=0, tiled=True)
    attended = attend(
        inbound,
        lengths,
        after(page_table, outbound)[0],
        cosine,
        sine,
        key_pages[0],
        value_pages[0],
        per_query,
        per_key,
    )
    (w_front,) = fetch((after(w_out, attended), (0, width // 32 * 10)), limit=48)
    returned = lax.all_to_all(attended, AXES, split_axis=0, concat_axis=0, tiled=True)
    returned = returned.reshape(all_slots, per_query)
    summed = scatter_sum(grid, place_a, place_b, returned, w_out, w_front, width // 32 * 21)
    return narrow(wide(hidden_in) + summed)


def solution(mesh):
    placed = (
        P(("groups", "tp", "attn"), None),
        P(),
        P(None, ("tp", "attn")),
        P(None, ("tp", "attn")),
        P(None, ("tp", "attn")),
        P(("tp", "attn"), None),
        P(("groups", "tp", "attn"), None, None, None),
        P(("groups", "tp", "attn"), None, None, None),
        P(("groups", "tp", "attn"), None, None),
        P("groups"),
        P("groups"),
    )
    return jax.shard_map(
        on_device,
        mesh=mesh,
        in_specs=placed,
        out_specs=P(("groups", "tp", "attn"), None),
        check_vma=False,
    )
```

```python
import functools

import jax
import jax.numpy as jnp
import numpy as np
from jax import lax
from jax.experimental import pallas as pl
from jax.experimental.pallas import tpu as pltpu
from jax.sharding import PartitionSpec as P

HEAD = 128
AXES = ("tp", "attn")

epsilon = 1e-05
rope_base = 500000.0


class Grid:
    def __init__(self):
        self.half = lax.axis_size("tp") // 4
        self.sizes = (self.half, 2, 2, lax.axis_size("attn"))
        self.size = int(np.prod(self.sizes))

    def shifted(self, place, moves):
        return np.ravel_multi_index(
            tuple((p + m) % n for p, m, n in zip(place, moves, self.sizes)), self.sizes
        )

    def send(self, x, half=0, pair=0, near=0, core=0):
        pairs = [
            (i, int(self.shifted(np.unravel_index(i, self.sizes), (half, pair, near, core))))
            for i in range(self.size)
        ]
        return lax.ppermute(x, AXES, pairs)

    def moves(self, order):
        counts = [self.sizes[axis] for axis in order]
        places = []
        for steps in np.ndindex(*counts):
            move = [0, 0, 0, 0]
            for axis, step in zip(order, steps):
                move[axis] = step
            places.append(tuple(move))
        return places


HALF, PAIR, NEAR, CORE = range(4)
ORDER_A = (CORE, NEAR, PAIR, HALF)
ORDER_B = (CORE, PAIR, HALF, NEAR)


def after(x, *earlier):
    return lax.optimization_barrier((x, *earlier))[0]


def gather_rows(grid, xa, xb, first, second):
    beside_b = grid.send(xb, near=1)
    line_a = jnp.concatenate(
        [xa]
        + [
            grid.send(xa, half=half, pair=pair)
            for pair in range(2)
            for half in range(grid.half)
            if half or pair
        ],
        axis=0,
    )
    pair_b = jnp.concatenate([xb, beside_b], axis=0)
    line_a, pair_b, first = lax.optimization_barrier((line_a, pair_b, first(xa)))
    beside_a = grid.send(line_a, near=1)
    parts_b = [pair_b] + [
        grid.send(pair_b, half=half, pair=pair)
        for pair in range(2)
        for half in range(grid.half)
        if half or pair
    ]
    beside_a, parts_b, second = lax.optimization_barrier((beside_a, parts_b, second(pair_b)))
    parts_a = [line_a, beside_a]
    parts_a += [grid.send(part, core=1) for part in parts_a]
    parts_b += [grid.send(part, core=1) for part in parts_b]
    return parts_a, parts_b, first, second


def narrow(x):
    return x.astype(jnp.bfloat16)


def wide(x):
    return x.astype(jnp.float32)


def product_kernel(
    cuts,
    place_a,
    place_b,
    returned,
    w_out,
    w_front,
    away_a,
    keep_a,
    away_b,
    keep_b,
    held,
    sems,
):
    front = w_front.shape[1]
    copies = []
    for i, (start, stop) in enumerate(cuts):
        copy = None
        if start >= front:
            size = pl.ds(start, stop - start), pl.ds(start - front, stop - start)
            copy = pltpu.make_async_copy(
                w_out.at[:, size[0]], held.at[:, size[1]], sems.at[i]
            )
            copy.start()
        copies.append(copy)
    slots = lax.broadcasted_iota(jnp.int32, (returned.shape[0], place_a.shape[1]), 0)

    def picked(place):
        route = jnp.where(slots == place[...], 1.0, 0.0).astype(jnp.bfloat16)
        rows = lax.dot_general(
            route, returned[...], (((0,), (0,)), ((), ())), preferred_element_type=jnp.float32
        )
        return rows.astype(jnp.bfloat16)

    rows_a, rows_b = picked(place_a), picked(place_b)
    half = keep_a.shape[0]
    middle = keep_a.shape[1]
    for copy, (start, stop) in zip(copies, cuts):
        if copy is not None:
            copy.wait()
        rows, away, keep = (rows_a, away_a, keep_a) if start < middle else (rows_b, away_b, keep_b)
        w = w_front[:, start:stop] if copy is None else held[:, start - front : stop - front]
        x = jnp.dot(rows, w, preferred_element_type=jnp.float32)
        begin = start if start < middle else start - middle
        here = slice(begin, begin + stop - start)
        keep[:, here] = x[:half]
        away[:, here] = x[half:].astype(jnp.bfloat16)


def product(place_a, place_b, returned, w_out, w_front, cut):
    rows = place_a.shape[1]
    depth, width = w_out.shape
    cuts = []
    front = w_front.shape[1]
    for start, stop in ((0, front), (front, cut), (cut, width)):
        while start < stop:
            cuts.append((start, min(start + 1024, stop)))
            start = cuts[-1][1]
    vmem = pl.BlockSpec(memory_space=pltpu.VMEM)
    out = []
    for size in (cut, width - cut):
        out.append(jax.ShapeDtypeStruct((rows // 2, size), jnp.bfloat16))
        out.append(jax.ShapeDtypeStruct((rows // 2, size), jnp.float32))
    return pl.pallas_call(
        functools.partial(product_kernel, tuple(cuts)),
        in_specs=[vmem, vmem, vmem, pl.BlockSpec(memory_space=pl.ANY), vmem],
        out_specs=[vmem] * 4,
        out_shape=out,
        scratch_shapes=[
            pltpu.VMEM((depth, width - front), jnp.bfloat16),
            pltpu.SemaphoreType.DMA((len(cuts),)),
        ],
        compiler_params=pltpu.CompilerParams(vmem_limit_bytes=48 * 2**20),
        cost_estimate=pl.CostEstimate(
            flops=2 * rows * depth * width, bytes_accessed=2 * depth * width, transcendentals=0
        ),
        name="product",
    )(place_a, place_b, returned, w_out, w_front)


def scatter_sum(grid, place_a, place_b, returned, w_out, w_front, cut):
    def pieces(x):
        size = x.shape[0] // 2 // grid.half
        return x[:size], [narrow(x[i * size : (i + 1) * size]) for i in range(1, 2 * grid.half)]

    def direct(sent):
        return [
            grid.send(x, half=i % grid.half, pair=i // grid.half)
            for i, x in enumerate(sent, start=1)
        ]

    def total(x, parts):
        for part in parts:
            x = x + wide(part)
        return x

    away_a, keep_a, away_b, keep_b = product(place_a, place_b, returned, w_out, w_front, cut)
    xa = keep_a + wide(grid.send(away_a, core=1))
    middle = xa.shape[0] // 2
    sent_a = narrow(xa[middle:])
    got_a = grid.send(sent_a, near=1)
    xb = keep_b + wide(grid.send(after(away_b, sent_a), core=1))
    xb, sent = pieces(xb)
    got_b = direct(sent)
    got_a, got_b[0] = lax.optimization_barrier((got_a, got_b[0]))
    xa, sent = pieces(xa[:middle] + wide(got_a))
    parts_a = direct(sent)
    xb = total(xb, got_b)
    middle = xb.shape[0] // 2
    sent_b = after(narrow(xb[middle:]), *sent)
    xa = total(xa, parts_a)
    xb = xb[:middle] + wide(after(grid.send(sent_b, near=1), xa))
    return jnp.concatenate([xa, xb], axis=1)


def norm_kernel(x, gain, *refs):
    outs, (rows, gains, sems) = refs[:-3], refs[-3:]
    copies = [
        pltpu.make_async_copy(x, rows, sems.at[0]),
        pltpu.make_async_copy(gain, gains, sems.at[1]),
    ]
    for copy in copies:
        copy.start()
    copies[0].wait()
    inputs = rows[...].astype(jnp.float32)
    factor = lax.rsqrt(jnp.mean(inputs * inputs, axis=1, keepdims=True) + epsilon)
    copies[1].wait()
    normed = (inputs * factor * gains[...]).astype(jnp.bfloat16)
    start = 0
    for out in outs:
        out[...] = normed[:, start : start + out.shape[1]]
        start += out.shape[1]


def norm(x, gain, widths):
    vmem = pl.BlockSpec(memory_space=pltpu.VMEM)
    hbm = pl.BlockSpec(memory_space=pl.ANY)
    return pl.pallas_call(
        norm_kernel,
        in_specs=[hbm, hbm],
        out_specs=[vmem] * len(widths),
        out_shape=[jax.ShapeDtypeStruct((x.shape[0], w), jnp.bfloat16) for w in widths],
        scratch_shapes=[
            pltpu.VMEM(x.shape, jnp.bfloat16),
            pltpu.VMEM((1, x.shape[1]), jnp.float32),
            pltpu.SemaphoreType.DMA((2,)),
        ],
        compiler_params=pltpu.CompilerParams(vmem_limit_bytes=60 * 2**20),
        name="norm",
    )(x, gain.reshape(1, -1))


def placing_kernel(sizes, slots, orders, kv_owner, *outs):
    requests = kv_owner.shape[1]
    row = lax.broadcasted_iota(jnp.int32, (requests, requests), 0)
    column = lax.broadcasted_iota(jnp.int32, (requests, requests), 1)

    def upright(x):
        return jnp.sum(jnp.where(row == column, x, 0.0), axis=1, keepdims=True)

    owner = kv_owner[...].astype(jnp.float32)
    earlier = (upright(owner) == owner) & (row < column)
    slot = jnp.sum(jnp.where(earlier, 1.0, 0.0), axis=0, keepdims=True)
    place = owner * slots + slot
    upright_place = upright(place)

    tp = lax.axis_index("tp")
    me = (lax.div(tp, 4), lax.rem(lax.div(tp, 2), 2), lax.rem(tp, 2), lax.axis_index("attn"))
    rows_dev = requests // int(np.prod(sizes))
    lane = lax.broadcasted_iota(jnp.int32, (1, requests), 1)
    for order, out in zip(orders, outs):
        if order is None:
            out[...] = place.astype(jnp.int32)
            continue
        if not order:
            out[...] = (tp * sizes[CORE] + me[CORE]) * slots + lane
            continue
        sign, axes = order
        rest = lax.div(lane, rows_dev)
        where = [None] * len(sizes)
        for axis in reversed(axes):
            move = lax.rem(rest, sizes[axis])
            rest = lax.div(rest, sizes[axis])
            where[axis] = lax.rem(me[axis] + sizes[axis] + sign * move, sizes[axis])
        block = where[0]
        for axis in range(1, len(sizes)):
            block = block * sizes[axis] + where[axis]
        source = block * rows_dev + lax.rem(lane, rows_dev)
        moved = jnp.sum(jnp.where(row == source, upright_place, 0.0), axis=0, keepdims=True)
        out[...] = moved.astype(jnp.int32)


def placing(kv_owner, sizes, slots, orders):
    requests = kv_owner.shape[0]
    vmem = pl.BlockSpec(memory_space=pltpu.VMEM)
    return pl.pallas_call(
        functools.partial(placing_kernel, sizes, slots, orders),
        in_specs=[vmem],
        out_specs=[vmem] * len(orders),
        out_shape=[jax.ShapeDtypeStruct((1, requests), jnp.int32)] * len(orders),
        compiler_params=pltpu.CompilerParams(vmem_limit_bytes=16 * 2**20),
        name="placing",
    )(kv_owner.reshape(1, requests))


def fetch_kernel(starts, *refs):
    count = len(starts)
    sems = refs[-1]
    copies = []
    for i, start in enumerate(starts):
        source, target = refs[i], refs[count + i]
        if start is not None:
            columns = pl.ds(start, target.shape[-1])
            source = source.at[(slice(None),) * (len(target.shape) - 1) + (columns,)]
        copies.append(pltpu.make_async_copy(source, target, sems.at[i]))
        copies[-1].start()
    for copy in copies:
        copy.wait()


def fetch(*wanted, limit):
    arrays = [x for x, _ in wanted]
    starts = [columns and columns[0] for _, columns in wanted]
    out = [
        jax.ShapeDtypeStruct(x.shape[:-1] + (columns[1],) if columns else x.shape, x.dtype)
        for x, columns in wanted
    ]
    return pl.pallas_call(
        functools.partial(fetch_kernel, starts),
        in_specs=[pl.BlockSpec(memory_space=pl.ANY)] * len(arrays),
        out_specs=[pl.BlockSpec(memory_space=pltpu.VMEM)] * len(arrays),
        out_shape=out,
        scratch_shapes=[pltpu.SemaphoreType.DMA((len(arrays),))],
        compiler_params=pltpu.CompilerParams(vmem_limit_bytes=limit * 2**20),
        cost_estimate=pl.CostEstimate(
            flops=0, bytes_accessed=sum(x.size * 4 for x in out), transcendentals=0
        ),
        name="fetch",
    )(*arrays)


def project_kernel(first, last, order, start, block, *refs):
    count = len(refs) - 4 - (not first) - last
    parts, (wq, w_kv), refs = refs[:count], refs[count : count + 2], refs[count + 2 :]
    if not first:
        before, refs = refs[0], refs[1:]
    if last:
        place, refs = refs[0], refs[1:]
    out, total = refs
    step = pl.program_id(0)
    per_query = wq.shape[1]

    @pl.when(step == 0)
    def _():
        total[...] = jnp.zeros_like(total) if first else before[...]

    here = pl.ds(pl.multiple_of(step * block, block), block)
    there = pl.ds(pl.multiple_of(start + step * block, block), block)
    x = jnp.concatenate([part[:, here] for part in parts], axis=0)
    products = [
        jnp.dot(x, wq[there, :], preferred_element_type=jnp.float32),
        lax.dot_general(x, w_kv[:, there], (((1,), (1,)), ((), ())), preferred_element_type=jnp.float32),
    ]
    size = x.shape[0] // len(order)
    for product, columns in zip(products, (slice(0, per_query), slice(per_query, None))):
        for i, place_i in enumerate(order):
            total[place_i * size : (place_i + 1) * size, columns] += product[
                i * size : (i + 1) * size
            ]

    @pl.when(step == pl.num_programs(0) - 1)
    def _():
        if last:
            rows = lax.broadcasted_iota(jnp.int32, (out.shape[0], place.shape[1]), 0)
            route = jnp.where(rows == place[...], 1.0, 0.0).astype(jnp.bfloat16)
            moved = jnp.dot(
                route, total[...].astype(jnp.bfloat16), preferred_element_type=jnp.float32
            )
            out[...] = moved.astype(jnp.bfloat16)
        else:
            out[...] = total[...]


def project(start, parts, order, w_query, w_kv_t, before, place, slots):
    row_width = w_query.shape[1] + w_kv_t.shape[0]
    width = parts[0].shape[1]
    block = width
    rows = sum(part.shape[0] for part in parts)
    first, last = before is None, place is not None
    vmem = pl.BlockSpec(memory_space=pltpu.VMEM)
    args = [*parts, w_query, w_kv_t]
    specs = [vmem] * len(parts)
    specs += [
        vmem,
        vmem,
    ]
    if not first:
        args.append(before)
        specs.append(vmem)
    if last:
        args.append(place)
        specs.append(vmem)
        out = jax.ShapeDtypeStruct((slots, row_width), jnp.bfloat16)
    else:
        out = jax.ShapeDtypeStruct((rows, row_width), jnp.float32)
    return pl.pallas_call(
        functools.partial(project_kernel, first, last, order, start, block),
        grid=(width // block,),
        in_specs=specs,
        out_specs=vmem,
        out_shape=out,
        scratch_shapes=[pltpu.VMEM((rows, row_width), jnp.float32)],
        compiler_params=pltpu.CompilerParams(vmem_limit_bytes=24 * 2**20),
        cost_estimate=pl.CostEstimate(
            flops=2 * rows * width * row_width,
            bytes_accessed=2 * width * row_width,
            transcendentals=0,
        ),
        name="project",
    )(*args)


def attend_kernel(
    per_query,
    per_key,
    table,
    lengths,
    inbound,
    cosine,
    sine,
    key_pages,
    value_pages,
    out,
    key_pool,
    value_pool,
    sems,
    key_new,
    query_rot,
    value_own,
    chance,
    mixed,
):
    owners, slots, _ = inbound.shape
    pages = table.shape[1]
    page, kv_width = key_pages.shape[1:]
    kv_heads = kv_width // HEAD
    heads_dev = per_query // HEAD
    heads = owners * heads_dev
    pair = 2 * heads // kv_heads
    pairs = kv_heads // 2
    span = pages * page
    pieces = owners // kv_heads
    batches = query_rot.shape[1]
    batch = slots // batches

    cuts = 8
    size = key_pages.shape[0] // cuts
    width = kv_width // 2
    for i, (pool, on_chip) in enumerate(((key_pages, key_pool), (value_pages, value_pool))):
        for half in range(2):
            for cut in range(cuts):
                part = pl.ds(cut * size, size)
                pltpu.make_async_copy(
                    pool.at[part, :, pl.ds(half * width, width)],
                    on_chip.at[half, part],
                    sems.at[i, half],
                ).start()

    def arrived(on_chip, i, p):
        half, inside = divmod(p * 2 * HEAD, width)
        if inside == 0:
            pltpu.make_async_copy(on_chip.at[half], on_chip.at[half], sems.at[i, half]).wait()
        return on_chip.at[half], slice(inside, inside + 2 * HEAD)

    def held(pool, slot, columns):
        return [pool[table[slot, j], :, columns] for j in range(pages)]

    cos = cosine[...]
    sin = sine[...]

    def turn(x):
        return (x * cos + pltpu.roll(x, HEAD // 2, 1) * sin).astype(jnp.bfloat16)

    for source in range(owners):
        for j in range(heads_dev):
            x = inbound[source, :, j * HEAD : (j + 1) * HEAD].astype(jnp.float32)
            x = turn(x).astype(jnp.float32)
            head = source * heads_dev + j
            for b in range(batches):
                rows = pl.ds(head % pair * batch, batch)
                query_rot[head // pair, b, rows] = x[b * batch : (b + 1) * batch]

    piece = lax.broadcasted_iota(jnp.int32, (slots, HEAD), 1) // per_key
    for g in range(kv_heads):
        key = jnp.zeros((slots, HEAD), jnp.float32)
        value = jnp.zeros((slots, HEAD), jnp.float32)
        for j in range(pieces):
            tile = inbound[g * pieces + j, :, per_query : per_query + HEAD].astype(jnp.float32)
            shift = j * per_key
            back = (shift - per_key) % HEAD
            key = jnp.where(piece == j, pltpu.roll(tile, shift, 1) if shift else tile, key)
            value = jnp.where(piece == j, pltpu.roll(tile, back, 1) if back else tile, value)
        key_new[:, g * HEAD : (g + 1) * HEAD] = turn(key)
        value_own[g] = value

    scale = HEAD ** (-0.5)
    columns = pair * batch
    row = lax.broadcasted_iota(jnp.int32, (span, columns), 0)
    place = lax.broadcasted_iota(jnp.int32, (span, columns), 1) % batch
    own_row = lax.broadcasted_iota(jnp.int32, (slots, columns), 0)
    own_place = lax.broadcasted_iota(jnp.int32, (slots, columns), 1) % batch
    first = lax.broadcasted_iota(jnp.int32, (HEAD, columns), 1) < columns // 2
    same = lax.broadcasted_iota(jnp.int32, (columns, columns), 0) == lax.broadcasted_iota(
        jnp.int32, (columns, columns), 1
    )

    own_chances = {}
    for p in range(pairs):
        key_half, columns_p = arrived(key_pool, 0, p)
        for b in range(batches):
            valid = row < lengths[b]
            turned = query_rot[p, b].T.astype(jnp.bfloat16)
            none = jnp.zeros_like(turned)
            wide = jnp.concatenate(
                [jnp.where(first, turned, none), jnp.where(first, none, turned)], axis=0
            )
            keys = []
            for s in range(batch):
                keys += held(key_half, b * batch + s, columns_p)
            keys.append(key_new[:, p * 2 * HEAD : (p + 1) * 2 * HEAD])
            products = jnp.dot(
                jnp.concatenate(keys, axis=0), wide, preferred_element_type=jnp.float32
            )
            scores = products[:span]
            for s in range(1, batch):
                scores = jnp.where(place == s, products[s * span : (s + 1) * span], scores)
            own = jnp.where(own_row == own_place + b * batch, products[batch * span :], 0.0)
            own = jnp.sum(own, axis=0, keepdims=True) * scale
            masked = jnp.where(valid, scores * scale, -1e30)
            top = jnp.maximum(jnp.max(masked, axis=0, keepdims=True), own)
            terms = jnp.where(valid, jnp.exp(masked - top), 0.0)
            own_term = jnp.exp(own - top)
            total = jnp.sum(terms, axis=0, keepdims=True) + own_term
            chance[p, b] = (terms / total).T.astype(jnp.bfloat16).astype(jnp.float32)
            own_chance = (own_term / total).astype(jnp.bfloat16).astype(jnp.float32)
            own_chances[p, b] = jnp.sum(
                jnp.where(same, own_chance, 0.0), axis=1, keepdims=True
            )

    for p in range(pairs):
        value_half, columns_p = arrived(value_pool, 1, p)
        for b in range(batches):
            for s in range(batch):
                mine = chance[p, b, pl.ds(s, pair, stride=batch)].astype(jnp.bfloat16)
                values = held(value_half, b * batch + s, columns_p)
                both = jnp.dot(
                    mine, jnp.concatenate(values, axis=0), preferred_element_type=jnp.float32
                )
                result = jnp.concatenate(
                    [both[: pair // 2, :HEAD], both[pair // 2 :, HEAD:]], axis=0
                )
                mixed[p, b, pl.ds(s, pair, stride=batch)] = result
        for j in range(pair):
            head = p * pair + j
            g = head * kv_heads // heads
            halves = []
            for b in range(batches):
                rows = slice(j * batch, (j + 1) * batch)
                own_value = value_own[g, b * batch : (b + 1) * batch]
                halves.append(mixed[p, b, rows] + own_chances[p, b][rows] * own_value)
            column = head % heads_dev * HEAD
            out[head // heads_dev, :, column : column + HEAD] = jnp.concatenate(
                halves, axis=0
            ).astype(jnp.bfloat16)


def attend(inbound, lengths, table, cosine, sine, key_pages, value_pages, per_query, per_key):
    owners, slots, _ = inbound.shape
    pages = table.shape[1]
    page, kv_width = key_pages.shape[1:]
    kv_heads = kv_width // HEAD
    heads = owners * (per_query // HEAD)
    span = pages * page
    pair = 2 * heads // kv_heads
    pairs = kv_heads // 2
    batches = slots * pair // HEAD
    batch = slots // batches
    columns = pair * batch
    lengths = jnp.tile(lengths.reshape(batches, 1, batch), (1, 1, pair))
    smem = pl.BlockSpec(memory_space=pltpu.SMEM)
    vmem = pl.BlockSpec(memory_space=pltpu.VMEM)
    hbm = pl.BlockSpec(memory_space=pl.ANY)
    return pl.pallas_call(
        functools.partial(attend_kernel, per_query, per_key),
        in_specs=[smem, vmem, vmem, vmem, vmem, hbm, hbm],
        out_specs=vmem,
        out_shape=jax.ShapeDtypeStruct((owners, slots, per_query), jnp.bfloat16),
        scratch_shapes=[
            pltpu.VMEM((2, *key_pages.shape[:2], kv_width // 2), jnp.bfloat16),
            pltpu.VMEM((2, *key_pages.shape[:2], kv_width // 2), jnp.bfloat16),
            pltpu.SemaphoreType.DMA((2, 2)),
            pltpu.VMEM((slots, kv_width), jnp.bfloat16),
            pltpu.VMEM((pairs, batches, columns, HEAD), jnp.float32),
            pltpu.VMEM((kv_heads, slots, HEAD), jnp.float32),
            pltpu.VMEM((pairs, batches, columns, span), jnp.float32),
            pltpu.VMEM((pairs, batches, columns, HEAD), jnp.float32),
        ],
        compiler_params=pltpu.CompilerParams(vmem_limit_bytes=52 * 2**20),
        cost_estimate=pl.CostEstimate(
            flops=8 * slots * heads * span * HEAD,
            bytes_accessed=4 * slots * span * kv_width,
            transcendentals=slots * heads * span,
        ),
        name="attend",
    )(table, lengths, inbound, cosine, sine, key_pages, value_pages)


def on_device(
    hidden_in,
    norm_gain,
    w_query,
    w_key,
    w_value,
    w_out,
    key_pages,
    value_pages,
    page_table,
    kv_owner,
    cached,
):
    grid = Grid()
    owners = grid.size
    slot_count = page_table.shape[1]
    per_query = w_query.shape[1]
    per_key = w_key.shape[1]
    row_width = per_query + -(-2 * per_key // HEAD) * HEAD
    requests = kv_owner.shape[0]
    rows_dev = requests // owners
    width = hidden_in.shape[1]
    all_slots = owners * slot_count

    moves_a = grid.moves(ORDER_A)
    order_b = [moves_a.index(move) for move in grid.moves(ORDER_B)]
    cut = width // 16 * 11
    xa, xb = norm(hidden_in, norm_gain, (cut, width - cut))

    def first(x):
        orders = (None, (-1, ORDER_A), (1, ORDER_A), (1, ORDER_B), ())
        places = placing(after(kv_owner, x), grid.sizes, slot_count, orders)
        pieces = [after(w_key, x).T, w_value.T]
        spare = row_width - per_query - 2 * per_key
        if spare:
            pieces.append(jnp.zeros((spare, width), w_key.dtype))
        return places, jnp.concatenate(pieces, axis=0)

    def second(x):
        return fetch((after(w_query, x), None), limit=44)[0]

    parts_a, parts_b, others, w_query = gather_rows(grid, xa, xb, first, second)
    (place, place_in, place_a, place_b, mine), w_kv_t = others
    plain = list(range(owners))
    total = project(0, parts_a, plain, w_query, w_kv_t, None, None, all_slots)
    total = project(cut, parts_b, order_b, w_query, w_kv_t, total, place_in, all_slots)
    outbound = total.reshape(owners, slot_count, row_width)
    place = after(place, outbound).reshape(requests)
    mine = mine[0, :slot_count]
    lengths = jnp.sum(jnp.where(place[:, None] == mine[None, :], cached[:, None], 0), axis=0)
    halfway = HEAD // 2
    offsets = jnp.arange(halfway, dtype=jnp.float32)
    frequency = rope_base ** (-(2.0 * offsets) / HEAD)
    angles = lengths.astype(jnp.float32)[:, None] * frequency
    cosine_part = jnp.cos(angles)
    sine_part = jnp.sin(angles)
    cosine = jnp.concatenate([cosine_part, cosine_part], axis=1)
    sine = jnp.concatenate([-sine_part, sine_part], axis=1)
    inbound = lax.all_to_all(outbound, AXES, split_axis=0, concat_axis=0, tiled=True)
    attended = attend(
        inbound,
        lengths,
        after(page_table, outbound)[0],
        cosine,
        sine,
        key_pages[0],
        value_pages[0],
        per_query,
        per_key,
    )
    (w_front,) = fetch((after(w_out, attended), (0, width // 32 * 10)), limit=48)
    returned = lax.all_to_all(attended, AXES, split_axis=0, concat_axis=0, tiled=True)
    returned = returned.reshape(all_slots, per_query)
    summed = scatter_sum(grid, place_a, place_b, returned, w_out, w_front, width // 32 * 21)
    return narrow(wide(hidden_in) + summed)


def solution(mesh):
    placed = (
        P(("groups", "tp", "attn"), None),
        P(),
        P(None, ("tp", "attn")),
        P(None, ("tp", "attn")),
        P(None, ("tp", "attn")),
        P(("tp", "attn"), None),
        P(("groups", "tp", "attn"), None, None, None),
        P(("groups", "tp", "attn"), None, None, None),
        P(("groups", "tp", "attn"), None, None),
        P("groups"),
        P("groups"),
    )
    return jax.shard_map(
        on_device,
        mesh=mesh,
        in_specs=placed,
        out_specs=P(("groups", "tp", "attn"), None),
        check_vma=False,
    )
```

```python
import functools

import jax
import jax.numpy as jnp
import numpy as np
from jax import lax
from jax.experimental import pallas as pl
from jax.experimental.pallas import tpu as pltpu
from jax.sharding import PartitionSpec as P

HEAD = 128
AXES = ("tp", "attn")

epsilon = 1e-05
rope_base = 500000.0


class Grid:
    def __init__(self):
        self.half = lax.axis_size("tp") // 4
        self.sizes = (self.half, 2, 2, lax.axis_size("attn"))
        self.size = int(np.prod(self.sizes))

    def shifted(self, place, moves):
        return np.ravel_multi_index(
            tuple((p + m) % n for p, m, n in zip(place, moves, self.sizes)), self.sizes
        )

    def send(self, x, half=0, pair=0, near=0, core=0):
        pairs = [
            (i, int(self.shifted(np.unravel_index(i, self.sizes), (half, pair, near, core))))
            for i in range(self.size)
        ]
        return lax.ppermute(x, AXES, pairs)

    def moves(self, order):
        counts = [self.sizes[axis] for axis in order]
        places = []
        for steps in np.ndindex(*counts):
            move = [0, 0, 0, 0]
            for axis, step in zip(order, steps):
                move[axis] = step
            places.append(tuple(move))
        return places


HALF, PAIR, NEAR, CORE = range(4)
ORDER_A = (CORE, NEAR, PAIR, HALF)
ORDER_B = (CORE, PAIR, HALF, NEAR)


def after(x, *earlier):
    return lax.optimization_barrier((x, *earlier))[0]


def gather_rows(grid, xa, xb, first, second):
    beside_b = grid.send(xb, near=1)
    line_a = jnp.concatenate(
        [xa]
        + [
            grid.send(xa, half=half, pair=pair)
            for pair in range(2)
            for half in range(grid.half)
            if half or pair
        ],
        axis=0,
    )
    pair_b = jnp.concatenate([xb, beside_b], axis=0)
    line_a, pair_b, first = lax.optimization_barrier((line_a, pair_b, first(xa)))
    beside_a = grid.send(line_a, near=1)
    parts_b = [pair_b] + [
        grid.send(pair_b, half=half, pair=pair)
        for pair in range(2)
        for half in range(grid.half)
        if half or pair
    ]
    beside_a, parts_b, second = lax.optimization_barrier((beside_a, parts_b, second(pair_b)))
    parts_a = [line_a, beside_a]
    parts_a += [grid.send(part, core=1) for part in parts_a]
    parts_b += [grid.send(part, core=1) for part in parts_b]
    return parts_a, parts_b, first, second


def narrow(x):
    return x.astype(jnp.bfloat16)


def wide(x):
    return x.astype(jnp.float32)


def product_kernel(
    cuts,
    place_a,
    place_b,
    returned,
    w_out,
    w_front,
    away_a,
    keep_a,
    away_b,
    keep_b,
    held,
    sems,
):
    front = w_front.shape[1]
    copies = []
    for i, (start, stop) in enumerate(cuts):
        copy = None
        if start >= front:
            size = pl.ds(start, stop - start), pl.ds(start - front, stop - start)
            copy = pltpu.make_async_copy(
                w_out.at[:, size[0]], held.at[:, size[1]], sems.at[i]
            )
            copy.start()
        copies.append(copy)
    slots = lax.broadcasted_iota(jnp.int32, (returned.shape[0], place_a.shape[1]), 0)

    def picked(place):
        route = jnp.where(slots == place[...], 1.0, 0.0).astype(jnp.bfloat16)
        rows = lax.dot_general(
            route, returned[...], (((0,), (0,)), ((), ())), preferred_element_type=jnp.float32
        )
        return rows.astype(jnp.bfloat16)

    rows_a, rows_b = picked(place_a), picked(place_b)
    half = keep_a.shape[0]
    middle = keep_a.shape[1]
    for copy, (start, stop) in zip(copies, cuts):
        if copy is not None:
            copy.wait()
        rows, away, keep = (rows_a, away_a, keep_a) if start < middle else (rows_b, away_b, keep_b)
        w = w_front[:, start:stop] if copy is None else held[:, start - front : stop - front]
        x = jnp.dot(rows, w, preferred_element_type=jnp.float32)
        begin = start if start < middle else start - middle
        here = slice(begin, begin + stop - start)
        keep[:, here] = x[:half]
        away[:, here] = x[half:].astype(jnp.bfloat16)


def product(place_a, place_b, returned, w_out, w_front, cut):
    rows = place_a.shape[1]
    depth, width = w_out.shape
    cuts = []
    front = w_front.shape[1]
    for start, stop in ((0, front), (front, cut), (cut, width)):
        while start < stop:
            cuts.append((start, min(start + 1024, stop)))
            start = cuts[-1][1]
    vmem = pl.BlockSpec(memory_space=pltpu.VMEM)
    out = []
    for size in (cut, width - cut):
        out.append(jax.ShapeDtypeStruct((rows // 2, size), jnp.bfloat16))
        out.append(jax.ShapeDtypeStruct((rows // 2, size), jnp.float32))
    return pl.pallas_call(
        functools.partial(product_kernel, tuple(cuts)),
        in_specs=[vmem, vmem, vmem, pl.BlockSpec(memory_space=pl.ANY), vmem],
        out_specs=[vmem] * 4,
        out_shape=out,
        scratch_shapes=[
            pltpu.VMEM((depth, width - front), jnp.bfloat16),
            pltpu.SemaphoreType.DMA((len(cuts),)),
        ],
        compiler_params=pltpu.CompilerParams(vmem_limit_bytes=48 * 2**20),
        cost_estimate=pl.CostEstimate(
            flops=2 * rows * depth * width, bytes_accessed=2 * depth * width, transcendentals=0
        ),
        name="product",
    )(place_a, place_b, returned, w_out, w_front)


def scatter_sum(grid, place_a, place_b, returned, w_out, w_front, cut):
    def pieces(x):
        size = x.shape[0] // 2 // grid.half
        return x[:size], [narrow(x[i * size : (i + 1) * size]) for i in range(1, 2 * grid.half)]

    def direct(sent):
        return [
            grid.send(x, half=i % grid.half, pair=i // grid.half)
            for i, x in enumerate(sent, start=1)
        ]

    def total(x, parts):
        for part in parts:
            x = x + wide(part)
        return x

    away_a, keep_a, away_b, keep_b = product(place_a, place_b, returned, w_out, w_front, cut)
    xa = keep_a + wide(grid.send(away_a, core=1))
    middle = xa.shape[0] // 2
    sent_a = narrow(xa[middle:])
    got_a = grid.send(sent_a, near=1)
    xb = keep_b + wide(grid.send(after(away_b, sent_a), core=1))
    xb, sent = pieces(xb)
    got_b = direct(sent)
    got_a, got_b[0] = lax.optimization_barrier((got_a, got_b[0]))
    xa, sent = pieces(xa[:middle] + wide(got_a))
    parts_a = direct(sent)
    xb = total(xb, got_b)
    middle = xb.shape[0] // 2
    sent_b = after(narrow(xb[middle:]), *sent)
    xa = total(xa, parts_a)
    xb = xb[:middle] + wide(after(grid.send(sent_b, near=1), xa))
    return jnp.concatenate([xa, xb], axis=1)


def norm_kernel(x, gain, *refs):
    outs, (rows, gains, sems) = refs[:-3], refs[-3:]
    copies = [
        pltpu.make_async_copy(x, rows, sems.at[0]),
        pltpu.make_async_copy(gain, gains, sems.at[1]),
    ]
    for copy in copies:
        copy.start()
    copies[0].wait()
    inputs = rows[...].astype(jnp.float32)
    factor = lax.rsqrt(jnp.mean(inputs * inputs, axis=1, keepdims=True) + epsilon)
    copies[1].wait()
    normed = (inputs * factor * gains[...]).astype(jnp.bfloat16)
    start = 0
    for out in outs:
        out[...] = normed[:, start : start + out.shape[1]]
        start += out.shape[1]


def norm(x, gain, widths):
    vmem = pl.BlockSpec(memory_space=pltpu.VMEM)
    hbm = pl.BlockSpec(memory_space=pl.ANY)
    return pl.pallas_call(
        norm_kernel,
        in_specs=[hbm, hbm],
        out_specs=[vmem] * len(widths),
        out_shape=[jax.ShapeDtypeStruct((x.shape[0], w), jnp.bfloat16) for w in widths],
        scratch_shapes=[
            pltpu.VMEM(x.shape, jnp.bfloat16),
            pltpu.VMEM((1, x.shape[1]), jnp.float32),
            pltpu.SemaphoreType.DMA((2,)),
        ],
        compiler_params=pltpu.CompilerParams(vmem_limit_bytes=60 * 2**20),
        name="norm",
    )(x, gain.reshape(1, -1))


def placing_kernel(sizes, slots, orders, kv_owner, *outs):
    requests = kv_owner.shape[1]
    row = lax.broadcasted_iota(jnp.int32, (requests, requests), 0)
    column = lax.broadcasted_iota(jnp.int32, (requests, requests), 1)

    def upright(x):
        return jnp.sum(jnp.where(row == column, x, 0.0), axis=1, keepdims=True)

    tp = lax.axis_index("tp")
    me = (lax.div(tp, 4), lax.rem(lax.div(tp, 2), 2), lax.rem(tp, 2), lax.axis_index("attn"))
    cores = sizes[CORE]
    chip = lax.div(kv_owner[...], cores)
    core = lax.rem(lax.rem(kv_owner[...], cores) + cores - me[CORE], cores)

    owner = kv_owner[...].astype(jnp.float32)
    earlier = (upright(owner) == owner) & (row < column)
    slot = jnp.sum(jnp.where(earlier, 1.0, 0.0), axis=0, keepdims=True)
    place = (chip * cores + core).astype(jnp.float32) * slots + slot
    chips = int(np.prod(sizes)) // cores
    by_core = (core * chips + chip).astype(jnp.float32) * slots + slot
    upright_place, upright_by_core = upright(place), upright(by_core)
    rows_dev = requests // int(np.prod(sizes))
    lane = lax.broadcasted_iota(jnp.int32, (1, requests), 1)
    for order, out in zip(orders, outs):
        if order is None:
            out[...] = place.astype(jnp.int32)
            continue
        if not order:
            out[...] = tp * cores * slots + lane
            continue
        sign, axes = order
        rest = lax.div(lane, rows_dev)
        where = [None] * len(sizes)
        for axis in reversed(axes):
            move = lax.rem(rest, sizes[axis])
            rest = lax.div(rest, sizes[axis])
            where[axis] = lax.rem(me[axis] + sizes[axis] + sign * move, sizes[axis])
        block = where[0]
        for axis in range(1, len(sizes)):
            block = block * sizes[axis] + where[axis]
        source = block * rows_dev + lax.rem(lane, rows_dev)
        wanted = upright_by_core if sign < 0 else upright_place
        moved = jnp.sum(jnp.where(row == source, wanted, 0.0), axis=0, keepdims=True)
        out[...] = moved.astype(jnp.int32)


def placing(kv_owner, sizes, slots, orders):
    requests = kv_owner.shape[0]
    vmem = pl.BlockSpec(memory_space=pltpu.VMEM)
    return pl.pallas_call(
        functools.partial(placing_kernel, sizes, slots, orders),
        in_specs=[vmem],
        out_specs=[vmem] * len(orders),
        out_shape=[jax.ShapeDtypeStruct((1, requests), jnp.int32)] * len(orders),
        compiler_params=pltpu.CompilerParams(vmem_limit_bytes=16 * 2**20),
        name="placing",
    )(kv_owner.reshape(1, requests))


def fetch_kernel(starts, *refs):
    count = len(starts)
    sems = refs[-1]
    copies = []
    for i, start in enumerate(starts):
        source, target = refs[i], refs[count + i]
        if start is not None:
            columns = pl.ds(start, target.shape[-1])
            source = source.at[(slice(None),) * (len(target.shape) - 1) + (columns,)]
        copies.append(pltpu.make_async_copy(source, target, sems.at[i]))
        copies[-1].start()
    for copy in copies:
        copy.wait()


def fetch(*wanted, limit):
    arrays = [x for x, _ in wanted]
    starts = [columns and columns[0] for _, columns in wanted]
    out = [
        jax.ShapeDtypeStruct(x.shape[:-1] + (columns[1],) if columns else x.shape, x.dtype)
        for x, columns in wanted
    ]
    return pl.pallas_call(
        functools.partial(fetch_kernel, starts),
        in_specs=[pl.BlockSpec(memory_space=pl.ANY)] * len(arrays),
        out_specs=[pl.BlockSpec(memory_space=pltpu.VMEM)] * len(arrays),
        out_shape=out,
        scratch_shapes=[pltpu.SemaphoreType.DMA((len(arrays),))],
        compiler_params=pltpu.CompilerParams(vmem_limit_bytes=limit * 2**20),
        cost_estimate=pl.CostEstimate(
            flops=0, bytes_accessed=sum(x.size * 4 for x in out), transcendentals=0
        ),
        name="fetch",
    )(*arrays)


def project_kernel(first, last, order, start, block, *refs):
    count = len(refs) - 4 - (not first) - 2 * last
    parts, (wq, w_kv), refs = refs[:count], refs[count : count + 2], refs[count + 2 :]
    if not first:
        before, refs = refs[0], refs[1:]
    if last:
        place, refs = refs[0], refs[1:]
    outs, total = refs[:-1], refs[-1]
    out = outs[0]
    step = pl.program_id(0)
    per_query = wq.shape[1]

    @pl.when(step == 0)
    def _():
        total[...] = jnp.zeros_like(total) if first else before[...]

    here = pl.ds(pl.multiple_of(step * block, block), block)
    there = pl.ds(pl.multiple_of(start + step * block, block), block)
    x = jnp.concatenate([part[:, here] for part in parts], axis=0)
    products = [
        jnp.dot(x, wq[there, :], preferred_element_type=jnp.float32),
        lax.dot_general(x, w_kv[:, there], (((1,), (1,)), ((), ())), preferred_element_type=jnp.float32),
    ]
    size = x.shape[0] // len(order)
    for product, columns in zip(products, (slice(0, per_query), slice(per_query, None))):
        for i, place_i in enumerate(order):
            total[place_i * size : (place_i + 1) * size, columns] += product[
                i * size : (i + 1) * size
            ]

    @pl.when(step == pl.num_programs(0) - 1)
    def _():
        if last:
            rows = lax.broadcasted_iota(jnp.int32, (out.shape[0], place.shape[1]), 0)
            for i, part in enumerate(outs):
                here = rows + i * out.shape[0] == place[...]
                route = jnp.where(here, 1.0, 0.0).astype(jnp.bfloat16)
                moved = jnp.dot(
                    route, total[...].astype(jnp.bfloat16), preferred_element_type=jnp.float32
                )
                part[...] = moved.astype(jnp.bfloat16)
        else:
            out[...] = total[...]


def project(start, parts, order, w_query, w_kv_t, before, place, slots):
    row_width = w_query.shape[1] + w_kv_t.shape[0]
    width = parts[0].shape[1]
    block = width
    rows = sum(part.shape[0] for part in parts)
    first, last = before is None, place is not None
    vmem = pl.BlockSpec(memory_space=pltpu.VMEM)
    args = [*parts, w_query, w_kv_t]
    specs = [vmem] * len(parts)
    specs += [
        vmem,
        vmem,
    ]
    if not first:
        args.append(before)
        specs.append(vmem)
    if last:
        args.append(place)
        specs.append(vmem)
        out = [jax.ShapeDtypeStruct((slots // 2, row_width), jnp.bfloat16)] * 2
    else:
        out = [jax.ShapeDtypeStruct((rows, row_width), jnp.float32)]
    return pl.pallas_call(
        functools.partial(project_kernel, first, last, order, start, block),
        grid=(width // block,),
        in_specs=specs,
        out_specs=[vmem] * len(out),
        out_shape=out,
        scratch_shapes=[pltpu.VMEM((rows, row_width), jnp.float32)],
        compiler_params=pltpu.CompilerParams(vmem_limit_bytes=24 * 2**20),
        cost_estimate=pl.CostEstimate(
            flops=2 * rows * width * row_width,
            bytes_accessed=2 * width * row_width,
            transcendentals=0,
        ),
        name="project",
    )(*args)


def attend_kernel(
    per_query,
    per_key,
    table,
    lengths,
    inbound,
    cosine,
    sine,
    key_pages,
    value_pages,
    out_own,
    out_other,
    key_pool,
    value_pool,
    sems,
    key_new,
    query_rot,
    value_own,
    chance,
    mixed,
):
    owners, slots, _ = inbound.shape
    pages = table.shape[1]
    page, kv_width = key_pages.shape[1:]
    kv_heads = kv_width // HEAD
    heads_dev = per_query // HEAD
    heads = owners * heads_dev
    pair = 2 * heads // kv_heads
    pairs = kv_heads // 2
    span = pages * page
    pieces = owners // kv_heads
    batches = query_rot.shape[1]
    batch = slots // batches

    cuts = 16
    size = key_pages.shape[0] // cuts

    def fetch_pool(pool, on_chip, sem):
        for cut in range(cuts):
            part = pl.ds(cut * size, size)
            pltpu.make_async_copy(pool.at[part], on_chip.at[part], sem).start()

    fetch_pool(key_pages, key_pool, sems.at[0])
    fetch_pool(value_pages, value_pool, sems.at[1])

    def held(pool, slot, columns):
        return [pool[table[slot, j], :, columns] for j in range(pages)]

    cos = cosine[...]
    sin = sine[...]

    def turn(x):
        return (x * cos + pltpu.roll(x, HEAD // 2, 1) * sin).astype(jnp.bfloat16)

    for source in range(owners):
        for j in range(heads_dev):
            x = inbound[source, :, j * HEAD : (j + 1) * HEAD].astype(jnp.float32)
            x = turn(x).astype(jnp.float32)
            head = source * heads_dev + j
            for b in range(batches):
                rows = pl.ds(head % pair * batch, batch)
                query_rot[head // pair, b, rows] = x[b * batch : (b + 1) * batch]

    piece = lax.broadcasted_iota(jnp.int32, (slots, HEAD), 1) // per_key
    straight = jnp.broadcast_to(lax.axis_index("attn") == 0, (slots, HEAD))

    def by_core(x):
        other = jnp.where(
            piece % 2 == 0, pltpu.roll(x, HEAD - per_key, 1), pltpu.roll(x, per_key, 1)
        )
        return jnp.where(straight, x, other)

    for g in range(kv_heads):
        key = jnp.zeros((slots, HEAD), jnp.float32)
        value = jnp.zeros((slots, HEAD), jnp.float32)
        for j in range(pieces):
            tile = inbound[g * pieces + j, :, per_query : per_query + HEAD].astype(jnp.float32)
            shift = j * per_key
            back = (shift - per_key) % HEAD
            key = jnp.where(piece == j, pltpu.roll(tile, shift, 1) if shift else tile, key)
            value = jnp.where(piece == j, pltpu.roll(tile, back, 1) if back else tile, value)
        key_new[:, g * HEAD : (g + 1) * HEAD] = turn(by_core(key))
        value_own[g] = by_core(value)

    scale = HEAD ** (-0.5)
    columns = pair * batch
    row = lax.broadcasted_iota(jnp.int32, (span, columns), 0)
    place = lax.broadcasted_iota(jnp.int32, (span, columns), 1) % batch
    own_row = lax.broadcasted_iota(jnp.int32, (slots, columns), 0)
    own_place = lax.broadcasted_iota(jnp.int32, (slots, columns), 1) % batch
    first = lax.broadcasted_iota(jnp.int32, (HEAD, columns), 1) < columns // 2
    same = lax.broadcasted_iota(jnp.int32, (columns, columns), 0) == lax.broadcasted_iota(
        jnp.int32, (columns, columns), 1
    )

    own_chances = {}
    pltpu.make_async_copy(key_pool, key_pool, sems.at[0]).wait()
    for p in range(pairs):
        columns_p = slice(p * 2 * HEAD, (p + 1) * 2 * HEAD)
        for b in range(batches):
            valid = row < lengths[b]
            turned = query_rot[p, b].T.astype(jnp.bfloat16)
            none = jnp.zeros_like(turned)
            wide = jnp.concatenate(
                [jnp.where(first, turned, none), jnp.where(first, none, turned)], axis=0
            )
            keys = []
            for s in range(batch):
                keys += held(key_pool, b * batch + s, columns_p)
            keys.append(key_new[:, columns_p])
            products = jnp.dot(
                jnp.concatenate(keys, axis=0), wide, preferred_element_type=jnp.float32
            )
            scores = products[:span]
            for s in range(1, batch):
                scores = jnp.where(place == s, products[s * span : (s + 1) * span], scores)
            own = jnp.where(own_row == own_place + b * batch, products[batch * span :], 0.0)
            own = jnp.sum(own, axis=0, keepdims=True) * scale
            masked = jnp.where(valid, scores * scale, -1e30)
            top = jnp.maximum(jnp.max(masked, axis=0, keepdims=True), own)
            terms = jnp.where(valid, jnp.exp(masked - top), 0.0)
            own_term = jnp.exp(own - top)
            total = jnp.sum(terms, axis=0, keepdims=True) + own_term
            chance[p, b] = (terms / total).T.astype(jnp.bfloat16).astype(jnp.float32)
            own_chance = (own_term / total).astype(jnp.bfloat16).astype(jnp.float32)
            own_chances[p, b] = jnp.sum(
                jnp.where(same, own_chance, 0.0), axis=1, keepdims=True
            )

    pltpu.make_async_copy(value_pool, value_pool, sems.at[1]).wait()
    for p in range(pairs):
        columns_p = slice(p * 2 * HEAD, (p + 1) * 2 * HEAD)
        for b in range(batches):
            for s in range(batch):
                mine = chance[p, b, pl.ds(s, pair, stride=batch)].astype(jnp.bfloat16)
                values = held(value_pool, b * batch + s, columns_p)
                both = jnp.dot(
                    mine, jnp.concatenate(values, axis=0), preferred_element_type=jnp.float32
                )
                result = jnp.concatenate(
                    [both[: pair // 2, :HEAD], both[pair // 2 :, HEAD:]], axis=0
                )
                mixed[p, b, pl.ds(s, pair, stride=batch)] = result
        for j in range(pair):
            head = p * pair + j
            g = head * kv_heads // heads
            halves = []
            for b in range(batches):
                rows = slice(j * batch, (j + 1) * batch)
                own_value = value_own[g, b * batch : (b + 1) * batch]
                halves.append(mixed[p, b, rows] + own_chances[p, b][rows] * own_value)
            column = head % heads_dev * HEAD
            target = head // heads_dev
            out = out_other if target % 2 else out_own
            out[target // 2, :, column : column + HEAD] = jnp.concatenate(
                halves, axis=0
            ).astype(jnp.bfloat16)


def attend(inbound, lengths, table, cosine, sine, key_pages, value_pages, per_query, per_key):
    owners, slots, _ = inbound.shape
    pages = table.shape[1]
    page, kv_width = key_pages.shape[1:]
    kv_heads = kv_width // HEAD
    heads = owners * (per_query // HEAD)
    span = pages * page
    pair = 2 * heads // kv_heads
    pairs = kv_heads // 2
    batches = slots * pair // HEAD
    batch = slots // batches
    columns = pair * batch
    lengths = jnp.tile(lengths.reshape(batches, 1, batch), (1, 1, pair))
    smem = pl.BlockSpec(memory_space=pltpu.SMEM)
    vmem = pl.BlockSpec(memory_space=pltpu.VMEM)
    hbm = pl.BlockSpec(memory_space=pl.ANY)
    return pl.pallas_call(
        functools.partial(attend_kernel, per_query, per_key),
        in_specs=[smem, vmem, vmem, vmem, vmem, hbm, hbm],
        out_specs=[vmem, vmem],
        out_shape=[jax.ShapeDtypeStruct((owners // 2, slots, per_query), jnp.bfloat16)] * 2,
        scratch_shapes=[
            pltpu.VMEM(key_pages.shape, jnp.bfloat16),
            pltpu.VMEM(value_pages.shape, jnp.bfloat16),
            pltpu.SemaphoreType.DMA((2,)),
            pltpu.VMEM((slots, kv_width), jnp.bfloat16),
            pltpu.VMEM((pairs, batches, columns, HEAD), jnp.float32),
            pltpu.VMEM((kv_heads, slots, HEAD), jnp.float32),
            pltpu.VMEM((pairs, batches, columns, span), jnp.float32),
            pltpu.VMEM((pairs, batches, columns, HEAD), jnp.float32),
        ],
        compiler_params=pltpu.CompilerParams(vmem_limit_bytes=52 * 2**20),
        cost_estimate=pl.CostEstimate(
            flops=8 * slots * heads * span * HEAD,
            bytes_accessed=4 * slots * span * kv_width,
            transcendentals=slots * heads * span,
        ),
        name="attend",
    )(table, lengths, inbound, cosine, sine, key_pages, value_pages)


def on_device(
    hidden_in,
    norm_gain,
    w_query,
    w_key,
    w_value,
    w_out,
    key_pages,
    value_pages,
    page_table,
    kv_owner,
    cached,
):
    grid = Grid()
    owners = grid.size
    slot_count = page_table.shape[1]
    per_query = w_query.shape[1]
    per_key = w_key.shape[1]
    row_width = per_query + -(-2 * per_key // HEAD) * HEAD
    requests = kv_owner.shape[0]
    rows_dev = requests // owners
    width = hidden_in.shape[1]
    all_slots = owners * slot_count

    moves_a = grid.moves(ORDER_A)
    order_b = [moves_a.index(move) for move in grid.moves(ORDER_B)]
    cut = width // 16 * 11
    xa, xb = norm(hidden_in, norm_gain, (cut, width - cut))

    def first(x):
        orders = (None, (-1, ORDER_A), (1, ORDER_A), (1, ORDER_B), ())
        places = placing(after(kv_owner, x), grid.sizes, slot_count, orders)
        pieces = [after(w_key, x).T, w_value.T]
        spare = row_width - per_query - 2 * per_key
        if spare:
            pieces.append(jnp.zeros((spare, width), w_key.dtype))
        return places, jnp.concatenate(pieces, axis=0)

    def second(x):
        return fetch((after(w_query, x), None), limit=44)[0]

    parts_a, parts_b, others, w_query = gather_rows(grid, xa, xb, first, second)
    (place, place_in, place_a, place_b, mine), w_kv_t = others
    plain = list(range(owners))
    (total,) = project(0, parts_a, plain, w_query, w_kv_t, None, None, all_slots)
    outbound, other = project(
        cut, parts_b, order_b, w_query, w_kv_t, total, place_in, all_slots
    )
    chips = owners // 2

    def exchange(own, other):
        other = grid.send(other, core=1)
        both = [x.reshape(chips, slot_count, x.shape[-1]) for x in (own, other)]
        both = jnp.concatenate(both, axis=1)
        return lax.all_to_all(both, "tp", split_axis=0, concat_axis=0, tiled=True), both

    place = after(place, outbound).reshape(requests)
    mine = mine[0, :slot_count]
    lengths = jnp.sum(jnp.where(place[:, None] == mine[None, :], cached[:, None], 0), axis=0)
    halfway = HEAD // 2
    offsets = jnp.arange(halfway, dtype=jnp.float32)
    frequency = rope_base ** (-(2.0 * offsets) / HEAD)
    angles = lengths.astype(jnp.float32)[:, None] * frequency
    cosine_part = jnp.cos(angles)
    sine_part = jnp.sin(angles)
    cosine = jnp.concatenate([cosine_part, cosine_part], axis=1)
    sine = jnp.concatenate([-sine_part, sine_part], axis=1)
    inbound, _ = exchange(outbound, other)
    inbound = inbound.reshape(owners, slot_count, row_width)
    attended, other = attend(
        inbound,
        lengths,
        after(page_table, outbound)[0],
        cosine,
        sine,
        key_pages[0],
        value_pages[0],
        per_query,
        per_key,
    )
    returned, sent = exchange(attended, other)
    (w_front,) = fetch((after(w_out, sent), (0, width // 32 * 10)), limit=48)
    returned = returned.reshape(all_slots, per_query)
    summed = scatter_sum(grid, place_a, place_b, returned, w_out, w_front, width // 32 * 21)
    return narrow(wide(hidden_in) + summed)


def solution(mesh):
    placed = (
        P(("groups", "tp", "attn"), None),
        P(),
        P(None, ("tp", "attn")),
        P(None, ("tp", "attn")),
        P(None, ("tp", "attn")),
        P(("tp", "attn"), None),
        P(("groups", "tp", "attn"), None, None, None),
        P(("groups", "tp", "attn"), None, None, None),
        P(("groups", "tp", "attn"), None, None),
        P("groups"),
        P("groups"),
    )
    return jax.shard_map(
        on_device,
        mesh=mesh,
        in_specs=placed,
        out_specs=P(("groups", "tp", "attn"), None),
        check_vma=False,
    )
```

```python
import functools

import jax
import jax.numpy as jnp
import numpy as np
from jax import lax
from jax.experimental import pallas as pl
from jax.experimental.pallas import tpu as pltpu
from jax.sharding import PartitionSpec as P

HEAD = 128
AXES = ("tp", "attn")

epsilon = 1e-05
rope_base = 500000.0


class Grid:
    def __init__(self):
        self.half = lax.axis_size("tp") // 4
        self.sizes = (self.half, 2, 2, lax.axis_size("attn"))
        self.size = int(np.prod(self.sizes))

    def shifted(self, place, moves):
        return np.ravel_multi_index(
            tuple((p + m) % n for p, m, n in zip(place, moves, self.sizes)), self.sizes
        )

    def send(self, x, half=0, pair=0, near=0, core=0):
        pairs = [
            (i, int(self.shifted(np.unravel_index(i, self.sizes), (half, pair, near, core))))
            for i in range(self.size)
        ]
        return lax.ppermute(x, AXES, pairs)

    def moves(self, order):
        counts = [self.sizes[axis] for axis in order]
        places = []
        for steps in np.ndindex(*counts):
            move = [0, 0, 0, 0]
            for axis, step in zip(order, steps):
                move[axis] = step
            places.append(tuple(move))
        return places


HALF, PAIR, NEAR, CORE = range(4)
ORDER_A = (CORE, NEAR, PAIR, HALF)
ORDER_B = (CORE, PAIR, HALF, NEAR)


def after(x, *earlier):
    return lax.optimization_barrier((x, *earlier))[0]


def gather_rows(grid, xa, xb, first, second):
    beside_b = grid.send(xb, near=1)
    line_a = jnp.concatenate(
        [xa]
        + [
            grid.send(xa, half=half, pair=pair)
            for pair in range(2)
            for half in range(grid.half)
            if half or pair
        ],
        axis=0,
    )
    pair_b = jnp.concatenate([xb, beside_b], axis=0)
    line_a, pair_b, first = lax.optimization_barrier((line_a, pair_b, first(xa)))
    beside_a = grid.send(line_a, near=1)
    parts_b = [pair_b] + [
        grid.send(pair_b, half=half, pair=pair)
        for pair in range(2)
        for half in range(grid.half)
        if half or pair
    ]
    beside_a, parts_b, second = lax.optimization_barrier((beside_a, parts_b, second(pair_b)))
    parts_a = [line_a, beside_a]
    parts_a += [grid.send(part, core=1) for part in parts_a]
    parts_b += [grid.send(part, core=1) for part in parts_b]
    return parts_a, parts_b, first, second


def narrow(x):
    return x.astype(jnp.bfloat16)


def wide(x):
    return x.astype(jnp.float32)


def product_kernel(
    cuts,
    place_a,
    place_b,
    returned,
    w_out,
    w_front,
    away_a,
    keep_a,
    away_b,
    keep_b,
    held,
    sems,
):
    front = w_front.shape[1]
    copies = []
    for i, (start, stop) in enumerate(cuts):
        copy = None
        if start >= front:
            size = pl.ds(start, stop - start), pl.ds(start - front, stop - start)
            copy = pltpu.make_async_copy(
                w_out.at[:, size[0]], held.at[:, size[1]], sems.at[i]
            )
            copy.start()
        copies.append(copy)
    slots = lax.broadcasted_iota(jnp.int32, (returned.shape[0], place_a.shape[1]), 0)

    def picked(place):
        route = jnp.where(slots == place[...], 1.0, 0.0).astype(jnp.bfloat16)
        rows = lax.dot_general(
            route, returned[...], (((0,), (0,)), ((), ())), preferred_element_type=jnp.float32
        )
        return rows.astype(jnp.bfloat16)

    rows_a, rows_b = picked(place_a), picked(place_b)
    half = keep_a.shape[0]
    middle = keep_a.shape[1]
    for copy, (start, stop) in zip(copies, cuts):
        if copy is not None:
            copy.wait()
        rows, away, keep = (rows_a, away_a, keep_a) if start < middle else (rows_b, away_b, keep_b)
        w = w_front[:, start:stop] if copy is None else held[:, start - front : stop - front]
        x = jnp.dot(rows, w, preferred_element_type=jnp.float32)
        begin = start if start < middle else start - middle
        here = slice(begin, begin + stop - start)
        keep[:, here] = x[:half]
        away[:, here] = x[half:].astype(jnp.bfloat16)


def product(place_a, place_b, returned, w_out, w_front, cut):
    rows = place_a.shape[1]
    depth, width = w_out.shape
    cuts = []
    front = w_front.shape[1]
    for start, stop in ((0, front), (front, cut), (cut, width)):
        while start < stop:
            cuts.append((start, min(start + 1024, stop)))
            start = cuts[-1][1]
    vmem = pl.BlockSpec(memory_space=pltpu.VMEM)
    out = []
    for size in (cut, width - cut):
        out.append(jax.ShapeDtypeStruct((rows // 2, size), jnp.bfloat16))
        out.append(jax.ShapeDtypeStruct((rows // 2, size), jnp.float32))
    return pl.pallas_call(
        functools.partial(product_kernel, tuple(cuts)),
        in_specs=[vmem, vmem, vmem, pl.BlockSpec(memory_space=pl.ANY), vmem],
        out_specs=[vmem] * 4,
        out_shape=out,
        scratch_shapes=[
            pltpu.VMEM((depth, width - front), jnp.bfloat16),
            pltpu.SemaphoreType.DMA((len(cuts),)),
        ],
        compiler_params=pltpu.CompilerParams(vmem_limit_bytes=48 * 2**20),
        cost_estimate=pl.CostEstimate(
            flops=2 * rows * depth * width, bytes_accessed=2 * depth * width, transcendentals=0
        ),
        name="product",
    )(place_a, place_b, returned, w_out, w_front)


def scatter_sum(grid, place_a, place_b, returned, w_out, w_front, cut):
    def pieces(x):
        size = x.shape[0] // 2 // grid.half
        return x[:size], [narrow(x[i * size : (i + 1) * size]) for i in range(1, 2 * grid.half)]

    def direct(sent):
        return [
            grid.send(x, half=i % grid.half, pair=i // grid.half)
            for i, x in enumerate(sent, start=1)
        ]

    def total(x, parts):
        for part in parts:
            x = x + wide(part)
        return x

    away_a, keep_a, away_b, keep_b = product(place_a, place_b, returned, w_out, w_front, cut)
    xa = keep_a + wide(grid.send(away_a, core=1))
    middle = xa.shape[0] // 2
    sent_a = narrow(xa[middle:])
    got_a = grid.send(sent_a, near=1)
    xb = keep_b + wide(grid.send(after(away_b, sent_a), core=1))
    xb, sent = pieces(xb)
    got_b = direct(sent)
    got_a, got_b[0] = lax.optimization_barrier((got_a, got_b[0]))
    xa, sent = pieces(xa[:middle] + wide(got_a))
    parts_a = direct(sent)
    xb = total(xb, got_b)
    middle = xb.shape[0] // 2
    sent_b = after(narrow(xb[middle:]), *sent)
    xa = total(xa, parts_a)
    xb = xb[:middle] + wide(after(grid.send(sent_b, near=1), xa))
    return jnp.concatenate([xa, xb], axis=1)


def norm_kernel(x, gain, *refs):
    outs, (rows, gains, sems) = refs[:-3], refs[-3:]
    copies = [
        pltpu.make_async_copy(x, rows, sems.at[0]),
        pltpu.make_async_copy(gain, gains, sems.at[1]),
    ]
    for copy in copies:
        copy.start()
    copies[0].wait()
    inputs = rows[...].astype(jnp.float32)
    factor = lax.rsqrt(jnp.mean(inputs * inputs, axis=1, keepdims=True) + epsilon)
    copies[1].wait()
    normed = (inputs * factor * gains[...]).astype(jnp.bfloat16)
    start = 0
    for out in outs:
        out[...] = normed[:, start : start + out.shape[1]]
        start += out.shape[1]


def norm(x, gain, widths):
    vmem = pl.BlockSpec(memory_space=pltpu.VMEM)
    hbm = pl.BlockSpec(memory_space=pl.ANY)
    return pl.pallas_call(
        norm_kernel,
        in_specs=[hbm, hbm],
        out_specs=[vmem] * len(widths),
        out_shape=[jax.ShapeDtypeStruct((x.shape[0], w), jnp.bfloat16) for w in widths],
        scratch_shapes=[
            pltpu.VMEM(x.shape, jnp.bfloat16),
            pltpu.VMEM((1, x.shape[1]), jnp.float32),
            pltpu.SemaphoreType.DMA((2,)),
        ],
        compiler_params=pltpu.CompilerParams(vmem_limit_bytes=60 * 2**20),
        name="norm",
    )(x, gain.reshape(1, -1))


def placing_kernel(sizes, slots, orders, kv_owner, *outs):
    requests = kv_owner.shape[1]
    row = lax.broadcasted_iota(jnp.int32, (requests, requests), 0)
    column = lax.broadcasted_iota(jnp.int32, (requests, requests), 1)

    def upright(x):
        return jnp.sum(jnp.where(row == column, x, 0.0), axis=1, keepdims=True)

    owner = kv_owner[...].astype(jnp.float32)
    earlier = (upright(owner) == owner) & (row < column)
    slot = jnp.sum(jnp.where(earlier, 1.0, 0.0), axis=0, keepdims=True)
    place = owner * slots + slot
    upright_place = upright(place)

    tp = lax.axis_index("tp")
    me = (lax.div(tp, 4), lax.rem(lax.div(tp, 2), 2), lax.rem(tp, 2), lax.axis_index("attn"))
    rows_dev = requests // int(np.prod(sizes))
    lane = lax.broadcasted_iota(jnp.int32, (1, requests), 1)
    for order, out in zip(orders, outs):
        if order is None:
            out[...] = place.astype(jnp.int32)
            continue
        if not order:
            out[...] = (tp * sizes[CORE] + me[CORE]) * slots + lane
            continue
        sign, axes = order
        rest = lax.div(lane, rows_dev)
        where = [None] * len(sizes)
        for axis in reversed(axes):
            move = lax.rem(rest, sizes[axis])
            rest = lax.div(rest, sizes[axis])
            where[axis] = lax.rem(me[axis] + sizes[axis] + sign * move, sizes[axis])
        block = where[0]
        for axis in range(1, len(sizes)):
            block = block * sizes[axis] + where[axis]
        source = block * rows_dev + lax.rem(lane, rows_dev)
        moved = jnp.sum(jnp.where(row == source, upright_place, 0.0), axis=0, keepdims=True)
        out[...] = moved.astype(jnp.int32)


def placing(kv_owner, sizes, slots, orders):
    requests = kv_owner.shape[0]
    vmem = pl.BlockSpec(memory_space=pltpu.VMEM)
    return pl.pallas_call(
        functools.partial(placing_kernel, sizes, slots, orders),
        in_specs=[vmem],
        out_specs=[vmem] * len(orders),
        out_shape=[jax.ShapeDtypeStruct((1, requests), jnp.int32)] * len(orders),
        compiler_params=pltpu.CompilerParams(vmem_limit_bytes=16 * 2**20),
        name="placing",
    )(kv_owner.reshape(1, requests))


def fetch_kernel(starts, *refs):
    count = len(starts)
    sems = refs[-1]
    copies = []
    for i, start in enumerate(starts):
        source, target = refs[i], refs[count + i]
        if start is not None:
            columns = pl.ds(start, target.shape[-1])
            source = source.at[(slice(None),) * (len(target.shape) - 1) + (columns,)]
        copies.append(pltpu.make_async_copy(source, target, sems.at[i]))
        copies[-1].start()
    for copy in copies:
        copy.wait()


def fetch(*wanted, limit):
    arrays = [x for x, _ in wanted]
    starts = [columns and columns[0] for _, columns in wanted]
    out = [
        jax.ShapeDtypeStruct(x.shape[:-1] + (columns[1],) if columns else x.shape, x.dtype)
        for x, columns in wanted
    ]
    return pl.pallas_call(
        functools.partial(fetch_kernel, starts),
        in_specs=[pl.BlockSpec(memory_space=pl.ANY)] * len(arrays),
        out_specs=[pl.BlockSpec(memory_space=pltpu.VMEM)] * len(arrays),
        out_shape=out,
        scratch_shapes=[pltpu.SemaphoreType.DMA((len(arrays),))],
        compiler_params=pltpu.CompilerParams(vmem_limit_bytes=limit * 2**20),
        cost_estimate=pl.CostEstimate(
            flops=0, bytes_accessed=sum(x.size * 4 for x in out), transcendentals=0
        ),
        name="fetch",
    )(*arrays)


def project_kernel(count, order, *refs):
    parts_a, parts_b, (wq, w_kv, place, out) = refs[:count], refs[count:-4], refs[-4:]

    def products(parts, features):
        x = jnp.concatenate([part[...] for part in parts], axis=0)
        query = jnp.dot(x, wq[features, :], preferred_element_type=jnp.float32)
        key_value = lax.dot_general(
            x, w_kv[:, features], (((1,), (1,)), ((), ())), preferred_element_type=jnp.float32
        )
        return jnp.concatenate([query, key_value], axis=1)

    cut = parts_a[0].shape[1]
    total = products(parts_a, slice(0, cut))
    part_b = products(parts_b, slice(cut, wq.shape[0]))
    size = part_b.shape[0] // len(order)
    blocks = [order.index(i) for i in range(len(order))]
    total += jnp.concatenate([part_b[i * size : (i + 1) * size] for i in blocks], axis=0)
    rows = lax.broadcasted_iota(jnp.int32, (out.shape[0], place.shape[1]), 0)
    route = jnp.where(rows == place[...], 1.0, 0.0).astype(jnp.bfloat16)
    moved = jnp.dot(route, total.astype(jnp.bfloat16), preferred_element_type=jnp.float32)
    out[...] = moved.astype(jnp.bfloat16)


def project(parts_a, parts_b, order, w_query, w_kv_t, place, slots):
    rows = place.shape[1]
    width = w_query.shape[0]
    row_width = w_query.shape[1] + w_kv_t.shape[0]
    args = [*parts_a, *parts_b, w_query, w_kv_t, place]
    vmem = pl.BlockSpec(memory_space=pltpu.VMEM)
    return pl.pallas_call(
        functools.partial(project_kernel, len(parts_a), order),
        in_specs=[vmem] * len(args),
        out_specs=vmem,
        out_shape=jax.ShapeDtypeStruct((slots, row_width), jnp.bfloat16),
        compiler_params=pltpu.CompilerParams(vmem_limit_bytes=24 * 2**20),
        cost_estimate=pl.CostEstimate(
            flops=2 * rows * width * row_width,
            bytes_accessed=2 * width * row_width,
            transcendentals=0,
        ),
        name="project",
    )(*args)


def attend_kernel(
    per_query,
    per_key,
    table,
    lengths,
    inbound,
    cosine,
    sine,
    key_pages,
    value_pages,
    out,
    key_pool,
    value_pool,
    sems,
    key_new,
    query_rot,
    value_own,
    chance,
    mixed,
):
    owners, slots, _ = inbound.shape
    pages = table.shape[1]
    page, kv_width = key_pages.shape[1:]
    kv_heads = kv_width // HEAD
    heads_dev = per_query // HEAD
    heads = owners * heads_dev
    pair = 2 * heads // kv_heads
    pairs = kv_heads // 2
    span = pages * page
    pieces = owners // kv_heads
    batches = query_rot.shape[1]
    batch = slots // batches

    cuts = 16
    size = key_pages.shape[0] // cuts

    def fetch_pool(pool, on_chip, sem):
        for cut in range(cuts):
            part = pl.ds(cut * size, size)
            pltpu.make_async_copy(pool.at[part], on_chip.at[part], sem).start()

    fetch_pool(key_pages, key_pool, sems.at[0])
    fetch_pool(value_pages, value_pool, sems.at[1])

    def held(pool, slot, columns):
        return [pool[table[slot, j], :, columns] for j in range(pages)]

    cos = cosine[...]
    sin = sine[...]

    def turn(x):
        return (x * cos + pltpu.roll(x, HEAD // 2, 1) * sin).astype(jnp.bfloat16)

    for source in range(owners):
        for j in range(heads_dev):
            x = inbound[source, :, j * HEAD : (j + 1) * HEAD].astype(jnp.float32)
            x = turn(x).astype(jnp.float32)
            head = source * heads_dev + j
            for b in range(batches):
                rows = pl.ds(head % pair * batch, batch)
                query_rot[head // pair, b, rows] = x[b * batch : (b + 1) * batch]

    piece = lax.broadcasted_iota(jnp.int32, (slots, HEAD), 1) // per_key
    for g in range(kv_heads):
        key = jnp.zeros((slots, HEAD), jnp.float32)
        value = jnp.zeros((slots, HEAD), jnp.float32)
        for j in range(pieces):
            tile = inbound[g * pieces + j, :, per_query : per_query + HEAD].astype(jnp.float32)
            shift = j * per_key
            back = (shift - per_key) % HEAD
            key = jnp.where(piece == j, pltpu.roll(tile, shift, 1) if shift else tile, key)
            value = jnp.where(piece == j, pltpu.roll(tile, back, 1) if back else tile, value)
        key_new[:, g * HEAD : (g + 1) * HEAD] = turn(key)
        value_own[g] = value

    scale = HEAD ** (-0.5)
    columns = pair * batch
    row = lax.broadcasted_iota(jnp.int32, (span, columns), 0)
    place = lax.broadcasted_iota(jnp.int32, (span, columns), 1) % batch
    own_row = lax.broadcasted_iota(jnp.int32, (slots, columns), 0)
    own_place = lax.broadcasted_iota(jnp.int32, (slots, columns), 1) % batch
    first = lax.broadcasted_iota(jnp.int32, (HEAD, columns), 1) < columns // 2
    same = lax.broadcasted_iota(jnp.int32, (columns, columns), 0) == lax.broadcasted_iota(
        jnp.int32, (columns, columns), 1
    )

    own_chances = {}
    pltpu.make_async_copy(key_pool, key_pool, sems.at[0]).wait()
    for p in range(pairs):
        columns_p = slice(p * 2 * HEAD, (p + 1) * 2 * HEAD)
        for b in range(batches):
            valid = row < lengths[b]
            turned = query_rot[p, b].T.astype(jnp.bfloat16)
            none = jnp.zeros_like(turned)
            wide = jnp.concatenate(
                [jnp.where(first, turned, none), jnp.where(first, none, turned)], axis=0
            )
            keys = []
            for s in range(batch):
                keys += held(key_pool, b * batch + s, columns_p)
            keys.append(key_new[:, columns_p])
            products = jnp.dot(
                jnp.concatenate(keys, axis=0), wide, preferred_element_type=jnp.float32
            )
            scores = products[:span]
            for s in range(1, batch):
                scores = jnp.where(place == s, products[s * span : (s + 1) * span], scores)
            own = jnp.where(own_row == own_place + b * batch, products[batch * span :], 0.0)
            own = jnp.sum(own, axis=0, keepdims=True) * scale
            masked = jnp.where(valid, scores * scale, -1e30)
            top = jnp.maximum(jnp.max(masked, axis=0, keepdims=True), own)
            terms = jnp.where(valid, jnp.exp(masked - top), 0.0)
            own_term = jnp.exp(own - top)
            total = jnp.sum(terms, axis=0, keepdims=True) + own_term
            chance[p, b] = (terms / total).T.astype(jnp.bfloat16).astype(jnp.float32)
            own_chance = (own_term / total).astype(jnp.bfloat16).astype(jnp.float32)
            own_chances[p, b] = jnp.sum(
                jnp.where(same, own_chance, 0.0), axis=1, keepdims=True
            )

    pltpu.make_async_copy(value_pool, value_pool, sems.at[1]).wait()
    for p in range(pairs):
        columns_p = slice(p * 2 * HEAD, (p + 1) * 2 * HEAD)
        for b in range(batches):
            for s in range(batch):
                mine = chance[p, b, pl.ds(s, pair, stride=batch)].astype(jnp.bfloat16)
                values = held(value_pool, b * batch + s, columns_p)
                both = jnp.dot(
                    mine, jnp.concatenate(values, axis=0), preferred_element_type=jnp.float32
                )
                result = jnp.concatenate(
                    [both[: pair // 2, :HEAD], both[pair // 2 :, HEAD:]], axis=0
                )
                mixed[p, b, pl.ds(s, pair, stride=batch)] = result
        for j in range(pair):
            head = p * pair + j
            g = head * kv_heads // heads
            halves = []
            for b in range(batches):
                rows = slice(j * batch, (j + 1) * batch)
                own_value = value_own[g, b * batch : (b + 1) * batch]
                halves.append(mixed[p, b, rows] + own_chances[p, b][rows] * own_value)
            column = head % heads_dev * HEAD
            out[head // heads_dev, :, column : column + HEAD] = jnp.concatenate(
                halves, axis=0
            ).astype(jnp.bfloat16)


def attend(inbound, lengths, table, cosine, sine, key_pages, value_pages, per_query, per_key):
    owners, slots, _ = inbound.shape
    pages = table.shape[1]
    page, kv_width = key_pages.shape[1:]
    kv_heads = kv_width // HEAD
    heads = owners * (per_query // HEAD)
    span = pages * page
    pair = 2 * heads // kv_heads
    pairs = kv_heads // 2
    batches = slots * pair // HEAD
    batch = slots // batches
    columns = pair * batch
    lengths = jnp.tile(lengths.reshape(batches, 1, batch), (1, 1, pair))
    smem = pl.BlockSpec(memory_space=pltpu.SMEM)
    vmem = pl.BlockSpec(memory_space=pltpu.VMEM)
    hbm = pl.BlockSpec(memory_space=pl.ANY)
    return pl.pallas_call(
        functools.partial(attend_kernel, per_query, per_key),
        in_specs=[smem, vmem, vmem, vmem, vmem, hbm, hbm],
        out_specs=vmem,
        out_shape=jax.ShapeDtypeStruct((owners, slots, per_query), jnp.bfloat16),
        scratch_shapes=[
            pltpu.VMEM(key_pages.shape, jnp.bfloat16),
            pltpu.VMEM(value_pages.shape, jnp.bfloat16),
            pltpu.SemaphoreType.DMA((2,)),
            pltpu.VMEM((slots, kv_width), jnp.bfloat16),
            pltpu.VMEM((pairs, batches, columns, HEAD), jnp.float32),
            pltpu.VMEM((kv_heads, slots, HEAD), jnp.float32),
            pltpu.VMEM((pairs, batches, columns, span), jnp.float32),
            pltpu.VMEM((pairs, batches, columns, HEAD), jnp.float32),
        ],
        compiler_params=pltpu.CompilerParams(vmem_limit_bytes=52 * 2**20),
        cost_estimate=pl.CostEstimate(
            flops=8 * slots * heads * span * HEAD,
            bytes_accessed=4 * slots * span * kv_width,
            transcendentals=slots * heads * span,
        ),
        name="attend",
    )(table, lengths, inbound, cosine, sine, key_pages, value_pages)


def on_device(
    hidden_in,
    norm_gain,
    w_query,
    w_key,
    w_value,
    w_out,
    key_pages,
    value_pages,
    page_table,
    kv_owner,
    cached,
):
    grid = Grid()
    owners = grid.size
    slot_count = page_table.shape[1]
    per_query = w_query.shape[1]
    per_key = w_key.shape[1]
    row_width = per_query + -(-2 * per_key // HEAD) * HEAD
    requests = kv_owner.shape[0]
    rows_dev = requests // owners
    width = hidden_in.shape[1]
    all_slots = owners * slot_count

    moves_a = grid.moves(ORDER_A)
    order_b = [moves_a.index(move) for move in grid.moves(ORDER_B)]
    cut = width // 32 * 23
    xa, xb = norm(hidden_in, norm_gain, (cut, width - cut))

    def first(x):
        orders = (None, (-1, ORDER_A), (1, ORDER_A), (1, ORDER_B), ())
        places = placing(after(kv_owner, x), grid.sizes, slot_count, orders)
        pieces = [after(w_key, x).T, w_value.T]
        spare = row_width - per_query - 2 * per_key
        if spare:
            pieces.append(jnp.zeros((spare, width), w_key.dtype))
        return places, jnp.concatenate(pieces, axis=0)

    def second(x):
        return fetch((after(w_query, x), None), limit=44)[0]

    parts_a, parts_b, others, w_query = gather_rows(grid, xa, xb, first, second)
    (place, place_in, place_a, place_b, mine), w_kv_t = others
    total = project(parts_a, parts_b, order_b, w_query, w_kv_t, place_in, all_slots)
    outbound = total.reshape(owners, slot_count, row_width)
    place = after(place, outbound).reshape(requests)
    mine = mine[0, :slot_count]
    lengths = jnp.sum(jnp.where(place[:, None] == mine[None, :], cached[:, None], 0), axis=0)
    halfway = HEAD // 2
    offsets = jnp.arange(halfway, dtype=jnp.float32)
    frequency = rope_base ** (-(2.0 * offsets) / HEAD)
    angles = lengths.astype(jnp.float32)[:, None] * frequency
    cosine_part = jnp.cos(angles)
    sine_part = jnp.sin(angles)
    cosine = jnp.concatenate([cosine_part, cosine_part], axis=1)
    sine = jnp.concatenate([-sine_part, sine_part], axis=1)
    inbound = lax.all_to_all(outbound, AXES, split_axis=0, concat_axis=0, tiled=True)
    attended = attend(
        inbound,
        lengths,
        after(page_table, outbound)[0],
        cosine,
        sine,
        key_pages[0],
        value_pages[0],
        per_query,
        per_key,
    )
    (w_front,) = fetch((after(w_out, attended), (0, width // 32 * 11)), limit=48)
    returned = lax.all_to_all(attended, AXES, split_axis=0, concat_axis=0, tiled=True)
    returned = returned.reshape(all_slots, per_query)
    summed = scatter_sum(grid, place_a, place_b, returned, w_out, w_front, width // 32 * 21)
    return narrow(wide(hidden_in) + summed)


def solution(mesh):
    placed = (
        P(("groups", "tp", "attn"), None),
        P(),
        P(None, ("tp", "attn")),
        P(None, ("tp", "attn")),
        P(None, ("tp", "attn")),
        P(("tp", "attn"), None),
        P(("groups", "tp", "attn"), None, None, None),
        P(("groups", "tp", "attn"), None, None, None),
        P(("groups", "tp", "attn"), None, None),
        P("groups"),
        P("groups"),
    )
    return jax.shard_map(
        on_device,
        mesh=mesh,
        in_specs=placed,
        out_specs=P(("groups", "tp", "attn"), None),
        check_vma=False,
    )
```

```python
import functools

import jax
import jax.numpy as jnp
import numpy as np
from jax import lax
from jax.experimental import pallas as pl
from jax.experimental.pallas import tpu as pltpu
from jax.sharding import PartitionSpec as P

HEAD = 128
AXES = ("tp", "attn")

epsilon = 1e-05
rope_base = 500000.0


class Grid:
    def __init__(self):
        self.half = lax.axis_size("tp") // 4
        self.sizes = (self.half, 2, 2, lax.axis_size("attn"))
        self.size = int(np.prod(self.sizes))

    def shifted(self, place, moves):
        return np.ravel_multi_index(
            tuple((p + m) % n for p, m, n in zip(place, moves, self.sizes)), self.sizes
        )

    def send(self, x, half=0, pair=0, near=0, core=0):
        pairs = [
            (i, int(self.shifted(np.unravel_index(i, self.sizes), (half, pair, near, core))))
            for i in range(self.size)
        ]
        return lax.ppermute(x, AXES, pairs)

    def moves(self, order):
        counts = [self.sizes[axis] for axis in order]
        places = []
        for steps in np.ndindex(*counts):
            move = [0, 0, 0, 0]
            for axis, step in zip(order, steps):
                move[axis] = step
            places.append(tuple(move))
        return places


HALF, PAIR, NEAR, CORE = range(4)
ORDER_A = (CORE, NEAR, PAIR, HALF)
ORDER_B = (CORE, PAIR, HALF, NEAR)


def after(x, *earlier):
    return lax.optimization_barrier((x, *earlier))[0]


def gather_rows(grid, xa, xb, first, second):
    beside_b = grid.send(xb, near=1)
    line_a = jnp.concatenate(
        [xa]
        + [
            grid.send(xa, half=half, pair=pair)
            for pair in range(2)
            for half in range(grid.half)
            if half or pair
        ],
        axis=0,
    )
    pair_b = jnp.concatenate([xb, beside_b], axis=0)
    line_a, pair_b, first = lax.optimization_barrier((line_a, pair_b, first(xa)))
    beside_a = grid.send(line_a, near=1)
    parts_b = [pair_b] + [
        grid.send(pair_b, half=half, pair=pair)
        for pair in range(2)
        for half in range(grid.half)
        if half or pair
    ]
    beside_a, parts_b, second = lax.optimization_barrier((beside_a, parts_b, second(pair_b)))
    parts_a = [line_a, beside_a]
    parts_a += [grid.send(part, core=1) for part in parts_a]
    parts_b += [grid.send(part, core=1) for part in parts_b]
    return parts_a, parts_b, first, second


def narrow(x):
    return x.astype(jnp.bfloat16)


def wide(x):
    return x.astype(jnp.float32)


def product_kernel(
    cuts,
    place_a,
    place_b,
    returned,
    w_out,
    w_front,
    away_a,
    keep_a,
    away_b,
    keep_b,
    held,
    sems,
):
    front = w_front.shape[1]
    copies = []
    for i, (start, stop) in enumerate(cuts):
        copy = None
        if start >= front:
            size = pl.ds(start, stop - start), pl.ds(start - front, stop - start)
            copy = pltpu.make_async_copy(
                w_out.at[:, size[0]], held.at[:, size[1]], sems.at[i]
            )
            copy.start()
        copies.append(copy)
    slots = lax.broadcasted_iota(jnp.int32, (returned.shape[0], place_a.shape[1]), 0)

    def picked(place):
        route = jnp.where(slots == place[...], 1.0, 0.0).astype(jnp.bfloat16)
        rows = lax.dot_general(
            route, returned[...], (((0,), (0,)), ((), ())), preferred_element_type=jnp.float32
        )
        return rows.astype(jnp.bfloat16)

    rows_a, rows_b = picked(place_a), picked(place_b)
    half = keep_a.shape[0]
    middle = keep_a.shape[1]
    for copy, (start, stop) in zip(copies, cuts):
        if copy is not None:
            copy.wait()
        rows, away, keep = (rows_a, away_a, keep_a) if start < middle else (rows_b, away_b, keep_b)
        w = w_front[:, start:stop] if copy is None else held[:, start - front : stop - front]
        x = jnp.dot(rows, w, preferred_element_type=jnp.float32)
        begin = start if start < middle else start - middle
        here = slice(begin, begin + stop - start)
        keep[:, here] = x[:half]
        away[:, here] = x[half:].astype(jnp.bfloat16)


def product(place_a, place_b, returned, w_out, w_front, cut):
    rows = place_a.shape[1]
    depth, width = w_out.shape
    cuts = []
    front = w_front.shape[1]
    for start, stop in ((0, front), (front, cut), (cut, width)):
        while start < stop:
            cuts.append((start, min(start + 1024, stop)))
            start = cuts[-1][1]
    vmem = pl.BlockSpec(memory_space=pltpu.VMEM)
    out = []
    for size in (cut, width - cut):
        out.append(jax.ShapeDtypeStruct((rows // 2, size), jnp.bfloat16))
        out.append(jax.ShapeDtypeStruct((rows // 2, size), jnp.float32))
    return pl.pallas_call(
        functools.partial(product_kernel, tuple(cuts)),
        in_specs=[vmem, vmem, vmem, pl.BlockSpec(memory_space=pl.ANY), vmem],
        out_specs=[vmem] * 4,
        out_shape=out,
        scratch_shapes=[
            pltpu.VMEM((depth, width - front), jnp.bfloat16),
            pltpu.SemaphoreType.DMA((len(cuts),)),
        ],
        compiler_params=pltpu.CompilerParams(vmem_limit_bytes=48 * 2**20),
        cost_estimate=pl.CostEstimate(
            flops=2 * rows * depth * width, bytes_accessed=2 * depth * width, transcendentals=0
        ),
        name="product",
    )(place_a, place_b, returned, w_out, w_front)


def scatter_sum(grid, place_a, place_b, returned, w_out, w_front, cut):
    def pieces(x):
        size = x.shape[0] // 2 // grid.half
        return x[:size], [narrow(x[i * size : (i + 1) * size]) for i in range(1, 2 * grid.half)]

    def direct(sent):
        return [
            grid.send(x, half=i % grid.half, pair=i // grid.half)
            for i, x in enumerate(sent, start=1)
        ]

    def total(x, parts):
        for part in parts:
            x = x + wide(part)
        return x

    away_a, keep_a, away_b, keep_b = product(place_a, place_b, returned, w_out, w_front, cut)
    xa = keep_a + wide(grid.send(away_a, core=1))
    middle = xa.shape[0] // 2
    sent_a = narrow(xa[middle:])
    got_a = grid.send(sent_a, near=1)
    xb = keep_b + wide(grid.send(after(away_b, sent_a), core=1))
    xb, sent = pieces(xb)
    got_b = direct(sent)
    got_a, got_b[0] = lax.optimization_barrier((got_a, got_b[0]))
    xa, sent = pieces(xa[:middle] + wide(got_a))
    parts_a = direct(sent)
    xb = total(xb, got_b)
    middle = xb.shape[0] // 2
    sent_b = after(narrow(xb[middle:]), *sent)
    xa = total(xa, parts_a)
    xb = xb[:middle] + wide(after(grid.send(sent_b, near=1), xa))
    return jnp.concatenate([xa, xb], axis=1)


def norm_kernel(x, gain, *refs):
    outs, (rows, gains, sems) = refs[:-3], refs[-3:]
    copies = [
        pltpu.make_async_copy(x, rows, sems.at[0]),
        pltpu.make_async_copy(gain, gains, sems.at[1]),
    ]
    for copy in copies:
        copy.start()
    copies[0].wait()
    inputs = rows[...].astype(jnp.float32)
    factor = lax.rsqrt(jnp.mean(inputs * inputs, axis=1, keepdims=True) + epsilon)
    copies[1].wait()
    normed = (inputs * factor * gains[...]).astype(jnp.bfloat16)
    start = 0
    for out in outs:
        out[...] = normed[:, start : start + out.shape[1]]
        start += out.shape[1]


def norm(x, gain, widths):
    vmem = pl.BlockSpec(memory_space=pltpu.VMEM)
    hbm = pl.BlockSpec(memory_space=pl.ANY)
    return pl.pallas_call(
        norm_kernel,
        in_specs=[hbm, hbm],
        out_specs=[vmem] * len(widths),
        out_shape=[jax.ShapeDtypeStruct((x.shape[0], w), jnp.bfloat16) for w in widths],
        scratch_shapes=[
            pltpu.VMEM(x.shape, jnp.bfloat16),
            pltpu.VMEM((1, x.shape[1]), jnp.float32),
            pltpu.SemaphoreType.DMA((2,)),
        ],
        compiler_params=pltpu.CompilerParams(vmem_limit_bytes=60 * 2**20),
        name="norm",
    )(x, gain.reshape(1, -1))


def placing_kernel(sizes, slots, orders, kv_owner, *outs):
    requests = kv_owner.shape[1]
    row = lax.broadcasted_iota(jnp.int32, (requests, requests), 0)
    column = lax.broadcasted_iota(jnp.int32, (requests, requests), 1)

    def upright(x):
        return jnp.sum(jnp.where(row == column, x, 0.0), axis=1, keepdims=True)

    owner = kv_owner[...].astype(jnp.float32)
    earlier = (upright(owner) == owner) & (row < column)
    slot = jnp.sum(jnp.where(earlier, 1.0, 0.0), axis=0, keepdims=True)
    place = owner * slots + slot
    upright_place = upright(place)

    tp = lax.axis_index("tp")
    me = (lax.div(tp, 4), lax.rem(lax.div(tp, 2), 2), lax.rem(tp, 2), lax.axis_index("attn"))
    rows_dev = requests // int(np.prod(sizes))
    lane = lax.broadcasted_iota(jnp.int32, (1, requests), 1)
    for order, out in zip(orders, outs):
        if order is None:
            out[...] = place.astype(jnp.int32)
            continue
        if not order:
            out[...] = (tp * sizes[CORE] + me[CORE]) * slots + lane
            continue
        sign, axes = order
        rest = lax.div(lane, rows_dev)
        where = [None] * len(sizes)
        for axis in reversed(axes):
            move = lax.rem(rest, sizes[axis])
            rest = lax.div(rest, sizes[axis])
            where[axis] = lax.rem(me[axis] + sizes[axis] + sign * move, sizes[axis])
        block = where[0]
        for axis in range(1, len(sizes)):
            block = block * sizes[axis] + where[axis]
        source = block * rows_dev + lax.rem(lane, rows_dev)
        moved = jnp.sum(jnp.where(row == source, upright_place, 0.0), axis=0, keepdims=True)
        out[...] = moved.astype(jnp.int32)


def placing(kv_owner, sizes, slots, orders):
    requests = kv_owner.shape[0]
    vmem = pl.BlockSpec(memory_space=pltpu.VMEM)
    return pl.pallas_call(
        functools.partial(placing_kernel, sizes, slots, orders),
        in_specs=[vmem],
        out_specs=[vmem] * len(orders),
        out_shape=[jax.ShapeDtypeStruct((1, requests), jnp.int32)] * len(orders),
        compiler_params=pltpu.CompilerParams(vmem_limit_bytes=16 * 2**20),
        name="placing",
    )(kv_owner.reshape(1, requests))


def fetch_kernel(starts, *refs):
    count = len(starts)
    sems = refs[-1]
    copies = []
    for i, start in enumerate(starts):
        source, target = refs[i], refs[count + i]
        if start is not None:
            columns = pl.ds(start, target.shape[-1])
            source = source.at[(slice(None),) * (len(target.shape) - 1) + (columns,)]
        copies.append(pltpu.make_async_copy(source, target, sems.at[i]))
        copies[-1].start()
    for copy in copies:
        copy.wait()


def fetch(*wanted, limit):
    arrays = [x for x, _ in wanted]
    starts = [columns and columns[0] for _, columns in wanted]
    out = [
        jax.ShapeDtypeStruct(x.shape[:-1] + (columns[1],) if columns else x.shape, x.dtype)
        for x, columns in wanted
    ]
    return pl.pallas_call(
        functools.partial(fetch_kernel, starts),
        in_specs=[pl.BlockSpec(memory_space=pl.ANY)] * len(arrays),
        out_specs=[pl.BlockSpec(memory_space=pltpu.VMEM)] * len(arrays),
        out_shape=out,
        scratch_shapes=[pltpu.SemaphoreType.DMA((len(arrays),))],
        compiler_params=pltpu.CompilerParams(vmem_limit_bytes=limit * 2**20),
        cost_estimate=pl.CostEstimate(
            flops=0, bytes_accessed=sum(x.size * 4 for x in out), transcendentals=0
        ),
        name="fetch",
    )(*arrays)


def project_kernel(first, last, order, start, block, *refs):
    count = len(refs) - 4 - (not first) - last
    parts, (wq, w_kv), refs = refs[:count], refs[count : count + 2], refs[count + 2 :]
    if not first:
        before, refs = refs[0], refs[1:]
    if last:
        place, refs = refs[0], refs[1:]
    out, total = refs
    step = pl.program_id(0)
    per_query = wq.shape[1]

    @pl.when(step == 0)
    def _():
        total[...] = jnp.zeros_like(total) if first else before[...]

    here = pl.ds(pl.multiple_of(step * block, block), block)
    there = pl.ds(pl.multiple_of(start + step * block, block), block)
    x = jnp.concatenate([part[:, here] for part in parts], axis=0)
    products = [
        jnp.dot(x, wq[there, :], preferred_element_type=jnp.float32),
        lax.dot_general(x, w_kv[:, there], (((1,), (1,)), ((), ())), preferred_element_type=jnp.float32),
    ]
    size = x.shape[0] // len(order)
    for product, columns in zip(products, (slice(0, per_query), slice(per_query, None))):
        for i, place_i in enumerate(order):
            total[place_i * size : (place_i + 1) * size, columns] += product[
                i * size : (i + 1) * size
            ]

    @pl.when(step == pl.num_programs(0) - 1)
    def _():
        if last:
            rows = lax.broadcasted_iota(jnp.int32, (out.shape[0], place.shape[1]), 0)
            route = jnp.where(rows == place[...], 1.0, 0.0).astype(jnp.bfloat16)
            moved = jnp.dot(
                route, total[...].astype(jnp.bfloat16), preferred_element_type=jnp.float32
            )
            out[...] = moved.astype(jnp.bfloat16)
        else:
            out[...] = total[...]


def project(start, parts, order, w_query, w_kv_t, before, place, slots):
    row_width = w_query.shape[1] + w_kv_t.shape[0]
    width = parts[0].shape[1]
    block = width
    rows = sum(part.shape[0] for part in parts)
    first, last = before is None, place is not None
    vmem = pl.BlockSpec(memory_space=pltpu.VMEM)
    args = [*parts, w_query, w_kv_t]
    specs = [vmem] * len(parts)
    specs += [
        vmem,
        vmem,
    ]
    if not first:
        args.append(before)
        specs.append(vmem)
    if last:
        args.append(place)
        specs.append(vmem)
        out = jax.ShapeDtypeStruct((slots, row_width), jnp.bfloat16)
    else:
        out = jax.ShapeDtypeStruct((rows, row_width), jnp.float32)
    return pl.pallas_call(
        functools.partial(project_kernel, first, last, order, start, block),
        grid=(width // block,),
        in_specs=specs,
        out_specs=vmem,
        out_shape=out,
        scratch_shapes=[pltpu.VMEM((rows, row_width), jnp.float32)],
        compiler_params=pltpu.CompilerParams(vmem_limit_bytes=24 * 2**20),
        cost_estimate=pl.CostEstimate(
            flops=2 * rows * width * row_width,
            bytes_accessed=2 * width * row_width,
            transcendentals=0,
        ),
        name="project",
    )(*args)


def attend_kernel(
    per_query,
    per_key,
    table,
    lengths,
    inbound,
    cosine,
    sine,
    key_pages,
    value_pages,
    out,
    key_pool,
    value_pool,
    sems,
    key_new,
    query_tile,
    query_rot,
    value_own,
    chance,
    mixed,
):
    owners, slots, _ = inbound.shape
    pages = table.shape[1]
    page, kv_width = key_pages.shape[1:]
    kv_heads = kv_width // HEAD
    heads_dev = per_query // HEAD
    heads = owners * heads_dev
    pair = 2 * heads // kv_heads
    pairs = kv_heads // 2
    span = pages * page
    pieces = owners // kv_heads
    batches = query_rot.shape[1]
    batch = slots // batches

    cuts = 16
    size = key_pages.shape[0] // cuts

    def fetch_pool(pool, on_chip, sem):
        for cut in range(cuts):
            part = pl.ds(cut * size, size)
            pltpu.make_async_copy(pool.at[part], on_chip.at[part], sem).start()

    fetch_pool(key_pages, key_pool, sems.at[0])

    def held(pool, slot, columns):
        return [pool[table[slot, j], :, columns] for j in range(pages)]

    cos = cosine[...]
    sin = sine[...]

    def turn(x):
        return (x * cos + pltpu.roll(x, HEAD // 2, 1) * sin).astype(jnp.bfloat16)

    for source in range(owners):
        for j in range(heads_dev):
            x = inbound[source, :, j * HEAD : (j + 1) * HEAD].astype(jnp.float32)
            x = turn(x).astype(jnp.float32)
            head = source * heads_dev + j
            for b in range(batches):
                rows = pl.ds(head % pair * batch, batch)
                query_rot[head // pair, b, rows] = x[b * batch : (b + 1) * batch]

    piece = lax.broadcasted_iota(jnp.int32, (slots, HEAD), 1) // per_key
    for g in range(kv_heads):
        key = jnp.zeros((slots, HEAD), jnp.float32)
        value = jnp.zeros((slots, HEAD), jnp.float32)
        for j in range(pieces):
            tile = inbound[g * pieces + j, :, per_query : per_query + HEAD].astype(jnp.float32)
            shift = j * per_key
            back = (shift - per_key) % HEAD
            key = jnp.where(piece == j, pltpu.roll(tile, shift, 1) if shift else tile, key)
            value = jnp.where(piece == j, pltpu.roll(tile, back, 1) if back else tile, value)
        key_new[:, g * HEAD : (g + 1) * HEAD] = turn(key)
        value_own[g] = value

    scale = HEAD ** (-0.5)
    columns = pair * batch
    row = lax.broadcasted_iota(jnp.int32, (span, columns), 0)
    place = lax.broadcasted_iota(jnp.int32, (span, columns), 1) % batch
    own_row = lax.broadcasted_iota(jnp.int32, (slots, columns), 0)
    own_place = lax.broadcasted_iota(jnp.int32, (slots, columns), 1) % batch
    first = lax.broadcasted_iota(jnp.int32, (HEAD, columns), 1) < columns // 2
    same = lax.broadcasted_iota(jnp.int32, (columns, columns), 0) == lax.broadcasted_iota(
        jnp.int32, (columns, columns), 1
    )

    own_chances = {}
    for p in range(pairs):
        for b in range(batches):
            turned = query_rot[p, b].T.astype(jnp.bfloat16)
            none = jnp.zeros_like(turned)
            query_tile[p, b, :HEAD] = jnp.where(first, turned, none)
            query_tile[p, b, HEAD:] = jnp.where(first, none, turned)

    fetch_pool(value_pages, value_pool, sems.at[1])
    pltpu.make_async_copy(key_pool, key_pool, sems.at[0]).wait()
    for p in range(pairs):
        columns_p = slice(p * 2 * HEAD, (p + 1) * 2 * HEAD)
        for b in range(batches):
            valid = row < lengths[b]
            keys = []
            for s in range(batch):
                keys += held(key_pool, b * batch + s, columns_p)
            keys.append(key_new[:, columns_p])
            products = jnp.dot(
                jnp.concatenate(keys, axis=0),
                query_tile[p, b],
                preferred_element_type=jnp.float32,
            )
            scores = products[:span]
            for s in range(1, batch):
                scores = jnp.where(place == s, products[s * span : (s + 1) * span], scores)
            own = jnp.where(own_row == own_place + b * batch, products[batch * span :], 0.0)
            own = jnp.sum(own, axis=0, keepdims=True) * scale
            masked = jnp.where(valid, scores * scale, -1e30)
            top = jnp.maximum(jnp.max(masked, axis=0, keepdims=True), own)
            terms = jnp.where(valid, jnp.exp(masked - top), 0.0)
            own_term = jnp.exp(own - top)
            total = jnp.sum(terms, axis=0, keepdims=True) + own_term
            chance[p, b] = (terms / total).T.astype(jnp.bfloat16).astype(jnp.float32)
            own_chance = (own_term / total).astype(jnp.bfloat16).astype(jnp.float32)
            own_chances[p, b] = jnp.sum(
                jnp.where(same, own_chance, 0.0), axis=1, keepdims=True
            )

    pltpu.make_async_copy(value_pool, value_pool, sems.at[1]).wait()
    for p in range(pairs):
        columns_p = slice(p * 2 * HEAD, (p + 1) * 2 * HEAD)
        for b in range(batches):
            for s in range(batch):
                mine = chance[p, b, pl.ds(s, pair, stride=batch)].astype(jnp.bfloat16)
                values = held(value_pool, b * batch + s, columns_p)
                both = jnp.dot(
                    mine, jnp.concatenate(values, axis=0), preferred_element_type=jnp.float32
                )
                result = jnp.concatenate(
                    [both[: pair // 2, :HEAD], both[pair // 2 :, HEAD:]], axis=0
                )
                mixed[p, b, pl.ds(s, pair, stride=batch)] = result
        for j in range(pair):
            head = p * pair + j
            g = head * kv_heads // heads
            halves = []
            for b in range(batches):
                rows = slice(j * batch, (j + 1) * batch)
                own_value = value_own[g, b * batch : (b + 1) * batch]
                halves.append(mixed[p, b, rows] + own_chances[p, b][rows] * own_value)
            column = head % heads_dev * HEAD
            out[head // heads_dev, :, column : column + HEAD] = jnp.concatenate(
                halves, axis=0
            ).astype(jnp.bfloat16)


def attend(inbound, lengths, table, cosine, sine, key_pages, value_pages, per_query, per_key):
    owners, slots, _ = inbound.shape
    pages = table.shape[1]
    page, kv_width = key_pages.shape[1:]
    kv_heads = kv_width // HEAD
    heads = owners * (per_query // HEAD)
    span = pages * page
    pair = 2 * heads // kv_heads
    pairs = kv_heads // 2
    batches = slots * pair // HEAD
    batch = slots // batches
    columns = pair * batch
    lengths = jnp.tile(lengths.reshape(batches, 1, batch), (1, 1, pair))
    smem = pl.BlockSpec(memory_space=pltpu.SMEM)
    vmem = pl.BlockSpec(memory_space=pltpu.VMEM)
    hbm = pl.BlockSpec(memory_space=pl.ANY)
    return pl.pallas_call(
        functools.partial(attend_kernel, per_query, per_key),
        in_specs=[smem, vmem, vmem, vmem, vmem, hbm, hbm],
        out_specs=vmem,
        out_shape=jax.ShapeDtypeStruct((owners, slots, per_query), jnp.bfloat16),
        scratch_shapes=[
            pltpu.VMEM(key_pages.shape, jnp.bfloat16),
            pltpu.VMEM(value_pages.shape, jnp.bfloat16),
            pltpu.SemaphoreType.DMA((2,)),
            pltpu.VMEM((slots, kv_width), jnp.bfloat16),
            pltpu.VMEM((pairs, batches, 2 * HEAD, columns), jnp.bfloat16),
            pltpu.VMEM((pairs, batches, columns, HEAD), jnp.float32),
            pltpu.VMEM((kv_heads, slots, HEAD), jnp.float32),
            pltpu.VMEM((pairs, batches, columns, span), jnp.float32),
            pltpu.VMEM((pairs, batches, columns, HEAD), jnp.float32),
        ],
        compiler_params=pltpu.CompilerParams(vmem_limit_bytes=52 * 2**20),
        cost_estimate=pl.CostEstimate(
            flops=8 * slots * heads * span * HEAD,
            bytes_accessed=4 * slots * span * kv_width,
            transcendentals=slots * heads * span,
        ),
        name="attend",
    )(table, lengths, inbound, cosine, sine, key_pages, value_pages)


def on_device(
    hidden_in,
    norm_gain,
    w_query,
    w_key,
    w_value,
    w_out,
    key_pages,
    value_pages,
    page_table,
    kv_owner,
    cached,
):
    grid = Grid()
    owners = grid.size
    slot_count = page_table.shape[1]
    per_query = w_query.shape[1]
    per_key = w_key.shape[1]
    row_width = per_query + -(-2 * per_key // HEAD) * HEAD
    requests = kv_owner.shape[0]
    rows_dev = requests // owners
    width = hidden_in.shape[1]
    all_slots = owners * slot_count

    moves_a = grid.moves(ORDER_A)
    order_b = [moves_a.index(move) for move in grid.moves(ORDER_B)]
    cut = width // 16 * 11
    xa, xb = norm(hidden_in, norm_gain, (cut, width - cut))

    def first(x):
        orders = (None, (-1, ORDER_A), (1, ORDER_A), (1, ORDER_B), ())
        places = placing(after(kv_owner, x), grid.sizes, slot_count, orders)
        pieces = [after(w_key, x).T, w_value.T]
        spare = row_width - per_query - 2 * per_key
        if spare:
            pieces.append(jnp.zeros((spare, width), w_key.dtype))
        return places, jnp.concatenate(pieces, axis=0)

    def second(x):
        return fetch((after(w_query, x), None), limit=44)[0]

    parts_a, parts_b, others, w_query = gather_rows(grid, xa, xb, first, second)
    (place, place_in, place_a, place_b, mine), w_kv_t = others
    plain = list(range(owners))
    total = project(0, parts_a, plain, w_query, w_kv_t, None, None, all_slots)
    total = project(cut, parts_b, order_b, w_query, w_kv_t, total, place_in, all_slots)
    outbound = total.reshape(owners, slot_count, row_width)
    place = after(place, outbound).reshape(requests)
    mine = mine[0, :slot_count]
    lengths = jnp.sum(jnp.where(place[:, None] == mine[None, :], cached[:, None], 0), axis=0)
    halfway = HEAD // 2
    offsets = jnp.arange(halfway, dtype=jnp.float32)
    frequency = rope_base ** (-(2.0 * offsets) / HEAD)
    angles = lengths.astype(jnp.float32)[:, None] * frequency
    cosine_part = jnp.cos(angles)
    sine_part = jnp.sin(angles)
    cosine = jnp.concatenate([cosine_part, cosine_part], axis=1)
    sine = jnp.concatenate([-sine_part, sine_part], axis=1)
    inbound = lax.all_to_all(outbound, AXES, split_axis=0, concat_axis=0, tiled=True)
    attended = attend(
        inbound,
        lengths,
        after(page_table, outbound)[0],
        cosine,
        sine,
        key_pages[0],
        value_pages[0],
        per_query,
        per_key,
    )
    (w_front,) = fetch((after(w_out, attended), (0, width // 32 * 10)), limit=48)
    returned = lax.all_to_all(attended, AXES, split_axis=0, concat_axis=0, tiled=True)
    returned = returned.reshape(all_slots, per_query)
    summed = scatter_sum(grid, place_a, place_b, returned, w_out, w_front, width // 32 * 21)
    return narrow(wide(hidden_in) + summed)


def solution(mesh):
    placed = (
        P(("groups", "tp", "attn"), None),
        P(),
        P(None, ("tp", "attn")),
        P(None, ("tp", "attn")),
        P(None, ("tp", "attn")),
        P(("tp", "attn"), None),
        P(("groups", "tp", "attn"), None, None, None),
        P(("groups", "tp", "attn"), None, None, None),
        P(("groups", "tp", "attn"), None, None),
        P("groups"),
        P("groups"),
    )
    return jax.shard_map(
        on_device,
        mesh=mesh,
        in_specs=placed,
        out_specs=P(("groups", "tp", "attn"), None),
        check_vma=False,
    )
```

```python
import functools

import jax
import jax.numpy as jnp
import numpy as np
from jax import lax
from jax.experimental import pallas as pl
from jax.experimental.pallas import tpu as pltpu
from jax.sharding import PartitionSpec as P

HEAD = 128
AXES = ("tp", "attn")

epsilon = 1e-05
rope_base = 500000.0


class Grid:
    def __init__(self):
        self.half = lax.axis_size("tp") // 4
        self.sizes = (self.half, 2, 2, lax.axis_size("attn"))
        self.size = int(np.prod(self.sizes))

    def shifted(self, place, moves):
        return np.ravel_multi_index(
            tuple((p + m) % n for p, m, n in zip(place, moves, self.sizes)), self.sizes
        )

    def send(self, x, half=0, pair=0, near=0, core=0):
        pairs = [
            (i, int(self.shifted(np.unravel_index(i, self.sizes), (half, pair, near, core))))
            for i in range(self.size)
        ]
        return lax.ppermute(x, AXES, pairs)

    def moves(self, order):
        counts = [self.sizes[axis] for axis in order]
        places = []
        for steps in np.ndindex(*counts):
            move = [0, 0, 0, 0]
            for axis, step in zip(order, steps):
                move[axis] = step
            places.append(tuple(move))
        return places


HALF, PAIR, NEAR, CORE = range(4)
ORDER_A = (CORE, NEAR, PAIR, HALF)
ORDER_B = (CORE, PAIR, HALF, NEAR)


def after(x, *earlier):
    return lax.optimization_barrier((x, *earlier))[0]


def gather_rows(grid, xa, xb, first, second):
    beside_b = grid.send(xb, near=1)
    line_a = jnp.concatenate(
        [xa]
        + [
            grid.send(xa, half=half, pair=pair)
            for pair in range(2)
            for half in range(grid.half)
            if half or pair
        ],
        axis=0,
    )
    pair_b = jnp.concatenate([xb, beside_b], axis=0)
    line_a, pair_b, first = lax.optimization_barrier((line_a, pair_b, first(xa)))
    beside_a = grid.send(line_a, near=1)
    parts_b = [pair_b] + [
        grid.send(pair_b, half=half, pair=pair)
        for pair in range(2)
        for half in range(grid.half)
        if half or pair
    ]
    beside_a, parts_b, second = lax.optimization_barrier((beside_a, parts_b, second(pair_b)))
    parts_a = [line_a, beside_a]
    parts_a += [grid.send(part, core=1) for part in parts_a]
    parts_b += [grid.send(part, core=1) for part in parts_b]
    return parts_a, parts_b, first, second


def narrow(x):
    return x.astype(jnp.bfloat16)


def wide(x):
    return x.astype(jnp.float32)


def product_kernel(
    cuts,
    place_a,
    place_b,
    returned,
    w_out,
    w_front,
    away_a,
    keep_a,
    away_b,
    keep_b,
    held,
    sems,
):
    front = w_front.shape[1]
    copies = []
    for i, (start, stop) in enumerate(cuts):
        copy = None
        if start >= front:
            size = pl.ds(start, stop - start), pl.ds(start - front, stop - start)
            copy = pltpu.make_async_copy(
                w_out.at[:, size[0]], held.at[:, size[1]], sems.at[i]
            )
            copy.start()
        copies.append(copy)
    slots = lax.broadcasted_iota(jnp.int32, (returned.shape[0], place_a.shape[1]), 0)

    def picked(place):
        route = jnp.where(slots == place[...], 1.0, 0.0).astype(jnp.bfloat16)
        rows = lax.dot_general(
            route, returned[...], (((0,), (0,)), ((), ())), preferred_element_type=jnp.float32
        )
        return rows.astype(jnp.bfloat16)

    rows_a, rows_b = picked(place_a), picked(place_b)
    half = keep_a.shape[0]
    middle = keep_a.shape[1]
    for copy, (start, stop) in zip(copies, cuts):
        if copy is not None:
            copy.wait()
        rows, away, keep = (rows_a, away_a, keep_a) if start < middle else (rows_b, away_b, keep_b)
        w = w_front[:, start:stop] if copy is None else held[:, start - front : stop - front]
        x = jnp.dot(rows, w, preferred_element_type=jnp.float32)
        begin = start if start < middle else start - middle
        here = slice(begin, begin + stop - start)
        keep[:, here] = x[:half]
        away[:, here] = x[half:].astype(jnp.bfloat16)


def product(place_a, place_b, returned, w_out, w_front, cut):
    rows = place_a.shape[1]
    depth, width = w_out.shape
    cuts = []
    front = w_front.shape[1]
    for start, stop in ((0, front), (front, cut), (cut, width)):
        while start < stop:
            cuts.append((start, min(start + 1024, stop)))
            start = cuts[-1][1]
    vmem = pl.BlockSpec(memory_space=pltpu.VMEM)
    out = []
    for size in (cut, width - cut):
        out.append(jax.ShapeDtypeStruct((rows // 2, size), jnp.bfloat16))
        out.append(jax.ShapeDtypeStruct((rows // 2, size), jnp.float32))
    return pl.pallas_call(
        functools.partial(product_kernel, tuple(cuts)),
        in_specs=[vmem, vmem, vmem, pl.BlockSpec(memory_space=pl.ANY), vmem],
        out_specs=[vmem] * 4,
        out_shape=out,
        scratch_shapes=[
            pltpu.VMEM((depth, width - front), jnp.bfloat16),
            pltpu.SemaphoreType.DMA((len(cuts),)),
        ],
        compiler_params=pltpu.CompilerParams(vmem_limit_bytes=48 * 2**20),
        cost_estimate=pl.CostEstimate(
            flops=2 * rows * depth * width, bytes_accessed=2 * depth * width, transcendentals=0
        ),
        name="product",
    )(place_a, place_b, returned, w_out, w_front)


def scatter_sum(grid, place_a, place_b, returned, w_out, w_front, cut):
    def pieces(x):
        size = x.shape[0] // 2 // grid.half
        return x[:size], [narrow(x[i * size : (i + 1) * size]) for i in range(1, 2 * grid.half)]

    def direct(sent):
        return [
            grid.send(x, half=i % grid.half, pair=i // grid.half)
            for i, x in enumerate(sent, start=1)
        ]

    def total(x, parts):
        for part in parts:
            x = x + wide(part)
        return x

    away_a, keep_a, away_b, keep_b = product(place_a, place_b, returned, w_out, w_front, cut)
    xa = keep_a + wide(grid.send(away_a, core=1))
    middle = xa.shape[0] // 2
    sent_a = narrow(xa[middle:])
    got_a = grid.send(sent_a, near=1)
    xb = keep_b + wide(grid.send(after(away_b, sent_a), core=1))
    xb, sent = pieces(xb)
    got_b = direct(sent)
    got_a, got_b[0] = lax.optimization_barrier((got_a, got_b[0]))
    xa, sent = pieces(xa[:middle] + wide(got_a))
    parts_a = direct(sent)
    xb = total(xb, got_b)
    middle = xb.shape[0] // 2
    sent_b = after(narrow(xb[middle:]), *sent)
    xa = total(xa, parts_a)
    xb = xb[:middle] + wide(after(grid.send(sent_b, near=1), xa))
    return jnp.concatenate([xa, xb], axis=1)


def norm_kernel(x, gain, *refs):
    outs, (rows, gains, sems) = refs[:-3], refs[-3:]
    copies = [
        pltpu.make_async_copy(x, rows, sems.at[0]),
        pltpu.make_async_copy(gain, gains, sems.at[1]),
    ]
    for copy in copies:
        copy.start()
    copies[0].wait()
    inputs = rows[...].astype(jnp.float32)
    factor = lax.rsqrt(jnp.mean(inputs * inputs, axis=1, keepdims=True) + epsilon)
    copies[1].wait()
    normed = (inputs * factor * gains[...]).astype(jnp.bfloat16)
    start = 0
    for out in outs:
        out[...] = normed[:, start : start + out.shape[1]]
        start += out.shape[1]


def norm(x, gain, widths):
    vmem = pl.BlockSpec(memory_space=pltpu.VMEM)
    hbm = pl.BlockSpec(memory_space=pl.ANY)
    return pl.pallas_call(
        norm_kernel,
        in_specs=[hbm, hbm],
        out_specs=[vmem] * len(widths),
        out_shape=[jax.ShapeDtypeStruct((x.shape[0], w), jnp.bfloat16) for w in widths],
        scratch_shapes=[
            pltpu.VMEM(x.shape, jnp.bfloat16),
            pltpu.VMEM((1, x.shape[1]), jnp.float32),
            pltpu.SemaphoreType.DMA((2,)),
        ],
        compiler_params=pltpu.CompilerParams(vmem_limit_bytes=60 * 2**20),
        name="norm",
    )(x, gain.reshape(1, -1))


def placing_kernel(sizes, slots, orders, kv_owner, *outs):
    requests = kv_owner.shape[1]
    row = lax.broadcasted_iota(jnp.int32, (requests, requests), 0)
    column = lax.broadcasted_iota(jnp.int32, (requests, requests), 1)

    def upright(x):
        return jnp.sum(jnp.where(row == column, x, 0.0), axis=1, keepdims=True)

    owner = kv_owner[...].astype(jnp.float32)
    earlier = (upright(owner) == owner) & (row < column)
    slot = jnp.sum(jnp.where(earlier, 1.0, 0.0), axis=0, keepdims=True)
    place = owner * slots + slot
    upright_place = upright(place)

    tp = lax.axis_index("tp")
    me = (lax.div(tp, 4), lax.rem(lax.div(tp, 2), 2), lax.rem(tp, 2), lax.axis_index("attn"))
    rows_dev = requests // int(np.prod(sizes))
    lane = lax.broadcasted_iota(jnp.int32, (1, requests), 1)
    for order, out in zip(orders, outs):
        if order is None:
            out[...] = place.astype(jnp.int32)
            continue
        if not order:
            out[...] = (tp * sizes[CORE] + me[CORE]) * slots + lane
            continue
        sign, axes = order
        rest = lax.div(lane, rows_dev)
        where = [None] * len(sizes)
        for axis in reversed(axes):
            move = lax.rem(rest, sizes[axis])
            rest = lax.div(rest, sizes[axis])
            where[axis] = lax.rem(me[axis] + sizes[axis] + sign * move, sizes[axis])
        block = where[0]
        for axis in range(1, len(sizes)):
            block = block * sizes[axis] + where[axis]
        source = block * rows_dev + lax.rem(lane, rows_dev)
        moved = jnp.sum(jnp.where(row == source, upright_place, 0.0), axis=0, keepdims=True)
        out[...] = moved.astype(jnp.int32)


def placing(kv_owner, sizes, slots, orders):
    requests = kv_owner.shape[0]
    vmem = pl.BlockSpec(memory_space=pltpu.VMEM)
    return pl.pallas_call(
        functools.partial(placing_kernel, sizes, slots, orders),
        in_specs=[vmem],
        out_specs=[vmem] * len(orders),
        out_shape=[jax.ShapeDtypeStruct((1, requests), jnp.int32)] * len(orders),
        compiler_params=pltpu.CompilerParams(vmem_limit_bytes=16 * 2**20),
        name="placing",
    )(kv_owner.reshape(1, requests))


def fetch_kernel(starts, *refs):
    count = len(starts)
    sems = refs[-1]
    copies = []
    for i, start in enumerate(starts):
        source, target = refs[i], refs[count + i]
        if start is not None:
            columns = pl.ds(start, target.shape[-1])
            source = source.at[(slice(None),) * (len(target.shape) - 1) + (columns,)]
        copies.append(pltpu.make_async_copy(source, target, sems.at[i]))
        copies[-1].start()
    for copy in copies:
        copy.wait()


def fetch(*wanted, limit):
    arrays = [x for x, _ in wanted]
    starts = [columns and columns[0] for _, columns in wanted]
    out = [
        jax.ShapeDtypeStruct(x.shape[:-1] + (columns[1],) if columns else x.shape, x.dtype)
        for x, columns in wanted
    ]
    return pl.pallas_call(
        functools.partial(fetch_kernel, starts),
        in_specs=[pl.BlockSpec(memory_space=pl.ANY)] * len(arrays),
        out_specs=[pl.BlockSpec(memory_space=pltpu.VMEM)] * len(arrays),
        out_shape=out,
        scratch_shapes=[pltpu.SemaphoreType.DMA((len(arrays),))],
        compiler_params=pltpu.CompilerParams(vmem_limit_bytes=limit * 2**20),
        cost_estimate=pl.CostEstimate(
            flops=0, bytes_accessed=sum(x.size * 4 for x in out), transcendentals=0
        ),
        name="fetch",
    )(*arrays)


def project_kernel(first, last, order, start, block, *refs):
    count = len(refs) - 4 - (not first) - last
    parts, (wq, w_kv), refs = refs[:count], refs[count : count + 2], refs[count + 2 :]
    if not first:
        before, refs = refs[0], refs[1:]
    if last:
        place, refs = refs[0], refs[1:]
    out, total = refs
    step = pl.program_id(0)
    per_query = wq.shape[1]

    @pl.when(step == 0)
    def _():
        total[...] = jnp.zeros_like(total) if first else before[...]

    here = pl.ds(pl.multiple_of(step * block, block), block)
    there = pl.ds(pl.multiple_of(start + step * block, block), block)
    x = jnp.concatenate([part[:, here] for part in parts], axis=0)
    products = [
        jnp.dot(x, wq[there, :], preferred_element_type=jnp.float32),
        lax.dot_general(x, w_kv[:, there], (((1,), (1,)), ((), ())), preferred_element_type=jnp.float32),
    ]
    size = x.shape[0] // len(order)
    for product, columns in zip(products, (slice(0, per_query), slice(per_query, None))):
        for i, place_i in enumerate(order):
            total[place_i * size : (place_i + 1) * size, columns] += product[
                i * size : (i + 1) * size
            ]

    @pl.when(step == pl.num_programs(0) - 1)
    def _():
        if last:
            rows = lax.broadcasted_iota(jnp.int32, (out.shape[0], place.shape[1]), 0)
            route = jnp.where(rows == place[...], 1.0, 0.0).astype(jnp.bfloat16)
            moved = jnp.dot(
                route, total[...].astype(jnp.bfloat16), preferred_element_type=jnp.float32
            )
            out[...] = moved.astype(jnp.bfloat16)
        else:
            out[...] = total[...]


def project(start, parts, order, w_query, w_kv_t, before, place, slots):
    row_width = w_query.shape[1] + w_kv_t.shape[0]
    width = parts[0].shape[1]
    block = width
    rows = sum(part.shape[0] for part in parts)
    first, last = before is None, place is not None
    vmem = pl.BlockSpec(memory_space=pltpu.VMEM)
    args = [*parts, w_query, w_kv_t]
    specs = [vmem] * len(parts)
    specs += [
        vmem,
        vmem,
    ]
    if not first:
        args.append(before)
        specs.append(vmem)
    if last:
        args.append(place)
        specs.append(vmem)
        out = jax.ShapeDtypeStruct((slots, row_width), jnp.bfloat16)
    else:
        out = jax.ShapeDtypeStruct((rows, row_width), jnp.float32)
    return pl.pallas_call(
        functools.partial(project_kernel, first, last, order, start, block),
        grid=(width // block,),
        in_specs=specs,
        out_specs=vmem,
        out_shape=out,
        scratch_shapes=[pltpu.VMEM((rows, row_width), jnp.float32)],
        compiler_params=pltpu.CompilerParams(vmem_limit_bytes=24 * 2**20),
        cost_estimate=pl.CostEstimate(
            flops=2 * rows * width * row_width,
            bytes_accessed=2 * width * row_width,
            transcendentals=0,
        ),
        name="project",
    )(*args)


def attend_kernel(
    per_query,
    per_key,
    table,
    lengths,
    inbound,
    cosine,
    sine,
    key_pages,
    value_pages,
    out,
    key_pool,
    value_pool,
    sems,
    key_new,
    query_tile,
    query_rot,
    value_own,
    chance,
    mixed,
):
    owners, slots, _ = inbound.shape
    pages = table.shape[1]
    page, kv_width = key_pages.shape[1:]
    kv_heads = kv_width // HEAD
    heads_dev = per_query // HEAD
    heads = owners * heads_dev
    pair = 2 * heads // kv_heads
    pairs = kv_heads // 2
    span = pages * page
    pieces = owners // kv_heads
    batches = query_rot.shape[1]
    batch = slots // batches

    cuts = 16
    size = key_pages.shape[0] // cuts

    def fetch_pool(pool, on_chip, sem):
        for cut in range(cuts):
            part = pl.ds(cut * size, size)
            pltpu.make_async_copy(pool.at[part], on_chip.at[part], sem).start()

    fetch_pool(key_pages, key_pool, sems.at[0])
    fetch_pool(value_pages, value_pool, sems.at[1])

    def held(pool, slot, columns):
        return [pool[table[slot, j], :, columns] for j in range(pages)]

    cos = cosine[...]
    sin = sine[...]

    def turn(x):
        return (x * cos + pltpu.roll(x, HEAD // 2, 1) * sin).astype(jnp.bfloat16)

    for source in range(owners):
        for j in range(heads_dev):
            x = inbound[source, :, j * HEAD : (j + 1) * HEAD].astype(jnp.float32)
            x = turn(x).astype(jnp.float32)
            head = source * heads_dev + j
            for b in range(batches):
                rows = pl.ds(head % pair * batch, batch)
                query_rot[head // pair, b, rows] = x[b * batch : (b + 1) * batch]

    piece = lax.broadcasted_iota(jnp.int32, (slots, HEAD), 1) // per_key
    for g in range(kv_heads):
        key = jnp.zeros((slots, HEAD), jnp.float32)
        value = jnp.zeros((slots, HEAD), jnp.float32)
        for j in range(pieces):
            tile = inbound[g * pieces + j, :, per_query : per_query + HEAD].astype(jnp.float32)
            shift = j * per_key
            back = (shift - per_key) % HEAD
            key = jnp.where(piece == j, pltpu.roll(tile, shift, 1) if shift else tile, key)
            value = jnp.where(piece == j, pltpu.roll(tile, back, 1) if back else tile, value)
        key_new[:, g * HEAD : (g + 1) * HEAD] = turn(key)
        value_own[g] = value

    scale = HEAD ** (-0.5)
    columns = pair * batch
    row = lax.broadcasted_iota(jnp.int32, (span, columns), 0)
    place = lax.broadcasted_iota(jnp.int32, (span, columns), 1) % batch
    own_row = lax.broadcasted_iota(jnp.int32, (slots, columns), 0)
    own_place = lax.broadcasted_iota(jnp.int32, (slots, columns), 1) % batch
    first = lax.broadcasted_iota(jnp.int32, (HEAD, columns), 1) < columns // 2
    same = lax.broadcasted_iota(jnp.int32, (columns, columns), 0) == lax.broadcasted_iota(
        jnp.int32, (columns, columns), 1
    )

    own_chances = {}
    for p in range(pairs):
        for b in range(batches):
            turned = query_rot[p, b].T.astype(jnp.bfloat16)
            none = jnp.zeros_like(turned)
            query_tile[p, b, :HEAD] = jnp.where(first, turned, none)
            query_tile[p, b, HEAD:] = jnp.where(first, none, turned)

    pltpu.make_async_copy(key_pool, key_pool, sems.at[0]).wait()
    for p in range(pairs):
        columns_p = slice(p * 2 * HEAD, (p + 1) * 2 * HEAD)
        for b in range(batches):
            valid = row < lengths[b]
            keys = []
            for s in range(batch):
                keys += held(key_pool, b * batch + s, columns_p)
            keys.append(key_new[:, columns_p])
            products = jnp.dot(
                jnp.concatenate(keys, axis=0),
                query_tile[p, b],
                preferred_element_type=jnp.float32,
            )
            scores = products[:span]
            for s in range(1, batch):
                scores = jnp.where(place == s, products[s * span : (s + 1) * span], scores)
            own = jnp.where(own_row == own_place + b * batch, products[batch * span :], 0.0)
            own = jnp.sum(own, axis=0, keepdims=True) * scale
            masked = jnp.where(valid, scores * scale, -1e30)
            top = jnp.maximum(jnp.max(masked, axis=0, keepdims=True), own)
            terms = jnp.where(valid, jnp.exp(masked - top), 0.0)
            own_term = jnp.exp(own - top)
            total = jnp.sum(terms, axis=0, keepdims=True) + own_term
            chance[p, b] = (terms / total).T.astype(jnp.bfloat16).astype(jnp.float32)
            own_chance = (own_term / total).astype(jnp.bfloat16).astype(jnp.float32)
            own_chances[p, b] = jnp.sum(
                jnp.where(same, own_chance, 0.0), axis=1, keepdims=True
            )

    pltpu.make_async_copy(value_pool, value_pool, sems.at[1]).wait()
    for p in range(pairs):
        columns_p = slice(p * 2 * HEAD, (p + 1) * 2 * HEAD)
        for b in range(batches):
            for s in range(batch):
                mine = chance[p, b, pl.ds(s, pair, stride=batch)].astype(jnp.bfloat16)
                values = held(value_pool, b * batch + s, columns_p)
                both = jnp.dot(
                    mine, jnp.concatenate(values, axis=0), preferred_element_type=jnp.float32
                )
                result = jnp.concatenate(
                    [both[: pair // 2, :HEAD], both[pair // 2 :, HEAD:]], axis=0
                )
                mixed[p, b, pl.ds(s, pair, stride=batch)] = result
        for j in range(pair):
            head = p * pair + j
            g = head * kv_heads // heads
            halves = []
            for b in range(batches):
                rows = slice(j * batch, (j + 1) * batch)
                own_value = value_own[g, b * batch : (b + 1) * batch]
                halves.append(mixed[p, b, rows] + own_chances[p, b][rows] * own_value)
            column = head % heads_dev * HEAD
            out[head // heads_dev, :, column : column + HEAD] = jnp.concatenate(
                halves, axis=0
            ).astype(jnp.bfloat16)


def attend(inbound, lengths, table, cosine, sine, key_pages, value_pages, per_query, per_key):
    owners, slots, _ = inbound.shape
    pages = table.shape[1]
    page, kv_width = key_pages.shape[1:]
    kv_heads = kv_width // HEAD
    heads = owners * (per_query // HEAD)
    span = pages * page
    pair = 2 * heads // kv_heads
    pairs = kv_heads // 2
    batches = slots * pair // HEAD
    batch = slots // batches
    columns = pair * batch
    lengths = jnp.tile(lengths.reshape(batches, 1, batch), (1, 1, pair))
    smem = pl.BlockSpec(memory_space=pltpu.SMEM)
    vmem = pl.BlockSpec(memory_space=pltpu.VMEM)
    hbm = pl.BlockSpec(memory_space=pl.ANY)
    return pl.pallas_call(
        functools.partial(attend_kernel, per_query, per_key),
        in_specs=[smem, vmem, vmem, vmem, vmem, hbm, hbm],
        out_specs=vmem,
        out_shape=jax.ShapeDtypeStruct((owners, slots, per_query), jnp.bfloat16),
        scratch_shapes=[
            pltpu.VMEM(key_pages.shape, jnp.bfloat16),
            pltpu.VMEM(value_pages.shape, jnp.bfloat16),
            pltpu.SemaphoreType.DMA((2,)),
            pltpu.VMEM((slots, kv_width), jnp.bfloat16),
            pltpu.VMEM((pairs, batches, 2 * HEAD, columns), jnp.bfloat16),
            pltpu.VMEM((pairs, batches, columns, HEAD), jnp.float32),
            pltpu.VMEM((kv_heads, slots, HEAD), jnp.float32),
            pltpu.VMEM((pairs, batches, columns, span), jnp.float32),
            pltpu.VMEM((pairs, batches, columns, HEAD), jnp.float32),
        ],
        compiler_params=pltpu.CompilerParams(vmem_limit_bytes=52 * 2**20),
        cost_estimate=pl.CostEstimate(
            flops=8 * slots * heads * span * HEAD,
            bytes_accessed=4 * slots * span * kv_width,
            transcendentals=slots * heads * span,
        ),
        name="attend",
    )(table, lengths, inbound, cosine, sine, key_pages, value_pages)


def on_device(
    hidden_in,
    norm_gain,
    w_query,
    w_key,
    w_value,
    w_out,
    key_pages,
    value_pages,
    page_table,
    kv_owner,
    cached,
):
    grid = Grid()
    owners = grid.size
    slot_count = page_table.shape[1]
    per_query = w_query.shape[1]
    per_key = w_key.shape[1]
    row_width = per_query + -(-2 * per_key // HEAD) * HEAD
    requests = kv_owner.shape[0]
    rows_dev = requests // owners
    width = hidden_in.shape[1]
    all_slots = owners * slot_count

    moves_a = grid.moves(ORDER_A)
    order_b = [moves_a.index(move) for move in grid.moves(ORDER_B)]
    cut = width // 16 * 11
    xa, xb = norm(hidden_in, norm_gain, (cut, width - cut))

    def first(x):
        orders = (None, (-1, ORDER_A), (1, ORDER_A), (1, ORDER_B), ())
        places = placing(after(kv_owner, x), grid.sizes, slot_count, orders)
        pieces = [after(w_key, x).T, w_value.T]
        spare = row_width - per_query - 2 * per_key
        if spare:
            pieces.append(jnp.zeros((spare, width), w_key.dtype))
        return places, jnp.concatenate(pieces, axis=0)

    def second(x):
        return fetch((after(w_query, x), None), limit=44)[0]

    parts_a, parts_b, others, w_query = gather_rows(grid, xa, xb, first, second)
    (place, place_in, place_a, place_b, mine), w_kv_t = others
    plain = list(range(owners))
    total = project(0, parts_a, plain, w_query, w_kv_t, None, None, all_slots)
    total = project(cut, parts_b, order_b, w_query, w_kv_t, total, place_in, all_slots)
    outbound = total.reshape(owners, slot_count, row_width)
    place = after(place, outbound).reshape(requests)
    mine = mine[0, :slot_count]
    lengths = jnp.sum(jnp.where(place[:, None] == mine[None, :], cached[:, None], 0), axis=0)
    halfway = HEAD // 2
    offsets = jnp.arange(halfway, dtype=jnp.float32)
    frequency = rope_base ** (-(2.0 * offsets) / HEAD)
    angles = lengths.astype(jnp.float32)[:, None] * frequency
    cosine_part = jnp.cos(angles)
    sine_part = jnp.sin(angles)
    cosine = jnp.concatenate([cosine_part, cosine_part], axis=1)
    sine = jnp.concatenate([-sine_part, sine_part], axis=1)
    inbound = lax.all_to_all(outbound, AXES, split_axis=0, concat_axis=0, tiled=True)
    attended = attend(
        inbound,
        lengths,
        after(page_table, outbound)[0],
        cosine,
        sine,
        key_pages[0],
        value_pages[0],
        per_query,
        per_key,
    )
    (w_front,) = fetch((after(w_out, attended), (0, width // 32 * 10)), limit=48)
    returned = lax.all_to_all(attended, AXES, split_axis=0, concat_axis=0, tiled=True)
    returned = returned.reshape(all_slots, per_query)
    summed = scatter_sum(grid, place_a, place_b, returned, w_out, w_front, width // 32 * 21)
    return narrow(wide(hidden_in) + summed)


def solution(mesh):
    placed = (
        P(("groups", "tp", "attn"), None),
        P(),
        P(None, ("tp", "attn")),
        P(None, ("tp", "attn")),
        P(None, ("tp", "attn")),
        P(("tp", "attn"), None),
        P(("groups", "tp", "attn"), None, None, None),
        P(("groups", "tp", "attn"), None, None, None),
        P(("groups", "tp", "attn"), None, None),
        P("groups"),
        P("groups"),
    )
    return jax.shard_map(
        on_device,
        mesh=mesh,
        in_specs=placed,
        out_specs=P(("groups", "tp", "attn"), None),
        check_vma=False,
    )
```

```python
import functools

import jax
import jax.numpy as jnp
import numpy as np
from jax import lax
from jax.experimental import pallas as pl
from jax.experimental.pallas import tpu as pltpu
from jax.sharding import PartitionSpec as P

HEAD = 128
AXES = ("tp", "attn")

epsilon = 1e-05
rope_base = 500000.0


class Grid:
    def __init__(self):
        self.half = lax.axis_size("tp") // 4
        self.sizes = (self.half, 2, 2, lax.axis_size("attn"))
        self.size = int(np.prod(self.sizes))

    def shifted(self, place, moves):
        return np.ravel_multi_index(
            tuple((p + m) % n for p, m, n in zip(place, moves, self.sizes)), self.sizes
        )

    def send(self, x, half=0, pair=0, near=0, core=0):
        pairs = [
            (i, int(self.shifted(np.unravel_index(i, self.sizes), (half, pair, near, core))))
            for i in range(self.size)
        ]
        return lax.ppermute(x, AXES, pairs)

    def moves(self, order):
        counts = [self.sizes[axis] for axis in order]
        places = []
        for steps in np.ndindex(*counts):
            move = [0, 0, 0, 0]
            for axis, step in zip(order, steps):
                move[axis] = step
            places.append(tuple(move))
        return places


HALF, PAIR, NEAR, CORE = range(4)
ORDER_A = (CORE, NEAR, PAIR, HALF)
ORDER_B = (CORE, PAIR, HALF, NEAR)


def after(x, *earlier):
    return lax.optimization_barrier((x, *earlier))[0]


def gather_rows(grid, xa, xb, first, second):
    beside_b = grid.send(xb, near=1)
    line_a = jnp.concatenate(
        [xa]
        + [
            grid.send(xa, half=half, pair=pair)
            for pair in range(2)
            for half in range(grid.half)
            if half or pair
        ],
        axis=0,
    )
    pair_b = jnp.concatenate([xb, beside_b], axis=0)
    line_a, pair_b, first = lax.optimization_barrier((line_a, pair_b, first(xa)))
    beside_a = grid.send(line_a, near=1)
    parts_b = [pair_b] + [
        grid.send(pair_b, half=half, pair=pair)
        for pair in range(2)
        for half in range(grid.half)
        if half or pair
    ]
    beside_a, parts_b, second = lax.optimization_barrier((beside_a, parts_b, second(pair_b)))
    parts_a = [line_a, beside_a]
    parts_a += [grid.send(part, core=1) for part in parts_a]
    parts_b += [grid.send(part, core=1) for part in parts_b]
    return parts_a, parts_b, first, second


def narrow(x):
    return x.astype(jnp.bfloat16)


def wide(x):
    return x.astype(jnp.float32)


def product_kernel(
    cuts,
    place_a,
    place_b,
    returned,
    w_out,
    w_front,
    away_a,
    keep_a,
    away_b,
    keep_b,
    held,
    sems,
):
    front = w_front.shape[1]
    copies = []
    for i, (start, stop) in enumerate(cuts):
        copy = None
        if start >= front:
            size = pl.ds(start, stop - start), pl.ds(start - front, stop - start)
            copy = pltpu.make_async_copy(
                w_out.at[:, size[0]], held.at[:, size[1]], sems.at[i]
            )
            copy.start()
        copies.append(copy)
    slots = lax.broadcasted_iota(jnp.int32, (returned.shape[0], place_a.shape[1]), 0)

    def picked(place):
        route = jnp.where(slots == place[...], 1.0, 0.0).astype(jnp.bfloat16)
        rows = lax.dot_general(
            route, returned[...], (((0,), (0,)), ((), ())), preferred_element_type=jnp.float32
        )
        return rows.astype(jnp.bfloat16)

    rows_a, rows_b = picked(place_a), picked(place_b)
    half = keep_a.shape[0]
    middle = keep_a.shape[1]
    for copy, (start, stop) in zip(copies, cuts):
        if copy is not None:
            copy.wait()
        rows, away, keep = (rows_a, away_a, keep_a) if start < middle else (rows_b, away_b, keep_b)
        w = w_front[:, start:stop] if copy is None else held[:, start - front : stop - front]
        x = jnp.dot(rows, w, preferred_element_type=jnp.float32)
        begin = start if start < middle else start - middle
        here = slice(begin, begin + stop - start)
        keep[:, here] = x[:half]
        away[:, here] = x[half:].astype(jnp.bfloat16)


def product(place_a, place_b, returned, w_out, w_front, cut):
    rows = place_a.shape[1]
    depth, width = w_out.shape
    cuts = []
    front = w_front.shape[1]
    for start, stop in ((0, front), (front, cut), (cut, width)):
        while start < stop:
            cuts.append((start, min(start + 1024, stop)))
            start = cuts[-1][1]
    vmem = pl.BlockSpec(memory_space=pltpu.VMEM)
    out = []
    for size in (cut, width - cut):
        out.append(jax.ShapeDtypeStruct((rows // 2, size), jnp.bfloat16))
        out.append(jax.ShapeDtypeStruct((rows // 2, size), jnp.float32))
    return pl.pallas_call(
        functools.partial(product_kernel, tuple(cuts)),
        in_specs=[vmem, vmem, vmem, pl.BlockSpec(memory_space=pl.ANY), vmem],
        out_specs=[vmem] * 4,
        out_shape=out,
        scratch_shapes=[
            pltpu.VMEM((depth, width - front), jnp.bfloat16),
            pltpu.SemaphoreType.DMA((len(cuts),)),
        ],
        compiler_params=pltpu.CompilerParams(vmem_limit_bytes=48 * 2**20),
        cost_estimate=pl.CostEstimate(
            flops=2 * rows * depth * width, bytes_accessed=2 * depth * width, transcendentals=0
        ),
        name="product",
    )(place_a, place_b, returned, w_out, w_front)


def scatter_sum(grid, place_a, place_b, returned, w_out, w_front, cut):
    def pieces(x):
        size = x.shape[0] // 2 // grid.half
        return x[:size], [narrow(x[i * size : (i + 1) * size]) for i in range(1, 2 * grid.half)]

    def direct(sent):
        return [
            grid.send(x, half=i % grid.half, pair=i // grid.half)
            for i, x in enumerate(sent, start=1)
        ]

    def total(x, parts):
        for part in parts:
            x = x + wide(part)
        return x

    away_a, keep_a, away_b, keep_b = product(place_a, place_b, returned, w_out, w_front, cut)
    xa = keep_a + wide(grid.send(away_a, core=1))
    middle = xa.shape[0] // 2
    sent_a = narrow(xa[middle:])
    got_a = grid.send(sent_a, near=1)
    xb = keep_b + wide(grid.send(after(away_b, sent_a), core=1))
    xb, sent = pieces(xb)
    got_b = direct(sent)
    got_a, got_b[0] = lax.optimization_barrier((got_a, got_b[0]))
    xa, sent = pieces(xa[:middle] + wide(got_a))
    parts_a = direct(sent)
    xb = total(xb, got_b)
    middle = xb.shape[0] // 2
    sent_b = after(narrow(xb[middle:]), *sent)
    xa = total(xa, parts_a)
    xb = xb[:middle] + wide(after(grid.send(sent_b, near=1), xa))
    return jnp.concatenate([xa, xb], axis=1)


def norm_kernel(x, gain, *refs):
    outs, (rows, gains, sems) = refs[:-3], refs[-3:]
    copies = [
        pltpu.make_async_copy(x, rows, sems.at[0]),
        pltpu.make_async_copy(gain, gains, sems.at[1]),
    ]
    for copy in copies:
        copy.start()
    copies[0].wait()
    inputs = rows[...].astype(jnp.float32)
    factor = lax.rsqrt(jnp.mean(inputs * inputs, axis=1, keepdims=True) + epsilon)
    copies[1].wait()
    normed = (inputs * factor * gains[...]).astype(jnp.bfloat16)
    start = 0
    for out in outs:
        out[...] = normed[:, start : start + out.shape[1]]
        start += out.shape[1]


def norm(x, gain, widths):
    vmem = pl.BlockSpec(memory_space=pltpu.VMEM)
    hbm = pl.BlockSpec(memory_space=pl.ANY)
    return pl.pallas_call(
        norm_kernel,
        in_specs=[hbm, hbm],
        out_specs=[vmem] * len(widths),
        out_shape=[jax.ShapeDtypeStruct((x.shape[0], w), jnp.bfloat16) for w in widths],
        scratch_shapes=[
            pltpu.VMEM(x.shape, jnp.bfloat16),
            pltpu.VMEM((1, x.shape[1]), jnp.float32),
            pltpu.SemaphoreType.DMA((2,)),
        ],
        compiler_params=pltpu.CompilerParams(vmem_limit_bytes=60 * 2**20),
        name="norm",
    )(x, gain.reshape(1, -1))


def placing_kernel(sizes, slots, orders, kv_owner, *outs):
    requests = kv_owner.shape[1]
    row = lax.broadcasted_iota(jnp.int32, (requests, requests), 0)
    column = lax.broadcasted_iota(jnp.int32, (requests, requests), 1)

    def upright(x):
        return jnp.sum(jnp.where(row == column, x, 0.0), axis=1, keepdims=True)

    owner = kv_owner[...].astype(jnp.float32)
    earlier = (upright(owner) == owner) & (row < column)
    slot = jnp.sum(jnp.where(earlier, 1.0, 0.0), axis=0, keepdims=True)
    place = owner * slots + slot
    upright_place = upright(place)

    tp = lax.axis_index("tp")
    me = (lax.div(tp, 4), lax.rem(lax.div(tp, 2), 2), lax.rem(tp, 2), lax.axis_index("attn"))
    rows_dev = requests // int(np.prod(sizes))
    lane = lax.broadcasted_iota(jnp.int32, (1, requests), 1)
    for order, out in zip(orders, outs):
        if order is None:
            out[...] = place.astype(jnp.int32)
            continue
        if not order:
            out[...] = (tp * sizes[CORE] + me[CORE]) * slots + lane
            continue
        sign, axes = order
        rest = lax.div(lane, rows_dev)
        where = [None] * len(sizes)
        for axis in reversed(axes):
            move = lax.rem(rest, sizes[axis])
            rest = lax.div(rest, sizes[axis])
            where[axis] = lax.rem(me[axis] + sizes[axis] + sign * move, sizes[axis])
        block = where[0]
        for axis in range(1, len(sizes)):
            block = block * sizes[axis] + where[axis]
        source = block * rows_dev + lax.rem(lane, rows_dev)
        moved = jnp.sum(jnp.where(row == source, upright_place, 0.0), axis=0, keepdims=True)
        out[...] = moved.astype(jnp.int32)


def placing(kv_owner, sizes, slots, orders):
    requests = kv_owner.shape[0]
    vmem = pl.BlockSpec(memory_space=pltpu.VMEM)
    return pl.pallas_call(
        functools.partial(placing_kernel, sizes, slots, orders),
        in_specs=[vmem],
        out_specs=[vmem] * len(orders),
        out_shape=[jax.ShapeDtypeStruct((1, requests), jnp.int32)] * len(orders),
        compiler_params=pltpu.CompilerParams(vmem_limit_bytes=16 * 2**20),
        name="placing",
    )(kv_owner.reshape(1, requests))


def fetch_kernel(starts, *refs):
    count = len(starts)
    sems = refs[-1]
    copies = []
    for i, start in enumerate(starts):
        source, target = refs[i], refs[count + i]
        if start is not None:
            columns = pl.ds(start, target.shape[-1])
            source = source.at[(slice(None),) * (len(target.shape) - 1) + (columns,)]
        copies.append(pltpu.make_async_copy(source, target, sems.at[i]))
        copies[-1].start()
    for copy in copies:
        copy.wait()


def fetch(*wanted, limit):
    arrays = [x for x, _ in wanted]
    starts = [columns and columns[0] for _, columns in wanted]
    out = [
        jax.ShapeDtypeStruct(x.shape[:-1] + (columns[1],) if columns else x.shape, x.dtype)
        for x, columns in wanted
    ]
    return pl.pallas_call(
        functools.partial(fetch_kernel, starts),
        in_specs=[pl.BlockSpec(memory_space=pl.ANY)] * len(arrays),
        out_specs=[pl.BlockSpec(memory_space=pltpu.VMEM)] * len(arrays),
        out_shape=out,
        scratch_shapes=[pltpu.SemaphoreType.DMA((len(arrays),))],
        compiler_params=pltpu.CompilerParams(vmem_limit_bytes=limit * 2**20),
        cost_estimate=pl.CostEstimate(
            flops=0, bytes_accessed=sum(x.size * 4 for x in out), transcendentals=0
        ),
        name="fetch",
    )(*arrays)


def project_kernel(first, last, order, start, block, *refs):
    count = len(refs) - 4 - (not first) - last
    parts, (wq, w_kv), refs = refs[:count], refs[count : count + 2], refs[count + 2 :]
    if not first:
        before, refs = refs[0], refs[1:]
    if last:
        place, refs = refs[0], refs[1:]
    out, total = refs
    step = pl.program_id(0)
    per_query = wq.shape[1]

    @pl.when(step == 0)
    def _():
        total[...] = jnp.zeros_like(total) if first else before[...]

    here = pl.ds(pl.multiple_of(step * block, block), block)
    there = pl.ds(pl.multiple_of(start + step * block, block), block)
    x = jnp.concatenate([part[:, here] for part in parts], axis=0)
    products = [
        jnp.dot(x, wq[there, :], preferred_element_type=jnp.float32),
        lax.dot_general(x, w_kv[:, there], (((1,), (1,)), ((), ())), preferred_element_type=jnp.float32),
    ]
    size = x.shape[0] // len(order)
    for product, columns in zip(products, (slice(0, per_query), slice(per_query, None))):
        for i, place_i in enumerate(order):
            total[place_i * size : (place_i + 1) * size, columns] += product[
                i * size : (i + 1) * size
            ]

    @pl.when(step == pl.num_programs(0) - 1)
    def _():
        if last:
            rows = lax.broadcasted_iota(jnp.int32, (out.shape[0], place.shape[1]), 0)
            route = jnp.where(rows == place[...], 1.0, 0.0).astype(jnp.bfloat16)
            moved = jnp.dot(
                route, total[...].astype(jnp.bfloat16), preferred_element_type=jnp.float32
            )
            out[...] = moved.astype(jnp.bfloat16)
        else:
            out[...] = total[...]


def project(start, parts, order, w_query, w_kv_t, before, place, slots):
    row_width = w_query.shape[1] + w_kv_t.shape[0]
    width = parts[0].shape[1]
    block = width
    rows = sum(part.shape[0] for part in parts)
    first, last = before is None, place is not None
    vmem = pl.BlockSpec(memory_space=pltpu.VMEM)
    args = [*parts, w_query, w_kv_t]
    specs = [vmem] * len(parts)
    specs += [
        vmem,
        vmem,
    ]
    if not first:
        args.append(before)
        specs.append(vmem)
    if last:
        args.append(place)
        specs.append(vmem)
        out = jax.ShapeDtypeStruct((slots, row_width), jnp.bfloat16)
    else:
        out = jax.ShapeDtypeStruct((rows, row_width), jnp.float32)
    return pl.pallas_call(
        functools.partial(project_kernel, first, last, order, start, block),
        grid=(width // block,),
        in_specs=specs,
        out_specs=vmem,
        out_shape=out,
        scratch_shapes=[pltpu.VMEM((rows, row_width), jnp.float32)],
        compiler_params=pltpu.CompilerParams(vmem_limit_bytes=24 * 2**20),
        cost_estimate=pl.CostEstimate(
            flops=2 * rows * width * row_width,
            bytes_accessed=2 * width * row_width,
            transcendentals=0,
        ),
        name="project",
    )(*args)


def attend_kernel(
    per_query,
    per_key,
    table,
    lengths,
    inbound,
    cosine,
    sine,
    key_pages,
    value_pages,
    out,
    key_pool,
    value_pool,
    sems,
    key_new,
    query_rot,
    value_own,
    chance,
    mixed,
):
    owners, slots, _ = inbound.shape
    pages = table.shape[1]
    page, kv_width = key_pages.shape[1:]
    kv_heads = kv_width // HEAD
    heads_dev = per_query // HEAD
    heads = owners * heads_dev
    pair = 2 * heads // kv_heads
    pairs = kv_heads // 2
    span = pages * page
    pieces = owners // kv_heads
    batches = query_rot.shape[1]
    batch = slots // batches

    cuts = 16
    size = key_pages.shape[0] // cuts

    def fetch_pool(pool, on_chip, sem):
        for cut in range(cuts):
            part = pl.ds(cut * size, size)
            pltpu.make_async_copy(pool.at[part], on_chip.at[part], sem).start()

    fetch_pool(key_pages, key_pool, sems.at[0])
    fetch_pool(value_pages, value_pool, sems.at[1])

    def held(pool, slot, columns):
        return [pool[table[slot, j], :, columns] for j in range(pages)]

    cos = cosine[...]
    sin = sine[...]

    def turn(x):
        return (x * cos + pltpu.roll(x, HEAD // 2, 1) * sin).astype(jnp.bfloat16)

    for source in range(owners):
        for j in range(heads_dev):
            x = inbound[source, :, j * HEAD : (j + 1) * HEAD].astype(jnp.float32)
            x = turn(x).astype(jnp.float32)
            head = source * heads_dev + j
            for b in range(batches):
                rows = pl.ds(head % pair * batch, batch)
                query_rot[head // pair, b, rows] = x[b * batch : (b + 1) * batch]

    piece = lax.broadcasted_iota(jnp.int32, (slots, HEAD), 1) // per_key
    for g in range(kv_heads):
        key = jnp.zeros((slots, HEAD), jnp.float32)
        value = jnp.zeros((slots, HEAD), jnp.float32)
        for j in range(pieces):
            tile = inbound[g * pieces + j, :, per_query : per_query + HEAD].astype(jnp.float32)
            shift = j * per_key
            back = (shift - per_key) % HEAD
            key = jnp.where(piece == j, pltpu.roll(tile, shift, 1) if shift else tile, key)
            value = jnp.where(piece == j, pltpu.roll(tile, back, 1) if back else tile, value)
        key_new[:, g * HEAD : (g + 1) * HEAD] = turn(key)
        value_own[g] = value

    scale = HEAD ** (-0.5)
    columns = pair * batch
    row = lax.broadcasted_iota(jnp.int32, (span, columns), 0)
    place = lax.broadcasted_iota(jnp.int32, (span, columns), 1) % batch
    own_row = lax.broadcasted_iota(jnp.int32, (slots, columns), 0)
    own_place = lax.broadcasted_iota(jnp.int32, (slots, columns), 1) % batch
    first = lax.broadcasted_iota(jnp.int32, (HEAD, columns), 1) < columns // 2
    same = lax.broadcasted_iota(jnp.int32, (columns, columns), 0) == lax.broadcasted_iota(
        jnp.int32, (columns, columns), 1
    )

    own_chances = {}
    pltpu.make_async_copy(key_pool, key_pool, sems.at[0]).wait()
    for p in range(pairs):
        columns_p = slice(p * 2 * HEAD, (p + 1) * 2 * HEAD)
        for b in range(batches):
            valid = row < lengths[b]
            turned = query_rot[p, b].T.astype(jnp.bfloat16)
            none = jnp.zeros_like(turned)
            wide = jnp.concatenate(
                [jnp.where(first, turned, none), jnp.where(first, none, turned)], axis=0
            )
            keys = []
            for s in range(batch):
                keys += held(key_pool, b * batch + s, columns_p)
            keys.append(key_new[:, columns_p])
            products = jnp.dot(
                jnp.concatenate(keys, axis=0), wide, preferred_element_type=jnp.float32
            )
            scores = products[:span]
            for s in range(1, batch):
                scores = jnp.where(place == s, products[s * span : (s + 1) * span], scores)
            own = jnp.where(own_row == own_place + b * batch, products[batch * span :], 0.0)
            own = jnp.sum(own, axis=0, keepdims=True) * scale
            masked = jnp.where(valid, scores * scale, -1e30)
            top = jnp.maximum(jnp.max(masked, axis=0, keepdims=True), own)
            terms = jnp.where(valid, jnp.exp(masked - top), 0.0)
            own_term = jnp.exp(own - top)
            total = jnp.sum(terms, axis=0, keepdims=True) + own_term
            chance[p, b] = (terms / total).T.astype(jnp.bfloat16).astype(jnp.float32)
            own_chance = (own_term / total).astype(jnp.bfloat16).astype(jnp.float32)
            own_chances[p, b] = jnp.sum(
                jnp.where(same, own_chance, 0.0), axis=1, keepdims=True
            )

    pltpu.make_async_copy(value_pool, value_pool, sems.at[1]).wait()
    for p in range(pairs):
        columns_p = slice(p * 2 * HEAD, (p + 1) * 2 * HEAD)
        for b in range(batches):
            for s in range(batch):
                mine = chance[p, b, pl.ds(s, pair, stride=batch)].astype(jnp.bfloat16)
                values = held(value_pool, b * batch + s, columns_p)
                both = jnp.dot(
                    mine, jnp.concatenate(values, axis=0), preferred_element_type=jnp.float32
                )
                result = jnp.concatenate(
                    [both[: pair // 2, :HEAD], both[pair // 2 :, HEAD:]], axis=0
                )
                mixed[p, b, pl.ds(s, pair, stride=batch)] = result
        for j in range(pair):
            head = p * pair + j
            g = head * kv_heads // heads
            halves = []
            for b in range(batches):
                rows = slice(j * batch, (j + 1) * batch)
                own_value = value_own[g, b * batch : (b + 1) * batch]
                halves.append(mixed[p, b, rows] + own_chances[p, b][rows] * own_value)
            column = head % heads_dev * HEAD
            out[head // heads_dev, :, column : column + HEAD] = jnp.concatenate(
                halves, axis=0
            ).astype(jnp.bfloat16)


def attend(inbound, lengths, table, cosine, sine, key_pages, value_pages, per_query, per_key):
    owners, slots, _ = inbound.shape
    pages = table.shape[1]
    page, kv_width = key_pages.shape[1:]
    kv_heads = kv_width // HEAD
    heads = owners * (per_query // HEAD)
    span = pages * page
    pair = 2 * heads // kv_heads
    pairs = kv_heads // 2
    batches = slots * pair // HEAD
    batch = slots // batches
    columns = pair * batch
    lengths = jnp.tile(lengths.reshape(batches, 1, batch), (1, 1, pair))
    smem = pl.BlockSpec(memory_space=pltpu.SMEM)
    vmem = pl.BlockSpec(memory_space=pltpu.VMEM)
    hbm = pl.BlockSpec(memory_space=pl.ANY)
    return pl.pallas_call(
        functools.partial(attend_kernel, per_query, per_key),
        in_specs=[smem, vmem, vmem, vmem, vmem, hbm, hbm],
        out_specs=vmem,
        out_shape=jax.ShapeDtypeStruct((owners, slots, per_query), jnp.bfloat16),
        scratch_shapes=[
            pltpu.VMEM(key_pages.shape, jnp.bfloat16),
            pltpu.VMEM(value_pages.shape, jnp.bfloat16),
            pltpu.SemaphoreType.DMA((2,)),
            pltpu.VMEM((slots, kv_width), jnp.bfloat16),
            pltpu.VMEM((pairs, batches, columns, HEAD), jnp.float32),
            pltpu.VMEM((kv_heads, slots, HEAD), jnp.float32),
            pltpu.VMEM((pairs, batches, columns, span), jnp.float32),
            pltpu.VMEM((pairs, batches, columns, HEAD), jnp.float32),
        ],
        compiler_params=pltpu.CompilerParams(vmem_limit_bytes=52 * 2**20),
        cost_estimate=pl.CostEstimate(
            flops=8 * slots * heads * span * HEAD,
            bytes_accessed=4 * slots * span * kv_width,
            transcendentals=slots * heads * span,
        ),
        name="attend",
    )(table, lengths, inbound, cosine, sine, key_pages, value_pages)


def on_device(
    hidden_in,
    norm_gain,
    w_query,
    w_key,
    w_value,
    w_out,
    key_pages,
    value_pages,
    page_table,
    kv_owner,
    cached,
):
    grid = Grid()
    owners = grid.size
    slot_count = page_table.shape[1]
    per_query = w_query.shape[1]
    per_key = w_key.shape[1]
    row_width = per_query + -(-2 * per_key // HEAD) * HEAD
    requests = kv_owner.shape[0]
    rows_dev = requests // owners
    width = hidden_in.shape[1]
    all_slots = owners * slot_count

    moves_a = grid.moves(ORDER_A)
    order_b = [moves_a.index(move) for move in grid.moves(ORDER_B)]
    cut = width // 16 * 11
    xa, xb = norm(hidden_in, norm_gain, (cut, width - cut))

    def first(x):
        orders = (None, (-1, ORDER_A), (1, ORDER_A), (1, ORDER_B), ())
        places = placing(after(kv_owner, x), grid.sizes, slot_count, orders)
        pieces = [after(w_key, x).T, w_value.T]
        spare = row_width - per_query - 2 * per_key
        if spare:
            pieces.append(jnp.zeros((spare, width), w_key.dtype))
        return places, jnp.concatenate(pieces, axis=0)

    def second(x):
        return fetch((after(w_query, x), None), limit=44)[0]

    parts_a, parts_b, others, w_query = gather_rows(grid, xa, xb, first, second)
    (place, place_in, place_a, place_b, mine), w_kv_t = others
    plain = list(range(owners))
    total = project(0, parts_a, plain, w_query, w_kv_t, None, None, all_slots)
    total = project(cut, parts_b, order_b, w_query, w_kv_t, total, place_in, all_slots)
    outbound = total.reshape(owners, slot_count, row_width)
    place = after(place, outbound).reshape(requests)
    mine = mine[0, :slot_count]
    lengths = jnp.sum(jnp.where(place[:, None] == mine[None, :], cached[:, None], 0), axis=0)
    halfway = HEAD // 2
    offsets = jnp.arange(halfway, dtype=jnp.float32)
    frequency = rope_base ** (-(2.0 * offsets) / HEAD)
    angles = lengths.astype(jnp.float32)[:, None] * frequency
    cosine_part = jnp.cos(angles)
    sine_part = jnp.sin(angles)
    cosine = jnp.concatenate([cosine_part, cosine_part], axis=1)
    sine = jnp.concatenate([-sine_part, sine_part], axis=1)
    inbound = lax.all_to_all(outbound, AXES, split_axis=0, concat_axis=0, tiled=True)
    attended = attend(
        inbound,
        lengths,
        after(page_table, outbound)[0],
        cosine,
        sine,
        key_pages[0],
        value_pages[0],
        per_query,
        per_key,
    )
    (w_front,) = fetch((after(w_out, attended), (0, width // 32 * 10)), limit=48)
    returned = lax.all_to_all(attended, AXES, split_axis=0, concat_axis=0, tiled=True)
    returned = returned.reshape(all_slots, per_query)
    summed = scatter_sum(grid, place_a, place_b, returned, w_out, w_front, width // 32 * 22)
    return narrow(wide(hidden_in) + summed)


def solution(mesh):
    placed = (
        P(("groups", "tp", "attn"), None),
        P(),
        P(None, ("tp", "attn")),
        P(None, ("tp", "attn")),
        P(None, ("tp", "attn")),
        P(("tp", "attn"), None),
        P(("groups", "tp", "attn"), None, None, None),
        P(("groups", "tp", "attn"), None, None, None),
        P(("groups", "tp", "attn"), None, None),
        P("groups"),
        P("groups"),
    )
    return jax.shard_map(
        on_device,
        mesh=mesh,
        in_specs=placed,
        out_specs=P(("groups", "tp", "attn"), None),
        check_vma=False,
    )
```
